32 devices in a mesh: dp: 4 (over y, core), ctx: 2 (over x), tensor: 4 (over z).
Axes of the slice: x: 2, y: 2, z: 4, core: 2. Of those that a mesh axis runs over, the one named last changes fastest.
Arguments:
- tokens: bfloat16 [16384, 2048], P(('dp', 'ctx')), may hold values from -6 to 6
- cotangent: bfloat16 [16384, 2048], P(('dp', 'ctx')), may hold values from -6 to 6
- span_order: int32 [4, 4], P('dp'), may hold values from 0 to 3, each once within a row
- norm_attn: float32 [2048], replicated, may hold values from 0.5 to 1.5
- w_query: bfloat16 [2048, 2048], P(None, 'tensor'), may hold values from -0.125 to 0.125
- w_key: bfloat16 [2048, 256], replicated, may hold values from -0.125 to 0.125
- w_value: bfloat16 [2048, 256], replicated, may hold values from -0.125 to 0.125
- w_output: bfloat16 [2048, 2048], P(None, 'tensor'), may hold values from -2 to 2
- norm_mlp: float32 [2048], replicated, may hold values from 0.5 to 1.5
- w_gate: bfloat16 [2048, 5632], P(None, 'tensor'), may hold values from -0.125 to 0.125
- w_up: bfloat16 [2048, 5632], P(None, 'tensor'), may hold values from -0.125 to 0.125
- w_down: bfloat16 [2048, 5632], P(None, 'tensor'), may hold values from -0.078125 to 0.078125
Outputs:
- mixed: bfloat16 [16384, 2048], P(('dp', 'ctx'))
- tokens_grad: bfloat16 [16384, 2048], P(('dp', 'ctx'))
- norm_attn_grad: float32 [2048], P(('dp', 'ctx'))
- w_query_grad: float32 [2048, 2048], P(('dp', 'ctx'), 'tensor')
- w_key_grad: float32 [2048, 256], P(('dp', 'ctx', 'tensor'))
- w_value_grad: float32 [2048, 256], P(('dp', 'ctx', 'tensor'))
- w_output_grad: float32 [2048, 2048], P(('dp', 'ctx'), 'tensor')
- norm_mlp_grad: float32 [2048], P(('dp', 'ctx'))
- w_gate_grad: float32 [2048, 5632], P(('dp', 'ctx'), 'tensor')
- w_up_grad: float32 [2048, 5632], P(('dp', 'ctx'), 'tensor')
- w_down_grad: float32 [2048, 5632], P(('dp', 'ctx'), 'tensor')
The draws below stay inside these ranges and needn't reach their ends.
Inputs may be any that keep to these rules, and one draw needn't show every extreme that they name: Each row is a permutation of the 4 blocks of one sequence, a permuted block order; slot j holds positions span_order[s, j] * 1024 onward, and index c of ctx holds slots 2c and 2c + 1.
All inputs are finite; a program needn't handle non-finite values.
Results may differ from the reference program's by a relative error of at most 0.023.
Values may be sent and summed in bfloat16 or wider, within the bound.
No kernel may reach another device: no remote copies, remote signals or barrier semaphores. Data moves between devices by JAX's collectives and lax.ppermute only.
A program may use at most 448 MiB of HBM per device.

```python
import jax
import jax.numpy as jnp
import numpy as np
from jax import lax

D = 2048
HQ = 32
KVH = 4
HD = 64
FF = 5632
LENGTH = 4096
QW = 2048
KW = 256
SPANS = 4
TOKENS = 16384
N_DP = 4
N_CTX = 2
N_TENSOR = 4


def with_spikes(array, stream_key, source, target, shards_of, factor):
    owner, partner = [(jnp.arange(array.shape[axis_at]) // (array.shape[axis_at] // shards_of)).reshape([-1 if axis == axis_at else 1 for axis in range(array.ndim)]) for axis_at in (source, target)]
    chosen = jax.random.permutation(stream_key, shards_of)[partner]
    strong = (owner == chosen) | (owner == (partner + shards_of // 2) % shards_of)
    return jnp.where(strong, factor * array, array)


def block_levels(stream_key, dims, split, least, top_value):
    level = 1.0
    for position, parts in split:
        steps = jax.random.uniform(jax.random.fold_in(jax.random.fold_in(stream_key, 6), position), (parts,), jnp.float32, least / len(split), top_value / len(split))
        level = level * jnp.repeat(jnp.exp(steps), dims[position] // parts).reshape((-1,) + (1,) * (len(dims) - 1 - position))
    return level


def normal_values(stream_key, shape, spread, limit, split=(), kind=jnp.bfloat16):
    entries = jax.random.normal(stream_key, shape, jnp.float32) * spread
    if len(split) > 0:
        entries = block_levels(stream_key, shape, split, -0.22, 0.18) * entries
    return jnp.clip(entries, min=-limit, max=limit).astype(kind)


def noise_with(rng, shape, scale, most, cuts, heavy, kind=jnp.bfloat16):
    entries = scale * jax.random.normal(rng, shape, jnp.float32)
    if cuts:
        entries = entries * block_levels(rng, shape, cuts, -0.22, 0.18)
    return jnp.clip(with_spikes(entries, jax.random.fold_in(rng, 3), *heavy), -most, most).astype(kind)


def setup_inputs(seed: int = 0) -> dict:
    seeds = jax.random.split(jax.random.key(seed), 13)
    return {
        "tokens": normal_values(seeds[0], (TOKENS, D), 1.0, 6.0, ((0, 8),)),
        "cotangent": noise_with(seeds[1], (TOKENS, D), 1.0, 6.0, ((0, 8),), (0, 1, 8, 2.0)),
        "span_order": jax.vmap(lambda own: jax.random.permutation(own, 2 * N_CTX))(jax.random.split(seeds[2], N_DP)).reshape((N_DP, SPANS)).astype(jnp.int32),
        "norm_attn": jnp.clip(1.0 + 0.1 * jax.random.normal(seeds[3], (D,), jnp.float32), 0.5, 1.5),
        "w_query": normal_values(seeds[4], (D, QW), D ** -0.5, 0.125, ((1, 4),)),
        "w_key": normal_values(seeds[5], (D, KW), D ** -0.5, 0.125),
        "w_value": normal_values(seeds[6], (D, KW), D ** -0.5, 0.125),
        "w_output": normal_values(seeds[7], (D, QW), (QW // 256) ** -0.5, 2.0, ((1, 4),)),
        "norm_mlp": jnp.clip(1.0 + 0.1 * jax.random.normal(seeds[8], (D,), jnp.float32), 0.5, 1.5),
        "w_gate": normal_values(seeds[9], (D, FF), D ** -0.5, 0.125, ((1, 4),)),
        "w_up": normal_values(seeds[10], (D, FF), D ** -0.5, 0.125, ((1, 4),)),
        "w_down": normal_values(seeds[11], (D, FF), FF ** -0.5, 0.078125, ((1, 4),)),
    }


@jax.custom_vjp
def low(v):
    return lax.optimization_barrier(v.astype(jnp.bfloat16)).astype(jnp.float32)

@jax.custom_vjp
def low_back(v):
    return v

def low_keep(v):
    return (low(v), None)

def low_pass(kept, grad):
    return (grad,)

def back_keep(v):
    return (v, None)

def back_low(kept, grad):
    return (low(grad),)
low.defvjp(low_keep, low_pass)
low_back.defvjp(back_keep, back_low)
epsilon = 1e-05
highest = lax.Precision.HIGHEST

def rms_norm(values, gain_vec):
    factor = lax.rsqrt(lax.optimization_barrier(jnp.mean(values * values, axis=-1, keepdims=True)) + epsilon)
    return values * factor * gain_vec

def rotate(values, positions):
    half_dim = values.shape[-1] // 2
    frequency = 10000.0 ** (-jnp.arange(half_dim, dtype=jnp.float32) / half_dim)
    angles = positions.astype(jnp.float32)[:, None] * frequency[None, :]
    cosine = jnp.cos(angles)[:, None, :]
    sine_part = jnp.sin(angles)[:, None, :]
    first_half = values[..., :half_dim]
    second_half = values[..., half_dim:]
    return jnp.concatenate([first_half * cosine - second_half * sine_part, second_half * cosine + first_half * sine_part], axis=-1)

def layer_forward(inputs, params, positions):
    norm_attn, w_query, w_key, w_value, w_output, norm_mlp, w_gate, w_up, w_down = params
    seq_len = inputs.shape[0]
    groups = N_TENSOR
    per_group = HQ // groups
    kv_pick = np.arange(N_TENSOR) * KVH // N_TENSOR
    normed = low(rms_norm(inputs, norm_attn))
    query_raw = low_back(jnp.dot(normed, w_query, precision=highest))
    query_rot = low(rotate(query_raw.reshape(seq_len, HQ, HD), positions))
    query_rot = query_rot.reshape(seq_len, groups, per_group, HD)
    key_heads = jnp.dot(normed, w_key, precision=highest).reshape(seq_len, KVH, HD)
    key_raw = low_back(jnp.take(key_heads, kv_pick, axis=1))
    key_rot = low(rotate(key_raw, positions))
    value_heads = jnp.dot(normed, w_value, precision=highest).reshape(seq_len, KVH, HD)
    value_low = low(low_back(jnp.take(value_heads, kv_pick, axis=1)))
    block_rows = min(512, seq_len)
    block_count = seq_len // block_rows
    score_scale = HD ** (-0.5)

    def attend(block_items):
        query_block, block_positions = block_items
        scores = low_back(jnp.einsum('bgpd,kgd->gpbk', query_block, key_rot, precision=highest) * score_scale)
        visible = positions[None, :] <= block_positions[:, None]
        scores = jnp.where(visible, scores, -1e+30)
        row_max = lax.optimization_barrier(jnp.max(scores, axis=-1, keepdims=True))
        weights = jnp.exp(scores - row_max)
        softmax_low = low(weights / lax.optimization_barrier(jnp.sum(weights, axis=-1, keepdims=True)))
        return jnp.einsum('gpbk,kgd->bgpd', softmax_low, value_low, precision=highest)
    blocks = lax.map(jax.checkpoint(attend), (query_rot.reshape(block_count, block_rows, groups, per_group, HD), positions.reshape(block_count, block_rows)))
    attention = low(low_back(blocks.reshape(seq_len, HQ * HD)))
    attn_out = low_back(jnp.dot(attention, w_output.T, precision=highest))
    middle = inputs + attn_out
    normed_mlp = low(rms_norm(middle, norm_mlp))
    gate_proj = low_back(jnp.dot(normed_mlp, w_gate, precision=highest))
    up_proj = low_back(jnp.dot(normed_mlp, w_up, precision=highest))
    hidden = low(jax.nn.silu(gate_proj) * up_proj)
    mlp_out = low_back(jnp.dot(hidden, w_down.T, precision=highest))
    return middle + mlp_out

def reference(tokens, cotangent, span_order, norm_attn, w_query, w_key, w_value, w_output, norm_mlp, w_gate, w_up, w_down):
    params = tuple((weight.astype(jnp.float32) for weight in (norm_attn, w_query, w_key, w_value, w_output, norm_mlp, w_gate, w_up, w_down)))
    span_len = LENGTH // (2 * N_CTX)

    def one_sequence(totals, seq_items):
        seq_tokens, seq_back, slot_order = seq_items
        positions = (slot_order[:, None].astype(jnp.int32) * span_len + jnp.arange(span_len, dtype=jnp.int32)[None, :]).reshape(-1).astype(jnp.int32)

        def forward(inputs, weights):
            return layer_forward(inputs, weights, positions)
        result, pullback = jax.vjp(forward, seq_tokens.astype(jnp.float32), params)
        grads = pullback(seq_back.astype(jnp.float32))
        totals = tuple((running + extra for running, extra in zip(totals, grads[1])))
        return (totals, (result.astype(jnp.bfloat16), grads[0].astype(jnp.bfloat16)))
    start = tuple((jnp.zeros(weight.shape, jnp.float32) for weight in params))
    totals, outputs = lax.scan(one_sequence, start, (tokens.reshape(N_DP, LENGTH, D), cotangent.reshape(N_DP, LENGTH, D), span_order))
    mixed = outputs[0].reshape(TOKENS, D)
    tokens_grad = outputs[1].reshape(TOKENS, D)
    return (mixed, tokens_grad, totals[0], totals[1], totals[2], totals[3], totals[4], totals[5], totals[6], totals[7], totals[8])
```

```python
import jax
import jax.numpy as jnp
import numpy as np
from jax import lax
from jax.experimental import pallas as pl
from jax.experimental.pallas import tpu as pltpu
from jax.sharding import PartitionSpec as P

NT = (((1,), (1,)), ((), ()))
F32 = jnp.float32
BF16 = jnp.bfloat16
HD = 64
GROUP = 256


def fwd_kernel(meta, q_ref, ka_ref, kb_ref, vt_ref, o_ref, lse_ref):
    span = q_ref.shape[0]
    group = min(GROUP, span)
    queries = q_ref[...]
    own = pl.multiple_of(meta[1 + meta[0]] * span, span)
    heads = []
    for keys_ref in (ka_ref, kb_ref):
        tops, sums = [], []
        for first in range(0, span, group):
            count = first + group
            rows = pl.ds(own, count)
            scores = lax.dot_general(
                keys_ref[rows, :], queries[first:count], NT, preferred_element_type=F32
            )
            key_at = lax.broadcasted_iota(jnp.int32, scores.shape, 0)
            row_at = lax.broadcasted_iota(jnp.int32, scores.shape, 1) + first
            scores = jnp.where(key_at <= row_at, scores, -1e30)
            top = jnp.max(scores, axis=0, keepdims=True)
            weights = jnp.exp(scores - top).astype(BF16)
            tops.append(top)
            sums.append(jnp.dot(vt_ref[:, rows], weights, preferred_element_type=F32))
        heads += [jnp.concatenate(tops, axis=1), jnp.concatenate(sums, axis=1)]

    def step(index, carry):
        rows = pl.ds(pl.multiple_of(meta[1 + index] * span, span), span)
        out = []
        for side, keys_ref in enumerate((ka_ref, kb_ref)):
            top, total = carry[2 * side : 2 * side + 2]
            scores = lax.dot_general(
                keys_ref[rows, :], queries, NT, preferred_element_type=F32
            )
            new_top = jnp.maximum(top, jnp.max(scores, axis=0, keepdims=True))
            weights = jnp.exp(scores - new_top).astype(BF16)
            total = total * jnp.exp(top - new_top) + jnp.dot(
                vt_ref[:, rows], weights, preferred_element_type=F32
            )
            out += [new_top, total]
        return tuple(out)

    top0, total0, top1, total1 = lax.fori_loop(0, meta[0], step, tuple(heads))
    norm0, norm1 = total0[HD : HD + 1], total1[HD : HD + 1]
    o_ref[...] = jnp.concatenate([total0[:HD] / norm0, total1[:HD] / norm1], axis=0).T.astype(BF16)
    lse_ref[0] = jnp.concatenate(
        [top0 + jnp.log(norm0), top1 + jnp.log(norm1), jnp.zeros((6, span), F32)], axis=0
    )


def attend(meta, queries, keys_a, keys_b, values_t, fraction=0.6):
    span, width = queries.shape
    pairs = width // 128
    length = keys_a.shape[0]
    whole = pl.BlockSpec((length, 128), lambda p, m: (0, 0))
    flops = int(4 * span * length * width * fraction)
    return pl.pallas_call(
        fwd_kernel,
        grid_spec=pltpu.PrefetchScalarGridSpec(
            num_scalar_prefetch=1,
            grid=(pairs,),
            in_specs=[
                pl.BlockSpec((span, 128), lambda p, m: (0, p)),
                whole,
                whole,
                pl.BlockSpec(values_t.shape, lambda p, m: (0, 0)),
            ],
            out_specs=[
                pl.BlockSpec((span, 128), lambda p, m: (0, p)),
                pl.BlockSpec((1, 8, span), lambda p, m: (p, 0, 0)),
            ],
        ),
        out_shape=[
            jax.ShapeDtypeStruct((span, width), BF16),
            jax.ShapeDtypeStruct((pairs, 8, span), F32),
        ],
        compiler_params=pltpu.CompilerParams(vmem_limit_bytes=56 * 2**20),
        cost_estimate=pl.CostEstimate(
            flops=4 * flops, bytes_accessed=2**23, transcendentals=0
        ),
        name="attend",
    )(meta, queries, keys_a, keys_b, values_t)


def bwd_kernel(
    meta,
    q_ref,
    o_ref,
    g_ref,
    lse_ref,
    ka_ref,
    kb_ref,
    va_ref,
    vb_ref,
    kt_ref,
    cos_ref,
    sin_ref,
    dk_in,
    dv_in,
    dq_ref,
    dk_ref,
    dv_ref,
):
    span = q_ref.shape[0]
    group = min(GROUP, span)

    @pl.when(pl.program_id(0) == 0)
    def _():
        dk_ref[...] = dk_in[...]
        dv_ref[...] = dv_in[...]

    queries, grads = q_ref[...], g_ref[...]
    left = lax.broadcasted_iota(jnp.int32, (span, 128), 1) < HD
    products = (grads.astype(F32) * o_ref[...].astype(F32)).T
    zero = jnp.zeros_like(queries)
    sides = []
    for side, (keys_ref, values_ref) in enumerate(((ka_ref, va_ref), (kb_ref, vb_ref))):
        mine = left if side == 0 else jnp.logical_not(left)
        delta = jnp.sum(products[side * HD : side * HD + HD], axis=0, keepdims=True)
        sides.append(
            (
                keys_ref,
                values_ref,
                jnp.where(mine, queries, zero),
                jnp.where(mine, grads, zero),
                lse_ref[0, side : side + 1, :],
                delta,
            )
        )

    def block(rows, columns, masked):
        first, count = columns
        cut = slice(first, first + count)
        dqs = []
        dk_add = dv_add = None
        for keys_ref, values_ref, q_mine, g_mine, lse, delta in sides:
            scores = lax.dot_general(
                keys_ref[rows, :], queries[cut], NT, preferred_element_type=F32
            )
            probs = jnp.exp(scores - lse[:, cut])
            if masked:
                key_at = lax.broadcasted_iota(jnp.int32, scores.shape, 0)
                row_at = lax.broadcasted_iota(jnp.int32, scores.shape, 1) + first
                probs = jnp.where(key_at <= row_at, probs, 0.0)
            grad_probs = lax.dot_general(
                values_ref[rows, :], grads[cut], NT, preferred_element_type=F32
            )
            grad_scores = (probs * (grad_probs - delta[:, cut])).astype(BF16)
            dv_new = jnp.dot(probs.astype(BF16), g_mine[cut], preferred_element_type=F32)
            dk_new = jnp.dot(grad_scores, q_mine[cut], preferred_element_type=F32)
            dv_add = dv_new if dv_add is None else dv_add + dv_new
            dk_add = dk_new if dk_add is None else dk_add + dk_new
            dqs.append(jnp.dot(kt_ref[:, rows], grad_scores, preferred_element_type=F32))
        dv_ref[rows, :] += dv_add
        dk_ref[rows, :] += dk_add
        return jnp.concatenate(dqs, axis=0)

    own = pl.multiple_of(meta[1 + meta[0]] * span, span)
    start = jnp.concatenate(
        [block(pl.ds(own, first + group), (first, group), True) for first in range(0, span, group)],
        axis=1,
    )
    half = min(512, span)

    def step(index, total):
        base = pl.multiple_of(meta[1 + index // (span // half)] * span, span)
        rows = pl.ds(pl.multiple_of(base + (index % (span // half)) * half, half), half)
        return total + block(rows, (0, span), False)

    dq = lax.fori_loop(0, meta[0] * (span // half), step, start).T * (HD**-0.5)
    low = (lax.broadcasted_iota(jnp.int32, (span, 128), 1) % HD) < HD // 2
    swapped = jnp.where(low, pltpu.roll(dq, 128 - HD // 2, 1), pltpu.roll(dq, HD // 2, 1))
    dq_ref[...] = (dq * cos_ref[...] - swapped * sin_ref[...]).astype(BF16)


def attend_back(
    meta, queries, outputs, grads, lse, ka, kb, va, vb, kt, cos, sin, dk, dv, fraction=0.6
):
    span, width = queries.shape
    pairs = width // 128
    length = ka.shape[0]
    whole = pl.BlockSpec((length, 128), lambda p, m: (0, 0))
    pair = pl.BlockSpec((span, 128), lambda p, m: (0, p))
    table = pl.BlockSpec((span, 128), lambda p, m: (0, 0))
    flops = int(10 * span * length * width * fraction)
    return pl.pallas_call(
        bwd_kernel,
        grid_spec=pltpu.PrefetchScalarGridSpec(
            num_scalar_prefetch=1,
            grid=(pairs,),
            in_specs=[
                pair,
                pair,
                pair,
                pl.BlockSpec((1, 8, span), lambda p, m: (p, 0, 0)),
                whole,
                whole,
                whole,
                whole,
                pl.BlockSpec(kt.shape, lambda p, m: (0, 0)),
                table,
                table,
                whole,
                whole,
            ],
            out_specs=[pair, whole, whole],
        ),
        out_shape=[
            jax.ShapeDtypeStruct((span, width), BF16),
            jax.ShapeDtypeStruct((length, 128), F32),
            jax.ShapeDtypeStruct((length, 128), F32),
        ],
        compiler_params=pltpu.CompilerParams(vmem_limit_bytes=58 * 2**20),
        cost_estimate=pl.CostEstimate(
            flops=4 * flops, bytes_accessed=2**24, transcendentals=0
        ),
        name="attend_back",
    )(meta, queries, outputs, grads, lse, ka, kb, va, vb, kt, cos, sin, dk, dv)

EPSILON = 1e-05


def line_gather(piece, place, target):
    size = lax.axis_size("tensor")
    me = lax.axis_index("tensor")
    target = place(target, piece, me)
    rights, lefts = [piece], [piece]
    for step in range(1, size):
        rights.append(
            lax.ppermute(rights[-1], "tensor", [(i, i + 1) for i in range(step - 1, size - 1)])
        )
        lefts.append(
            lax.ppermute(lefts[-1], "tensor", [(i, i - 1) for i in range(1, size - step + 1)])
        )
    for step in range(1, size):
        arrived = rights[step] + lefts[size - step]
        target = place(target, arrived, lax.rem(me - step + size, size))
    return target


def line_scatter(partial):
    size = lax.axis_size("tensor")
    me = lax.axis_index("tensor")
    rows = partial.shape[0] // size

    def part(index):
        index = jnp.clip(index, 0, size - 1)
        return lax.dynamic_slice_in_dim(partial, index * rows, rows, 0)

    right = left = None
    for step in range(1, size):
        send = part(size - step + me)
        if right is not None:
            send = send + right
        right = lax.ppermute(send, "tensor", [(i, i + 1) for i in range(step)])
        send = part(me + step - size)
        if left is not None:
            send = send + left
        left = lax.ppermute(send, "tensor", [(i, i - 1) for i in range(size - step, size)])
    total = part(me).astype(F32)
    if right is not None:
        total = total + right.astype(F32) + left.astype(F32)
    return total


def exchange(pick):
    size = lax.axis_size("tensor")
    me = lax.axis_index("tensor")
    own = pick(me)
    out = jnp.zeros((size, *own.shape), own.dtype)
    out = lax.dynamic_update_index_in_dim(out, own, me, 0)
    for shift in range(1, size):
        got = lax.ppermute(
            pick(lax.rem(me + shift, size)), "tensor", [(i, (i + shift) % size) for i in range(size)]
        )
        out = lax.dynamic_update_index_in_dim(out, got, lax.rem(me - shift + size, size), 0)
    return out


def gather_weight(weight):
    plane = lax.axis_size("dp") * lax.axis_size("ctx")
    index = lax.axis_index("dp") * lax.axis_size("ctx") + lax.axis_index("ctx")
    rows = weight.shape[0] // plane
    piece = lax.dynamic_slice_in_dim(weight, index * rows, rows, 0)
    column = lax.all_gather(piece, "tensor", axis=0, tiled=False)
    whole = lax.all_gather(column, ("dp", "ctx"), axis=0, tiled=False)
    return jnp.swapaxes(whole, 0, 1).reshape(lax.axis_size("tensor"), *weight.shape)


def swap_halves(weight):
    rows, columns = weight.shape
    return weight.reshape(rows, columns // HD, 2, HD // 2)[:, :, ::-1, :].reshape(rows, columns)


def dot(a, b):
    return jnp.dot(a, b, preferred_element_type=F32)


def dot_t(a, b):
    return jnp.einsum("rf,df->rd", a, b, preferred_element_type=F32)


def t_dot(a, b):
    return jnp.einsum("rd,rf->df", a, b, preferred_element_type=F32)


def body(
    tokens,
    cotangent,
    span_order,
    norm_attn,
    w_query,
    w_key,
    w_value,
    w_output,
    norm_mlp,
    w_gate,
    w_up,
    w_down,
):
    tok_rows, width = tokens.shape
    groups = lax.axis_size("tensor")
    member = lax.axis_index("tensor")
    n_ctx = lax.axis_size("ctx")
    ctx_index = lax.axis_index("ctx")
    features = w_query.shape[1]
    kv_count = w_key.shape[1] // HD
    kv_pick = np.arange(groups) * kv_count // groups
    kv_start = member * kv_count // groups * HD
    key_weight = lax.dynamic_slice_in_dim(w_key, kv_start, HD, 1)
    value_weight = lax.dynamic_slice_in_dim(w_value, kv_start, HD, 1)
    span = tok_rows // 2
    share = span // groups
    slots = range(2)

    swap = n_ctx == 2
    order = span_order[0]
    if swap:
        order = jnp.roll(order, -2 * ctx_index)
    n_spans = order.shape[0]
    places = jnp.arange(n_spans, dtype=jnp.int32)
    slot_of = jnp.sum(
        jnp.where(order[None, :] == places[:, None], places[None, :], 0), axis=1, dtype=jnp.int32
    )
    own_first = 0 if swap else 2 * ctx_index
    own_spans = lax.dynamic_slice_in_dim(order, own_first, 2)
    metas = [jnp.concatenate([own_spans[s : s + 1], slot_of]) for s in slots]

    positions = (own_spans[:, None] * span + jnp.arange(span, dtype=jnp.int32)[None, :]).reshape(-1)
    half = HD // 2
    frequency = 10000.0 ** (-jnp.arange(half, dtype=F32) / half)
    angles = positions.astype(F32)[:, None] * frequency[None, :]
    cos_part, sin_part = jnp.cos(angles), jnp.sin(angles)
    cos_head = jnp.concatenate([cos_part, cos_part], axis=1)
    sin_head = jnp.concatenate([-sin_part, sin_part], axis=1)
    cos_pair = jnp.concatenate([cos_head, cos_head], axis=1)
    sin_pair = jnp.concatenate([sin_head, sin_head], axis=1)

    output_whole = gather_weight(w_output)
    query_whole = gather_weight(w_query)

    inputs = tokens.astype(F32)
    inverse_one = lax.rsqrt(jnp.mean(inputs * inputs, axis=-1, keepdims=True) + EPSILON)
    normed = (inputs * inverse_one * norm_attn).astype(BF16)
    kv_raw = dot(normed, jnp.concatenate([key_weight, value_weight, swap_halves(key_weight)], axis=1))
    key_rot = kv_raw[:, :HD] * cos_head + kv_raw[:, 2 * HD :] * sin_head
    kv_own = jnp.concatenate([key_rot, kv_raw[:, HD : 2 * HD]], axis=1).astype(BF16)
    if swap:
        kv_other = lax.ppermute(kv_own, "ctx", [(0, 1), (1, 0)])
        kv_all = jnp.concatenate([kv_own, kv_other], axis=0)
    else:
        kv_all = lax.all_gather(kv_own, "ctx", axis=0, tiled=True)
    length = kv_all.shape[0]
    keys, values = kv_all[:, :HD], kv_all[:, HD:]
    blank = jnp.zeros_like(keys)
    keys_a = jnp.concatenate([keys, blank], axis=1)
    keys_b = jnp.concatenate([blank, keys], axis=1)
    values_a = jnp.concatenate([values, blank], axis=1)
    values_b = jnp.concatenate([blank, values], axis=1)
    keys_t = keys.T
    values_t = jnp.concatenate(
        [values.T, jnp.ones((1, length), BF16), jnp.zeros((15, length), BF16)], axis=0
    )

    query_raw = dot(normed, jnp.concatenate([w_query, swap_halves(w_query)], axis=1))
    tiles = features // 128
    queries = (
        (
            query_raw[:, :features] * jnp.tile(cos_pair, (1, tiles))
            + query_raw[:, features:] * jnp.tile(sin_pair, (1, tiles))
        )
        * HD**-0.5
    ).astype(BF16)

    def cut(array, slot):
        return array[slot * span : (slot + 1) * span]

    def own_rows(array):
        return lax.dynamic_slice_in_dim(array, member * share, share, 0)

    def by_row(target, piece, source):
        return lax.dynamic_update_slice_in_dim(target, piece, source * share, 0)

    attention, log_totals, whole_attention = [], [], []
    for s in slots:
        out, lse = attend(metas[s], cut(queries, s), keys_a, keys_b, values_t)
        attention.append(out)
        log_totals.append(lse)
        whole_attention.append(
            line_gather(
                out,
                lambda target, piece, source: lax.dynamic_update_index_in_dim(target, piece, source, 0),
                jnp.zeros((groups, span, features), BF16),
            )
        )

    parts = []
    for s in slots:
        middle = cut(inputs, s) + jnp.einsum(
            "trq,tdq->rd", whole_attention[s], output_whole, preferred_element_type=F32
        )
        inverse_two = lax.rsqrt(jnp.mean(middle * middle, axis=-1, keepdims=True) + EPSILON)
        normed_mlp = (middle * inverse_two * norm_mlp).astype(BF16)
        gate_proj = dot(normed_mlp, w_gate)
        up_proj = dot(normed_mlp, w_up)
        sigmoid_gate = jax.nn.sigmoid(gate_proj)
        hidden = (gate_proj * sigmoid_gate * up_proj).astype(BF16)
        grad_hidden = dot(cut(cotangent, s), w_down)
        grad_gate = (
            grad_hidden * up_proj * sigmoid_gate * (1.0 + gate_proj * (1.0 - sigmoid_gate))
        ).astype(BF16)
        grad_up = (grad_hidden * gate_proj * sigmoid_gate).astype(BF16)
        grad_part = (dot_t(grad_gate, w_gate) + dot_t(grad_up, w_up)).astype(BF16)
        mlp_part = dot_t(hidden, w_down).astype(BF16)
        parts.append(
            (own_rows(middle), own_rows(inverse_two), normed_mlp, hidden, grad_gate, grad_up)
            + (grad_part, mlp_part)
        )

    mlp_gain = jnp.zeros((width,), F32)
    grad_middles, grad_lows, grad_attention = [], [], []
    for s in slots:
        middle, inverse_two = parts[s][:2]
        grad_normed_mlp = line_scatter(parts[s][6])
        mlp_gain = mlp_gain + jnp.sum(grad_normed_mlp * middle * inverse_two, axis=0)
        scaled_two = grad_normed_mlp * norm_mlp
        grad_middle = (
            own_rows(cut(cotangent, s)).astype(F32)
            + inverse_two * scaled_two
            - middle * inverse_two**3 * jnp.mean(scaled_two * middle, axis=-1, keepdims=True)
        )
        grad_middles.append(grad_middle)
        grad_low = grad_middle.astype(BF16)
        grad_lows.append(grad_low)
        blocks = jnp.einsum(
            "rd,tdq->trq", grad_low, output_whole, preferred_element_type=F32
        ).astype(BF16)
        grad_attention.append(
            exchange(lambda j: lax.dynamic_index_in_dim(blocks, j, 0, keepdims=False)).reshape(
                span, features
            )
        )

    normed_mlp, hidden, grad_gate, grad_up = (
        jnp.concatenate([parts[s][i] for s in slots], axis=0) for i in range(2, 6)
    )

    def plane_sum(gradient):
        return lax.psum_scatter(
            gradient.astype(BF16), ("dp", "ctx"), scatter_dimension=0, tiled=True
        ).astype(F32)

    gate_grad = plane_sum(t_dot(normed_mlp, grad_gate))
    up_grad = plane_sum(t_dot(normed_mlp, grad_up))
    down_grad = plane_sum(t_dot(cotangent, hidden))

    mixed = jnp.zeros((tok_rows, width), BF16)
    for s in slots:
        mixed_share = (parts[s][0] + line_scatter(parts[s][7])).astype(BF16)
        mixed = line_gather(
            mixed_share,
            lambda target, piece, source: lax.dynamic_update_slice_in_dim(
                target, piece, s * span + source * share, 0
            ),
            mixed,
        )

    dk = jnp.zeros((length, 128), F32)
    dv = jnp.zeros((length, 128), F32)
    grad_queries, exchanged = [], []
    for s in slots:
        grad_query, dk, dv = attend_back(
            metas[s],
            cut(queries, s),
            attention[s],
            grad_attention[s],
            log_totals[s],
            keys_a,
            keys_b,
            values_a,
            values_b,
            keys_t,
            cut(cos_pair, s),
            cut(sin_pair, s),
            dk,
            dv,
        )
        grad_queries.append(grad_query)
        exchanged.append(
            exchange(lambda j: lax.dynamic_slice_in_dim(grad_query, j * share, share, 0))
        )
    kv_sums = jnp.concatenate([dk[:, :HD] + dk[:, HD:], dv[:, :HD] + dv[:, HD:]], axis=1)
    if swap:
        sent = lax.ppermute(kv_sums[tok_rows:].astype(BF16), "ctx", [(0, 1), (1, 0)])
        kv_grad = kv_sums[:tok_rows] + sent.astype(F32)
    else:
        kv_grad = lax.psum_scatter(
            kv_sums.astype(BF16), "ctx", scatter_dimension=0, tiled=True
        ).astype(F32)
    grad_key = kv_grad[:, :HD]
    swapped = jnp.concatenate([grad_key[:, half:], grad_key[:, :half]], axis=1)
    grad_kv_raw = jnp.concatenate(
        [grad_key * cos_head - swapped * sin_head, kv_grad[:, HD:]], axis=1
    ).astype(BF16)
    kv_exchanged = [
        exchange(
            lambda j: lax.dynamic_slice_in_dim(grad_kv_raw, s * span + j * share, share, 0)
        )
        for s in slots
    ]
    kv_whole = jnp.stack(
        [
            jnp.concatenate(
                [w_key[:, h * HD : (h + 1) * HD], w_value[:, h * HD : (h + 1) * HD]], axis=1
            )
            for h in kv_pick
        ]
    )

    attn_gain = jnp.zeros((width,), F32)
    tokens_grad = jnp.zeros((tok_rows, width), BF16)
    for s in slots:
        grad_normed = jnp.einsum(
            "trq,tdq->rd", exchanged[s], query_whole, preferred_element_type=F32
        ) + jnp.einsum("trq,tdq->rd", kv_exchanged[s], kv_whole, preferred_element_type=F32)
        inputs_own = own_rows(cut(inputs, s))
        inverse_own = own_rows(cut(inverse_one, s))
        attn_gain = attn_gain + jnp.sum(grad_normed * inputs_own * inverse_own, axis=0)
        scaled_one = grad_normed * norm_attn
        grad_inputs = (
            grad_middles[s]
            + inverse_own * scaled_one
            - inputs_own
            * inverse_own**3
            * jnp.mean(scaled_one * inputs_own, axis=-1, keepdims=True)
        ).astype(BF16)
        tokens_grad = line_gather(
            grad_inputs,
            lambda target, piece, source: lax.dynamic_update_slice_in_dim(
                target, piece, s * span + source * share, 0
            ),
            tokens_grad,
        )

    low_rows = jnp.concatenate(grad_lows, axis=0)
    attention_rows = jnp.concatenate(
        [lax.dynamic_slice_in_dim(whole, member * share, share, 1) for whole in whole_attention],
        axis=1,
    )
    output_part = jnp.einsum("rd,trq->dtq", low_rows, attention_rows, preferred_element_type=F32)
    output_plane = lax.psum_scatter(
        output_part.astype(BF16).reshape(width, groups * features),
        ("dp", "ctx"),
        scatter_dimension=0,
        tiled=True,
    )
    output_grad = jnp.sum(
        exchange(
            lambda j: lax.dynamic_slice_in_dim(output_plane, j * features, features, 1)
        ).astype(F32),
        axis=0,
    )

    query_part = t_dot(normed, jnp.concatenate(grad_queries, axis=0))
    kv_part = t_dot(normed, grad_kv_raw)
    query_kv = plane_sum(jnp.concatenate([query_part, kv_part], axis=1))
    query_grad = query_kv[:, :features]
    kv_rows = query_kv.shape[0] // groups
    kv_plane = query_kv[:, features:].astype(BF16)
    kv_blocks = exchange(
        lambda j: lax.dynamic_slice_in_dim(kv_plane, j * kv_rows, kv_rows, 0)
    ).astype(F32)
    key_heads, value_heads = [], []
    for h in range(kv_count):
        members = [g for g in range(groups) if kv_pick[g] == h]
        total = jnp.zeros((kv_rows, 2 * HD), F32)
        for g in members:
            total = total + kv_blocks[g]
        key_heads.append(total[:, :HD])
        value_heads.append(total[:, HD:])
    key_grad = jnp.concatenate(key_heads, axis=1)
    value_grad = jnp.concatenate(value_heads, axis=1)

    gains = lax.psum(jnp.stack([attn_gain, mlp_gain]), ("dp", "ctx", "tensor"))
    plane = lax.axis_size("dp") * n_ctx
    plane_index = lax.axis_index("dp") * n_ctx + ctx_index
    gains = lax.dynamic_slice_in_dim(gains, plane_index * (width // plane), width // plane, 1)
    return (
        mixed,
        tokens_grad,
        gains[0],
        query_grad,
        key_grad,
        value_grad,
        output_grad,
        gains[1],
        gate_grad,
        up_grad,
        down_grad,
    )


def solution(mesh):
    placed = (
        P(("dp", "ctx"), None),
        P(("dp", "ctx"), None),
        P("dp", None),
        P(),
        P(None, "tensor"),
        P(),
        P(),
        P(None, "tensor"),
        P(),
        P(None, "tensor"),
        P(None, "tensor"),
        P(None, "tensor"),
    )
    return jax.shard_map(
        body,
        mesh=mesh,
        in_specs=placed,
        out_specs=(
            P(("dp", "ctx"), None),
            P(("dp", "ctx"), None),
            P(("dp", "ctx")),
            P(("dp", "ctx"), "tensor"),
            P(("dp", "ctx", "tensor"), None),
            P(("dp", "ctx", "tensor"), None),
            P(("dp", "ctx"), "tensor"),
            P(("dp", "ctx")),
            P(("dp", "ctx"), "tensor"),
            P(("dp", "ctx"), "tensor"),
            P(("dp", "ctx"), "tensor"),
        ),
        check_vma=False,
    )
```

```python
import jax
import jax.numpy as jnp
import numpy as np
from jax import lax
from jax.experimental import pallas as pl
from jax.experimental.pallas import tpu as pltpu
from jax.sharding import PartitionSpec as P

NT = (((1,), (1,)), ((), ()))
F32 = jnp.float32
BF16 = jnp.bfloat16
HD = 64
GROUP = 256
EPSILON = 1e-05
LIGHT = pl.CostEstimate(flops=1, bytes_accessed=1, transcendentals=0)


def turn(values, cos, sin):
    low = (lax.broadcasted_iota(jnp.int32, values.shape, 1) % HD) < HD // 2
    other = jnp.where(
        low, pltpu.roll(values, 128 - HD // 2, 1), pltpu.roll(values, HD // 2, 1)
    )
    return values * cos + other * sin


def project_kernel(
    tokens_ref, gain_ref, kv_weight, q_weight, cos_ref, sin_ref, kv_ref, q_ref, normed_ref
):
    inputs = tokens_ref[...].astype(F32)
    inverse = lax.rsqrt(jnp.mean(inputs * inputs, axis=-1, keepdims=True) + EPSILON)
    normed = (inputs * inverse * gain_ref[...]).astype(BF16)
    normed_ref[...] = normed
    cos, sin = cos_ref[...], sin_ref[...]
    pair = jnp.dot(normed, kv_weight[...], preferred_element_type=F32)
    is_key = lax.broadcasted_iota(jnp.int32, pair.shape, 1) < HD
    kv_ref[...] = jnp.where(is_key, turn(pair, cos, sin), pair).astype(BF16)
    raw = jnp.dot(normed, q_weight[...], preferred_element_type=F32)
    for first in range(0, q_ref.shape[1], 128):
        pair = raw[:, first : first + 128]
        q_ref[:, first : first + 128] = (turn(pair, cos, sin) * HD**-0.5).astype(BF16)


def project(tokens, gain, kv_weight, q_weight, cos, sin):
    rows, width = tokens.shape
    columns = q_weight.shape[1]
    block = 256
    return pl.pallas_call(
        project_kernel,
        grid=(rows // block,),
        in_specs=[
            pl.BlockSpec((block, width), lambda i: (i, 0)),
            pl.BlockSpec((1, width), lambda i: (0, 0)),
            pl.BlockSpec((width, 128), lambda i: (0, 0)),
            pl.BlockSpec((width, columns), lambda i: (0, 0)),
            pl.BlockSpec((block, 128), lambda i: (i, 0)),
            pl.BlockSpec((block, 128), lambda i: (i, 0)),
        ],
        out_specs=[
            pl.BlockSpec((block, 128), lambda i: (i, 0)),
            pl.BlockSpec((block, columns), lambda i: (i, 0)),
            pl.BlockSpec((block, width), lambda i: (i, 0)),
        ],
        out_shape=[
            jax.ShapeDtypeStruct((rows, 128), BF16),
            jax.ShapeDtypeStruct((rows, columns), BF16),
            jax.ShapeDtypeStruct((rows, width), BF16),
        ],
        compiler_params=pltpu.CompilerParams(vmem_limit_bytes=48 * 2**20),
        cost_estimate=LIGHT,
        name="project",
    )(tokens, gain.reshape(1, width), kv_weight, q_weight, cos, sin)


def fwd_kernel(offsets, meta, q_ref, ka_ref, kb_ref, vt_ref, o_ref, lse_ref):
    half = q_ref.shape[0] // 2
    span = 2 * half
    group = min(GROUP, half)
    pairs = q_ref.shape[1] // 128
    for part, offset in enumerate(offsets):
        at = slice(part * half, part * half + half)
        queries = [q_ref[at, p * 128 : p * 128 + 128] for p in range(pairs)]
        chains = [(p, keys_ref) for p in range(pairs) for keys_ref in (ka_ref, kb_ref)]
        seen = meta[part]
        own = pl.multiple_of(meta[2 + seen] * span, span)
        heads = []
        for p, keys_ref in chains:
            tops, sums = [], []
            for first in range(0, half, group):
                count = offset + first + group
                rows = pl.ds(own, count)
                scores = lax.dot_general(
                    keys_ref[rows, :],
                    queries[p][first : first + group],
                    NT,
                    preferred_element_type=F32,
                )
                key_at = lax.broadcasted_iota(jnp.int32, scores.shape, 0)
                row_at = lax.broadcasted_iota(jnp.int32, scores.shape, 1) + (offset + first)
                scores = jnp.where(key_at <= row_at, scores, -1e30)
                top = jnp.max(scores, axis=0, keepdims=True)
                weights = jnp.exp(scores - top).astype(BF16)
                tops.append(top)
                sums.append(jnp.dot(vt_ref[:, rows], weights, preferred_element_type=F32))
            heads += [jnp.concatenate(tops, axis=1), jnp.concatenate(sums, axis=1)]

        def step(index, carry):
            rows = pl.ds(pl.multiple_of(meta[2 + index] * span, span), span)
            out = []
            for chain, (p, keys_ref) in enumerate(chains):
                top, total = carry[2 * chain : 2 * chain + 2]
                scores = lax.dot_general(
                    keys_ref[rows, :], queries[p], NT, preferred_element_type=F32
                )
                new_top = jnp.maximum(top, jnp.max(scores, axis=0, keepdims=True))
                weights = jnp.exp(scores - new_top).astype(BF16)
                total = total * jnp.exp(top - new_top) + jnp.dot(
                    vt_ref[:, rows], weights, preferred_element_type=F32
                )
                out += [new_top, total]
            return tuple(out)

        heads = lax.fori_loop(0, seen, step, tuple(heads))
        for p in range(pairs):
            top0, total0, top1, total1 = heads[4 * p : 4 * p + 4]
            norm0, norm1 = total0[HD : HD + 1], total1[HD : HD + 1]
            o_ref[at, p * 128 : p * 128 + 128] = (
                jnp.concatenate([total0[:HD] / norm0, total1[:HD] / norm1], axis=0).T.astype(BF16)
            )
            lse_ref[p, :, at] = jnp.concatenate(
                [top0 + jnp.log(norm0), top1 + jnp.log(norm1), jnp.zeros((6, half), F32)], axis=0
            )


def spread(kv_refs, ka_ref, kb_ref, va_ref, vb_ref, kt_ref, vt_ref):
    at = 0
    for kv_ref in kv_refs:
        rows = kv_ref.shape[0]
        block = min(512, rows)
        for first in range(0, rows, block):
            here = slice(at + first, at + first + block)
            pair = kv_ref[first : first + block, :].astype(F32)
            other = pltpu.roll(pair, HD, 1)
            left = lax.broadcasted_iota(jnp.int32, pair.shape, 1) < HD
            ka_ref[here, :] = jnp.where(left, pair, 0.0).astype(BF16)
            vb_ref[here, :] = jnp.where(left, 0.0, pair).astype(BF16)
            va_ref[here, :] = jnp.where(left, other, 0.0).astype(BF16)
            kb_ref[here, :] = jnp.where(left, 0.0, other).astype(BF16)
            turned = pair.T
            kt_ref[:, here] = turned[:HD].astype(BF16)
            ones = jnp.where(lax.broadcasted_iota(jnp.int32, (16, block), 0) == 0, 1.0, 0.0)
            vt_ref[:, here] = jnp.concatenate([turned[HD:], ones], axis=0).astype(BF16)
        at += rows


def attend_first(meta, offsets, queries, kv_own, kv_other):
    rows, width = queries.shape
    pairs = width // 128
    together = 2 if pairs % 2 == 0 else 1
    length = 2 * kv_own.shape[0]

    def whole(shape):
        return pl.BlockSpec(shape, lambda p, m: (0, 0))

    def kernel(meta, q_ref, own, other, o_ref, lse_ref, ka, kb, va, vb, kt, vt):
        @pl.when(pl.program_id(0) == 0)
        def _():
            spread((own, other), ka, kb, va, vb, kt, vt)

        fwd_kernel(offsets, meta, q_ref, ka, kb, vt, o_ref, lse_ref)

    wide = (length, 128)
    forms = [wide, wide, wide, wide, (HD, length), (HD + 16, length)]
    return pl.pallas_call(
        kernel,
        grid_spec=pltpu.PrefetchScalarGridSpec(
            num_scalar_prefetch=1,
            grid=(pairs // together,),
            in_specs=[
                pl.BlockSpec((rows, 128 * together), lambda p, m: (0, p)),
                whole(kv_own.shape),
                whole(kv_other.shape),
            ],
            out_specs=[
                pl.BlockSpec((rows, 128 * together), lambda p, m: (0, p)),
                pl.BlockSpec((together, 8, rows), lambda p, m: (p, 0, 0)),
            ]
            + [whole(form) for form in forms],
        ),
        out_shape=[
            jax.ShapeDtypeStruct((rows, width), BF16),
            jax.ShapeDtypeStruct((pairs, 8, rows), F32),
        ]
        + [jax.ShapeDtypeStruct(form, BF16) for form in forms],
        compiler_params=pltpu.CompilerParams(vmem_limit_bytes=58 * 2**20),
        cost_estimate=LIGHT,
        name="attend_first",
    )(meta, queries, kv_own, kv_other)


def attend(meta, offsets, queries, keys_a, keys_b, values_t):
    rows, width = queries.shape
    pairs = width // 128
    together = 2 if pairs % 2 == 0 else 1
    length = keys_a.shape[0]
    whole = pl.BlockSpec((length, 128), lambda p, m: (0, 0))

    def kernel(*refs):
        fwd_kernel(offsets, *refs)

    return pl.pallas_call(
        kernel,
        grid_spec=pltpu.PrefetchScalarGridSpec(
            num_scalar_prefetch=1,
            grid=(pairs // together,),
            in_specs=[
                pl.BlockSpec((rows, 128 * together), lambda p, m: (0, p)),
                whole,
                whole,
                pl.BlockSpec(values_t.shape, lambda p, m: (0, 0)),
            ],
            out_specs=[
                pl.BlockSpec((rows, 128 * together), lambda p, m: (0, p)),
                pl.BlockSpec((together, 8, rows), lambda p, m: (p, 0, 0)),
            ],
        ),
        out_shape=[
            jax.ShapeDtypeStruct((rows, width), BF16),
            jax.ShapeDtypeStruct((pairs, 8, rows), F32),
        ],
        compiler_params=pltpu.CompilerParams(vmem_limit_bytes=58 * 2**20),
        cost_estimate=LIGHT,
        name="attend",
    )(meta, queries, keys_a, keys_b, values_t)


def bwd_kernel(
    offsets,
    meta,
    q_ref,
    o_ref,
    g_ref,
    lse_ref,
    ka_ref,
    kb_ref,
    va_ref,
    vb_ref,
    kt_ref,
    cos_ref,
    sin_ref,
    dq_ref,
    dk_ref,
    dv_ref,
):
    half = q_ref.shape[0] // 2
    span = 2 * half
    group = min(GROUP, half)

    for part, offset in enumerate(offsets):
        at = slice(part * half, part * half + half)
        queries, grads = q_ref[at, :], g_ref[at, :]
        left = lax.broadcasted_iota(jnp.int32, (half, 128), 1) < HD
        products = (grads.astype(F32) * o_ref[at, :].astype(F32)).T
        zero = jnp.zeros_like(queries)
        sides = []
        for side, (keys_ref, values_ref) in enumerate(((ka_ref, va_ref), (kb_ref, vb_ref))):
            mine = left if side == 0 else jnp.logical_not(left)
            delta = jnp.sum(products[side * HD : side * HD + HD], axis=0, keepdims=True)
            sides.append(
                (
                    keys_ref,
                    values_ref,
                    jnp.where(mine, queries, zero),
                    jnp.where(mine, grads, zero),
                    lse_ref[0, side : side + 1, at],
                    delta,
                )
            )

        def block(rows, first, count, masked):
            cut = slice(first, first + count)
            dqs = []
            dk_add = dv_add = None
            for keys_ref, values_ref, q_mine, g_mine, lse, delta in sides:
                scores = lax.dot_general(
                    keys_ref[rows, :], queries[cut], NT, preferred_element_type=F32
                )
                probs = jnp.exp(scores - lse[:, cut])
                if masked:
                    key_at = lax.broadcasted_iota(jnp.int32, scores.shape, 0)
                    row_at = lax.broadcasted_iota(jnp.int32, scores.shape, 1) + (offset + first)
                    probs = jnp.where(key_at <= row_at, probs, 0.0)
                grad_probs = lax.dot_general(
                    values_ref[rows, :], grads[cut], NT, preferred_element_type=F32
                )
                grad_scores = (probs * (grad_probs - delta[:, cut])).astype(BF16)
                dv_new = jnp.dot(probs.astype(BF16), g_mine[cut], preferred_element_type=F32)
                dk_new = jnp.dot(grad_scores, q_mine[cut], preferred_element_type=F32)
                dv_add = dv_new if dv_add is None else dv_add + dv_new
                dk_add = dk_new if dk_add is None else dk_add + dk_new
                dqs.append(jnp.dot(kt_ref[:, rows], grad_scores, preferred_element_type=F32))
            dv_ref[rows, :] += dv_add
            dk_ref[rows, :] += dk_add
            return jnp.concatenate(dqs, axis=0)

        own = pl.multiple_of(meta[2 + meta[part]] * span, span)
        start = jnp.concatenate(
            [
                block(pl.ds(own, offset + first + group), first, group, True)
                for first in range(0, half, group)
            ],
            axis=1,
        )

        def step(index, total):
            rows = pl.ds(pl.multiple_of(meta[2 + index] * span, span), span)
            return total + block(rows, 0, half, False)

        dq = lax.fori_loop(0, meta[part], step, start).T * (HD**-0.5)
        dq_ref[at, :] = turn(dq, cos_ref[at, :], -sin_ref[at, :]).astype(BF16)


def back_specs(queries, forms):
    rows, width = queries.shape
    pair = pl.BlockSpec((rows, 128), lambda p, m: (0, p))
    table = pl.BlockSpec((rows, 128), lambda p, m: (0, 0))
    specs = [pair, pair, pair, pl.BlockSpec((1, 8, rows), lambda p, m: (p, 0, 0))]
    specs += [pl.BlockSpec(form.shape, lambda p, m: (0, 0)) for form in forms]
    return pair, specs + [table, table]


def attend_back_first(meta, offsets, queries, outputs, grads, lse, forms, cos, sin):
    length = forms[0].shape[0]
    pair, specs = back_specs(queries, forms)
    whole = pl.BlockSpec((length, 128), lambda p, m: (0, 0))

    def kernel(*refs):
        dk_ref, dv_ref = refs[-2:]

        @pl.when(pl.program_id(0) == 0)
        def _():
            dk_ref[...] = jnp.zeros(dk_ref.shape, F32)
            dv_ref[...] = jnp.zeros(dv_ref.shape, F32)

        bwd_kernel(offsets, *refs)

    return pl.pallas_call(
        kernel,
        grid_spec=pltpu.PrefetchScalarGridSpec(
            num_scalar_prefetch=1,
            grid=(queries.shape[1] // 128,),
            in_specs=specs,
            out_specs=[pair, whole, whole],
        ),
        out_shape=[
            jax.ShapeDtypeStruct(queries.shape, BF16),
            jax.ShapeDtypeStruct((length, 128), F32),
            jax.ShapeDtypeStruct((length, 128), F32),
        ],
        compiler_params=pltpu.CompilerParams(vmem_limit_bytes=58 * 2**20),
        cost_estimate=LIGHT,
        name="attend_back_first",
    )(meta, queries, outputs, grads, lse, *forms, cos, sin)


def attend_back_last(
    meta, offsets, queries, outputs, grads, lse, forms, cos, sin, dk, dv, all_cos, all_sin
):
    length = forms[0].shape[0]
    near = length // 2
    pair, specs = back_specs(queries, forms)
    whole = pl.BlockSpec((length, 128), lambda p, m: (0, 0))
    half = pl.BlockSpec((near, 128), lambda p, m: (0, 0))

    def kernel(*refs):
        dk_in, dv_in, cos_ref, sin_ref, dq_ref, near_ref, far_ref, dk_ref, dv_ref = refs[-9:]

        @pl.when(pl.program_id(0) == 0)
        def _():
            dk_ref[...] = dk_in[...]
            dv_ref[...] = dv_in[...]

        bwd_kernel(offsets, *refs[:-9], dq_ref, dk_ref, dv_ref)

        @pl.when(pl.program_id(0) == pl.num_programs(0) - 1)
        def _():
            block = min(512, near)
            for first in range(0, length, block):
                here = slice(first, first + block)
                dk_block, dv_block = dk_ref[here, :], dv_ref[here, :]
                dk_block = dk_block + pltpu.roll(dk_block, HD, 1)
                dv_block = dv_block + pltpu.roll(dv_block, HD, 1)
                left = lax.broadcasted_iota(jnp.int32, dk_block.shape, 1) < HD
                both = jnp.where(
                    left, turn(dk_block, cos_ref[here, :], -sin_ref[here, :]), dv_block
                )
                if first < near:
                    near_ref[here, :] = both
                else:
                    far_ref[first - near : first - near + block, :] = both.astype(BF16)

    return pl.pallas_call(
        kernel,
        grid_spec=pltpu.PrefetchScalarGridSpec(
            num_scalar_prefetch=1,
            grid=(queries.shape[1] // 128,),
            in_specs=specs + [whole] * 4,
            out_specs=[pair, half, half],
            scratch_shapes=[pltpu.VMEM((length, 128), F32), pltpu.VMEM((length, 128), F32)],
        ),
        out_shape=[
            jax.ShapeDtypeStruct(queries.shape, BF16),
            jax.ShapeDtypeStruct((near, 128), F32),
            jax.ShapeDtypeStruct((near, 128), BF16),
        ],
        compiler_params=pltpu.CompilerParams(vmem_limit_bytes=60 * 2**20),
        cost_estimate=LIGHT,
        name="attend_back_last",
    )(meta, queries, outputs, grads, lse, *forms, cos, sin, dk, dv, all_cos, all_sin)


def feed_kernel(
    gathered_ref,
    tokens_ref,
    cotangent_ref,
    gain_ref,
    output_weight,
    gate_weight,
    up_weight,
    down_weight,
    *refs,
):
    middle_ref, normed_ref, hidden_ref, gates_ref, down_ref, grad_ref = refs[-6:]
    middle = tokens_ref[...].astype(F32)
    for source in range(gathered_ref.shape[0]):
        middle = middle + lax.dot_general(
            gathered_ref[source], output_weight[source], NT, preferred_element_type=F32
        )
    middle_ref[...] = middle
    inverse = lax.rsqrt(jnp.mean(middle * middle, axis=-1, keepdims=True) + EPSILON)
    normed = (middle * inverse * gain_ref[...]).astype(BF16)
    normed_ref[...] = normed
    gate = jnp.dot(normed, gate_weight[...], preferred_element_type=F32)
    up = jnp.dot(normed, up_weight[...], preferred_element_type=F32)
    grad_hidden = jnp.dot(cotangent_ref[...], down_weight[...], preferred_element_type=F32)
    sigmoid = jax.nn.sigmoid(gate)
    hidden = (gate * sigmoid * up).astype(BF16)
    hidden_ref[...] = hidden
    grad_gate = (grad_hidden * up * sigmoid * (1.0 + gate * (1.0 - sigmoid))).astype(BF16)
    grad_up = (grad_hidden * gate * sigmoid).astype(BF16)
    units = hidden.shape[1]
    gates_ref[:, :units] = grad_gate
    gates_ref[:, units:] = grad_up
    down_ref[...] = lax.dot_general(
        hidden, down_weight[...], NT, preferred_element_type=F32
    ).astype(BF16)
    grad_ref[...] = (
        lax.dot_general(grad_gate, gate_weight[...], NT, preferred_element_type=F32)
        + lax.dot_general(grad_up, up_weight[...], NT, preferred_element_type=F32)
    ).astype(BF16)


def feed_forward(c, gathered, tokens, cotangent, gain, output_weight, weights, earlier):
    rows, width = tokens.shape
    units = weights[0].shape[1]
    block = min(256, rows // 4)
    quarter = rows // 4 // block
    if c:
        place = lambda i: (i + quarter, 0)
    else:
        place = lambda i: (jnp.where(i < quarter, i, i + 2 * quarter), 0)
    once = pl.Buffered(1)

    def natural(columns):
        return pl.BlockSpec((block, columns), place)

    def whole(array):
        zeros = (0,) * array.ndim
        return pl.BlockSpec(array.shape, lambda i: zeros, pipeline_mode=once)

    shapes = [
        jax.ShapeDtypeStruct((rows, width), F32),
        jax.ShapeDtypeStruct((rows, width), BF16),
        jax.ShapeDtypeStruct((rows, units), BF16),
        jax.ShapeDtypeStruct((rows, 2 * units), BF16),
        jax.ShapeDtypeStruct((rows, width), BF16),
    ]
    gain = gain.reshape(1, width)
    return pl.pallas_call(
        feed_kernel,
        grid=(2 * quarter,),
        in_specs=[
            pl.BlockSpec((gathered.shape[0], block, gathered.shape[2]), lambda i: (0, i, 0)),
            natural(width),
            natural(width),
            whole(gain),
            whole(output_weight),
        ]
        + [whole(weight) for weight in weights]
        + [pl.BlockSpec(memory_space=pl.ANY) for _ in earlier],
        out_specs=[natural(shape.shape[1]) for shape in shapes]
        + [pl.BlockSpec((block, width), lambda i: (i, 0))],
        out_shape=shapes + [jax.ShapeDtypeStruct((rows // 2, width), BF16)],
        input_output_aliases={8 + k: k for k in range(len(earlier))},
        compiler_params=pltpu.CompilerParams(vmem_limit_bytes=60 * 2**20),
        cost_estimate=LIGHT,
        name="feed_forward",
    )(gathered, tokens, cotangent, gain, output_weight, *weights, *earlier)


def quarter_row(row, c, half, span):
    if c:
        return half + row
    return row if row < half else row + span


def after(value, *earlier):
    return lax.optimization_barrier((value, earlier))[0]


def line_steps(size):
    return [
        (
            [(i, i + 1) for i in range(step - 1, size - 1)],
            [(i, i - 1) for i in range(1, size - step + 1)],
        )
        for step in range(1, size)
    ]


class Gather:
    def __init__(self, piece):
        self.piece = piece
        self.rights, self.lefts = [piece], [piece]
        self.hops = line_steps(lax.axis_size("tensor"))

    def step(self):
        done = len(self.rights) - 1
        if done < len(self.hops):
            to_right, to_left = self.hops[done]
            self.rights.append(lax.ppermute(self.rights[-1], "tensor", to_right))
            self.lefts.append(lax.ppermute(self.lefts[-1], "tensor", to_left))
        return self.rights[-1], self.lefts[-1]

    def held(self, pair):
        self.rights[-1], self.lefts[-1] = pair

    def collect(self, place, target):
        size = lax.axis_size("tensor")
        me = lax.axis_index("tensor")
        while len(self.rights) <= len(self.hops):
            self.step()
        target = place(target, self.piece, me)
        for step in range(1, size):
            arrived = self.rights[step] + self.lefts[size - step]
            target = place(target, arrived, lax.rem(me - step + size, size))
        return target


def send_blocks(pick, across=False):
    size = lax.axis_size("tensor")
    me = lax.axis_index("tensor")
    arrived = []
    for shift in range(size):
        block = pick(lax.rem(me + shift, size))
        if across:
            block = lax.ppermute(
                block,
                ("ctx", "tensor"),
                [
                    (c * size + i, (1 - c) * size + (i + shift) % size)
                    for c in range(2)
                    for i in range(size)
                ],
            )
        elif shift:
            block = lax.ppermute(block, "tensor", [(i, (i + shift) % size) for i in range(size)])
        arrived.append(block)
    return tuple(arrived)


def stack_blocks(arrived):
    size = len(arrived)
    me = lax.axis_index("tensor")
    out = jnp.zeros((size, *arrived[0].shape), arrived[0].dtype)
    for shift, block in enumerate(arrived):
        out = lax.dynamic_update_index_in_dim(out, block, lax.rem(me - shift + size, size), 0)
    return out


def pairwise(value, axis, step):
    size = lax.axis_size(axis)
    return value + lax.ppermute(value, axis, [(i, i ^ step) for i in range(size)])


def pair_steps():
    steps = []
    for axis in ("dp", "ctx", "tensor"):
        step = 1
        while step < lax.axis_size(axis):
            steps.append((axis, step))
            step *= 2
    return steps


def hold(*values):
    return lax.optimization_barrier(values)


def in_order(mine, other, upper):
    return jnp.concatenate(
        [jnp.where(upper == 0, mine, other), jnp.where(upper == 0, other, mine)], axis=1
    )


def rows_part(weight, index, count):
    rows = weight.shape[0] // count
    return lax.dynamic_slice_in_dim(weight, index * rows, rows, 0)


def by_source(target, piece, source):
    return lax.dynamic_update_index_in_dim(target, piece, source, 0)


def dot(a, b):
    return jnp.dot(a, b, preferred_element_type=F32)


def dot_t(a, b):
    return jnp.einsum("rf,df->rd", a, b, preferred_element_type=F32)


def t_dot(a, b):
    return jnp.einsum("rd,rf->df", a, b, preferred_element_type=F32)


def body(
    tokens,
    cotangent,
    span_order,
    norm_attn,
    w_query,
    w_key,
    w_value,
    w_output,
    norm_mlp,
    w_gate,
    w_up,
    w_down,
):
    tok_rows, width = tokens.shape
    groups = lax.axis_size("tensor")
    member = lax.axis_index("tensor")
    n_ctx = lax.axis_size("ctx")
    assert n_ctx == 2
    ctx_index = lax.axis_index("ctx")
    features = w_query.shape[1]
    kv_count = w_key.shape[1] // HD
    kv_pick = np.arange(groups) * kv_count // groups
    kv_start = member * kv_count // groups * HD
    key_weight = lax.dynamic_slice_in_dim(w_key, kv_start, HD, 1)
    value_weight = lax.dynamic_slice_in_dim(w_value, kv_start, HD, 1)
    span = tok_rows // 2
    half = span // 2
    share = span // groups
    over = [(0, 1), (1, 0)]
    chunks = range(2)

    def chunk(array, c):
        if c:
            return array[half : half + span]
        return jnp.concatenate([array[:half], array[half + span :]], axis=0)

    def natural(first, second):
        return jnp.concatenate([first[:half], second, first[half:]], axis=0)

    order = jnp.roll(span_order[0], -2 * ctx_index)
    places = jnp.arange(4, dtype=jnp.int32)
    slot_of = jnp.sum(
        jnp.where(order[None, :] == places[:, None], places[None, :], 0), axis=1, dtype=jnp.int32
    )
    metas = [jnp.concatenate([order[2 * c : 2 * c + 2], slot_of]) for c in chunks]
    offsets = [(0, half), (half, 0)]

    positions = (order[:, None] * span + jnp.arange(span, dtype=jnp.int32)[None, :]).reshape(-1)
    frequency = 10000.0 ** (-jnp.arange(HD // 2, dtype=F32) / (HD // 2))

    def table(positions):
        angles = frequency[:, None] * positions.astype(F32)[None, :]
        cos_part, sin_part = hold(jnp.cos(angles), jnp.sin(angles))
        cos_part, sin_part = cos_part.T, sin_part.T
        return (
            jnp.concatenate([cos_part] * 4, axis=1),
            jnp.concatenate([-sin_part, sin_part] * 2, axis=1),
        )

    cos_near, sin_near = table(positions[:tok_rows])

    upper = lax.axis_index("dp") % 2
    half_output = lax.all_gather(rows_part(w_output, upper, 2), "tensor", axis=0, tiled=False)
    beside = [(i, i ^ 1) for i in range(lax.axis_size("dp"))]

    kv_own, queries, normed = project(
        tokens,
        norm_attn,
        jnp.concatenate([key_weight, value_weight], axis=1),
        w_query,
        cos_near,
        sin_near,
    )
    kv_other = lax.ppermute(kv_own, "ctx", over)
    kv_own, kv_other, sent, kept, normed = hold(
        kv_own, kv_other, chunk(queries, 1), chunk(queries, 0), normed
    )
    length = 2 * tok_rows

    foreign = lax.ppermute(sent, "ctx", over)
    first, first_log, *forms = attend_first(metas[0], offsets[0], kept, kv_own, kv_other)
    first, first_log, foreign, forms = hold(first, first_log, foreign, forms)
    *forms, values_t = forms
    first_whole = lax.all_gather(first, "tensor", axis=0, tiled=False)

    other_output = lax.ppermute(half_output, "dp", beside)
    second, second_log = attend(metas[1], offsets[1], foreign, forms[0], forms[1], values_t)
    second, second_log, other_output, half_output = hold(
        second, second_log, other_output, half_output
    )
    output_whole = in_order(half_output, other_output, upper)

    cos_far, sin_far = table(after(positions[tok_rows:], second))
    cos_pair = jnp.concatenate([cos_near, cos_far], axis=0)
    sin_pair = jnp.concatenate([sin_near, sin_far], axis=0)
    tables = [(chunk(cos_near, 0), chunk(sin_near, 0)), (chunk(cos_far, 1), chunk(sin_far, 1))]
    second_home = lax.ppermute(second, "ctx", over)
    second_home, first_whole, output_whole, tables, cos_pair, sin_pair = hold(
        second_home, first_whole, output_whole, tables, cos_pair, sin_pair
    )
    second_whole = lax.all_gather(second_home, "tensor", axis=0, tiled=False)
    queries = [kept, foreign]
    attention = [first, second]
    log_totals = [first_log, second_log]

    row_of = [
        jnp.asarray([quarter_row(i * share, c, half, span) for i in range(groups)], jnp.int32)
        for c in chunks
    ]

    def own_rows(array, c):
        return lax.dynamic_slice_in_dim(array, row_of[c][member], share, 0)

    def to_attention(c, middle, grad_share):
        middle = own_rows(middle, c)
        inverse_two = lax.rsqrt(jnp.mean(middle * middle, axis=-1, keepdims=True) + EPSILON)
        grad_normed_mlp = grad_share.astype(F32)
        gain = jnp.sum(grad_normed_mlp * middle * inverse_two, axis=0)
        scaled_two = grad_normed_mlp * norm_mlp
        grad_middle = (
            own_rows(cotangent, c).astype(F32)
            + inverse_two * scaled_two
            - middle * inverse_two**3 * jnp.mean(scaled_two * middle, axis=-1, keepdims=True)
        )
        grad_low = grad_middle.astype(BF16)
        blocks = jnp.einsum(
            "rd,tdq->trq", grad_low, output_whole, preferred_element_type=F32
        ).astype(BF16)
        return gain, grad_middle, grad_low, blocks

    def block_of(blocks):
        return lambda j: lax.dynamic_index_in_dim(blocks, j, 0, keepdims=False)

    def rows_of(array):
        return lambda j: lax.dynamic_slice_in_dim(array, j * share, share, 0)

    def line_sum(array):
        return lax.psum_scatter(array, "tensor", scatter_dimension=0, tiled=True)

    def plane_sum(gradient):
        return lax.psum_scatter(
            gradient.astype(BF16), ("dp", "ctx"), scatter_dimension=0, tiled=True
        )

    query_gather = Gather(after(rows_part(w_query, 2 * upper + ctx_index, 4), first_whole))
    hop = query_gather.step()
    weights = (w_gate, w_up, w_down)
    fixed = (tokens, cotangent, norm_mlp, output_whole, weights)
    *fed, grad_first = feed_forward(0, first_whole, *fixed, ())
    fed, grad_first, second_whole, hop = hold(fed, grad_first, second_whole, hop)
    query_gather.held(hop)

    share_first = line_sum(grad_first)
    hop = query_gather.step()
    *fed, grad_second = feed_forward(1, second_whole, *fixed, fed)
    fed, grad_second, hop = hold(fed, grad_second, hop)
    query_gather.held(hop)
    middle, normed_mlp, hidden, gates, mlp_part = fed

    share_second = line_sum(grad_second)
    hop = query_gather.step()
    w_gates = t_dot(normed_mlp, gates).astype(BF16)
    w_gates, hop = hold(w_gates, hop)
    query_gather.held(hop)
    mlp_share = line_sum(after(mlp_part, w_gates))

    query_part = query_gather.collect(
        by_source, jnp.zeros((groups, w_query.shape[0] // 4, features), BF16)
    )
    part_over = lax.ppermute(query_part, "ctx", over)
    w_downs = t_dot(after(cotangent, w_gates), hidden).astype(BF16)
    w_downs, share_first, query_part, part_over = hold(
        w_downs, share_first, query_part, part_over
    )

    gain_first, middle_first, low_first, blocks = to_attention(0, middle, share_first)
    query_half = in_order(query_part, part_over, ctx_index)
    gain_first, middle_first, low_first, blocks, query_half = hold(
        gain_first, middle_first, low_first, blocks, query_half
    )

    came_first = send_blocks(block_of(blocks))
    other_half = lax.ppermute(query_half, "dp", beside)
    attention_rows = jnp.concatenate(
        [
            lax.dynamic_slice_in_dim(whole, member * share, share, 1)
            for whole in (first_whole, second_whole)
        ],
        axis=1,
    )
    attention_rows = jnp.swapaxes(attention_rows, 0, 1).reshape(2 * share, groups * features)
    n_part = tok_rows // groups
    middle_own = lax.dynamic_slice_in_dim(middle, member * n_part, n_part, 0)
    came_first, attention_rows, middle_own, query_half, other_half = hold(
        came_first, attention_rows, middle_own, query_half, other_half
    )
    query_whole = in_order(query_half, other_half, upper)
    grads_first = stack_blocks(came_first).reshape(span, features)
    query_whole, grads_first, share_second = hold(query_whole, grads_first, share_second)

    gain_second, middle_second, low_second, blocks = to_attention(1, middle, share_second)
    gain_second, middle_second, low_second, blocks = hold(
        gain_second, middle_second, low_second, blocks
    )

    def back_arguments(c, grads):
        return metas[c], offsets[c], queries[c], attention[c], grads, log_totals[c], forms, *tables[c]

    came_second = send_blocks(block_of(blocks), across=True)
    dq_first, dk, dv = attend_back_first(*back_arguments(0, grads_first))
    dq_first, dk, dv, came_second = hold(dq_first, dk, dv, came_second)

    rows_first = send_blocks(rows_of(dq_first))
    grads_second = stack_blocks(came_second).reshape(span, features)
    dq_second, kv_near, kv_far = attend_back_last(
        *back_arguments(1, grads_second), dk, dv, cos_pair, sin_pair
    )
    dq_second, kv_near, kv_far, rows_first, mlp_share = hold(
        dq_second, kv_near, kv_far, rows_first, mlp_share
    )
    gate_up_grad = plane_sum(after(w_gates, mlp_share))

    kv_sent = lax.ppermute(kv_far, "ctx", over)
    rows_second = send_blocks(rows_of(dq_second), across=True)
    dq_home = lax.ppermute(dq_second, "ctx", over)
    first_part = jnp.einsum(
        "trq,tdq->rd", stack_blocks(rows_first), query_whole, preferred_element_type=F32
    )
    kv_near, kv_sent, rows_second, first_part, dq_home = hold(
        kv_near, kv_sent, rows_second, first_part, dq_home
    )
    mixed_gather = Gather((middle_own + mlp_share.astype(F32)).astype(BF16))
    mixed_hop = mixed_gather.step()
    grad_kv_raw = (kv_near + kv_sent.astype(F32)).astype(BF16)
    kv_rows = send_blocks(
        lambda j: jnp.concatenate(
            [lax.dynamic_slice_in_dim(grad_kv_raw, row_of[c][j], share, 0) for c in chunks], axis=0
        )
    )
    second_part = jnp.einsum(
        "trq,tdq->rd", stack_blocks(rows_second), query_whole, preferred_element_type=F32
    )
    first_part, second_part, kv_rows, grad_kv_raw = hold(
        first_part, second_part, kv_rows, grad_kv_raw
    )
    kv_whole = jnp.stack(
        [
            jnp.concatenate(
                [w_key[:, h * HD : (h + 1) * HD], w_value[:, h * HD : (h + 1) * HD]], axis=1
            )
            for h in kv_pick
        ]
    )

    grad_normed = jnp.concatenate([first_part, second_part], axis=0) + jnp.einsum(
        "trq,tdq->rd", stack_blocks(kv_rows), kv_whole, preferred_element_type=F32
    )
    inputs_own = jnp.concatenate([own_rows(tokens, c) for c in chunks], axis=0).astype(F32)
    inverse_own = lax.rsqrt(jnp.mean(inputs_own * inputs_own, axis=-1, keepdims=True) + EPSILON)
    attn_gain = jnp.sum(grad_normed * inputs_own * inverse_own, axis=0)
    scaled_one = grad_normed * norm_attn
    grad_inputs = (
        jnp.concatenate([middle_first, middle_second], axis=0)
        + inverse_own * scaled_one
        - inputs_own * inverse_own**3 * jnp.mean(scaled_one * inputs_own, axis=-1, keepdims=True)
    ).astype(BF16)

    def put_rows(target, piece, source):
        for c in chunks:
            target = lax.dynamic_update_slice_in_dim(
                target, piece[c * share : (c + 1) * share], row_of[c][source], 0
            )
        return target

    gains = jnp.stack([attn_gain, gain_first + gain_second])
    grad_inputs, gains, low_first = hold(grad_inputs, gains, low_first)

    tokens_gather = Gather(grad_inputs)
    hop = tokens_gather.step()
    w_outs = t_dot(jnp.concatenate([low_first, low_second], axis=0), attention_rows).astype(BF16)
    query_kv = t_dot(
        normed, jnp.concatenate([natural(dq_first, dq_home), grad_kv_raw], axis=1)
    ).astype(BF16)
    rest = jnp.concatenate([w_downs, w_outs, query_kv], axis=1)
    hop, mixed_hop, rest, gate_up_grad = hold(hop, mixed_hop, rest, gate_up_grad)
    tokens_gather.held(hop)
    mixed_gather.held(mixed_hop)
    rest = plane_sum(rest)

    steps = pair_steps()
    hop, mixed_hop = tokens_gather.step(), mixed_gather.step()
    for axis, step in steps[:2]:
        gains = pairwise(gains, axis, step)
    hop, mixed_hop, gains = hold(hop, mixed_hop, gains)
    tokens_gather.held(hop)
    mixed_gather.held(mixed_hop)

    hop, mixed_hop = tokens_gather.step(), mixed_gather.step()
    for axis, step in steps[2:]:
        gains = pairwise(gains, axis, step)
    hop, mixed_hop, gains, rest = hold(hop, mixed_hop, gains, rest)
    tokens_gather.held(hop)
    mixed_gather.held(mixed_hop)

    tokens_grad = tokens_gather.collect(put_rows, jnp.zeros((tok_rows, width), BF16))
    hidden_units = w_down.shape[1]
    down_grad = rest[:, :hidden_units]
    rest = rest[:, hidden_units:]
    output_plane, query_kv = rest[:, : groups * features], rest[:, groups * features :]
    query_grad, kv_plane = query_kv[:, :features].astype(F32), query_kv[:, features:]
    output_rows = send_blocks(
        lambda j: lax.dynamic_slice_in_dim(output_plane, j * features, features, 1)
    )
    kv_share = query_kv.shape[0] // groups
    kv_blocks = send_blocks(
        lambda j: lax.dynamic_slice_in_dim(kv_plane, j * kv_share, kv_share, 0)
    )
    mixed = mixed_gather.collect(
        lambda target, piece, source: lax.dynamic_update_slice_in_dim(
            target, piece, source * n_part, 0
        ),
        jnp.zeros((tok_rows, width), BF16),
    )
    output_grad = jnp.sum(stack_blocks(output_rows).astype(F32), axis=0)

    kv_blocks = stack_blocks(kv_blocks).astype(F32)
    key_heads, value_heads = [], []
    for h in range(kv_count):
        total = jnp.zeros((kv_share, 2 * HD), F32)
        for g in range(groups):
            if kv_pick[g] == h:
                total = total + kv_blocks[g]
        key_heads.append(total[:, :HD])
        value_heads.append(total[:, HD:])
    key_grad = jnp.concatenate(key_heads, axis=1)
    value_grad = jnp.concatenate(value_heads, axis=1)

    plane = lax.axis_size("dp") * n_ctx
    plane_index = lax.axis_index("dp") * n_ctx + ctx_index
    gains = lax.dynamic_slice_in_dim(gains, plane_index * (width // plane), width // plane, 1)
    return (
        mixed,
        tokens_grad,
        gains[0],
        query_grad,
        key_grad,
        value_grad,
        output_grad,
        gains[1],
        gate_up_grad[:, :hidden_units].astype(F32),
        gate_up_grad[:, hidden_units:].astype(F32),
        down_grad.astype(F32),
    )


def solution(mesh):
    placed = (
        P(("dp", "ctx"), None),
        P(("dp", "ctx"), None),
        P("dp", None),
        P(),
        P(None, "tensor"),
        P(),
        P(),
        P(None, "tensor"),
        P(),
        P(None, "tensor"),
        P(None, "tensor"),
        P(None, "tensor"),
    )
    return jax.shard_map(
        body,
        mesh=mesh,
        in_specs=placed,
        out_specs=(
            P(("dp", "ctx"), None),
            P(("dp", "ctx"), None),
            P(("dp", "ctx")),
            P(("dp", "ctx"), "tensor"),
            P(("dp", "ctx", "tensor"), None),
            P(("dp", "ctx", "tensor"), None),
            P(("dp", "ctx"), "tensor"),
            P(("dp", "ctx")),
            P(("dp", "ctx"), "tensor"),
            P(("dp", "ctx"), "tensor"),
            P(("dp", "ctx"), "tensor"),
        ),
        check_vma=False,
    )
```

```python
import jax
import jax.numpy as jnp
import numpy as np
from jax import lax
from jax.experimental import pallas as pl
from jax.experimental.pallas import tpu as pltpu
from jax.sharding import PartitionSpec as P

NT = (((1,), (1,)), ((), ()))
F32 = jnp.float32
BF16 = jnp.bfloat16
HD = 64
GROUP = 256
EPSILON = 1e-05
LIGHT = pl.CostEstimate(flops=1, bytes_accessed=1, transcendentals=0)


def turn(values, cos, sin):
    low = (lax.broadcasted_iota(jnp.int32, values.shape, 1) % HD) < HD // 2
    other = jnp.where(
        low, pltpu.roll(values, 128 - HD // 2, 1), pltpu.roll(values, HD // 2, 1)
    )
    return values * cos + other * sin


def project_kernel(
    tokens_ref, gain_ref, kv_weight, q_weight, cos_ref, sin_ref, kv_ref, q_ref, normed_ref
):
    inputs = tokens_ref[...].astype(F32)
    inverse = lax.rsqrt(jnp.mean(inputs * inputs, axis=-1, keepdims=True) + EPSILON)
    normed = (inputs * inverse * gain_ref[...]).astype(BF16)
    normed_ref[...] = normed
    cos, sin = cos_ref[...], sin_ref[...]
    pair = jnp.dot(normed, kv_weight[...], preferred_element_type=F32)
    is_key = lax.broadcasted_iota(jnp.int32, pair.shape, 1) < HD
    kv_ref[...] = jnp.where(is_key, turn(pair, cos, sin), pair).astype(BF16)
    raw = jnp.dot(normed, q_weight[...], preferred_element_type=F32)
    for first in range(0, q_ref.shape[1], 128):
        pair = raw[:, first : first + 128]
        q_ref[:, first : first + 128] = (turn(pair, cos, sin) * HD**-0.5).astype(BF16)


def project(tokens, gain, kv_weight, q_weight, cos, sin):
    rows, width = tokens.shape
    columns = q_weight.shape[1]
    block = 256
    return pl.pallas_call(
        project_kernel,
        grid=(rows // block,),
        in_specs=[
            pl.BlockSpec((block, width), lambda i: (i, 0)),
            pl.BlockSpec((1, width), lambda i: (0, 0)),
            pl.BlockSpec((width, 128), lambda i: (0, 0)),
            pl.BlockSpec((width, columns), lambda i: (0, 0)),
            pl.BlockSpec((block, 128), lambda i: (i, 0)),
            pl.BlockSpec((block, 128), lambda i: (i, 0)),
        ],
        out_specs=[
            pl.BlockSpec((block, 128), lambda i: (i, 0)),
            pl.BlockSpec((block, columns), lambda i: (i, 0)),
            pl.BlockSpec((block, width), lambda i: (i, 0)),
        ],
        out_shape=[
            jax.ShapeDtypeStruct((rows, 128), BF16),
            jax.ShapeDtypeStruct((rows, columns), BF16),
            jax.ShapeDtypeStruct((rows, width), BF16),
        ],
        compiler_params=pltpu.CompilerParams(vmem_limit_bytes=48 * 2**20),
        cost_estimate=LIGHT,
        name="project",
    )(tokens, gain.reshape(1, width), kv_weight, q_weight, cos, sin)


def fwd_kernel(offsets, meta, q_ref, ka_ref, kb_ref, vt_ref, o_ref, lse_ref):
    half = q_ref.shape[0] // 2
    span = 2 * half
    group = min(GROUP, half)
    pairs = q_ref.shape[1] // 128
    for part, offset in enumerate(offsets):
        at = slice(part * half, part * half + half)
        queries = [q_ref[at, p * 128 : p * 128 + 128] for p in range(pairs)]
        chains = [(p, keys_ref) for p in range(pairs) for keys_ref in (ka_ref, kb_ref)]
        seen = meta[part]
        own = pl.multiple_of(meta[2 + seen] * span, span)
        heads = []
        for p, keys_ref in chains:
            tops, sums = [], []
            for first in range(0, half, group):
                count = offset + first + group
                rows = pl.ds(own, count)
                scores = lax.dot_general(
                    keys_ref[rows, :],
                    queries[p][first : first + group],
                    NT,
                    preferred_element_type=F32,
                )
                key_at = lax.broadcasted_iota(jnp.int32, scores.shape, 0)
                row_at = lax.broadcasted_iota(jnp.int32, scores.shape, 1) + (offset + first)
                scores = jnp.where(key_at <= row_at, scores, -1e30)
                top = jnp.max(scores, axis=0, keepdims=True)
                weights = jnp.exp(scores - top).astype(BF16)
                tops.append(top)
                sums.append(jnp.dot(vt_ref[:, rows], weights, preferred_element_type=F32))
            heads += [jnp.concatenate(tops, axis=1), jnp.concatenate(sums, axis=1)]

        def step(index, carry):
            rows = pl.ds(pl.multiple_of(meta[2 + index] * span, span), span)
            out = []
            for chain, (p, keys_ref) in enumerate(chains):
                top, total = carry[2 * chain : 2 * chain + 2]
                scores = lax.dot_general(
                    keys_ref[rows, :], queries[p], NT, preferred_element_type=F32
                )
                new_top = jnp.maximum(top, jnp.max(scores, axis=0, keepdims=True))
                weights = jnp.exp(scores - new_top).astype(BF16)
                total = total * jnp.exp(top - new_top) + jnp.dot(
                    vt_ref[:, rows], weights, preferred_element_type=F32
                )
                out += [new_top, total]
            return tuple(out)

        heads = lax.fori_loop(0, seen, step, tuple(heads))
        for p in range(pairs):
            top0, total0, top1, total1 = heads[4 * p : 4 * p + 4]
            norm0, norm1 = total0[HD : HD + 1], total1[HD : HD + 1]
            o_ref[at, p * 128 : p * 128 + 128] = (
                jnp.concatenate([total0[:HD] / norm0, total1[:HD] / norm1], axis=0).T.astype(BF16)
            )
            lse_ref[p, :, at] = jnp.concatenate(
                [top0 + jnp.log(norm0), top1 + jnp.log(norm1), jnp.zeros((6, half), F32)], axis=0
            )


def spread(kv_refs, ka_ref, kb_ref, va_ref, vb_ref, kt_ref, vt_ref):
    at = 0
    for kv_ref in kv_refs:
        rows = kv_ref.shape[0]
        block = min(512, rows)
        for first in range(0, rows, block):
            here = slice(at + first, at + first + block)
            pair = kv_ref[first : first + block, :].astype(F32)
            other = pltpu.roll(pair, HD, 1)
            left = lax.broadcasted_iota(jnp.int32, pair.shape, 1) < HD
            ka_ref[here, :] = jnp.where(left, pair, 0.0).astype(BF16)
            vb_ref[here, :] = jnp.where(left, 0.0, pair).astype(BF16)
            va_ref[here, :] = jnp.where(left, other, 0.0).astype(BF16)
            kb_ref[here, :] = jnp.where(left, 0.0, other).astype(BF16)
            turned = pair.T
            kt_ref[:, here] = turned[:HD].astype(BF16)
            ones = jnp.where(lax.broadcasted_iota(jnp.int32, (16, block), 0) == 0, 1.0, 0.0)
            vt_ref[:, here] = jnp.concatenate([turned[HD:], ones], axis=0).astype(BF16)
        at += rows


def attend_cost(rows, length, width):
    return pl.CostEstimate(
        flops=8 * rows * length * width, bytes_accessed=2**23, transcendentals=0
    )


def attend_first(meta, offsets, queries, kv_own, kv_other):
    rows, width = queries.shape
    pairs = width // 128
    together = 2 if pairs % 2 == 0 else 1
    length = 2 * kv_own.shape[0]

    def whole(shape):
        return pl.BlockSpec(shape, lambda p, m: (0, 0))

    def kernel(meta, q_ref, own, other, o_ref, lse_ref, ka, kb, va, vb, kt, vt):
        @pl.when(pl.program_id(0) == 0)
        def _():
            spread((own, other), ka, kb, va, vb, kt, vt)

        fwd_kernel(offsets, meta, q_ref, ka, kb, vt, o_ref, lse_ref)

    wide = (length, 128)
    forms = [wide, wide, wide, wide, (HD, length), (HD + 16, length)]
    return pl.pallas_call(
        kernel,
        grid_spec=pltpu.PrefetchScalarGridSpec(
            num_scalar_prefetch=1,
            grid=(pairs // together,),
            in_specs=[
                pl.BlockSpec((rows, 128 * together), lambda p, m: (0, p)),
                whole(kv_own.shape),
                whole(kv_other.shape),
            ],
            out_specs=[
                pl.BlockSpec((rows, 128 * together), lambda p, m: (0, p)),
                pl.BlockSpec((together, 8, rows), lambda p, m: (p, 0, 0)),
            ]
            + [whole(form) for form in forms],
        ),
        out_shape=[
            jax.ShapeDtypeStruct((rows, width), BF16),
            jax.ShapeDtypeStruct((pairs, 8, rows), F32),
        ]
        + [jax.ShapeDtypeStruct(form, BF16) for form in forms],
        compiler_params=pltpu.CompilerParams(vmem_limit_bytes=58 * 2**20),
        cost_estimate=attend_cost(rows, length, width),
        name="attend_first",
    )(meta, queries, kv_own, kv_other)


def attend(meta, offsets, queries, keys_a, keys_b, values_t):
    rows, width = queries.shape
    pairs = width // 128
    together = 2 if pairs % 2 == 0 else 1
    length = keys_a.shape[0]
    whole = pl.BlockSpec((length, 128), lambda p, m: (0, 0))

    def kernel(*refs):
        fwd_kernel(offsets, *refs)

    return pl.pallas_call(
        kernel,
        grid_spec=pltpu.PrefetchScalarGridSpec(
            num_scalar_prefetch=1,
            grid=(pairs // together,),
            in_specs=[
                pl.BlockSpec((rows, 128 * together), lambda p, m: (0, p)),
                whole,
                whole,
                pl.BlockSpec(values_t.shape, lambda p, m: (0, 0)),
            ],
            out_specs=[
                pl.BlockSpec((rows, 128 * together), lambda p, m: (0, p)),
                pl.BlockSpec((together, 8, rows), lambda p, m: (p, 0, 0)),
            ],
        ),
        out_shape=[
            jax.ShapeDtypeStruct((rows, width), BF16),
            jax.ShapeDtypeStruct((pairs, 8, rows), F32),
        ],
        compiler_params=pltpu.CompilerParams(vmem_limit_bytes=58 * 2**20),
        cost_estimate=attend_cost(rows, length, width),
        name="attend",
    )(meta, queries, keys_a, keys_b, values_t)


def bwd_kernel(
    offsets,
    meta,
    q_ref,
    o_ref,
    g_ref,
    lse_ref,
    ka_ref,
    kb_ref,
    va_ref,
    vb_ref,
    kt_ref,
    cos_ref,
    sin_ref,
    dq_ref,
    dk_ref,
    dv_ref,
):
    half = q_ref.shape[0] // 2
    span = 2 * half
    group = min(GROUP, half)

    for part, offset in enumerate(offsets):
        at = slice(part * half, part * half + half)
        queries, grads = q_ref[at, :], g_ref[at, :]
        left = lax.broadcasted_iota(jnp.int32, (half, 128), 1) < HD
        products = (grads.astype(F32) * o_ref[at, :].astype(F32)).T
        zero = jnp.zeros_like(queries)
        sides = []
        for side, (keys_ref, values_ref) in enumerate(((ka_ref, va_ref), (kb_ref, vb_ref))):
            mine = left if side == 0 else jnp.logical_not(left)
            delta = jnp.sum(products[side * HD : side * HD + HD], axis=0, keepdims=True)
            sides.append(
                (
                    keys_ref,
                    values_ref,
                    jnp.where(mine, queries, zero),
                    jnp.where(mine, grads, zero),
                    lse_ref[0, side : side + 1, at],
                    delta,
                )
            )

        def block(rows, first, count, masked):
            cut = slice(first, first + count)
            dqs = []
            dk_add = dv_add = None
            for keys_ref, values_ref, q_mine, g_mine, lse, delta in sides:
                scores = lax.dot_general(
                    keys_ref[rows, :], queries[cut], NT, preferred_element_type=F32
                )
                probs = jnp.exp(scores - lse[:, cut])
                if masked:
                    key_at = lax.broadcasted_iota(jnp.int32, scores.shape, 0)
                    row_at = lax.broadcasted_iota(jnp.int32, scores.shape, 1) + (offset + first)
                    probs = jnp.where(key_at <= row_at, probs, 0.0)
                grad_probs = lax.dot_general(
                    values_ref[rows, :], grads[cut], NT, preferred_element_type=F32
                )
                grad_scores = (probs * (grad_probs - delta[:, cut])).astype(BF16)
                dv_new = jnp.dot(probs.astype(BF16), g_mine[cut], preferred_element_type=F32)
                dk_new = jnp.dot(grad_scores, q_mine[cut], preferred_element_type=F32)
                dv_add = dv_new if dv_add is None else dv_add + dv_new
                dk_add = dk_new if dk_add is None else dk_add + dk_new
                dqs.append(jnp.dot(kt_ref[:, rows], grad_scores, preferred_element_type=F32))
            dv_ref[rows, :] += dv_add
            dk_ref[rows, :] += dk_add
            return jnp.concatenate(dqs, axis=0)

        own = pl.multiple_of(meta[2 + meta[part]] * span, span)
        start = jnp.concatenate(
            [
                block(pl.ds(own, offset + first + group), first, group, True)
                for first in range(0, half, group)
            ],
            axis=1,
        )

        def step(index, total):
            rows = pl.ds(pl.multiple_of(meta[2 + index] * span, span), span)
            return total + block(rows, 0, half, False)

        dq = lax.fori_loop(0, meta[part], step, start).T * (HD**-0.5)
        dq_ref[at, :] = turn(dq, cos_ref[at, :], -sin_ref[at, :]).astype(BF16)


def back_specs(queries, forms):
    rows, width = queries.shape
    pair = pl.BlockSpec((rows, 128), lambda p, m: (0, p))
    table = pl.BlockSpec((rows, 128), lambda p, m: (0, 0))
    specs = [pair, pair, pair, pl.BlockSpec((1, 8, rows), lambda p, m: (p, 0, 0))]
    specs += [pl.BlockSpec(form.shape, lambda p, m: (0, 0)) for form in forms]
    return pair, specs + [table, table]


def attend_back_first(meta, offsets, queries, outputs, grads, lse, forms, cos, sin):
    length = forms[0].shape[0]
    pair, specs = back_specs(queries, forms)
    whole = pl.BlockSpec((length, 128), lambda p, m: (0, 0))

    def kernel(*refs):
        dk_ref, dv_ref = refs[-2:]

        @pl.when(pl.program_id(0) == 0)
        def _():
            dk_ref[...] = jnp.zeros(dk_ref.shape, F32)
            dv_ref[...] = jnp.zeros(dv_ref.shape, F32)

        bwd_kernel(offsets, *refs)

    return pl.pallas_call(
        kernel,
        grid_spec=pltpu.PrefetchScalarGridSpec(
            num_scalar_prefetch=1,
            grid=(queries.shape[1] // 128,),
            in_specs=specs,
            out_specs=[pair, whole, whole],
        ),
        out_shape=[
            jax.ShapeDtypeStruct(queries.shape, BF16),
            jax.ShapeDtypeStruct((length, 128), F32),
            jax.ShapeDtypeStruct((length, 128), F32),
        ],
        compiler_params=pltpu.CompilerParams(vmem_limit_bytes=58 * 2**20),
        cost_estimate=LIGHT,
        name="attend_back_first",
    )(meta, queries, outputs, grads, lse, *forms, cos, sin)


def attend_back_last(
    meta, offsets, queries, outputs, grads, lse, forms, cos, sin, dk, dv, all_cos, all_sin
):
    length = forms[0].shape[0]
    near = length // 2
    pair, specs = back_specs(queries, forms)
    whole = pl.BlockSpec((length, 128), lambda p, m: (0, 0))
    half = pl.BlockSpec((near, 128), lambda p, m: (0, 0))

    def kernel(*refs):
        dk_in, dv_in, cos_ref, sin_ref, dq_ref, near_ref, far_ref, dk_ref, dv_ref = refs[-9:]

        @pl.when(pl.program_id(0) == 0)
        def _():
            dk_ref[...] = dk_in[...]
            dv_ref[...] = dv_in[...]

        bwd_kernel(offsets, *refs[:-9], dq_ref, dk_ref, dv_ref)

        @pl.when(pl.program_id(0) == pl.num_programs(0) - 1)
        def _():
            block = min(512, near)
            for first in range(0, length, block):
                here = slice(first, first + block)
                dk_block, dv_block = dk_ref[here, :], dv_ref[here, :]
                dk_block = dk_block + pltpu.roll(dk_block, HD, 1)
                dv_block = dv_block + pltpu.roll(dv_block, HD, 1)
                left = lax.broadcasted_iota(jnp.int32, dk_block.shape, 1) < HD
                both = jnp.where(
                    left, turn(dk_block, cos_ref[here, :], -sin_ref[here, :]), dv_block
                )
                if first < near:
                    near_ref[here, :] = both
                else:
                    far_ref[first - near : first - near + block, :] = both.astype(BF16)

    return pl.pallas_call(
        kernel,
        grid_spec=pltpu.PrefetchScalarGridSpec(
            num_scalar_prefetch=1,
            grid=(queries.shape[1] // 128,),
            in_specs=specs + [whole] * 4,
            out_specs=[pair, half, half],
            scratch_shapes=[pltpu.VMEM((length, 128), F32), pltpu.VMEM((length, 128), F32)],
        ),
        out_shape=[
            jax.ShapeDtypeStruct(queries.shape, BF16),
            jax.ShapeDtypeStruct((near, 128), F32),
            jax.ShapeDtypeStruct((near, 128), BF16),
        ],
        compiler_params=pltpu.CompilerParams(vmem_limit_bytes=60 * 2**20),
        cost_estimate=LIGHT,
        name="attend_back_last",
    )(meta, queries, outputs, grads, lse, *forms, cos, sin, dk, dv, all_cos, all_sin)


def feed_kernel(
    gathered_ref,
    tokens_ref,
    cotangent_ref,
    gain_ref,
    output_weight,
    gate_weight,
    up_weight,
    down_weight,
    *refs,
):
    middle_ref, normed_ref, hidden_ref, gates_ref, down_ref, grad_ref = refs[-6:]
    middle = tokens_ref[...].astype(F32)
    for source in range(gathered_ref.shape[0]):
        middle = middle + lax.dot_general(
            gathered_ref[source], output_weight[source], NT, preferred_element_type=F32
        )
    middle_ref[...] = middle
    inverse = lax.rsqrt(jnp.mean(middle * middle, axis=-1, keepdims=True) + EPSILON)
    normed = (middle * inverse * gain_ref[...]).astype(BF16)
    normed_ref[...] = normed
    gate = jnp.dot(normed, gate_weight[...], preferred_element_type=F32)
    up = jnp.dot(normed, up_weight[...], preferred_element_type=F32)
    grad_hidden = jnp.dot(cotangent_ref[...], down_weight[...], preferred_element_type=F32)
    sigmoid = jax.nn.sigmoid(gate)
    hidden = (gate * sigmoid * up).astype(BF16)
    hidden_ref[...] = hidden
    grad_gate = (grad_hidden * up * sigmoid * (1.0 + gate * (1.0 - sigmoid))).astype(BF16)
    grad_up = (grad_hidden * gate * sigmoid).astype(BF16)
    units = hidden.shape[1]
    gates_ref[:, :units] = grad_gate
    gates_ref[:, units:] = grad_up
    down_ref[...] = lax.dot_general(
        hidden, down_weight[...], NT, preferred_element_type=F32
    ).astype(BF16)
    grad_ref[...] = (
        lax.dot_general(grad_gate, gate_weight[...], NT, preferred_element_type=F32)
        + lax.dot_general(grad_up, up_weight[...], NT, preferred_element_type=F32)
    ).astype(BF16)


def feed_forward(c, gathered, tokens, cotangent, gain, output_weight, weights, earlier):
    rows, width = tokens.shape
    units = weights[0].shape[1]
    block = min(256, rows // 4)
    quarter = rows // 4 // block
    if c:
        place = lambda i: (i + quarter, 0)
    else:
        place = lambda i: (jnp.where(i < quarter, i, i + 2 * quarter), 0)
    once = pl.Buffered(1)

    def natural(columns):
        return pl.BlockSpec((block, columns), place)

    def whole(array):
        zeros = (0,) * array.ndim
        return pl.BlockSpec(array.shape, lambda i: zeros, pipeline_mode=once)

    shapes = [
        jax.ShapeDtypeStruct((rows, width), F32),
        jax.ShapeDtypeStruct((rows, width), BF16),
        jax.ShapeDtypeStruct((rows, units), BF16),
        jax.ShapeDtypeStruct((rows, 2 * units), BF16),
        jax.ShapeDtypeStruct((rows, width), BF16),
    ]
    gain = gain.reshape(1, width)
    return pl.pallas_call(
        feed_kernel,
        grid=(2 * quarter,),
        in_specs=[
            pl.BlockSpec((gathered.shape[0], block, gathered.shape[2]), lambda i: (0, i, 0)),
            natural(width),
            natural(width),
            whole(gain),
            whole(output_weight),
        ]
        + [whole(weight) for weight in weights]
        + [pl.BlockSpec(memory_space=pl.ANY) for _ in earlier],
        out_specs=[natural(shape.shape[1]) for shape in shapes]
        + [pl.BlockSpec((block, width), lambda i: (i, 0))],
        out_shape=shapes + [jax.ShapeDtypeStruct((rows // 2, width), BF16)],
        input_output_aliases={8 + k: k for k in range(len(earlier))},
        compiler_params=pltpu.CompilerParams(vmem_limit_bytes=60 * 2**20),
        cost_estimate=LIGHT,
        name="feed_forward",
    )(gathered, tokens, cotangent, gain, output_weight, *weights, *earlier)


def join_kernel(order, rows_ref, near_ref, far_ref, out_ref):
    piece = pl.program_id(0)

    def total(weight_ref):
        result = None
        for source in range(rows_ref.shape[0]):
            part = lax.dot_general(
                rows_ref[source], weight_ref[0, source], NT, preferred_element_type=F32
            )
            result = part if result is None else result + part
        out_ref[...] = result

    @pl.when(piece < 2)
    def _():
        total(near_ref)

    @pl.when(piece >= 2)
    def _():
        total(far_ref)


def join(order, rows, near, far):
    size, count, features = rows.shape
    columns = near.shape[2]
    return pl.pallas_call(
        join_kernel,
        grid_spec=pltpu.PrefetchScalarGridSpec(
            num_scalar_prefetch=1,
            grid=(4,),
            in_specs=[
                pl.BlockSpec(rows.shape, lambda p, order: (0, 0, 0)),
                pl.BlockSpec(
                    (1, size, columns, features), lambda p, order: (jnp.minimum(p, 1), 0, 0, 0)
                ),
                pl.BlockSpec(
                    (1, size, columns, features), lambda p, order: (jnp.maximum(p - 2, 0), 0, 0, 0)
                ),
            ],
            out_specs=pl.BlockSpec((count, columns), lambda p, order: (0, order[p])),
        ),
        out_shape=jax.ShapeDtypeStruct((count, 4 * columns), F32),
        compiler_params=pltpu.CompilerParams(vmem_limit_bytes=32 * 2**20),
        cost_estimate=LIGHT,
        name="join",
    )(order, rows, near, far)


def arrange_kernel(order, near_ref, far_ref, out_ref):
    piece = pl.program_id(0)

    @pl.when(piece < 2)
    def _():
        out_ref[...] = near_ref[0]

    @pl.when(piece >= 2)
    def _():
        out_ref[...] = far_ref[0]


def arrange(order, near, far):
    size, rows, features = near.shape[1:]
    return pl.pallas_call(
        arrange_kernel,
        grid_spec=pltpu.PrefetchScalarGridSpec(
            num_scalar_prefetch=1,
            grid=(4,),
            in_specs=[
                pl.BlockSpec(
                    (1, size, rows, features), lambda p, order: (jnp.minimum(p, 1), 0, 0, 0)
                ),
                pl.BlockSpec(
                    (1, size, rows, features), lambda p, order: (jnp.maximum(p - 2, 0), 0, 0, 0)
                ),
            ],
            out_specs=pl.BlockSpec((size, rows, features), lambda p, order: (0, order[p], 0)),
        ),
        out_shape=jax.ShapeDtypeStruct((size, 4 * rows, features), near.dtype),
        compiler_params=pltpu.CompilerParams(vmem_limit_bytes=32 * 2**20),
        cost_estimate=LIGHT,
        name="arrange",
    )(order, near, far)


def quarter_row(row, c, half, span):
    if c:
        return half + row
    return row if row < half else row + span


def after(value, *earlier):
    return lax.optimization_barrier((value, earlier))[0]


def line_steps(size):
    return [
        (
            [(i, i + 1) for i in range(step - 1, size - 1)],
            [(i, i - 1) for i in range(1, size - step + 1)],
        )
        for step in range(1, size)
    ]


class Gather:
    def __init__(self, piece):
        self.piece = piece
        self.rights, self.lefts = [piece], [piece]
        self.hops = line_steps(lax.axis_size("tensor"))

    def step(self):
        done = len(self.rights) - 1
        if done < len(self.hops):
            to_right, to_left = self.hops[done]
            self.rights.append(lax.ppermute(self.rights[-1], "tensor", to_right))
            self.lefts.append(lax.ppermute(self.lefts[-1], "tensor", to_left))
        return self.rights[-1], self.lefts[-1]

    def held(self, pair):
        self.rights[-1], self.lefts[-1] = pair

    def place_hop(self, place, target, hop):
        size = lax.axis_size("tensor")
        me = lax.axis_index("tensor")
        if hop == 0:
            return place(target, self.piece, me)
        right, left = self.rights[hop], self.lefts[hop]
        from_left, from_right = me >= hop, me + hop < size
        if 2 * hop >= size:
            piece = jnp.where(from_left, right, jnp.where(from_right, left, self.piece))
            source = jnp.where(from_left, me - hop, jnp.where(from_right, me + hop, me))
            return place(target, piece, source)
        target = place(
            target, jnp.where(from_left, right, self.piece), jnp.where(from_left, me - hop, me)
        )
        return place(
            target, jnp.where(from_right, left, self.piece), jnp.where(from_right, me + hop, me)
        )

    def collect(self, place, target):
        while len(self.rights) <= len(self.hops):
            self.step()
        for hop in range(len(self.rights)):
            target = self.place_hop(place, target, hop)
        return target


def send_blocks(pick, across=False):
    size = lax.axis_size("tensor")
    me = lax.axis_index("tensor")
    arrived = []
    for shift in range(size):
        block = pick(lax.rem(me + shift, size))
        if across:
            block = lax.ppermute(
                block,
                ("ctx", "tensor"),
                [
                    (c * size + i, (1 - c) * size + (i + shift) % size)
                    for c in range(2)
                    for i in range(size)
                ],
            )
        elif shift:
            block = lax.ppermute(block, "tensor", [(i, (i + shift) % size) for i in range(size)])
        arrived.append(block)
    return tuple(arrived)


def stack_blocks(arrived):
    size = len(arrived)
    me = lax.axis_index("tensor")
    out = jnp.zeros((size, *arrived[0].shape), arrived[0].dtype)
    for shift, block in enumerate(arrived):
        out = lax.dynamic_update_index_in_dim(out, block, lax.rem(me - shift + size, size), 0)
    return out


def pairwise(value, axis, step):
    size = lax.axis_size(axis)
    return value + lax.ppermute(value, axis, [(i, i ^ step) for i in range(size)])


def pair_steps():
    steps = []
    for axis in ("dp", "ctx", "tensor"):
        step = 1
        while step < lax.axis_size(axis):
            steps.append((axis, step))
            step *= 2
    return steps


def hold(*values):
    return lax.optimization_barrier(values)


def rows_part(weight, index, count):
    rows = weight.shape[0] // count
    return lax.dynamic_slice_in_dim(weight, index * rows, rows, 0)


def by_source(target, piece, source):
    return lax.dynamic_update_index_in_dim(target, piece, source, 0)


def dot(a, b):
    return jnp.dot(a, b, preferred_element_type=F32)


def dot_t(a, b):
    return jnp.einsum("rf,df->rd", a, b, preferred_element_type=F32)


def t_dot(a, b):
    return jnp.einsum("rd,rf->df", a, b, preferred_element_type=F32)


def body(
    tokens,
    cotangent,
    span_order,
    norm_attn,
    w_query,
    w_key,
    w_value,
    w_output,
    norm_mlp,
    w_gate,
    w_up,
    w_down,
):
    tok_rows, width = tokens.shape
    groups = lax.axis_size("tensor")
    member = lax.axis_index("tensor")
    n_ctx = lax.axis_size("ctx")
    assert n_ctx == 2
    ctx_index = lax.axis_index("ctx")
    features = w_query.shape[1]
    kv_count = w_key.shape[1] // HD
    kv_pick = np.arange(groups) * kv_count // groups
    kv_start = member * kv_count // groups * HD
    key_weight = lax.dynamic_slice_in_dim(w_key, kv_start, HD, 1)
    value_weight = lax.dynamic_slice_in_dim(w_value, kv_start, HD, 1)
    span = tok_rows // 2
    half = span // 2
    share = span // groups
    over = [(0, 1), (1, 0)]
    chunks = range(2)

    def chunk(array, c):
        if c:
            return array[half : half + span]
        return jnp.concatenate([array[:half], array[half + span :]], axis=0)

    def natural(first, second):
        return jnp.concatenate([first[:half], second, first[half:]], axis=0)

    order = jnp.roll(span_order[0], -2 * ctx_index)
    places = jnp.arange(4, dtype=jnp.int32)
    slot_of = jnp.sum(
        jnp.where(order[None, :] == places[:, None], places[None, :], 0), axis=1, dtype=jnp.int32
    )
    metas = [jnp.concatenate([order[2 * c : 2 * c + 2], slot_of]) for c in chunks]
    offsets = [(0, half), (half, 0)]

    positions = (order[:, None] * span + jnp.arange(span, dtype=jnp.int32)[None, :]).reshape(-1)
    frequency = 10000.0 ** (-jnp.arange(HD // 2, dtype=F32) / (HD // 2))

    def table(positions):
        angles = frequency[:, None] * positions.astype(F32)[None, :]
        cos_part, sin_part = hold(jnp.cos(angles), jnp.sin(angles))
        cos_part, sin_part = cos_part.T, sin_part.T
        return (
            jnp.concatenate([cos_part] * 4, axis=1),
            jnp.concatenate([-sin_part, sin_part] * 2, axis=1),
        )

    cos_near, sin_near = table(positions[:tok_rows])

    upper = lax.axis_index("dp") % 2
    beside = [(i, i ^ 1) for i in range(lax.axis_size("dp"))]
    quarters = jnp.stack(
        [
            2 * upper + ctx_index,
            2 * upper + 1 - ctx_index,
            2 - 2 * upper + ctx_index,
            3 - 2 * upper - ctx_index,
        ]
    ).astype(jnp.int32)

    def quarter_gather(weight):
        return Gather(rows_part(weight, 2 * upper + ctx_index, 4))

    def quarter_collect(gather):
        return gather.collect(by_source, jnp.zeros((groups, *gather.piece.shape), BF16))

    output_gather = quarter_gather(w_output)
    hop = output_gather.step()

    kv_own, queries, normed = project(
        tokens,
        norm_attn,
        jnp.concatenate([key_weight, value_weight], axis=1),
        w_query,
        cos_near,
        sin_near,
    )
    kv_own, queries, normed, hop, quarters = hold(kv_own, queries, normed, hop, quarters)
    output_gather.held(hop)
    kv_other = lax.ppermute(kv_own, "ctx", over)
    hop = output_gather.step()
    kv_own, kv_other, sent, kept, normed, hop = hold(
        kv_own, kv_other, chunk(queries, 1), chunk(queries, 0), normed, hop
    )
    output_gather.held(hop)
    length = 2 * tok_rows

    foreign = lax.ppermute(sent, "ctx", over)
    hop = output_gather.step()
    first, first_log, *forms = attend_first(metas[0], offsets[0], kept, kv_own, kv_other)
    first, first_log, foreign, forms, hop = hold(first, first_log, foreign, forms, hop)
    output_gather.held(hop)
    *forms, values_t = forms
    first_whole = lax.all_gather(first, "tensor", axis=0, tiled=False)

    output_part = quarter_collect(output_gather)
    output_over = lax.ppermute(output_part, "ctx", over)
    second, second_log = attend(metas[1], offsets[1], foreign, forms[0], forms[1], values_t)
    second, second_log, output_part, output_over = hold(
        second, second_log, output_part, output_over
    )

    output_near = jnp.stack([output_part, output_over])
    output_far = lax.ppermute(output_near, "dp", beside)
    cos_far, sin_far = table(after(positions[tok_rows:], second))
    cos_pair = jnp.concatenate([cos_near, cos_far], axis=0)
    sin_pair = jnp.concatenate([sin_near, sin_far], axis=0)
    tables = [(chunk(cos_near, 0), chunk(sin_near, 0)), (chunk(cos_far, 1), chunk(sin_far, 1))]
    second_home = lax.ppermute(second, "ctx", over)
    second_home, output_near, output_far, tables, cos_pair, sin_pair = hold(
        second_home, output_near, output_far, tables, cos_pair, sin_pair
    )
    second_whole = lax.all_gather(second_home, "tensor", axis=0, tiled=False)
    output_whole = arrange(quarters, output_near, output_far)
    output_whole, first_whole = hold(output_whole, first_whole)
    queries = [kept, foreign]
    attention = [first, second]
    log_totals = [first_log, second_log]

    row_of = [
        jnp.asarray([quarter_row(i * share, c, half, span) for i in range(groups)], jnp.int32)
        for c in chunks
    ]

    def own_rows(array, c):
        return lax.dynamic_slice_in_dim(array, row_of[c][member], share, 0)

    def to_attention(c, middle, grad_share):
        middle = own_rows(middle, c)
        inverse_two = lax.rsqrt(jnp.mean(middle * middle, axis=-1, keepdims=True) + EPSILON)
        grad_normed_mlp = grad_share.astype(F32)
        gain = jnp.sum(grad_normed_mlp * middle * inverse_two, axis=0)
        scaled_two = grad_normed_mlp * norm_mlp
        grad_middle = (
            own_rows(cotangent, c).astype(F32)
            + inverse_two * scaled_two
            - middle * inverse_two**3 * jnp.mean(scaled_two * middle, axis=-1, keepdims=True)
        )
        grad_low = grad_middle.astype(BF16)
        blocks = jnp.einsum(
            "rd,tdq->trq", grad_low, output_whole, preferred_element_type=F32
        ).astype(BF16)
        return gain, grad_middle, grad_low, blocks

    def block_of(blocks):
        return lambda j: lax.dynamic_index_in_dim(blocks, j, 0, keepdims=False)

    def rows_of(array):
        return lambda j: lax.dynamic_slice_in_dim(array, j * share, share, 0)

    def line_sum(array):
        return lax.psum_scatter(array, "tensor", scatter_dimension=0, tiled=True)

    def plane_sum(gradient):
        return lax.psum_scatter(
            gradient.astype(BF16), ("dp", "ctx"), scatter_dimension=0, tiled=True
        )

    query_gather = quarter_gather(after(w_query, first_whole))
    hop = query_gather.step()
    weights = (w_gate, w_up, w_down)
    fixed = (tokens, cotangent, norm_mlp, output_whole, weights)
    *fed, grad_first = feed_forward(0, first_whole, *fixed, ())
    fed, grad_first, second_whole, hop = hold(fed, grad_first, second_whole, hop)
    query_gather.held(hop)

    share_first = line_sum(grad_first)
    hop = query_gather.step()
    *fed, grad_second = feed_forward(1, second_whole, *fixed, fed)
    fed, grad_second, hop = hold(fed, grad_second, hop)
    query_gather.held(hop)
    middle, normed_mlp, hidden, gates, mlp_part = fed

    share_second = line_sum(grad_second)
    hop = query_gather.step()
    w_gates = t_dot(normed_mlp, gates).astype(BF16)
    w_gates, hop, share_first = hold(w_gates, hop, share_first)
    query_gather.held(hop)

    gain_first, middle_first, low_first, blocks = to_attention(0, middle, share_first)
    gain_first, middle_first, low_first, blocks, hidden = hold(
        gain_first, middle_first, low_first, blocks, hidden
    )

    came_first = send_blocks(block_of(blocks))
    query_part = quarter_collect(query_gather)
    query_over = lax.ppermute(query_part, "ctx", over)
    w_downs = t_dot(cotangent, hidden).astype(BF16)
    n_part = tok_rows // groups
    middle_own = lax.dynamic_slice_in_dim(middle, member * n_part, n_part, 0)
    came_first, middle_own, query_part, query_over, w_downs = hold(
        came_first, middle_own, query_part, query_over, w_downs
    )

    def back_arguments(c, grads):
        return metas[c], offsets[c], queries[c], attention[c], grads, log_totals[c], forms, *tables[c]

    query_near = jnp.stack([query_part, query_over])
    query_far = lax.ppermute(query_near, "dp", beside)
    grads_first = stack_blocks(came_first).reshape(span, features)
    dq_first, dk, dv = attend_back_first(*back_arguments(0, grads_first))
    dq_first, dk, dv, query_near, query_far, share_second = hold(
        dq_first, dk, dv, query_near, query_far, share_second
    )

    gain_second, middle_second, low_second, blocks = to_attention(1, middle, share_second)
    gain_second, middle_second, low_second, blocks = hold(
        gain_second, middle_second, low_second, blocks
    )

    came_second = send_blocks(block_of(blocks), across=True)
    attention_rows = jnp.concatenate(
        [
            lax.dynamic_slice_in_dim(whole, member * share, share, 1)
            for whole in (first_whole, second_whole)
        ],
        axis=1,
    )
    attention_rows = jnp.swapaxes(attention_rows, 0, 1).reshape(2 * share, groups * features)
    w_outs = t_dot(jnp.concatenate([low_first, low_second], axis=0), attention_rows).astype(BF16)
    came_second, w_outs = hold(came_second, w_outs)
    mlp_share = line_sum(after(mlp_part, came_second))

    rows_first = send_blocks(rows_of(dq_first))
    grads_second = stack_blocks(came_second).reshape(span, features)
    dq_second, kv_near, kv_far = attend_back_last(
        *back_arguments(1, grads_second), dk, dv, cos_pair, sin_pair
    )
    dq_second, kv_near, kv_far, rows_first = hold(dq_second, kv_near, kv_far, rows_first)

    kv_sent = lax.ppermute(kv_far, "ctx", over)
    rows_second = send_blocks(rows_of(dq_second), across=True)
    first_part = join(quarters, stack_blocks(rows_first), query_near, query_far)
    kv_near, kv_sent, rows_second, first_part = hold(kv_near, kv_sent, rows_second, first_part)
    grad_kv_raw = (kv_near + kv_sent.astype(F32)).astype(BF16)
    kv_rows = send_blocks(
        lambda j: jnp.concatenate(
            [lax.dynamic_slice_in_dim(grad_kv_raw, row_of[c][j], share, 0) for c in chunks], axis=0
        )
    )
    second_part = join(quarters, stack_blocks(rows_second), query_near, query_far)
    first_part, second_part, kv_rows, grad_kv_raw = hold(
        first_part, second_part, kv_rows, grad_kv_raw
    )
    kv_whole = jnp.stack(
        [
            jnp.concatenate(
                [w_key[:, h * HD : (h + 1) * HD], w_value[:, h * HD : (h + 1) * HD]], axis=1
            )
            for h in kv_pick
        ]
    )

    grad_normed = jnp.concatenate([first_part, second_part], axis=0) + jnp.einsum(
        "trq,tdq->rd", stack_blocks(kv_rows), kv_whole, preferred_element_type=F32
    )
    inputs_own = jnp.concatenate([own_rows(tokens, c) for c in chunks], axis=0).astype(F32)
    inverse_own = lax.rsqrt(jnp.mean(inputs_own * inputs_own, axis=-1, keepdims=True) + EPSILON)
    attn_gain = jnp.sum(grad_normed * inputs_own * inverse_own, axis=0)
    scaled_one = grad_normed * norm_attn
    grad_inputs = (
        jnp.concatenate([middle_first, middle_second], axis=0)
        + inverse_own * scaled_one
        - inputs_own * inverse_own**3 * jnp.mean(scaled_one * inputs_own, axis=-1, keepdims=True)
    ).astype(BF16)

    def put_rows(target, piece, source):
        for c in chunks:
            target = lax.dynamic_update_slice_in_dim(
                target, piece[c * share : (c + 1) * share], row_of[c][source], 0
            )
        return target

    gains = jnp.stack([attn_gain, gain_first + gain_second])
    mixed_share = (middle_own + mlp_share.astype(F32)).astype(BF16)
    grad_inputs, gains, dq_second, mixed_share, w_gates = hold(
        grad_inputs, gains, dq_second, mixed_share, w_gates
    )
    gate_up_grad = plane_sum(w_gates)

    def put_share(target, piece, source):
        return lax.dynamic_update_slice_in_dim(target, piece, source * n_part, 0)

    tokens_gather, mixed_gather = Gather(grad_inputs), Gather(mixed_share)
    tokens_grad = jnp.zeros((tok_rows, width), BF16)
    mixed = jnp.zeros((tok_rows, width), BF16)
    hop, mixed_hop = tokens_gather.step(), mixed_gather.step()
    dq_home = lax.ppermute(dq_second, "ctx", over)
    query_kv = t_dot(
        normed, jnp.concatenate([natural(dq_first, dq_home), grad_kv_raw], axis=1)
    ).astype(BF16)
    rest = jnp.concatenate([w_downs, w_outs, query_kv], axis=1)
    tokens_grad = tokens_gather.place_hop(put_rows, tokens_grad, 0)
    mixed = mixed_gather.place_hop(put_share, mixed, 0)
    hop, mixed_hop, rest, tokens_grad, mixed = hold(hop, mixed_hop, rest, tokens_grad, mixed)
    tokens_gather.held(hop)
    mixed_gather.held(mixed_hop)
    rest = plane_sum(rest)

    steps = pair_steps()
    hop, mixed_hop = tokens_gather.step(), mixed_gather.step()
    for axis, step in steps[:2]:
        gains = pairwise(gains, axis, step)
    tokens_grad = tokens_gather.place_hop(put_rows, tokens_grad, 1)
    mixed = mixed_gather.place_hop(put_share, mixed, 1)
    hop, mixed_hop, gains, tokens_grad, mixed = hold(hop, mixed_hop, gains, tokens_grad, mixed)
    tokens_gather.held(hop)
    mixed_gather.held(mixed_hop)

    hop, mixed_hop = tokens_gather.step(), mixed_gather.step()
    for axis, step in steps[2:]:
        gains = pairwise(gains, axis, step)
    tokens_grad = tokens_gather.place_hop(put_rows, tokens_grad, 2)
    mixed = mixed_gather.place_hop(put_share, mixed, 2)
    hidden_units = w_down.shape[1]
    down_grad = rest[:, :hidden_units]
    rest = rest[:, hidden_units:]
    output_plane, query_kv = rest[:, : groups * features], rest[:, groups * features :]
    query_grad, kv_plane = query_kv[:, :features].astype(F32), query_kv[:, features:]
    output_rows = send_blocks(
        lambda j: lax.dynamic_slice_in_dim(output_plane, j * features, features, 1)
    )
    kv_share = query_kv.shape[0] // groups
    kv_blocks = send_blocks(
        lambda j: lax.dynamic_slice_in_dim(kv_plane, j * kv_share, kv_share, 0)
    )
    hop, mixed_hop, gains, tokens_grad, mixed, output_rows, kv_blocks = hold(
        hop, mixed_hop, gains, tokens_grad, mixed, output_rows, kv_blocks
    )
    tokens_gather.held(hop)
    mixed_gather.held(mixed_hop)
    for hop in range(3, groups):
        while len(tokens_gather.rights) <= hop:
            tokens_gather.step()
            mixed_gather.step()
        tokens_grad = tokens_gather.place_hop(put_rows, tokens_grad, hop)
        mixed = mixed_gather.place_hop(put_share, mixed, hop)
    output_grad = jnp.sum(stack_blocks(output_rows).astype(F32), axis=0)

    kv_blocks = stack_blocks(kv_blocks).astype(F32)
    key_heads, value_heads = [], []
    for h in range(kv_count):
        total = jnp.zeros((kv_share, 2 * HD), F32)
        for g in range(groups):
            if kv_pick[g] == h:
                total = total + kv_blocks[g]
        key_heads.append(total[:, :HD])
        value_heads.append(total[:, HD:])
    key_grad = jnp.concatenate(key_heads, axis=1)
    value_grad = jnp.concatenate(value_heads, axis=1)

    plane = lax.axis_size("dp") * n_ctx
    plane_index = lax.axis_index("dp") * n_ctx + ctx_index
    gains = lax.dynamic_slice_in_dim(gains, plane_index * (width // plane), width // plane, 1)
    return (
        mixed,
        tokens_grad,
        gains[0],
        query_grad,
        key_grad,
        value_grad,
        output_grad,
        gains[1],
        gate_up_grad[:, :hidden_units].astype(F32),
        gate_up_grad[:, hidden_units:].astype(F32),
        down_grad.astype(F32),
    )


def solution(mesh):
    placed = (
        P(("dp", "ctx"), None),
        P(("dp", "ctx"), None),
        P("dp", None),
        P(),
        P(None, "tensor"),
        P(),
        P(),
        P(None, "tensor"),
        P(),
        P(None, "tensor"),
        P(None, "tensor"),
        P(None, "tensor"),
    )
    return jax.shard_map(
        body,
        mesh=mesh,
        in_specs=placed,
        out_specs=(
            P(("dp", "ctx"), None),
            P(("dp", "ctx"), None),
            P(("dp", "ctx")),
            P(("dp", "ctx"), "tensor"),
            P(("dp", "ctx", "tensor"), None),
            P(("dp", "ctx", "tensor"), None),
            P(("dp", "ctx"), "tensor"),
            P(("dp", "ctx")),
            P(("dp", "ctx"), "tensor"),
            P(("dp", "ctx"), "tensor"),
            P(("dp", "ctx"), "tensor"),
        ),
        check_vma=False,
    )
```

```python
import jax
import jax.numpy as jnp
import numpy as np
from jax import lax
from jax.experimental import pallas as pl
from jax.experimental.pallas import tpu as pltpu
from jax.sharding import PartitionSpec as P

NT = (((1,), (1,)), ((), ()))
F32 = jnp.float32
BF16 = jnp.bfloat16
HD = 64
GROUP = 256
EPSILON = 1e-05
LIGHT = pl.CostEstimate(flops=1, bytes_accessed=1, transcendentals=0)


def turn(values, cos, sin):
    low = (lax.broadcasted_iota(jnp.int32, values.shape, 1) % HD) < HD // 2
    other = jnp.where(
        low, pltpu.roll(values, 128 - HD // 2, 1), pltpu.roll(values, HD // 2, 1)
    )
    return values * cos + other * sin


def project_kernel(
    head, tokens_ref, gain_ref, k_weight, v_weight, q_weight, cos_ref, sin_ref, kv_ref, q_ref, normed_ref
):
    inputs = tokens_ref[...].astype(F32)
    inverse = lax.rsqrt(jnp.mean(inputs * inputs, axis=-1, keepdims=True) + EPSILON)
    normed = (inputs * inverse * gain_ref[...]).astype(BF16)
    normed_ref[...] = normed
    cos, sin = cos_ref[...], sin_ref[...]
    first = head[0] % 2 == 0
    key = jnp.dot(normed, k_weight[...], preferred_element_type=F32)
    value = jnp.dot(normed, v_weight[...], preferred_element_type=F32)
    key = jnp.where(first, key, pltpu.roll(key, HD, 1))
    value = jnp.where(first, pltpu.roll(value, HD, 1), value)
    is_key = lax.broadcasted_iota(jnp.int32, key.shape, 1) < HD
    kv_ref[...] = jnp.where(is_key, turn(key, cos, sin), value).astype(BF16)
    raw = jnp.dot(normed, q_weight[...], preferred_element_type=F32)
    for start in range(0, q_ref.shape[1], 128):
        pair = raw[:, start : start + 128]
        q_ref[:, start : start + 128] = (turn(pair, cos, sin) * HD**-0.5).astype(BF16)


def project(head, tokens, gain, k_weight, v_weight, q_weight, cos, sin):
    rows, width = tokens.shape
    columns = q_weight.shape[1]
    block = 256
    two_heads = pl.BlockSpec((width, 128), lambda i, head: (0, head[0] // 2))
    return pl.pallas_call(
        project_kernel,
        grid_spec=pltpu.PrefetchScalarGridSpec(
            num_scalar_prefetch=1,
            grid=(rows // block,),
            in_specs=[
                pl.BlockSpec((block, width), lambda i, head: (i, 0)),
                pl.BlockSpec((1, width), lambda i, head: (0, 0)),
                two_heads,
                two_heads,
                pl.BlockSpec((width, columns), lambda i, head: (0, 0)),
                pl.BlockSpec((block, 128), lambda i, head: (i, 0)),
                pl.BlockSpec((block, 128), lambda i, head: (i, 0)),
            ],
            out_specs=[
                pl.BlockSpec((block, 128), lambda i, head: (i, 0)),
                pl.BlockSpec((block, columns), lambda i, head: (i, 0)),
                pl.BlockSpec((block, width), lambda i, head: (i, 0)),
            ],
        ),
        out_shape=[
            jax.ShapeDtypeStruct((rows, 128), BF16),
            jax.ShapeDtypeStruct((rows, columns), BF16),
            jax.ShapeDtypeStruct((rows, width), BF16),
        ],
        compiler_params=pltpu.CompilerParams(vmem_limit_bytes=48 * 2**20),
        cost_estimate=LIGHT,
        name="project",
    )(head, tokens, gain.reshape(1, width), k_weight, v_weight, q_weight, cos, sin)


def fwd_kernel(offsets, meta, q_ref, ka_ref, kb_ref, vt_ref, o_ref, lse_ref):
    half = q_ref.shape[0] // 2
    span = 2 * half
    group = min(GROUP, half)
    pairs = q_ref.shape[1] // 128
    for part, offset in enumerate(offsets):
        at = slice(part * half, part * half + half)
        queries = [q_ref[at, p * 128 : p * 128 + 128] for p in range(pairs)]
        chains = [(p, keys_ref) for p in range(pairs) for keys_ref in (ka_ref, kb_ref)]
        seen = meta[part]
        own = pl.multiple_of(meta[2 + seen] * span, span)
        heads = []
        for p, keys_ref in chains:
            tops, sums = [], []
            for first in range(0, half, group):
                count = offset + first + group
                rows = pl.ds(own, count)
                scores = lax.dot_general(
                    keys_ref[rows, :],
                    queries[p][first : first + group],
                    NT,
                    preferred_element_type=F32,
                )
                key_at = lax.broadcasted_iota(jnp.int32, scores.shape, 0)
                row_at = lax.broadcasted_iota(jnp.int32, scores.shape, 1) + (offset + first)
                scores = jnp.where(key_at <= row_at, scores, -1e30)
                top = jnp.max(scores, axis=0, keepdims=True)
                weights = jnp.exp(scores - top).astype(BF16)
                tops.append(top)
                sums.append(jnp.dot(vt_ref[:, rows], weights, preferred_element_type=F32))
            heads += [jnp.concatenate(tops, axis=1), jnp.concatenate(sums, axis=1)]

        def step(index, carry):
            rows = pl.ds(pl.multiple_of(meta[2 + index] * span, span), span)
            out = []
            for chain, (p, keys_ref) in enumerate(chains):
                top, total = carry[2 * chain : 2 * chain + 2]
                scores = lax.dot_general(
                    keys_ref[rows, :], queries[p], NT, preferred_element_type=F32
                )
                new_top = jnp.maximum(top, jnp.max(scores, axis=0, keepdims=True))
                weights = jnp.exp(scores - new_top).astype(BF16)
                total = total * jnp.exp(top - new_top) + jnp.dot(
                    vt_ref[:, rows], weights, preferred_element_type=F32
                )
                out += [new_top, total]
            return tuple(out)

        heads = lax.fori_loop(0, seen, step, tuple(heads))
        for p in range(pairs):
            top0, total0, top1, total1 = heads[4 * p : 4 * p + 4]
            norm0, norm1 = total0[HD : HD + 1], total1[HD : HD + 1]
            o_ref[at, p * 128 : p * 128 + 128] = (
                jnp.concatenate([total0[:HD] / norm0, total1[:HD] / norm1], axis=0).T.astype(BF16)
            )
            lse_ref[p, :, at] = jnp.concatenate(
                [top0 + jnp.log(norm0), top1 + jnp.log(norm1), jnp.zeros((6, half), F32)], axis=0
            )


def spread(kv_refs, ka_ref, kb_ref, va_ref, vb_ref, kt_ref, vt_ref):
    at = 0
    for kv_ref in kv_refs:
        rows = kv_ref.shape[0]
        block = min(512, rows)
        for first in range(0, rows, block):
            here = slice(at + first, at + first + block)
            pair = kv_ref[first : first + block, :].astype(F32)
            other = pltpu.roll(pair, HD, 1)
            left = lax.broadcasted_iota(jnp.int32, pair.shape, 1) < HD
            ka_ref[here, :] = jnp.where(left, pair, 0.0).astype(BF16)
            vb_ref[here, :] = jnp.where(left, 0.0, pair).astype(BF16)
            va_ref[here, :] = jnp.where(left, other, 0.0).astype(BF16)
            kb_ref[here, :] = jnp.where(left, 0.0, other).astype(BF16)
            turned = pair.T
            kt_ref[:, here] = turned[:HD].astype(BF16)
            ones = jnp.where(lax.broadcasted_iota(jnp.int32, (16, block), 0) == 0, 1.0, 0.0)
            vt_ref[:, here] = jnp.concatenate([turned[HD:], ones], axis=0).astype(BF16)
        at += rows


def attend_cost(rows, length, width):
    return pl.CostEstimate(
        flops=8 * rows * length * width, bytes_accessed=2**23, transcendentals=0
    )


def attend_first(meta, offsets, queries, kv_own, kv_other):
    rows, width = queries.shape
    pairs = width // 128
    together = 2 if pairs % 2 == 0 else 1
    length = 2 * kv_own.shape[0]

    def whole(shape):
        return pl.BlockSpec(shape, lambda p, m: (0, 0))

    def kernel(meta, q_ref, own, other, o_ref, lse_ref, ka, kb, va, vb, kt, vt):
        @pl.when(pl.program_id(0) == 0)
        def _():
            spread((own, other), ka, kb, va, vb, kt, vt)

        fwd_kernel(offsets, meta, q_ref, ka, kb, vt, o_ref, lse_ref)

    wide = (length, 128)
    forms = [wide, wide, wide, wide, (HD, length), (HD + 16, length)]
    return pl.pallas_call(
        kernel,
        grid_spec=pltpu.PrefetchScalarGridSpec(
            num_scalar_prefetch=1,
            grid=(pairs // together,),
            in_specs=[
                pl.BlockSpec((rows, 128 * together), lambda p, m: (0, p)),
                whole(kv_own.shape),
                whole(kv_other.shape),
            ],
            out_specs=[
                pl.BlockSpec((rows, 128 * together), lambda p, m: (0, p)),
                pl.BlockSpec((together, 8, rows), lambda p, m: (p, 0, 0)),
            ]
            + [whole(form) for form in forms],
        ),
        out_shape=[
            jax.ShapeDtypeStruct((rows, width), BF16),
            jax.ShapeDtypeStruct((pairs, 8, rows), F32),
        ]
        + [jax.ShapeDtypeStruct(form, BF16) for form in forms],
        compiler_params=pltpu.CompilerParams(vmem_limit_bytes=58 * 2**20),
        cost_estimate=attend_cost(rows, length, width),
        name="attend_first",
    )(meta, queries, kv_own, kv_other)


def attend(meta, offsets, queries, keys_a, keys_b, values_t):
    rows, width = queries.shape
    pairs = width // 128
    together = 2 if pairs % 2 == 0 else 1
    length = keys_a.shape[0]
    whole = pl.BlockSpec((length, 128), lambda p, m: (0, 0))

    def kernel(*refs):
        fwd_kernel(offsets, *refs)

    return pl.pallas_call(
        kernel,
        grid_spec=pltpu.PrefetchScalarGridSpec(
            num_scalar_prefetch=1,
            grid=(pairs // together,),
            in_specs=[
                pl.BlockSpec((rows, 128 * together), lambda p, m: (0, p)),
                whole,
                whole,
                pl.BlockSpec(values_t.shape, lambda p, m: (0, 0)),
            ],
            out_specs=[
                pl.BlockSpec((rows, 128 * together), lambda p, m: (0, p)),
                pl.BlockSpec((together, 8, rows), lambda p, m: (p, 0, 0)),
            ],
        ),
        out_shape=[
            jax.ShapeDtypeStruct((rows, width), BF16),
            jax.ShapeDtypeStruct((pairs, 8, rows), F32),
        ],
        compiler_params=pltpu.CompilerParams(vmem_limit_bytes=58 * 2**20),
        cost_estimate=attend_cost(rows, length, width),
        name="attend",
    )(meta, queries, keys_a, keys_b, values_t)


def bwd_kernel(
    offsets,
    meta,
    q_ref,
    o_ref,
    g_ref,
    lse_ref,
    ka_ref,
    kb_ref,
    va_ref,
    vb_ref,
    kt_ref,
    cos_ref,
    sin_ref,
    dq_ref,
    dk_ref,
    dv_ref,
):
    half = q_ref.shape[0] // 2
    span = 2 * half
    group = min(GROUP, half)

    for part, offset in enumerate(offsets):
        at = slice(part * half, part * half + half)
        queries, grads = q_ref[at, :], g_ref[at, :]
        left = lax.broadcasted_iota(jnp.int32, (half, 128), 1) < HD
        products = (grads.astype(F32) * o_ref[at, :].astype(F32)).T
        zero = jnp.zeros_like(queries)
        sides = []
        for side, (keys_ref, values_ref) in enumerate(((ka_ref, va_ref), (kb_ref, vb_ref))):
            mine = left if side == 0 else jnp.logical_not(left)
            delta = jnp.sum(products[side * HD : side * HD + HD], axis=0, keepdims=True)
            sides.append(
                (
                    keys_ref,
                    values_ref,
                    jnp.where(mine, queries, zero),
                    jnp.where(mine, grads, zero),
                    lse_ref[0, side : side + 1, at],
                    delta,
                )
            )

        def block(rows, first, count, masked):
            cut = slice(first, first + count)
            dqs = []
            dk_add = dv_add = None
            for keys_ref, values_ref, q_mine, g_mine, lse, delta in sides:
                scores = lax.dot_general(
                    keys_ref[rows, :], queries[cut], NT, preferred_element_type=F32
                )
                probs = jnp.exp(scores - lse[:, cut])
                if masked:
                    key_at = lax.broadcasted_iota(jnp.int32, scores.shape, 0)
                    row_at = lax.broadcasted_iota(jnp.int32, scores.shape, 1) + (offset + first)
                    probs = jnp.where(key_at <= row_at, probs, 0.0)
                grad_probs = lax.dot_general(
                    values_ref[rows, :], grads[cut], NT, preferred_element_type=F32
                )
                grad_scores = (probs * (grad_probs - delta[:, cut])).astype(BF16)
                dv_new = jnp.dot(probs.astype(BF16), g_mine[cut], preferred_element_type=F32)
                dk_new = jnp.dot(grad_scores, q_mine[cut], preferred_element_type=F32)
                dv_add = dv_new if dv_add is None else dv_add + dv_new
                dk_add = dk_new if dk_add is None else dk_add + dk_new
                dqs.append(jnp.dot(kt_ref[:, rows], grad_scores, preferred_element_type=F32))
            dv_ref[rows, :] += dv_add
            dk_ref[rows, :] += dk_add
            return jnp.concatenate(dqs, axis=0)

        own = pl.multiple_of(meta[2 + meta[part]] * span, span)
        start = jnp.concatenate(
            [
                block(pl.ds(own, offset + first + group), first, group, True)
                for first in range(0, half, group)
            ],
            axis=1,
        )

        def step(index, total):
            rows = pl.ds(pl.multiple_of(meta[2 + index] * span, span), span)
            return total + block(rows, 0, half, False)

        dq = lax.fori_loop(0, meta[part], step, start).T * (HD**-0.5)
        dq_ref[at, :] = turn(dq, cos_ref[at, :], -sin_ref[at, :]).astype(BF16)


def back_specs(queries, forms):
    rows, width = queries.shape
    pair = pl.BlockSpec((rows, 128), lambda p, m: (0, p))
    table = pl.BlockSpec((rows, 128), lambda p, m: (0, 0))
    specs = [pair, pair, pair, pl.BlockSpec((1, 8, rows), lambda p, m: (p, 0, 0))]
    specs += [pl.BlockSpec(form.shape, lambda p, m: (0, 0)) for form in forms]
    return pair, specs + [table, table]


def attend_back_first(meta, offsets, queries, outputs, grads, lse, forms, cos, sin):
    length = forms[0].shape[0]
    pair, specs = back_specs(queries, forms)
    whole = pl.BlockSpec((length, 128), lambda p, m: (0, 0))

    def kernel(*refs):
        dk_ref, dv_ref = refs[-2:]

        @pl.when(pl.program_id(0) == 0)
        def _():
            dk_ref[...] = jnp.zeros(dk_ref.shape, F32)
            dv_ref[...] = jnp.zeros(dv_ref.shape, F32)

        bwd_kernel(offsets, *refs)

    return pl.pallas_call(
        kernel,
        grid_spec=pltpu.PrefetchScalarGridSpec(
            num_scalar_prefetch=1,
            grid=(queries.shape[1] // 128,),
            in_specs=specs,
            out_specs=[pair, whole, whole],
        ),
        out_shape=[
            jax.ShapeDtypeStruct(queries.shape, BF16),
            jax.ShapeDtypeStruct((length, 128), F32),
            jax.ShapeDtypeStruct((length, 128), F32),
        ],
        compiler_params=pltpu.CompilerParams(vmem_limit_bytes=58 * 2**20),
        cost_estimate=LIGHT,
        name="attend_back_first",
    )(meta, queries, outputs, grads, lse, *forms, cos, sin)


def attend_back_last(
    meta, offsets, queries, outputs, grads, lse, forms, cos, sin, dk, dv, all_cos, all_sin
):
    length = forms[0].shape[0]
    near = length // 2
    pair, specs = back_specs(queries, forms)
    whole = pl.BlockSpec((length, 128), lambda p, m: (0, 0))
    half = pl.BlockSpec((near, 128), lambda p, m: (0, 0))

    def kernel(*refs):
        dk_in, dv_in, cos_ref, sin_ref, dq_ref, near_ref, far_ref, dk_ref, dv_ref = refs[-9:]

        @pl.when(pl.program_id(0) == 0)
        def _():
            dk_ref[...] = dk_in[...]
            dv_ref[...] = dv_in[...]

        bwd_kernel(offsets, *refs[:-9], dq_ref, dk_ref, dv_ref)

        @pl.when(pl.program_id(0) == pl.num_programs(0) - 1)
        def _():
            block = min(512, near)
            for first in range(0, length, block):
                here = slice(first, first + block)
                dk_block, dv_block = dk_ref[here, :], dv_ref[here, :]
                dk_block = dk_block + pltpu.roll(dk_block, HD, 1)
                dv_block = dv_block + pltpu.roll(dv_block, HD, 1)
                left = lax.broadcasted_iota(jnp.int32, dk_block.shape, 1) < HD
                both = jnp.where(
                    left, turn(dk_block, cos_ref[here, :], -sin_ref[here, :]), dv_block
                )
                if first < near:
                    near_ref[here, :] = both
                else:
                    far_ref[first - near : first - near + block, :] = both.astype(BF16)

    return pl.pallas_call(
        kernel,
        grid_spec=pltpu.PrefetchScalarGridSpec(
            num_scalar_prefetch=1,
            grid=(queries.shape[1] // 128,),
            in_specs=specs + [whole] * 4,
            out_specs=[pair, half, half],
            scratch_shapes=[pltpu.VMEM((length, 128), F32), pltpu.VMEM((length, 128), F32)],
        ),
        out_shape=[
            jax.ShapeDtypeStruct(queries.shape, BF16),
            jax.ShapeDtypeStruct((near, 128), F32),
            jax.ShapeDtypeStruct((near, 128), BF16),
        ],
        compiler_params=pltpu.CompilerParams(vmem_limit_bytes=60 * 2**20),
        cost_estimate=LIGHT,
        name="attend_back_last",
    )(meta, queries, outputs, grads, lse, *forms, cos, sin, dk, dv, all_cos, all_sin)


def feed_kernel(
    gathered_ref,
    tokens_ref,
    cotangent_ref,
    gain_ref,
    output_weight,
    gate_weight,
    up_weight,
    down_weight,
    *refs,
):
    middle_ref, normed_ref, hidden_ref, gates_ref, down_ref, grad_ref = refs[-6:]
    middle = tokens_ref[...].astype(F32)
    for source in range(gathered_ref.shape[0]):
        middle = middle + lax.dot_general(
            gathered_ref[source], output_weight[source], NT, preferred_element_type=F32
        )
    middle_ref[...] = middle
    inverse = lax.rsqrt(jnp.mean(middle * middle, axis=-1, keepdims=True) + EPSILON)
    normed = (middle * inverse * gain_ref[...]).astype(BF16)
    normed_ref[...] = normed
    gate = jnp.dot(normed, gate_weight[...], preferred_element_type=F32)
    up = jnp.dot(normed, up_weight[...], preferred_element_type=F32)
    grad_hidden = jnp.dot(cotangent_ref[...], down_weight[...], preferred_element_type=F32)
    sigmoid = jax.nn.sigmoid(gate)
    hidden = (gate * sigmoid * up).astype(BF16)
    hidden_ref[...] = hidden
    grad_gate = (grad_hidden * up * sigmoid * (1.0 + gate * (1.0 - sigmoid))).astype(BF16)
    grad_up = (grad_hidden * gate * sigmoid).astype(BF16)
    units = hidden.shape[1]
    gates_ref[:, :units] = grad_gate
    gates_ref[:, units:] = grad_up
    down_ref[...] = lax.dot_general(
        hidden, down_weight[...], NT, preferred_element_type=F32
    ).astype(BF16)
    grad_ref[...] = (
        lax.dot_general(grad_gate, gate_weight[...], NT, preferred_element_type=F32)
        + lax.dot_general(grad_up, up_weight[...], NT, preferred_element_type=F32)
    ).astype(BF16)


def feed_forward(c, gathered, tokens, cotangent, gain, output_weight, weights, earlier):
    rows, width = tokens.shape
    units = weights[0].shape[1]
    block = min(256, rows // 4)
    quarter = rows // 4 // block
    if c:
        place = lambda i: (i + quarter, 0)
    else:
        place = lambda i: (jnp.where(i < quarter, i, i + 2 * quarter), 0)
    once = pl.Buffered(1)

    def natural(columns):
        return pl.BlockSpec((block, columns), place)

    def whole(array):
        zeros = (0,) * array.ndim
        return pl.BlockSpec(array.shape, lambda i: zeros, pipeline_mode=once)

    shapes = [
        jax.ShapeDtypeStruct((rows, width), F32),
        jax.ShapeDtypeStruct((rows, width), BF16),
        jax.ShapeDtypeStruct((rows, units), BF16),
        jax.ShapeDtypeStruct((rows, 2 * units), BF16),
        jax.ShapeDtypeStruct((rows, width), BF16),
    ]
    gain = gain.reshape(1, width)
    return pl.pallas_call(
        feed_kernel,
        grid=(2 * quarter,),
        in_specs=[
            pl.BlockSpec((gathered.shape[0], block, gathered.shape[2]), lambda i: (0, i, 0)),
            natural(width),
            natural(width),
            whole(gain),
            whole(output_weight),
        ]
        + [whole(weight) for weight in weights]
        + [pl.BlockSpec(memory_space=pl.ANY) for _ in earlier],
        out_specs=[natural(shape.shape[1]) for shape in shapes]
        + [pl.BlockSpec((block, width), lambda i: (i, 0))],
        out_shape=shapes + [jax.ShapeDtypeStruct((rows // 2, width), BF16)],
        input_output_aliases={8 + k: k for k in range(len(earlier))},
        compiler_params=pltpu.CompilerParams(vmem_limit_bytes=60 * 2**20),
        cost_estimate=LIGHT,
        name="feed_forward",
    )(gathered, tokens, cotangent, gain, output_weight, *weights, *earlier)


def part_specs(shape):
    return [pl.BlockSpec(shape, lambda p, order: (0, 0, 0)) for _ in range(4)]


def join_kernel(order, rows_ref, *refs):
    out_ref = refs[4]
    for part, weight_ref in enumerate(refs[:4]):

        @pl.when(pl.program_id(0) == part)
        def _():
            result = None
            for source in range(rows_ref.shape[0]):
                term = lax.dot_general(
                    rows_ref[source], weight_ref[source], NT, preferred_element_type=F32
                )
                result = term if result is None else result + term
            out_ref[...] = result


def join(order, rows, parts):
    size, count, features = rows.shape
    columns = parts[0].shape[1]
    return pl.pallas_call(
        join_kernel,
        grid_spec=pltpu.PrefetchScalarGridSpec(
            num_scalar_prefetch=1,
            grid=(4,),
            in_specs=[pl.BlockSpec(rows.shape, lambda p, order: (0, 0, 0))]
            + part_specs(parts[0].shape),
            out_specs=pl.BlockSpec((count, columns), lambda p, order: (0, order[p])),
        ),
        out_shape=jax.ShapeDtypeStruct((count, 4 * columns), F32),
        compiler_params=pltpu.CompilerParams(vmem_limit_bytes=48 * 2**20),
        cost_estimate=LIGHT,
        name="join",
    )(order, rows, *parts)


def arrange_kernel(order, *refs):
    for part, weight_ref in enumerate(refs[:4]):

        @pl.when(pl.program_id(0) == part)
        def _():
            refs[4][...] = weight_ref[...]


def arrange(order, parts):
    size, rows, features = parts[0].shape
    return pl.pallas_call(
        arrange_kernel,
        grid_spec=pltpu.PrefetchScalarGridSpec(
            num_scalar_prefetch=1,
            grid=(4,),
            in_specs=part_specs(parts[0].shape),
            out_specs=pl.BlockSpec((size, rows, features), lambda p, order: (0, order[p], 0)),
        ),
        out_shape=jax.ShapeDtypeStruct((size, 4 * rows, features), parts[0].dtype),
        compiler_params=pltpu.CompilerParams(vmem_limit_bytes=48 * 2**20),
        cost_estimate=LIGHT,
        name="arrange",
    )(order, *parts)


def quarter_row(row, c, half, span):
    if c:
        return half + row
    return row if row < half else row + span


def after(value, *earlier):
    return lax.optimization_barrier((value, earlier))[0]


def line_steps(size):
    return [
        (
            [(i, i + 1) for i in range(step - 1, size - 1)],
            [(i, i - 1) for i in range(1, size - step + 1)],
        )
        for step in range(1, size)
    ]


class Gather:
    def __init__(self, piece):
        self.piece = piece
        self.rights, self.lefts = [piece], [piece]
        self.hops = line_steps(lax.axis_size("tensor"))

    def step(self):
        done = len(self.rights) - 1
        if done < len(self.hops):
            to_right, to_left = self.hops[done]
            self.rights.append(lax.ppermute(self.rights[-1], "tensor", to_right))
            self.lefts.append(lax.ppermute(self.lefts[-1], "tensor", to_left))
        return self.rights[-1], self.lefts[-1]

    def held(self, pair):
        self.rights[-1], self.lefts[-1] = pair

    def place_hop(self, place, target, hop):
        size = lax.axis_size("tensor")
        me = lax.axis_index("tensor")
        if hop == 0:
            return place(target, self.piece, me)
        right, left = self.rights[hop], self.lefts[hop]
        from_left, from_right = me >= hop, me + hop < size
        if 2 * hop >= size:
            piece = jnp.where(from_left, right, jnp.where(from_right, left, self.piece))
            source = jnp.where(from_left, me - hop, jnp.where(from_right, me + hop, me))
            return place(target, piece, source)
        target = place(
            target, jnp.where(from_left, right, self.piece), jnp.where(from_left, me - hop, me)
        )
        return place(
            target, jnp.where(from_right, left, self.piece), jnp.where(from_right, me + hop, me)
        )

    def collect(self, place, target):
        while len(self.rights) <= len(self.hops):
            self.step()
        for hop in range(len(self.rights)):
            target = self.place_hop(place, target, hop)
        return target


def send_blocks(pick, across=False):
    size = lax.axis_size("tensor")
    me = lax.axis_index("tensor")
    arrived = []
    for shift in range(size):
        block = pick(lax.rem(me + shift, size))
        if across:
            block = lax.ppermute(
                block,
                ("ctx", "tensor"),
                [
                    (c * size + i, (1 - c) * size + (i + shift) % size)
                    for c in range(2)
                    for i in range(size)
                ],
            )
        elif shift:
            block = lax.ppermute(block, "tensor", [(i, (i + shift) % size) for i in range(size)])
        arrived.append(block)
    return tuple(arrived)


def stack_blocks(arrived):
    size = len(arrived)
    me = lax.axis_index("tensor")
    out = jnp.zeros((size, *arrived[0].shape), arrived[0].dtype)
    for shift, block in enumerate(arrived):
        out = lax.dynamic_update_index_in_dim(out, block, lax.rem(me - shift + size, size), 0)
    return out


def hold(*values):
    return lax.optimization_barrier(values)


def rows_part(weight, index, count):
    rows = weight.shape[0] // count
    return lax.dynamic_slice_in_dim(weight, index * rows, rows, 0)


def by_source(target, piece, source):
    return lax.dynamic_update_index_in_dim(target, piece, source, 0)


def dot(a, b):
    return jnp.dot(a, b, preferred_element_type=F32)


def dot_t(a, b):
    return jnp.einsum("rf,df->rd", a, b, preferred_element_type=F32)


def t_dot(a, b):
    return jnp.einsum("rd,rf->df", a, b, preferred_element_type=F32)


def body(
    tokens,
    cotangent,
    span_order,
    norm_attn,
    w_query,
    w_key,
    w_value,
    w_output,
    norm_mlp,
    w_gate,
    w_up,
    w_down,
):
    tok_rows, width = tokens.shape
    groups = lax.axis_size("tensor")
    member = lax.axis_index("tensor")
    n_ctx = lax.axis_size("ctx")
    assert n_ctx == 2
    ctx_index = lax.axis_index("ctx")
    features = w_query.shape[1]
    kv_count = w_key.shape[1] // HD
    kv_pick = np.arange(groups) * kv_count // groups
    head = (member * kv_count // groups).astype(jnp.int32).reshape(1)
    span = tok_rows // 2
    half = span // 2
    share = span // groups
    over = [(0, 1), (1, 0)]
    chunks = range(2)

    def chunk(array, c):
        if c:
            return array[half : half + span]
        return jnp.concatenate([array[:half], array[half + span :]], axis=0)

    def natural(first, second):
        return jnp.concatenate([first[:half], second, first[half:]], axis=0)

    order = jnp.roll(span_order[0], -2 * ctx_index)
    places = jnp.arange(4, dtype=jnp.int32)
    slot_of = jnp.sum(
        jnp.where(order[None, :] == places[:, None], places[None, :], 0), axis=1, dtype=jnp.int32
    )
    metas = [jnp.concatenate([order[2 * c : 2 * c + 2], slot_of]) for c in chunks]
    offsets = [(0, half), (half, 0)]

    positions = (order[:, None] * span + jnp.arange(span, dtype=jnp.int32)[None, :]).reshape(-1)
    frequency = 10000.0 ** (-jnp.arange(HD // 2, dtype=F32) / (HD // 2))

    def table(positions):
        angles = frequency[:, None] * positions.astype(F32)[None, :]
        cos_part, sin_part = hold(jnp.cos(angles), jnp.sin(angles))
        cos_part, sin_part = cos_part.T, sin_part.T
        return (
            jnp.concatenate([cos_part] * 4, axis=1),
            jnp.concatenate([-sin_part, sin_part] * 2, axis=1),
        )


    upper = lax.axis_index("dp") % 2
    beside = [(i, i ^ 1) for i in range(lax.axis_size("dp"))]
    quarters = jnp.stack(
        [
            2 * upper + ctx_index,
            2 * upper + 1 - ctx_index,
            2 - 2 * upper + ctx_index,
            3 - 2 * upper - ctx_index,
        ]
    ).astype(jnp.int32)

    def quarter_gather(weight):
        return Gather(rows_part(weight, 2 * upper + ctx_index, 4))

    def quarter_collect(gather):
        return gather.collect(by_source, jnp.zeros((groups, *gather.piece.shape), BF16))

    output_gather = quarter_gather(w_output)
    hop = output_gather.step()
    cos_near, sin_near = table(positions[:tok_rows])
    cos_near, sin_near, hop, quarters, head = hold(cos_near, sin_near, hop, quarters, head)
    output_gather.held(hop)
    hop = output_gather.step()

    kv_own, queries, normed = project(
        head, tokens, norm_attn, w_key, w_value, w_query, cos_near, sin_near
    )
    kv_own, queries, normed, hop = hold(kv_own, queries, normed, hop)
    output_gather.held(hop)
    kv_other = lax.ppermute(kv_own, "ctx", over)
    hop = output_gather.step()
    kv_own, kv_other, sent, kept, normed, hop = hold(
        kv_own, kv_other, chunk(queries, 1), chunk(queries, 0), normed, hop
    )
    output_gather.held(hop)
    length = 2 * tok_rows

    foreign = lax.ppermute(sent, "ctx", over)
    output_part = quarter_collect(output_gather)
    output_over = lax.ppermute(output_part, "ctx", over)
    first, first_log, *forms = attend_first(metas[0], offsets[0], kept, kv_own, kv_other)
    first, first_log, foreign, forms, output_near = hold(
        first, first_log, foreign, forms, (output_part, output_over)
    )
    *forms, values_t = forms
    first_whole = lax.all_gather(first, "tensor", axis=0, tiled=False)

    output_far = tuple(lax.ppermute(part, "dp", beside) for part in output_near)
    second, second_log = attend(metas[1], offsets[1], foreign, forms[0], forms[1], values_t)
    second, second_log, output_near, output_far = hold(
        second, second_log, output_near, output_far
    )

    cos_far, sin_far = table(after(positions[tok_rows:], second))
    cos_pair = jnp.concatenate([cos_near, cos_far], axis=0)
    sin_pair = jnp.concatenate([sin_near, sin_far], axis=0)
    tables = [(chunk(cos_near, 0), chunk(sin_near, 0)), (chunk(cos_far, 1), chunk(sin_far, 1))]
    second_home = lax.ppermute(second, "ctx", over)
    output_whole = arrange(quarters, output_near + output_far)
    second_home, output_whole, tables, cos_pair, sin_pair = hold(
        second_home, output_whole, tables, cos_pair, sin_pair
    )
    second_whole = lax.all_gather(second_home, "tensor", axis=0, tiled=False)
    queries = [kept, foreign]
    attention = [first, second]
    log_totals = [first_log, second_log]

    row_of = [
        jnp.asarray([quarter_row(i * share, c, half, span) for i in range(groups)], jnp.int32)
        for c in chunks
    ]

    def own_rows(array, c):
        return lax.dynamic_slice_in_dim(array, row_of[c][member], share, 0)

    def to_attention(c, middle, grad_share):
        middle = own_rows(middle, c)
        inverse_two = lax.rsqrt(jnp.mean(middle * middle, axis=-1, keepdims=True) + EPSILON)
        grad_normed_mlp = grad_share.astype(F32)
        gain = jnp.sum(grad_normed_mlp * middle * inverse_two, axis=0)
        scaled_two = grad_normed_mlp * norm_mlp
        grad_middle = (
            own_rows(cotangent, c).astype(F32)
            + inverse_two * scaled_two
            - middle * inverse_two**3 * jnp.mean(scaled_two * middle, axis=-1, keepdims=True)
        )
        grad_low = grad_middle.astype(BF16)
        blocks = jnp.einsum(
            "rd,tdq->trq", grad_low, output_whole, preferred_element_type=F32
        ).astype(BF16)
        return gain, grad_middle, grad_low, blocks

    def block_of(blocks):
        return lambda j: lax.dynamic_index_in_dim(blocks, j, 0, keepdims=False)

    def rows_of(array):
        return lambda j: lax.dynamic_slice_in_dim(array, j * share, share, 0)

    def line_sum(array):
        return lax.psum_scatter(array, "tensor", scatter_dimension=0, tiled=True)

    def plane_sum(gradient):
        return lax.psum_scatter(
            gradient.astype(BF16), ("dp", "ctx"), scatter_dimension=0, tiled=True
        )

    query_gather = quarter_gather(after(w_query, first_whole))
    hop = query_gather.step()
    weights = (w_gate, w_up, w_down)
    fixed = (tokens, cotangent, norm_mlp, output_whole, weights)
    *fed, grad_first = feed_forward(0, first_whole, *fixed, ())
    fed, grad_first, second_whole, hop = hold(fed, grad_first, second_whole, hop)
    query_gather.held(hop)

    share_first = line_sum(grad_first)
    hop = query_gather.step()
    *fed, grad_second = feed_forward(1, second_whole, *fixed, fed)
    fed, grad_second, hop = hold(fed, grad_second, hop)
    query_gather.held(hop)
    middle, normed_mlp, hidden, gates, mlp_part = fed

    share_second = line_sum(grad_second)
    hop = query_gather.step()
    w_gates = t_dot(normed_mlp, gates).astype(BF16)
    w_gates, hop, share_first = hold(w_gates, hop, share_first)
    query_gather.held(hop)

    gain_first, middle_first, low_first, blocks = to_attention(0, middle, share_first)
    gain_first, middle_first, low_first, blocks, hidden = hold(
        gain_first, middle_first, low_first, blocks, hidden
    )

    came_first = send_blocks(block_of(blocks))
    query_part = quarter_collect(query_gather)
    query_over = lax.ppermute(query_part, "ctx", over)
    w_downs = t_dot(cotangent, hidden).astype(BF16)
    n_part = tok_rows // groups
    middle_own = lax.dynamic_slice_in_dim(middle, member * n_part, n_part, 0)
    came_first, middle_own, query_part, query_over, w_downs = hold(
        came_first, middle_own, query_part, query_over, w_downs
    )

    def back_arguments(c, grads):
        return metas[c], offsets[c], queries[c], attention[c], grads, log_totals[c], forms, *tables[c]

    query_near = (query_part, query_over)
    query_far = tuple(lax.ppermute(part, "dp", beside) for part in query_near)
    grads_first = stack_blocks(came_first).reshape(span, features)
    dq_first, dk, dv = attend_back_first(*back_arguments(0, grads_first))
    dq_first, dk, dv, query_near, query_far, share_second = hold(
        dq_first, dk, dv, query_near, query_far, share_second
    )

    gain_second, middle_second, low_second, blocks = to_attention(1, middle, share_second)
    gain_second, middle_second, low_second, blocks = hold(
        gain_second, middle_second, low_second, blocks
    )

    came_second = send_blocks(block_of(blocks), across=True)
    attention_rows = jnp.concatenate(
        [
            lax.dynamic_slice_in_dim(whole, member * share, share, 1)
            for whole in (first_whole, second_whole)
        ],
        axis=1,
    )
    attention_rows = jnp.swapaxes(attention_rows, 0, 1).reshape(2 * share, groups * features)
    w_outs = t_dot(jnp.concatenate([low_first, low_second], axis=0), attention_rows).astype(BF16)
    came_second, w_outs = hold(came_second, w_outs)
    mlp_share = line_sum(after(mlp_part, came_second))

    rows_first = send_blocks(rows_of(dq_first))
    grads_second = stack_blocks(came_second).reshape(span, features)
    dq_second, kv_near, kv_far = attend_back_last(
        *back_arguments(1, grads_second), dk, dv, cos_pair, sin_pair
    )
    dq_second, kv_near, kv_far, rows_first = hold(dq_second, kv_near, kv_far, rows_first)

    def kv_share_of(array, j):
        return [lax.dynamic_slice_in_dim(array, row_of[c][j], share, 0) for c in chunks]

    kv_low = kv_near.astype(BF16)
    near_blocks = send_blocks(lambda j: jnp.concatenate(kv_share_of(kv_low, j), axis=1))
    far_blocks = send_blocks(
        lambda j: jnp.concatenate([rows_of(dq_second)(j), *kv_share_of(kv_far, j)], axis=1),
        across=True,
    )
    query_parts = query_near + query_far
    first_part = join(quarters, stack_blocks(rows_first), query_parts)
    near_blocks, far_blocks, first_part = hold(near_blocks, far_blocks, first_part)
    far_blocks = stack_blocks(far_blocks)
    kv_blocks = (
        stack_blocks(near_blocks).astype(F32) + far_blocks[:, :, features:].astype(F32)
    ).astype(BF16)
    kv_blocks = jnp.concatenate([kv_blocks[:, :, : 2 * HD], kv_blocks[:, :, 2 * HD :]], axis=1)
    second_part = join(quarters, far_blocks[:, :, :features], query_parts)
    kv_whole = jnp.stack(
        [
            jnp.concatenate(
                [w_key[:, h * HD : (h + 1) * HD], w_value[:, h * HD : (h + 1) * HD]], axis=1
            )
            for h in kv_pick
        ]
    )

    grad_normed = jnp.concatenate([first_part, second_part], axis=0) + jnp.einsum(
        "trq,tdq->rd", kv_blocks, kv_whole, preferred_element_type=F32
    )
    inputs_own = jnp.concatenate([own_rows(tokens, c) for c in chunks], axis=0).astype(F32)
    inverse_own = lax.rsqrt(jnp.mean(inputs_own * inputs_own, axis=-1, keepdims=True) + EPSILON)
    attn_gain = jnp.sum(grad_normed * inputs_own * inverse_own, axis=0)
    scaled_one = grad_normed * norm_attn
    grad_inputs = (
        jnp.concatenate([middle_first, middle_second], axis=0)
        + inverse_own * scaled_one
        - inputs_own * inverse_own**3 * jnp.mean(scaled_one * inputs_own, axis=-1, keepdims=True)
    ).astype(BF16)

    def put_rows(target, piece, source):
        for c in chunks:
            target = lax.dynamic_update_slice_in_dim(
                target, piece[c * share : (c + 1) * share], row_of[c][source], 0
            )
        return target

    gains = jnp.stack([attn_gain, gain_first + gain_second], axis=1).astype(BF16)
    grad_inputs, gains, dq_second, kv_far, kv_near, w_gates = hold(
        grad_inputs, gains, dq_second, kv_far, kv_near, w_gates
    )
    gate_up_grad = plane_sum(w_gates)

    def put_share(target, piece, source):
        return lax.dynamic_update_slice_in_dim(target, piece, source * n_part, 0)

    tokens_gather = Gather(grad_inputs)
    tokens_grad = jnp.zeros((tok_rows, width), BF16)
    mixed = jnp.zeros((tok_rows, width), BF16)
    hop = tokens_gather.step()
    kv_sent = lax.ppermute(kv_far, "ctx", over)
    dq_home = lax.ppermute(dq_second, "ctx", over)
    grad_kv_raw = (kv_near + kv_sent.astype(F32)).astype(BF16)
    query_kv = t_dot(
        normed, jnp.concatenate([natural(dq_first, dq_home), grad_kv_raw], axis=1)
    ).astype(BF16)
    gains = jnp.pad(gains, ((0, 0), (0, 126)))
    rest = jnp.concatenate([w_downs, w_outs, query_kv, gains], axis=1)
    tokens_grad = tokens_gather.place_hop(put_rows, tokens_grad, 0)
    hop, rest, tokens_grad = hold(hop, rest, tokens_grad)
    tokens_gather.held(hop)
    rest = plane_sum(rest)

    mixed_gather = Gather((middle_own + after(mlp_share, hop).astype(F32)).astype(BF16))
    hop, mixed_hop = tokens_gather.step(), mixed_gather.step()
    tokens_grad = tokens_gather.place_hop(put_rows, tokens_grad, 1)
    mixed = mixed_gather.place_hop(put_share, mixed, 0)
    hop, mixed_hop, tokens_grad, mixed, mixed_gather.piece = hold(
        hop, mixed_hop, tokens_grad, mixed, mixed_gather.piece
    )
    tokens_gather.held(hop)
    mixed_gather.held(mixed_hop)

    hop, mixed_hop = tokens_gather.step(), mixed_gather.step()
    tokens_grad = tokens_gather.place_hop(put_rows, tokens_grad, 2)
    mixed = mixed_gather.place_hop(put_share, mixed, 1)
    hidden_units = w_down.shape[1]
    rest = after(rest, tokens_gather.rights[-2])
    down_grad = rest[:, :hidden_units]
    output_plane = rest[:, hidden_units : hidden_units + groups * features]
    query_plane = rest[:, hidden_units + groups * features :]
    query_grad, small = query_plane[:, :features].astype(F32), query_plane[:, features:]
    blocks = send_blocks(
        lambda j: jnp.concatenate(
            [lax.dynamic_slice_in_dim(output_plane, j * features, features, 1), small], axis=1
        )
    )
    hop, mixed_hop, tokens_grad, mixed, blocks = hold(hop, mixed_hop, tokens_grad, mixed, blocks)
    tokens_gather.held(hop)
    mixed_gather.held(mixed_hop)

    hop = mixed_gather.step()
    if groups > 3:
        tokens_grad = tokens_gather.place_hop(put_rows, tokens_grad, 3)
    mixed = mixed_gather.place_hop(put_share, mixed, 2)
    blocks = stack_blocks(blocks).astype(F32)
    output_grad = jnp.sum(blocks[:, :, :features], axis=0)
    kv_share = blocks.shape[1] // groups
    kv_blocks = lax.dynamic_slice_in_dim(
        blocks[:, :, features : features + 2 * HD], member * kv_share, kv_share, 1
    )
    gains = jnp.sum(blocks[:, :, features + 2 * HD : features + 2 * HD + 2], axis=0).T
    hop, tokens_grad, mixed = hold(hop, tokens_grad, mixed)
    mixed_gather.held(hop)
    for count in range(3, groups):
        mixed = mixed_gather.place_hop(put_share, mixed, count)
        if count + 1 < groups:
            tokens_gather.step()
            mixed_gather.step()
            tokens_grad = tokens_gather.place_hop(put_rows, tokens_grad, count + 1)

    key_heads, value_heads = [], []
    for h in range(kv_count):
        total = jnp.zeros((kv_share, 2 * HD), F32)
        for g in range(groups):
            if kv_pick[g] == h:
                total = total + kv_blocks[g]
        key_heads.append(total[:, :HD])
        value_heads.append(total[:, HD:])
    key_grad = jnp.concatenate(key_heads, axis=1)
    value_grad = jnp.concatenate(value_heads, axis=1)

    return (
        mixed,
        tokens_grad,
        gains[0],
        query_grad,
        key_grad,
        value_grad,
        output_grad,
        gains[1],
        gate_up_grad[:, :hidden_units].astype(F32),
        gate_up_grad[:, hidden_units:].astype(F32),
        down_grad.astype(F32),
    )


def solution(mesh):
    placed = (
        P(("dp", "ctx"), None),
        P(("dp", "ctx"), None),
        P("dp", None),
        P(),
        P(None, "tensor"),
        P(),
        P(),
        P(None, "tensor"),
        P(),
        P(None, "tensor"),
        P(None, "tensor"),
        P(None, "tensor"),
    )
    return jax.shard_map(
        body,
        mesh=mesh,
        in_specs=placed,
        out_specs=(
            P(("dp", "ctx"), None),
            P(("dp", "ctx"), None),
            P(("dp", "ctx")),
            P(("dp", "ctx"), "tensor"),
            P(("dp", "ctx", "tensor"), None),
            P(("dp", "ctx", "tensor"), None),
            P(("dp", "ctx"), "tensor"),
            P(("dp", "ctx")),
            P(("dp", "ctx"), "tensor"),
            P(("dp", "ctx"), "tensor"),
            P(("dp", "ctx"), "tensor"),
        ),
        check_vma=False,
    )
```

```python
import jax
import jax.numpy as jnp
import numpy as np
from jax import lax
from jax.experimental import pallas as pl
from jax.experimental.pallas import tpu as pltpu
from jax.sharding import PartitionSpec as P

NT = (((1,), (1,)), ((), ()))
F32 = jnp.float32
BF16 = jnp.bfloat16
HD = 64
GROUP = 256
EPSILON = 1e-05
LIGHT = pl.CostEstimate(flops=1, bytes_accessed=1, transcendentals=0)


def turn(values, cos, sin):
    low = (lax.broadcasted_iota(jnp.int32, values.shape, 1) % HD) < HD // 2
    other = jnp.where(
        low, pltpu.roll(values, 128 - HD // 2, 1), pltpu.roll(values, HD // 2, 1)
    )
    return values * cos + other * sin


def project_kernel(
    head,
    tokens_ref,
    gain_ref,
    k_weight,
    v_weight,
    q_weight,
    cos_part,
    sin_part,
    kv_ref,
    q_ref,
    normed_ref,
    cos_ref,
    sin_ref,
):
    inputs = tokens_ref[...].astype(F32)
    inverse = lax.rsqrt(jnp.mean(inputs * inputs, axis=-1, keepdims=True) + EPSILON)
    normed = (inputs * inverse * gain_ref[...]).astype(BF16)
    normed_ref[...] = normed
    cos, sin = cos_part[...], sin_part[...]
    cos = jnp.concatenate([cos, cos, cos, cos], axis=0).T
    sin = jnp.concatenate([-sin, sin, -sin, sin], axis=0).T
    cos_ref[...] = cos
    sin_ref[...] = sin
    first = head[0] % 2 == 0
    key = jnp.dot(normed, k_weight[...], preferred_element_type=F32)
    value = jnp.dot(normed, v_weight[...], preferred_element_type=F32)
    key = jnp.where(first, key, pltpu.roll(key, HD, 1))
    value = jnp.where(first, pltpu.roll(value, HD, 1), value)
    is_key = lax.broadcasted_iota(jnp.int32, key.shape, 1) < HD
    kv_ref[...] = jnp.where(is_key, turn(key, cos, sin), value).astype(BF16)
    raw = jnp.dot(normed, q_weight[...], preferred_element_type=F32)
    for start in range(0, q_ref.shape[1], 128):
        pair = raw[:, start : start + 128]
        q_ref[:, start : start + 128] = (turn(pair, cos, sin) * HD**-0.5).astype(BF16)


def project(head, tokens, gain, k_weight, v_weight, q_weight, cos, sin):
    rows, width = tokens.shape
    columns = q_weight.shape[1]
    block = 256
    two_heads = pl.BlockSpec((width, 128), lambda i, head: (0, head[0] // 2))
    return pl.pallas_call(
        project_kernel,
        grid_spec=pltpu.PrefetchScalarGridSpec(
            num_scalar_prefetch=1,
            grid=(rows // block,),
            in_specs=[
                pl.BlockSpec((block, width), lambda i, head: (i, 0)),
                pl.BlockSpec((1, width), lambda i, head: (0, 0)),
                two_heads,
                two_heads,
                pl.BlockSpec((width, columns), lambda i, head: (0, 0)),
                pl.BlockSpec((HD // 2, block), lambda i, head: (0, i)),
                pl.BlockSpec((HD // 2, block), lambda i, head: (0, i)),
            ],
            out_specs=[
                pl.BlockSpec((block, 128), lambda i, head: (i, 0)),
                pl.BlockSpec((block, columns), lambda i, head: (i, 0)),
                pl.BlockSpec((block, width), lambda i, head: (i, 0)),
                pl.BlockSpec((block, 128), lambda i, head: (i, 0)),
                pl.BlockSpec((block, 128), lambda i, head: (i, 0)),
            ],
        ),
        out_shape=[
            jax.ShapeDtypeStruct((rows, 128), BF16),
            jax.ShapeDtypeStruct((rows, columns), BF16),
            jax.ShapeDtypeStruct((rows, width), BF16),
            jax.ShapeDtypeStruct((rows, 128), F32),
            jax.ShapeDtypeStruct((rows, 128), F32),
        ],
        compiler_params=pltpu.CompilerParams(vmem_limit_bytes=48 * 2**20),
        cost_estimate=LIGHT,
        name="project",
    )(head, tokens, gain.reshape(1, width), k_weight, v_weight, q_weight, cos, sin)


def fwd_kernel(offsets, meta, q_ref, ka_ref, kb_ref, vt_ref, o_ref, lse_ref):
    half = q_ref.shape[0] // 2
    span = 2 * half
    group = min(GROUP, half)
    pairs = q_ref.shape[1] // 128
    for part, offset in enumerate(offsets):
        at = slice(part * half, part * half + half)
        queries = [q_ref[at, p * 128 : p * 128 + 128] for p in range(pairs)]
        chains = [(p, keys_ref) for p in range(pairs) for keys_ref in (ka_ref, kb_ref)]
        seen = meta[part]
        own = pl.multiple_of(meta[2 + seen] * span, span)
        heads = []
        for p, keys_ref in chains:
            tops, sums = [], []
            for first in range(0, half, group):
                count = offset + first + group
                rows = pl.ds(own, count)
                scores = lax.dot_general(
                    keys_ref[rows, :],
                    queries[p][first : first + group],
                    NT,
                    preferred_element_type=F32,
                )
                key_at = lax.broadcasted_iota(jnp.int32, scores.shape, 0)
                row_at = lax.broadcasted_iota(jnp.int32, scores.shape, 1) + (offset + first)
                scores = jnp.where(key_at <= row_at, scores, -1e30)
                top = jnp.max(scores, axis=0, keepdims=True)
                weights = jnp.exp(scores - top).astype(BF16)
                tops.append(top)
                sums.append(jnp.dot(vt_ref[:, rows], weights, preferred_element_type=F32))
            heads += [jnp.concatenate(tops, axis=1), jnp.concatenate(sums, axis=1)]

        def step(index, carry):
            rows = pl.ds(pl.multiple_of(meta[2 + index] * span, span), span)
            out = []
            for chain, (p, keys_ref) in enumerate(chains):
                top, total = carry[2 * chain : 2 * chain + 2]
                scores = lax.dot_general(
                    keys_ref[rows, :], queries[p], NT, preferred_element_type=F32
                )
                new_top = jnp.maximum(top, jnp.max(scores, axis=0, keepdims=True))
                weights = jnp.exp(scores - new_top).astype(BF16)
                total = total * jnp.exp(top - new_top) + jnp.dot(
                    vt_ref[:, rows], weights, preferred_element_type=F32
                )
                out += [new_top, total]
            return tuple(out)

        heads = lax.fori_loop(0, seen, step, tuple(heads))
        for p in range(pairs):
            top0, total0, top1, total1 = heads[4 * p : 4 * p + 4]
            norm0, norm1 = total0[HD : HD + 1], total1[HD : HD + 1]
            o_ref[at, p * 128 : p * 128 + 128] = (
                jnp.concatenate([total0[:HD] / norm0, total1[:HD] / norm1], axis=0).T.astype(BF16)
            )
            lse_ref[p, :, at] = jnp.concatenate(
                [top0 + jnp.log(norm0), top1 + jnp.log(norm1), jnp.zeros((6, half), F32)], axis=0
            )


def spread(kv_refs, ka_ref, kb_ref, va_ref, vb_ref, kt_ref, vt_ref):
    at = 0
    for kv_ref in kv_refs:
        rows = kv_ref.shape[0]
        block = min(512, rows)
        for first in range(0, rows, block):
            here = slice(at + first, at + first + block)
            pair = kv_ref[first : first + block, :].astype(F32)
            other = pltpu.roll(pair, HD, 1)
            left = lax.broadcasted_iota(jnp.int32, pair.shape, 1) < HD
            ka_ref[here, :] = jnp.where(left, pair, 0.0).astype(BF16)
            vb_ref[here, :] = jnp.where(left, 0.0, pair).astype(BF16)
            va_ref[here, :] = jnp.where(left, other, 0.0).astype(BF16)
            kb_ref[here, :] = jnp.where(left, 0.0, other).astype(BF16)
            turned = pair.T
            kt_ref[:, here] = turned[:HD].astype(BF16)
            ones = jnp.where(lax.broadcasted_iota(jnp.int32, (16, block), 0) == 0, 1.0, 0.0)
            vt_ref[:, here] = jnp.concatenate([turned[HD:], ones], axis=0).astype(BF16)
        at += rows


def attend_cost(rows, length, width):
    return pl.CostEstimate(
        flops=8 * rows * length * width, bytes_accessed=2**23, transcendentals=0
    )


def attend_first(meta, offsets, queries, kv_own, kv_other):
    rows, width = queries.shape
    pairs = width // 128
    together = 2 if pairs % 2 == 0 else 1
    length = 2 * kv_own.shape[0]

    def whole(shape):
        return pl.BlockSpec(shape, lambda p, m: (0, 0))

    def kernel(meta, q_ref, own, other, o_ref, lse_ref, ka, kb, va, vb, kt, vt):
        @pl.when(pl.program_id(0) == 0)
        def _():
            spread((own, other), ka, kb, va, vb, kt, vt)

        fwd_kernel(offsets, meta, q_ref, ka, kb, vt, o_ref, lse_ref)

    wide = (length, 128)
    forms = [wide, wide, wide, wide, (HD, length), (HD + 16, length)]
    return pl.pallas_call(
        kernel,
        grid_spec=pltpu.PrefetchScalarGridSpec(
            num_scalar_prefetch=1,
            grid=(pairs // together,),
            in_specs=[
                pl.BlockSpec((rows, 128 * together), lambda p, m: (0, p)),
                whole(kv_own.shape),
                whole(kv_other.shape),
            ],
            out_specs=[
                pl.BlockSpec((rows, 128 * together), lambda p, m: (0, p)),
                pl.BlockSpec((together, 8, rows), lambda p, m: (p, 0, 0)),
            ]
            + [whole(form) for form in forms],
        ),
        out_shape=[
            jax.ShapeDtypeStruct((rows, width), BF16),
            jax.ShapeDtypeStruct((pairs, 8, rows), F32),
        ]
        + [jax.ShapeDtypeStruct(form, BF16) for form in forms],
        compiler_params=pltpu.CompilerParams(vmem_limit_bytes=58 * 2**20),
        cost_estimate=attend_cost(rows, length, width),
        name="attend_first",
    )(meta, queries, kv_own, kv_other)


def attend(meta, offsets, queries, keys_a, keys_b, values_t):
    rows, width = queries.shape
    pairs = width // 128
    together = 2 if pairs % 2 == 0 else 1
    length = keys_a.shape[0]
    whole = pl.BlockSpec((length, 128), lambda p, m: (0, 0))

    def kernel(*refs):
        fwd_kernel(offsets, *refs)

    return pl.pallas_call(
        kernel,
        grid_spec=pltpu.PrefetchScalarGridSpec(
            num_scalar_prefetch=1,
            grid=(pairs // together,),
            in_specs=[
                pl.BlockSpec((rows, 128 * together), lambda p, m: (0, p)),
                whole,
                whole,
                pl.BlockSpec(values_t.shape, lambda p, m: (0, 0)),
            ],
            out_specs=[
                pl.BlockSpec((rows, 128 * together), lambda p, m: (0, p)),
                pl.BlockSpec((together, 8, rows), lambda p, m: (p, 0, 0)),
            ],
        ),
        out_shape=[
            jax.ShapeDtypeStruct((rows, width), BF16),
            jax.ShapeDtypeStruct((pairs, 8, rows), F32),
        ],
        compiler_params=pltpu.CompilerParams(vmem_limit_bytes=58 * 2**20),
        cost_estimate=attend_cost(rows, length, width),
        name="attend",
    )(meta, queries, keys_a, keys_b, values_t)


def bwd_kernel(
    offsets,
    meta,
    q_ref,
    o_ref,
    g_ref,
    lse_ref,
    ka_ref,
    kb_ref,
    va_ref,
    vb_ref,
    kt_ref,
    cos_ref,
    sin_ref,
    dq_ref,
    dk_ref,
    dv_ref,
):
    half = q_ref.shape[0] // 2
    span = 2 * half
    group = min(GROUP, half)

    for part, offset in enumerate(offsets):
        at = slice(part * half, part * half + half)
        queries, grads = q_ref[at, :], g_ref[at, :]
        left = lax.broadcasted_iota(jnp.int32, (half, 128), 1) < HD
        products = (grads.astype(F32) * o_ref[at, :].astype(F32)).T
        zero = jnp.zeros_like(queries)
        sides = []
        for side, (keys_ref, values_ref) in enumerate(((ka_ref, va_ref), (kb_ref, vb_ref))):
            mine = left if side == 0 else jnp.logical_not(left)
            delta = jnp.sum(products[side * HD : side * HD + HD], axis=0, keepdims=True)
            sides.append(
                (
                    keys_ref,
                    values_ref,
                    jnp.where(mine, queries, zero),
                    jnp.where(mine, grads, zero),
                    lse_ref[0, side : side + 1, at],
                    delta,
                )
            )

        def block(rows, first, count, masked):
            cut = slice(first, first + count)
            dqs = []
            dk_add = dv_add = None
            for keys_ref, values_ref, q_mine, g_mine, lse, delta in sides:
                scores = lax.dot_general(
                    keys_ref[rows, :], queries[cut], NT, preferred_element_type=F32
                )
                probs = jnp.exp(scores - lse[:, cut])
                if masked:
                    key_at = lax.broadcasted_iota(jnp.int32, scores.shape, 0)
                    row_at = lax.broadcasted_iota(jnp.int32, scores.shape, 1) + (offset + first)
                    probs = jnp.where(key_at <= row_at, probs, 0.0)
                grad_probs = lax.dot_general(
                    values_ref[rows, :], grads[cut], NT, preferred_element_type=F32
                )
                grad_scores = (probs * (grad_probs - delta[:, cut])).astype(BF16)
                dv_new = jnp.dot(probs.astype(BF16), g_mine[cut], preferred_element_type=F32)
                dk_new = jnp.dot(grad_scores, q_mine[cut], preferred_element_type=F32)
                dv_add = dv_new if dv_add is None else dv_add + dv_new
                dk_add = dk_new if dk_add is None else dk_add + dk_new
                dqs.append(jnp.dot(kt_ref[:, rows], grad_scores, preferred_element_type=F32))
            dv_ref[rows, :] += dv_add
            dk_ref[rows, :] += dk_add
            return jnp.concatenate(dqs, axis=0)

        own = pl.multiple_of(meta[2 + meta[part]] * span, span)
        start = jnp.concatenate(
            [
                block(pl.ds(own, offset + first + group), first, group, True)
                for first in range(0, half, group)
            ],
            axis=1,
        )

        def step(index, total):
            rows = pl.ds(pl.multiple_of(meta[2 + index] * span, span), span)
            return total + block(rows, 0, half, False)

        dq = lax.fori_loop(0, meta[part], step, start).T * (HD**-0.5)
        dq_ref[at, :] = turn(dq, cos_ref[at, :], -sin_ref[at, :]).astype(BF16)


def back_specs(queries, forms):
    rows, width = queries.shape
    pair = pl.BlockSpec((rows, 128), lambda p, m: (0, p))
    table = pl.BlockSpec((rows, 128), lambda p, m: (0, 0))
    specs = [pair, pair, pair, pl.BlockSpec((1, 8, rows), lambda p, m: (p, 0, 0))]
    specs += [pl.BlockSpec(form.shape, lambda p, m: (0, 0)) for form in forms]
    return pair, specs + [table, table]


def attend_back_first(meta, offsets, queries, outputs, grads, lse, forms, cos, sin):
    length = forms[0].shape[0]
    pair, specs = back_specs(queries, forms)
    whole = pl.BlockSpec((length, 128), lambda p, m: (0, 0))

    def kernel(*refs):
        dk_ref, dv_ref = refs[-2:]

        @pl.when(pl.program_id(0) == 0)
        def _():
            dk_ref[...] = jnp.zeros(dk_ref.shape, F32)
            dv_ref[...] = jnp.zeros(dv_ref.shape, F32)

        bwd_kernel(offsets, *refs)

    return pl.pallas_call(
        kernel,
        grid_spec=pltpu.PrefetchScalarGridSpec(
            num_scalar_prefetch=1,
            grid=(queries.shape[1] // 128,),
            in_specs=specs,
            out_specs=[pair, whole, whole],
        ),
        out_shape=[
            jax.ShapeDtypeStruct(queries.shape, BF16),
            jax.ShapeDtypeStruct((length, 128), F32),
            jax.ShapeDtypeStruct((length, 128), F32),
        ],
        compiler_params=pltpu.CompilerParams(vmem_limit_bytes=58 * 2**20),
        cost_estimate=LIGHT,
        name="attend_back_first",
    )(meta, queries, outputs, grads, lse, *forms, cos, sin)


def attend_back_last(
    meta, offsets, queries, outputs, grads, lse, forms, cos, sin, dk, dv, all_cos, all_sin
):
    length = forms[0].shape[0]
    near = length // 2
    pair, specs = back_specs(queries, forms)
    whole = pl.BlockSpec((length, 128), lambda p, m: (0, 0))
    half = pl.BlockSpec((near, 128), lambda p, m: (0, 0))

    def kernel(*refs):
        dk_in, dv_in, cos_ref, sin_ref, dq_ref, near_ref, far_ref, dk_ref, dv_ref = refs[-9:]

        @pl.when(pl.program_id(0) == 0)
        def _():
            dk_ref[...] = dk_in[...]
            dv_ref[...] = dv_in[...]

        bwd_kernel(offsets, *refs[:-9], dq_ref, dk_ref, dv_ref)

        @pl.when(pl.program_id(0) == pl.num_programs(0) - 1)
        def _():
            block = min(512, near)
            for first in range(0, length, block):
                here = slice(first, first + block)
                dk_block, dv_block = dk_ref[here, :], dv_ref[here, :]
                dk_block = dk_block + pltpu.roll(dk_block, HD, 1)
                dv_block = dv_block + pltpu.roll(dv_block, HD, 1)
                left = lax.broadcasted_iota(jnp.int32, dk_block.shape, 1) < HD
                both = jnp.where(
                    left, turn(dk_block, cos_ref[here, :], -sin_ref[here, :]), dv_block
                )
                if first < near:
                    near_ref[here, :] = both
                else:
                    far_ref[first - near : first - near + block, :] = both.astype(BF16)

    return pl.pallas_call(
        kernel,
        grid_spec=pltpu.PrefetchScalarGridSpec(
            num_scalar_prefetch=1,
            grid=(queries.shape[1] // 128,),
            in_specs=specs + [whole] * 4,
            out_specs=[pair, half, half],
            scratch_shapes=[pltpu.VMEM((length, 128), F32), pltpu.VMEM((length, 128), F32)],
        ),
        out_shape=[
            jax.ShapeDtypeStruct(queries.shape, BF16),
            jax.ShapeDtypeStruct((near, 128), F32),
            jax.ShapeDtypeStruct((near, 128), BF16),
        ],
        compiler_params=pltpu.CompilerParams(vmem_limit_bytes=60 * 2**20),
        cost_estimate=LIGHT,
        name="attend_back_last",
    )(meta, queries, outputs, grads, lse, *forms, cos, sin, dk, dv, all_cos, all_sin)


def feed_kernel(
    gathered_ref,
    tokens_ref,
    cotangent_ref,
    gain_ref,
    output_weight,
    gate_weight,
    up_weight,
    down_weight,
    *refs,
):
    middle_ref, normed_ref, hidden_ref, gates_ref, down_ref, grad_ref = refs[-6:]
    middle = tokens_ref[...].astype(F32)
    for source in range(gathered_ref.shape[0]):
        middle = middle + lax.dot_general(
            gathered_ref[source], output_weight[source], NT, preferred_element_type=F32
        )
    middle_ref[...] = middle
    inverse = lax.rsqrt(jnp.mean(middle * middle, axis=-1, keepdims=True) + EPSILON)
    normed = (middle * inverse * gain_ref[...]).astype(BF16)
    normed_ref[...] = normed
    gate = jnp.dot(normed, gate_weight[...], preferred_element_type=F32)
    up = jnp.dot(normed, up_weight[...], preferred_element_type=F32)
    grad_hidden = jnp.dot(cotangent_ref[...], down_weight[...], preferred_element_type=F32)
    sigmoid = jax.nn.sigmoid(gate)
    hidden = (gate * sigmoid * up).astype(BF16)
    hidden_ref[...] = hidden
    grad_gate = (grad_hidden * up * sigmoid * (1.0 + gate * (1.0 - sigmoid))).astype(BF16)
    grad_up = (grad_hidden * gate * sigmoid).astype(BF16)
    units = hidden.shape[1]
    gates_ref[:, :units] = grad_gate
    gates_ref[:, units:] = grad_up
    down_ref[...] = lax.dot_general(
        hidden, down_weight[...], NT, preferred_element_type=F32
    ).astype(BF16)
    grad_ref[...] = (
        lax.dot_general(grad_gate, gate_weight[...], NT, preferred_element_type=F32)
        + lax.dot_general(grad_up, up_weight[...], NT, preferred_element_type=F32)
    ).astype(BF16)


def feed_forward(c, gathered, tokens, cotangent, gain, output_weight, weights, earlier):
    rows, width = tokens.shape
    units = weights[0].shape[1]
    block = min(256, rows // 4)
    quarter = rows // 4 // block
    if c:
        place = lambda i: (i + quarter, 0)
    else:
        place = lambda i: (jnp.where(i < quarter, i, i + 2 * quarter), 0)
    once = pl.Buffered(1)

    def natural(columns):
        return pl.BlockSpec((block, columns), place)

    def whole(array):
        zeros = (0,) * array.ndim
        return pl.BlockSpec(array.shape, lambda i: zeros, pipeline_mode=once)

    shapes = [
        jax.ShapeDtypeStruct((rows, width), F32),
        jax.ShapeDtypeStruct((rows, width), BF16),
        jax.ShapeDtypeStruct((rows, units), BF16),
        jax.ShapeDtypeStruct((rows, 2 * units), BF16),
        jax.ShapeDtypeStruct((rows, width), BF16),
    ]
    gain = gain.reshape(1, width)
    return pl.pallas_call(
        feed_kernel,
        grid=(2 * quarter,),
        in_specs=[
            pl.BlockSpec((gathered.shape[0], block, gathered.shape[2]), lambda i: (0, i, 0)),
            natural(width),
            natural(width),
            whole(gain),
            whole(output_weight),
        ]
        + [whole(weight) for weight in weights]
        + [pl.BlockSpec(memory_space=pl.ANY) for _ in earlier],
        out_specs=[natural(shape.shape[1]) for shape in shapes]
        + [pl.BlockSpec((block, width), lambda i: (i, 0))],
        out_shape=shapes + [jax.ShapeDtypeStruct((rows // 2, width), BF16)],
        input_output_aliases={8 + k: k for k in range(len(earlier))},
        compiler_params=pltpu.CompilerParams(vmem_limit_bytes=60 * 2**20),
        cost_estimate=LIGHT,
        name="feed_forward",
    )(gathered, tokens, cotangent, gain, output_weight, *weights, *earlier)


def part_specs(shape):
    return [pl.BlockSpec(shape, lambda p, order: (0, 0, 0)) for _ in range(4)]


def join_kernel(order, rows_ref, *refs):
    out_ref = refs[4]
    for part, weight_ref in enumerate(refs[:4]):

        @pl.when(pl.program_id(0) == part)
        def _():
            result = None
            for source in range(rows_ref.shape[0]):
                term = lax.dot_general(
                    rows_ref[source], weight_ref[source], NT, preferred_element_type=F32
                )
                result = term if result is None else result + term
            out_ref[...] = result


def join(order, rows, parts):
    size, count, features = rows.shape
    columns = parts[0].shape[1]
    return pl.pallas_call(
        join_kernel,
        grid_spec=pltpu.PrefetchScalarGridSpec(
            num_scalar_prefetch=1,
            grid=(4,),
            in_specs=[pl.BlockSpec(rows.shape, lambda p, order: (0, 0, 0))]
            + part_specs(parts[0].shape),
            out_specs=pl.BlockSpec((count, columns), lambda p, order: (0, order[p])),
        ),
        out_shape=jax.ShapeDtypeStruct((count, 4 * columns), F32),
        compiler_params=pltpu.CompilerParams(vmem_limit_bytes=48 * 2**20),
        cost_estimate=LIGHT,
        name="join",
    )(order, rows, *parts)


def arrange_kernel(order, *refs):
    for part, weight_ref in enumerate(refs[:-1]):

        @pl.when(pl.program_id(0) == part)
        def _():
            refs[-1][...] = weight_ref[...].reshape(refs[-1].shape)


def arrange(order, parts, shape, block, place):
    zeros = (0,) * parts[0].ndim
    return pl.pallas_call(
        arrange_kernel,
        grid_spec=pltpu.PrefetchScalarGridSpec(
            num_scalar_prefetch=1,
            grid=(len(parts),),
            in_specs=[pl.BlockSpec(parts[0].shape, lambda p, order: zeros) for _ in parts],
            out_specs=pl.BlockSpec(block, lambda p, order: place(order[p])),
        ),
        out_shape=jax.ShapeDtypeStruct(shape, parts[0].dtype),
        compiler_params=pltpu.CompilerParams(vmem_limit_bytes=48 * 2**20),
        cost_estimate=LIGHT,
        name="arrange",
    )(order, *parts)


def quarter_row(row, c, half, span):
    if c:
        return half + row
    return row if row < half else row + span


def after(value, *earlier):
    return lax.optimization_barrier((value, earlier))[0]


def line_steps(size):
    return [
        (
            [(i, i + 1) for i in range(step - 1, size - 1)],
            [(i, i - 1) for i in range(1, size - step + 1)],
        )
        for step in range(1, size)
    ]


class Gather:
    def __init__(self, piece):
        self.piece = piece
        self.rights, self.lefts = [piece], [piece]
        self.hops = line_steps(lax.axis_size("tensor"))

    def step(self):
        done = len(self.rights) - 1
        if done < len(self.hops):
            to_right, to_left = self.hops[done]
            self.rights.append(lax.ppermute(self.rights[-1], "tensor", to_right))
            self.lefts.append(lax.ppermute(self.lefts[-1], "tensor", to_left))
        return self.rights[-1], self.lefts[-1]

    def held(self, pair):
        self.rights[-1], self.lefts[-1] = pair

    def place_hop(self, place, target, hop):
        size = lax.axis_size("tensor")
        me = lax.axis_index("tensor")
        if hop == 0:
            return place(target, self.piece, me)
        right, left = self.rights[hop], self.lefts[hop]
        from_left, from_right = me >= hop, me + hop < size
        if 2 * hop >= size:
            piece = jnp.where(from_left, right, jnp.where(from_right, left, self.piece))
            source = jnp.where(from_left, me - hop, jnp.where(from_right, me + hop, me))
            return place(target, piece, source)
        target = place(
            target, jnp.where(from_left, right, self.piece), jnp.where(from_left, me - hop, me)
        )
        return place(
            target, jnp.where(from_right, left, self.piece), jnp.where(from_right, me + hop, me)
        )

    def whole(self):
        size = lax.axis_size("tensor")
        me = lax.axis_index("tensor")
        while len(self.rights) <= len(self.hops):
            self.step()
        parts, order = [self.piece], [me]
        for hop in range(1, size):
            for came, source in ((self.rights[hop], me - hop), (self.lefts[hop], me + hop)):
                parts.append(came)
                order.append(jnp.where((source >= 0) & (source < size), source, me))
        parts, order = parts[::-1], order[::-1]
        shape = self.piece.shape
        return arrange(
            jnp.stack(order).astype(jnp.int32),
            parts,
            (size, *shape),
            (1, *shape),
            lambda i: (i,) + (0,) * len(shape),
        )


def send_blocks(pick, across=False):
    size = lax.axis_size("tensor")
    me = lax.axis_index("tensor")
    arrived = []
    for shift in range(size):
        block = pick(lax.rem(me + shift, size))
        if across:
            block = lax.ppermute(
                block,
                ("ctx", "tensor"),
                [
                    (c * size + i, (1 - c) * size + (i + shift) % size)
                    for c in range(2)
                    for i in range(size)
                ],
            )
        elif shift:
            block = lax.ppermute(block, "tensor", [(i, (i + shift) % size) for i in range(size)])
        arrived.append(block)
    return tuple(arrived)


def stack_blocks(arrived):
    size = len(arrived)
    me = lax.axis_index("tensor")
    out = jnp.zeros((size, *arrived[0].shape), arrived[0].dtype)
    for shift, block in enumerate(arrived):
        out = lax.dynamic_update_index_in_dim(out, block, lax.rem(me - shift + size, size), 0)
    return out


def hold(*values):
    return lax.optimization_barrier(values)


def rows_part(weight, index, count):
    rows = weight.shape[0] // count
    return lax.dynamic_slice_in_dim(weight, index * rows, rows, 0)


def dot(a, b):
    return jnp.dot(a, b, preferred_element_type=F32)


def dot_t(a, b):
    return jnp.einsum("rf,df->rd", a, b, preferred_element_type=F32)


def t_dot(a, b):
    return jnp.einsum("rd,rf->df", a, b, preferred_element_type=F32)


def body(
    tokens,
    cotangent,
    span_order,
    norm_attn,
    w_query,
    w_key,
    w_value,
    w_output,
    norm_mlp,
    w_gate,
    w_up,
    w_down,
):
    tok_rows, width = tokens.shape
    groups = lax.axis_size("tensor")
    member = lax.axis_index("tensor")
    n_ctx = lax.axis_size("ctx")
    assert n_ctx == 2
    ctx_index = lax.axis_index("ctx")
    features = w_query.shape[1]
    kv_count = w_key.shape[1] // HD
    kv_pick = np.arange(groups) * kv_count // groups
    head = (member * kv_count // groups).astype(jnp.int32).reshape(1)
    span = tok_rows // 2
    half = span // 2
    share = span // groups
    over = [(0, 1), (1, 0)]
    chunks = range(2)

    def chunk(array, c):
        if c:
            return array[half : half + span]
        return jnp.concatenate([array[:half], array[half + span :]], axis=0)

    def natural(first, second):
        return jnp.concatenate([first[:half], second, first[half:]], axis=0)

    order = jnp.roll(span_order[0], -2 * ctx_index)
    places = jnp.arange(4, dtype=jnp.int32)
    slot_of = jnp.sum(
        jnp.where(order[None, :] == places[:, None], places[None, :], 0), axis=1, dtype=jnp.int32
    )
    metas = [jnp.concatenate([order[2 * c : 2 * c + 2], slot_of]) for c in chunks]
    offsets = [(0, half), (half, 0)]

    positions = (order[:, None] * span + jnp.arange(span, dtype=jnp.int32)[None, :]).reshape(-1)
    frequency = 10000.0 ** (-jnp.arange(HD // 2, dtype=F32) / (HD // 2))

    def table(positions):
        angles = frequency[:, None] * positions.astype(F32)[None, :]
        cos_part, sin_part = hold(jnp.cos(angles), jnp.sin(angles))
        cos_part, sin_part = cos_part.T, sin_part.T
        return (
            jnp.concatenate([cos_part] * 4, axis=1),
            jnp.concatenate([-sin_part, sin_part] * 2, axis=1),
        )


    upper = lax.axis_index("dp") % 2
    beside = [(i, i ^ 1) for i in range(lax.axis_size("dp"))]
    quarters = jnp.stack(
        [
            2 * upper + ctx_index,
            2 * upper + 1 - ctx_index,
            2 - 2 * upper + ctx_index,
            3 - 2 * upper - ctx_index,
        ]
    ).astype(jnp.int32)

    output_gather = Gather(rows_part(w_output, upper, 2))
    hop = output_gather.step()
    angles = frequency[:, None] * positions[:tok_rows].astype(F32)[None, :]
    cos_part, sin_part = hold(jnp.cos(angles), jnp.sin(angles))
    kv_own, queries, normed, cos_near, sin_near = project(
        head, tokens, norm_attn, w_key, w_value, w_query, cos_part, sin_part
    )
    kv_own, queries, normed, hop, quarters = hold(kv_own, queries, normed, hop, quarters)
    output_gather.held(hop)
    kv_other = lax.ppermute(kv_own, "ctx", over)
    hop = output_gather.step()
    kv_own, kv_other, sent, kept, normed, hop = hold(
        kv_own, kv_other, chunk(queries, 1), chunk(queries, 0), normed, hop
    )
    output_gather.held(hop)
    length = 2 * tok_rows

    foreign = lax.ppermute(sent, "ctx", over)
    hop = output_gather.step()
    first, first_log, *forms = attend_first(metas[0], offsets[0], kept, kv_own, kv_other)
    first, first_log, foreign, forms, hop = hold(first, first_log, foreign, forms, hop)
    output_gather.held(hop)
    *forms, values_t = forms
    first_whole = lax.all_gather(first, "tensor", axis=0, tiled=False)

    output_near = output_gather.whole()
    output_far = lax.ppermute(output_near, "dp", beside)
    second, second_log = attend(metas[1], offsets[1], foreign, forms[0], forms[1], values_t)
    second, second_log, output_near, output_far = hold(
        second, second_log, output_near, output_far
    )

    cos_far, sin_far = table(after(positions[tok_rows:], second))
    cos_pair = jnp.concatenate([cos_near, cos_far], axis=0)
    sin_pair = jnp.concatenate([sin_near, sin_far], axis=0)
    tables = [(chunk(cos_near, 0), chunk(sin_near, 0)), (chunk(cos_far, 1), chunk(sin_far, 1))]
    second_home = lax.ppermute(second, "ctx", over)
    half_rows = output_near.shape[1]
    output_whole = arrange(
        jnp.stack([upper, 1 - upper]).astype(jnp.int32),
        [output_near, output_far],
        (groups, 2 * half_rows, features),
        output_near.shape,
        lambda i: (0, i, 0),
    )
    second_home, output_whole, tables, cos_pair, sin_pair = hold(
        second_home, output_whole, tables, cos_pair, sin_pair
    )
    second_whole = lax.all_gather(second_home, "tensor", axis=0, tiled=False)
    queries = [kept, foreign]
    attention = [first, second]
    log_totals = [first_log, second_log]

    row_of = [
        jnp.asarray([quarter_row(i * share, c, half, span) for i in range(groups)], jnp.int32)
        for c in chunks
    ]

    def own_rows(array, c):
        return lax.dynamic_slice_in_dim(array, row_of[c][member], share, 0)

    def to_attention(c, middle, grad_share):
        middle = own_rows(middle, c)
        inverse_two = lax.rsqrt(jnp.mean(middle * middle, axis=-1, keepdims=True) + EPSILON)
        grad_normed_mlp = grad_share.astype(F32)
        gain = jnp.sum(grad_normed_mlp * middle * inverse_two, axis=0)
        scaled_two = grad_normed_mlp * norm_mlp
        grad_middle = (
            own_rows(cotangent, c).astype(F32)
            + inverse_two * scaled_two
            - middle * inverse_two**3 * jnp.mean(scaled_two * middle, axis=-1, keepdims=True)
        )
        grad_low = grad_middle.astype(BF16)
        blocks = jnp.einsum(
            "rd,tdq->trq", grad_low, output_whole, preferred_element_type=F32
        ).astype(BF16)
        return gain, grad_middle, grad_low, blocks

    def block_of(blocks):
        return lambda j: lax.dynamic_index_in_dim(blocks, j, 0, keepdims=False)

    def rows_of(array):
        return lambda j: lax.dynamic_slice_in_dim(array, j * share, share, 0)

    def line_sum(array):
        return lax.psum_scatter(array, "tensor", scatter_dimension=0, tiled=True)

    def plane_sum(gradient):
        return lax.psum_scatter(
            gradient.astype(BF16), ("dp", "ctx"), scatter_dimension=0, tiled=True
        )

    query_gather = Gather(rows_part(after(w_query, first_whole), 2 * upper + ctx_index, 4))
    hop = query_gather.step()
    weights = (w_gate, w_up, w_down)
    fixed = (tokens, cotangent, norm_mlp, output_whole, weights)
    *fed, grad_first = feed_forward(0, first_whole, *fixed, ())
    fed, grad_first, second_whole, hop = hold(fed, grad_first, second_whole, hop)
    query_gather.held(hop)

    share_first = line_sum(grad_first)
    hop = query_gather.step()
    *fed, grad_second = feed_forward(1, second_whole, *fixed, fed)
    fed, grad_second, hop = hold(fed, grad_second, hop)
    query_gather.held(hop)
    middle, normed_mlp, hidden, gates, mlp_part = fed

    share_second = line_sum(grad_second)
    hop = query_gather.step()
    w_gates = t_dot(normed_mlp, gates).astype(BF16)
    w_gates, hop, share_first = hold(w_gates, hop, share_first)
    query_gather.held(hop)

    mlp_share = line_sum(after(mlp_part, w_gates))

    gain_first, middle_first, low_first, blocks = to_attention(0, middle, share_first)
    query_part = query_gather.whole()
    gain_first, middle_first, low_first, blocks, hidden, query_part = hold(
        gain_first, middle_first, low_first, blocks, hidden, query_part
    )

    came_first = send_blocks(block_of(blocks))
    query_over = lax.ppermute(query_part, "ctx", over)
    w_downs = t_dot(cotangent, hidden).astype(BF16)
    n_part = tok_rows // groups
    middle_own = lax.dynamic_slice_in_dim(middle, member * n_part, n_part, 0)
    came_first, middle_own, query_part, query_over, w_downs = hold(
        came_first, middle_own, query_part, query_over, w_downs
    )

    query_near = (query_part, query_over)
    query_far = tuple(lax.ppermute(part, "dp", beside) for part in query_near)
    grads_first = stack_blocks(came_first).reshape(span, features)
    attention_rows = jnp.concatenate(
        [
            lax.dynamic_slice_in_dim(whole, member * share, share, 1)
            for whole in (first_whole, second_whole)
        ],
        axis=1,
    )
    attention_rows = jnp.swapaxes(attention_rows, 0, 1).reshape(2 * share, groups * features)
    query_near, query_far, grads_first, attention_rows, share_second = hold(
        query_near, query_far, grads_first, attention_rows, share_second
    )

    gain_second, middle_second, low_second, blocks = to_attention(1, middle, share_second)
    gain_second, middle_second, low_second, blocks = hold(
        gain_second, middle_second, low_second, blocks
    )

    def back_arguments(c, grads):
        return metas[c], offsets[c], queries[c], attention[c], grads, log_totals[c], forms, *tables[c]

    came_second = send_blocks(block_of(blocks), across=True)
    dq_first, dk, dv = attend_back_first(*back_arguments(0, grads_first))
    dq_first, dk, dv, came_second = hold(dq_first, dk, dv, came_second)

    rows_first = send_blocks(rows_of(dq_first))
    grads_second = stack_blocks(came_second).reshape(span, features)
    dq_second, kv_near, kv_far = attend_back_last(
        *back_arguments(1, grads_second), dk, dv, cos_pair, sin_pair
    )
    dq_second, kv_near, kv_far, rows_first = hold(dq_second, kv_near, kv_far, rows_first)

    def kv_share_of(array, j):
        return [lax.dynamic_slice_in_dim(array, row_of[c][j], share, 0) for c in chunks]

    kv_low = kv_near.astype(BF16)
    near_blocks = send_blocks(lambda j: jnp.concatenate(kv_share_of(kv_low, j), axis=1))
    far_blocks = send_blocks(
        lambda j: jnp.concatenate([rows_of(dq_second)(j), *kv_share_of(kv_far, j)], axis=1),
        across=True,
    )
    query_parts = query_near + query_far
    first_part = join(quarters, stack_blocks(rows_first), query_parts)
    w_outs = t_dot(jnp.concatenate([low_first, low_second], axis=0), attention_rows).astype(BF16)
    near_blocks, far_blocks, first_part, w_outs = hold(near_blocks, far_blocks, first_part, w_outs)
    far_blocks = stack_blocks(far_blocks)
    kv_blocks = (
        stack_blocks(near_blocks).astype(F32) + far_blocks[:, :, features:].astype(F32)
    ).astype(BF16)
    kv_blocks = jnp.concatenate([kv_blocks[:, :, : 2 * HD], kv_blocks[:, :, 2 * HD :]], axis=1)
    second_part = join(quarters, far_blocks[:, :, :features], query_parts)
    kv_whole = jnp.stack(
        [
            jnp.concatenate(
                [w_key[:, h * HD : (h + 1) * HD], w_value[:, h * HD : (h + 1) * HD]], axis=1
            )
            for h in kv_pick
        ]
    )

    grad_normed = jnp.concatenate([first_part, second_part], axis=0) + jnp.einsum(
        "trq,tdq->rd", kv_blocks, kv_whole, preferred_element_type=F32
    )
    inputs_own = jnp.concatenate([own_rows(tokens, c) for c in chunks], axis=0).astype(F32)
    inverse_own = lax.rsqrt(jnp.mean(inputs_own * inputs_own, axis=-1, keepdims=True) + EPSILON)
    attn_gain = jnp.sum(grad_normed * inputs_own * inverse_own, axis=0)
    scaled_one = grad_normed * norm_attn
    grad_inputs = (
        jnp.concatenate([middle_first, middle_second], axis=0)
        + inverse_own * scaled_one
        - inputs_own * inverse_own**3 * jnp.mean(scaled_one * inputs_own, axis=-1, keepdims=True)
    ).astype(BF16)

    def put_rows(target, piece, source):
        for c in chunks:
            target = lax.dynamic_update_slice_in_dim(
                target, piece[c * share : (c + 1) * share], row_of[c][source], 0
            )
        return target

    gains = jnp.stack([attn_gain, gain_first + gain_second], axis=1).astype(BF16)
    grad_inputs, gains, dq_second, kv_far, kv_near, w_gates = hold(
        grad_inputs, gains, dq_second, kv_far, kv_near, w_gates
    )
    gate_up_grad = plane_sum(w_gates)

    def put_share(target, piece, source):
        return lax.dynamic_update_slice_in_dim(target, piece, source * n_part, 0)

    mixed_share = (middle_own + mlp_share.astype(F32)).astype(BF16)
    tokens_gather, mixed_gather = Gather(grad_inputs), Gather(mixed_share)
    tokens_grad = jnp.zeros((tok_rows, width), BF16)
    mixed = jnp.zeros((tok_rows, width), BF16)
    hop, mixed_hop = tokens_gather.step(), mixed_gather.step()
    kv_sent = lax.ppermute(kv_far, "ctx", over)
    dq_home = lax.ppermute(dq_second, "ctx", over)
    grad_kv_raw = (kv_near + kv_sent.astype(F32)).astype(BF16)
    query_kv = t_dot(
        normed, jnp.concatenate([natural(dq_first, dq_home), grad_kv_raw], axis=1)
    ).astype(BF16)
    gains = jnp.pad(gains, ((0, 0), (0, 126)))
    rest = jnp.concatenate([w_downs, w_outs, query_kv, gains], axis=1)
    tokens_grad = tokens_gather.place_hop(put_rows, tokens_grad, 0)
    mixed = mixed_gather.place_hop(put_share, mixed, 0)
    hop, mixed_hop, rest, tokens_grad, mixed = hold(hop, mixed_hop, rest, tokens_grad, mixed)
    tokens_gather.held(hop)
    mixed_gather.held(mixed_hop)
    rest = plane_sum(rest)

    hop, mixed_hop = tokens_gather.step(), mixed_gather.step()
    tokens_grad = tokens_gather.place_hop(put_rows, tokens_grad, 1)
    mixed = mixed_gather.place_hop(put_share, mixed, 1)
    hop, mixed_hop, tokens_grad, mixed = hold(hop, mixed_hop, tokens_grad, mixed)
    tokens_gather.held(hop)
    mixed_gather.held(mixed_hop)

    hop = tokens_gather.step()
    tokens_grad = tokens_gather.place_hop(put_rows, tokens_grad, 2)
    mixed = mixed_gather.place_hop(put_share, mixed, 2)
    hop, tokens_grad, mixed = hold(hop, tokens_grad, mixed)
    tokens_gather.held(hop)

    mixed_hop = mixed_gather.step()
    if groups > 3:
        tokens_grad = tokens_gather.place_hop(put_rows, tokens_grad, 3)
    hidden_units = w_down.shape[1]
    rest = after(rest, hop)
    down_grad = rest[:, :hidden_units]
    output_plane = rest[:, hidden_units : hidden_units + groups * features]
    query_plane = rest[:, hidden_units + groups * features :]
    query_grad, small = query_plane[:, :features].astype(F32), query_plane[:, features:]
    blocks = send_blocks(
        lambda j: jnp.concatenate(
            [lax.dynamic_slice_in_dim(output_plane, j * features, features, 1), small], axis=1
        )
    )
    mixed_hop, tokens_grad, blocks = hold(mixed_hop, tokens_grad, blocks)
    mixed_gather.held(mixed_hop)
    blocks = stack_blocks(blocks).astype(F32)
    output_grad = jnp.sum(blocks[:, :, :features], axis=0)
    kv_share = blocks.shape[1] // groups
    kv_blocks = lax.dynamic_slice_in_dim(
        blocks[:, :, features : features + 2 * HD], member * kv_share, kv_share, 1
    )
    gains = jnp.sum(blocks[:, :, features + 2 * HD : features + 2 * HD + 2], axis=0).T
    for count in range(3, groups):
        mixed = mixed_gather.place_hop(put_share, mixed, count)
        if count + 1 < groups:
            tokens_gather.step()
            mixed_gather.step()
            tokens_grad = tokens_gather.place_hop(put_rows, tokens_grad, count + 1)

    key_heads, value_heads = [], []
    for h in range(kv_count):
        total = jnp.zeros((kv_share, 2 * HD), F32)
        for g in range(groups):
            if kv_pick[g] == h:
                total = total + kv_blocks[g]
        key_heads.append(total[:, :HD])
        value_heads.append(total[:, HD:])
    key_grad = jnp.concatenate(key_heads, axis=1)
    value_grad = jnp.concatenate(value_heads, axis=1)

    return (
        mixed,
        tokens_grad,
        gains[0],
        query_grad,
        key_grad,
        value_grad,
        output_grad,
        gains[1],
        gate_up_grad[:, :hidden_units].astype(F32),
        gate_up_grad[:, hidden_units:].astype(F32),
        down_grad.astype(F32),
    )


def solution(mesh):
    placed = (
        P(("dp", "ctx"), None),
        P(("dp", "ctx"), None),
        P("dp", None),
        P(),
        P(None, "tensor"),
        P(),
        P(),
        P(None, "tensor"),
        P(),
        P(None, "tensor"),
        P(None, "tensor"),
        P(None, "tensor"),
    )
    return jax.shard_map(
        body,
        mesh=mesh,
        in_specs=placed,
        out_specs=(
            P(("dp", "ctx"), None),
            P(("dp", "ctx"), None),
            P(("dp", "ctx")),
            P(("dp", "ctx"), "tensor"),
            P(("dp", "ctx", "tensor"), None),
            P(("dp", "ctx", "tensor"), None),
            P(("dp", "ctx"), "tensor"),
            P(("dp", "ctx")),
            P(("dp", "ctx"), "tensor"),
            P(("dp", "ctx"), "tensor"),
            P(("dp", "ctx"), "tensor"),
        ),
        check_vma=False,
    )
```

```python
import jax
import jax.numpy as jnp
import numpy as np
from jax import lax
from jax.experimental import pallas as pl
from jax.experimental.pallas import tpu as pltpu
from jax.sharding import PartitionSpec as P

NT = (((1,), (1,)), ((), ()))
F32 = jnp.float32
BF16 = jnp.bfloat16
HD = 64
GROUP = 256
EPSILON = 1e-05
LIGHT = pl.CostEstimate(flops=1, bytes_accessed=1, transcendentals=0)


def turn(values, cos, sin):
    low = (lax.broadcasted_iota(jnp.int32, values.shape, 1) % HD) < HD // 2
    other = jnp.where(
        low, pltpu.roll(values, 128 - HD // 2, 1), pltpu.roll(values, HD // 2, 1)
    )
    return values * cos + other * sin


def project_kernel(
    head,
    tokens_ref,
    gain_ref,
    k_weight,
    v_weight,
    q_weight,
    cos_part,
    sin_part,
    kv_ref,
    q_ref,
    normed_ref,
    cos_ref,
    sin_ref,
):
    inputs = tokens_ref[...].astype(F32)
    inverse = lax.rsqrt(jnp.mean(inputs * inputs, axis=-1, keepdims=True) + EPSILON)
    normed = (inputs * inverse * gain_ref[...]).astype(BF16)
    normed_ref[...] = normed
    cos, sin = cos_part[...], sin_part[...]
    cos = jnp.concatenate([cos, cos, cos, cos], axis=0).T
    sin = jnp.concatenate([-sin, sin, -sin, sin], axis=0).T
    cos_ref[...] = cos
    sin_ref[...] = sin
    first = head[0] % 2 == 0
    key = jnp.dot(normed, k_weight[...], preferred_element_type=F32)
    value = jnp.dot(normed, v_weight[...], preferred_element_type=F32)
    key = jnp.where(first, key, pltpu.roll(key, HD, 1))
    value = jnp.where(first, pltpu.roll(value, HD, 1), value)
    is_key = lax.broadcasted_iota(jnp.int32, key.shape, 1) < HD
    kv_ref[...] = jnp.where(is_key, turn(key, cos, sin), value).astype(BF16)
    raw = jnp.dot(normed, q_weight[...], preferred_element_type=F32)
    for start in range(0, q_ref.shape[1], 128):
        pair = raw[:, start : start + 128]
        q_ref[:, start : start + 128] = (turn(pair, cos, sin) * HD**-0.5).astype(BF16)


def project(head, tokens, gain, k_weight, v_weight, q_weight, cos, sin):
    rows, width = tokens.shape
    columns = q_weight.shape[1]
    block = 256
    two_heads = pl.BlockSpec((width, 128), lambda i, head: (0, head[0] // 2))
    return pl.pallas_call(
        project_kernel,
        grid_spec=pltpu.PrefetchScalarGridSpec(
            num_scalar_prefetch=1,
            grid=(rows // block,),
            in_specs=[
                pl.BlockSpec((block, width), lambda i, head: (i, 0)),
                pl.BlockSpec((1, width), lambda i, head: (0, 0)),
                two_heads,
                two_heads,
                pl.BlockSpec((width, columns), lambda i, head: (0, 0)),
                pl.BlockSpec((HD // 2, block), lambda i, head: (0, i)),
                pl.BlockSpec((HD // 2, block), lambda i, head: (0, i)),
            ],
            out_specs=[
                pl.BlockSpec((block, 128), lambda i, head: (i, 0)),
                pl.BlockSpec((block, columns), lambda i, head: (i, 0)),
                pl.BlockSpec((block, width), lambda i, head: (i, 0)),
                pl.BlockSpec((block, 128), lambda i, head: (i, 0)),
                pl.BlockSpec((block, 128), lambda i, head: (i, 0)),
            ],
        ),
        out_shape=[
            jax.ShapeDtypeStruct((rows, 128), BF16),
            jax.ShapeDtypeStruct((rows, columns), BF16),
            jax.ShapeDtypeStruct((rows, width), BF16),
            jax.ShapeDtypeStruct((rows, 128), F32),
            jax.ShapeDtypeStruct((rows, 128), F32),
        ],
        compiler_params=pltpu.CompilerParams(vmem_limit_bytes=48 * 2**20),
        cost_estimate=LIGHT,
        name="project",
    )(head, tokens, gain.reshape(1, width), k_weight, v_weight, q_weight, cos, sin)


def fwd_kernel(offsets, meta, q_ref, ka_ref, kb_ref, vt_ref, o_ref, lse_ref):
    half = q_ref.shape[0] // 2
    span = 2 * half
    group = min(GROUP, half)
    pairs = q_ref.shape[1] // 128
    for part, offset in enumerate(offsets):
        at = slice(part * half, part * half + half)
        queries = [q_ref[at, p * 128 : p * 128 + 128] for p in range(pairs)]
        chains = [(p, keys_ref) for p in range(pairs) for keys_ref in (ka_ref, kb_ref)]
        seen = meta[part]
        own = pl.multiple_of(meta[2 + seen] * span, span)
        heads = []
        for p, keys_ref in chains:
            tops, sums = [], []
            for first in range(0, half, group):
                count = offset + first + group
                rows = pl.ds(own, count)
                scores = lax.dot_general(
                    keys_ref[rows, :],
                    queries[p][first : first + group],
                    NT,
                    preferred_element_type=F32,
                )
                key_at = lax.broadcasted_iota(jnp.int32, scores.shape, 0)
                row_at = lax.broadcasted_iota(jnp.int32, scores.shape, 1) + (offset + first)
                scores = jnp.where(key_at <= row_at, scores, -1e30)
                top = jnp.max(scores, axis=0, keepdims=True)
                weights = jnp.exp(scores - top).astype(BF16)
                tops.append(top)
                sums.append(jnp.dot(vt_ref[:, rows], weights, preferred_element_type=F32))
            heads += [jnp.concatenate(tops, axis=1), jnp.concatenate(sums, axis=1)]

        def step(index, carry):
            rows = pl.ds(pl.multiple_of(meta[2 + index] * span, span), span)
            out = []
            for chain, (p, keys_ref) in enumerate(chains):
                top, total = carry[2 * chain : 2 * chain + 2]
                scores = lax.dot_general(
                    keys_ref[rows, :], queries[p], NT, preferred_element_type=F32
                )
                new_top = jnp.maximum(top, jnp.max(scores, axis=0, keepdims=True))
                weights = jnp.exp(scores - new_top).astype(BF16)
                total = total * jnp.exp(top - new_top) + jnp.dot(
                    vt_ref[:, rows], weights, preferred_element_type=F32
                )
                out += [new_top, total]
            return tuple(out)

        heads = lax.fori_loop(0, seen, step, tuple(heads))
        for p in range(pairs):
            top0, total0, top1, total1 = heads[4 * p : 4 * p + 4]
            norm0, norm1 = total0[HD : HD + 1], total1[HD : HD + 1]
            o_ref[at, p * 128 : p * 128 + 128] = (
                jnp.concatenate([total0[:HD] / norm0, total1[:HD] / norm1], axis=0).T.astype(BF16)
            )
            lse_ref[p, :, at] = jnp.concatenate(
                [top0 + jnp.log(norm0), top1 + jnp.log(norm1), jnp.zeros((6, half), F32)], axis=0
            )


def spread(kv_refs, ka_ref, kb_ref, va_ref, vb_ref, kt_ref, vt_ref):
    at = 0
    for kv_ref in kv_refs:
        rows = kv_ref.shape[0]
        block = min(512, rows)
        for first in range(0, rows, block):
            here = slice(at + first, at + first + block)
            pair = kv_ref[first : first + block, :].astype(F32)
            other = pltpu.roll(pair, HD, 1)
            left = lax.broadcasted_iota(jnp.int32, pair.shape, 1) < HD
            ka_ref[here, :] = jnp.where(left, pair, 0.0).astype(BF16)
            vb_ref[here, :] = jnp.where(left, 0.0, pair).astype(BF16)
            va_ref[here, :] = jnp.where(left, other, 0.0).astype(BF16)
            kb_ref[here, :] = jnp.where(left, 0.0, other).astype(BF16)
            turned = pair.T
            kt_ref[:, here] = turned[:HD].astype(BF16)
            ones = jnp.where(lax.broadcasted_iota(jnp.int32, (16, block), 0) == 0, 1.0, 0.0)
            vt_ref[:, here] = jnp.concatenate([turned[HD:], ones], axis=0).astype(BF16)
        at += rows


def attend_cost(rows, length, width):
    return pl.CostEstimate(
        flops=8 * rows * length * width, bytes_accessed=2**23, transcendentals=0
    )


def attend_first(meta, offsets, queries, kv_own, kv_other):
    rows, width = queries.shape
    pairs = width // 128
    together = 2 if pairs % 2 == 0 else 1
    length = 2 * kv_own.shape[0]

    def whole(shape):
        return pl.BlockSpec(shape, lambda p, m: (0, 0))

    def kernel(meta, q_ref, own, other, o_ref, lse_ref, ka, kb, va, vb, kt, vt):
        @pl.when(pl.program_id(0) == 0)
        def _():
            spread((own, other), ka, kb, va, vb, kt, vt)

        fwd_kernel(offsets, meta, q_ref, ka, kb, vt, o_ref, lse_ref)

    wide = (length, 128)
    forms = [wide, wide, wide, wide, (HD, length), (HD + 16, length)]
    return pl.pallas_call(
        kernel,
        grid_spec=pltpu.PrefetchScalarGridSpec(
            num_scalar_prefetch=1,
            grid=(pairs // together,),
            in_specs=[
                pl.BlockSpec((rows, 128 * together), lambda p, m: (0, p)),
                whole(kv_own.shape),
                whole(kv_other.shape),
            ],
            out_specs=[
                pl.BlockSpec((rows, 128 * together), lambda p, m: (0, p)),
                pl.BlockSpec((together, 8, rows), lambda p, m: (p, 0, 0)),
            ]
            + [whole(form) for form in forms],
        ),
        out_shape=[
            jax.ShapeDtypeStruct((rows, width), BF16),
            jax.ShapeDtypeStruct((pairs, 8, rows), F32),
        ]
        + [jax.ShapeDtypeStruct(form, BF16) for form in forms],
        compiler_params=pltpu.CompilerParams(vmem_limit_bytes=58 * 2**20),
        cost_estimate=attend_cost(rows, length, width),
        name="attend_first",
    )(meta, queries, kv_own, kv_other)


def attend(meta, offsets, queries, keys_a, keys_b, values_t):
    rows, width = queries.shape
    pairs = width // 128
    together = 2 if pairs % 2 == 0 else 1
    length = keys_a.shape[0]
    whole = pl.BlockSpec((length, 128), lambda p, m: (0, 0))

    def kernel(*refs):
        fwd_kernel(offsets, *refs)

    return pl.pallas_call(
        kernel,
        grid_spec=pltpu.PrefetchScalarGridSpec(
            num_scalar_prefetch=1,
            grid=(pairs // together,),
            in_specs=[
                pl.BlockSpec((rows, 128 * together), lambda p, m: (0, p)),
                whole,
                whole,
                pl.BlockSpec(values_t.shape, lambda p, m: (0, 0)),
            ],
            out_specs=[
                pl.BlockSpec((rows, 128 * together), lambda p, m: (0, p)),
                pl.BlockSpec((together, 8, rows), lambda p, m: (p, 0, 0)),
            ],
        ),
        out_shape=[
            jax.ShapeDtypeStruct((rows, width), BF16),
            jax.ShapeDtypeStruct((pairs, 8, rows), F32),
        ],
        compiler_params=pltpu.CompilerParams(vmem_limit_bytes=58 * 2**20),
        cost_estimate=attend_cost(rows, length, width),
        name="attend",
    )(meta, queries, keys_a, keys_b, values_t)


def bwd_kernel(
    offsets,
    meta,
    q_ref,
    o_ref,
    g_ref,
    lse_ref,
    ka_ref,
    kb_ref,
    va_ref,
    vb_ref,
    kt_ref,
    cos_ref,
    sin_ref,
    dq_ref,
    dk_ref,
    dv_ref,
):
    half = q_ref.shape[0] // 2
    span = 2 * half
    group = min(GROUP, half)

    for part, offset in enumerate(offsets):
        at = slice(part * half, part * half + half)
        queries, grads = q_ref[at, :], g_ref[at, :]
        left = lax.broadcasted_iota(jnp.int32, (half, 128), 1) < HD
        products = (grads.astype(F32) * o_ref[at, :].astype(F32)).T
        zero = jnp.zeros_like(queries)
        sides = []
        for side, (keys_ref, values_ref) in enumerate(((ka_ref, va_ref), (kb_ref, vb_ref))):
            mine = left if side == 0 else jnp.logical_not(left)
            delta = jnp.sum(products[side * HD : side * HD + HD], axis=0, keepdims=True)
            sides.append(
                (
                    keys_ref,
                    values_ref,
                    jnp.where(mine, queries, zero),
                    jnp.where(mine, grads, zero),
                    lse_ref[0, side : side + 1, at],
                    delta,
                )
            )

        def block(rows, first, count, masked):
            cut = slice(first, first + count)
            dqs = []
            dk_add = dv_add = None
            for keys_ref, values_ref, q_mine, g_mine, lse, delta in sides:
                scores = lax.dot_general(
                    keys_ref[rows, :], queries[cut], NT, preferred_element_type=F32
                )
                probs = jnp.exp(scores - lse[:, cut])
                if masked:
                    key_at = lax.broadcasted_iota(jnp.int32, scores.shape, 0)
                    row_at = lax.broadcasted_iota(jnp.int32, scores.shape, 1) + (offset + first)
                    probs = jnp.where(key_at <= row_at, probs, 0.0)
                grad_probs = lax.dot_general(
                    values_ref[rows, :], grads[cut], NT, preferred_element_type=F32
                )
                grad_scores = (probs * (grad_probs - delta[:, cut])).astype(BF16)
                dv_new = jnp.dot(probs.astype(BF16), g_mine[cut], preferred_element_type=F32)
                dk_new = jnp.dot(grad_scores, q_mine[cut], preferred_element_type=F32)
                dv_add = dv_new if dv_add is None else dv_add + dv_new
                dk_add = dk_new if dk_add is None else dk_add + dk_new
                dqs.append(jnp.dot(kt_ref[:, rows], grad_scores, preferred_element_type=F32))
            dv_ref[rows, :] += dv_add
            dk_ref[rows, :] += dk_add
            return jnp.concatenate(dqs, axis=0)

        own = pl.multiple_of(meta[2 + meta[part]] * span, span)
        start = jnp.concatenate(
            [
                block(pl.ds(own, offset + first + group), first, group, True)
                for first in range(0, half, group)
            ],
            axis=1,
        )

        def step(index, total):
            rows = pl.ds(pl.multiple_of(meta[2 + index] * span, span), span)
            return total + block(rows, 0, half, False)

        dq = lax.fori_loop(0, meta[part], step, start).T * (HD**-0.5)
        dq_ref[at, :] = turn(dq, cos_ref[at, :], -sin_ref[at, :]).astype(BF16)


def back_specs(queries, forms):
    rows, width = queries.shape
    pair = pl.BlockSpec((rows, 128), lambda p, m: (0, p))
    table = pl.BlockSpec((rows, 128), lambda p, m: (0, 0))
    specs = [pair, pair, pair, pl.BlockSpec((1, 8, rows), lambda p, m: (p, 0, 0))]
    specs += [pl.BlockSpec(form.shape, lambda p, m: (0, 0)) for form in forms]
    return pair, specs + [table, table]


def attend_back_first(meta, offsets, queries, outputs, grads, lse, forms, cos, sin):
    length = forms[0].shape[0]
    pair, specs = back_specs(queries, forms)
    whole = pl.BlockSpec((length, 128), lambda p, m: (0, 0))

    def kernel(*refs):
        dk_ref, dv_ref = refs[-2:]

        @pl.when(pl.program_id(0) == 0)
        def _():
            dk_ref[...] = jnp.zeros(dk_ref.shape, F32)
            dv_ref[...] = jnp.zeros(dv_ref.shape, F32)

        bwd_kernel(offsets, *refs)

    return pl.pallas_call(
        kernel,
        grid_spec=pltpu.PrefetchScalarGridSpec(
            num_scalar_prefetch=1,
            grid=(queries.shape[1] // 128,),
            in_specs=specs,
            out_specs=[pair, whole, whole],
        ),
        out_shape=[
            jax.ShapeDtypeStruct(queries.shape, BF16),
            jax.ShapeDtypeStruct((length, 128), F32),
            jax.ShapeDtypeStruct((length, 128), F32),
        ],
        compiler_params=pltpu.CompilerParams(vmem_limit_bytes=58 * 2**20),
        cost_estimate=LIGHT,
        name="attend_back_first",
    )(meta, queries, outputs, grads, lse, *forms, cos, sin)


def attend_back_last(
    meta, offsets, queries, outputs, grads, lse, forms, cos, sin, dk, dv, all_cos, all_sin
):
    length = forms[0].shape[0]
    near = length // 2
    pair, specs = back_specs(queries, forms)
    whole = pl.BlockSpec((length, 128), lambda p, m: (0, 0))
    half = pl.BlockSpec((near, 128), lambda p, m: (0, 0))

    def kernel(*refs):
        dk_in, dv_in, cos_ref, sin_ref, dq_ref, near_ref, far_ref, dk_ref, dv_ref = refs[-9:]

        @pl.when(pl.program_id(0) == 0)
        def _():
            dk_ref[...] = dk_in[...]
            dv_ref[...] = dv_in[...]

        bwd_kernel(offsets, *refs[:-9], dq_ref, dk_ref, dv_ref)

        @pl.when(pl.program_id(0) == pl.num_programs(0) - 1)
        def _():
            block = min(512, near)
            for first in range(0, length, block):
                here = slice(first, first + block)
                dk_block, dv_block = dk_ref[here, :], dv_ref[here, :]
                dk_block = dk_block + pltpu.roll(dk_block, HD, 1)
                dv_block = dv_block + pltpu.roll(dv_block, HD, 1)
                left = lax.broadcasted_iota(jnp.int32, dk_block.shape, 1) < HD
                both = jnp.where(
                    left, turn(dk_block, cos_ref[here, :], -sin_ref[here, :]), dv_block
                )
                if first < near:
                    near_ref[here, :] = both
                else:
                    far_ref[first - near : first - near + block, :] = both.astype(BF16)

    return pl.pallas_call(
        kernel,
        grid_spec=pltpu.PrefetchScalarGridSpec(
            num_scalar_prefetch=1,
            grid=(queries.shape[1] // 128,),
            in_specs=specs + [whole] * 4,
            out_specs=[pair, half, half],
            scratch_shapes=[pltpu.VMEM((length, 128), F32), pltpu.VMEM((length, 128), F32)],
        ),
        out_shape=[
            jax.ShapeDtypeStruct(queries.shape, BF16),
            jax.ShapeDtypeStruct((near, 128), F32),
            jax.ShapeDtypeStruct((near, 128), BF16),
        ],
        compiler_params=pltpu.CompilerParams(vmem_limit_bytes=60 * 2**20),
        cost_estimate=LIGHT,
        name="attend_back_last",
    )(meta, queries, outputs, grads, lse, *forms, cos, sin, dk, dv, all_cos, all_sin)


def feed_kernel(
    gathered_ref,
    tokens_ref,
    cotangent_ref,
    gain_ref,
    output_weight,
    gate_weight,
    up_weight,
    down_weight,
    *refs,
):
    middle_ref, normed_ref, hidden_ref, gates_ref, down_ref, grad_ref = refs[-6:]
    middle = tokens_ref[...].astype(F32)
    for source in range(gathered_ref.shape[0]):
        middle = middle + lax.dot_general(
            gathered_ref[source], output_weight[source], NT, preferred_element_type=F32
        )
    middle_ref[...] = middle
    inverse = lax.rsqrt(jnp.mean(middle * middle, axis=-1, keepdims=True) + EPSILON)
    normed = (middle * inverse * gain_ref[...]).astype(BF16)
    normed_ref[...] = normed
    gate = jnp.dot(normed, gate_weight[...], preferred_element_type=F32)
    up = jnp.dot(normed, up_weight[...], preferred_element_type=F32)
    grad_hidden = jnp.dot(cotangent_ref[...], down_weight[...], preferred_element_type=F32)
    sigmoid = jax.nn.sigmoid(gate)
    hidden = (gate * sigmoid * up).astype(BF16)
    hidden_ref[...] = hidden
    grad_gate = (grad_hidden * up * sigmoid * (1.0 + gate * (1.0 - sigmoid))).astype(BF16)
    grad_up = (grad_hidden * gate * sigmoid).astype(BF16)
    units = hidden.shape[1]
    gates_ref[:, :units] = grad_gate
    gates_ref[:, units:] = grad_up
    down_ref[...] = lax.dot_general(
        hidden, down_weight[...], NT, preferred_element_type=F32
    ).astype(BF16)
    grad_ref[...] = (
        lax.dot_general(grad_gate, gate_weight[...], NT, preferred_element_type=F32)
        + lax.dot_general(grad_up, up_weight[...], NT, preferred_element_type=F32)
    ).astype(BF16)


def feed_forward(c, gathered, tokens, cotangent, gain, output_weight, weights, earlier):
    rows, width = tokens.shape
    units = weights[0].shape[1]
    block = min(256, rows // 4)
    quarter = rows // 4 // block
    if c:
        place = lambda i: (i + quarter, 0)
    else:
        place = lambda i: (jnp.where(i < quarter, i, i + 2 * quarter), 0)
    once = pl.Buffered(1)

    def natural(columns):
        return pl.BlockSpec((block, columns), place)

    def whole(array):
        zeros = (0,) * array.ndim
        return pl.BlockSpec(array.shape, lambda i: zeros, pipeline_mode=once)

    shapes = [
        jax.ShapeDtypeStruct((rows, width), F32),
        jax.ShapeDtypeStruct((rows, width), BF16),
        jax.ShapeDtypeStruct((rows, units), BF16),
        jax.ShapeDtypeStruct((rows, 2 * units), BF16),
    ]
    gain = gain.reshape(1, width)
    return pl.pallas_call(
        feed_kernel,
        grid=(2 * quarter,),
        in_specs=[
            pl.BlockSpec((gathered.shape[0], block, gathered.shape[2]), lambda i: (0, i, 0)),
            natural(width),
            natural(width),
            whole(gain),
            whole(output_weight),
        ]
        + [whole(weight) for weight in weights]
        + [pl.BlockSpec(memory_space=pl.ANY) for _ in earlier],
        out_specs=[natural(shape.shape[1]) for shape in shapes]
        + [pl.BlockSpec((block, width), lambda i: (i, 0))] * 2,
        out_shape=shapes + [jax.ShapeDtypeStruct((rows // 2, width), BF16)] * 2,
        input_output_aliases={8 + k: k for k in range(len(earlier))},
        compiler_params=pltpu.CompilerParams(vmem_limit_bytes=60 * 2**20),
        cost_estimate=LIGHT,
        name="feed_forward",
    )(gathered, tokens, cotangent, gain, output_weight, *weights, *earlier)


def part_specs(shape):
    return [pl.BlockSpec(shape, lambda p, order: (0, 0, 0)) for _ in range(4)]


def join_kernel(order, rows_ref, *refs):
    out_ref = refs[4]
    for part, weight_ref in enumerate(refs[:4]):

        @pl.when(pl.program_id(0) == part)
        def _():
            result = None
            for source in range(rows_ref.shape[0]):
                term = lax.dot_general(
                    rows_ref[source], weight_ref[source], NT, preferred_element_type=F32
                )
                result = term if result is None else result + term
            out_ref[...] = result


def join(order, rows, parts):
    size, count, features = rows.shape
    columns = parts[0].shape[1]
    return pl.pallas_call(
        join_kernel,
        grid_spec=pltpu.PrefetchScalarGridSpec(
            num_scalar_prefetch=1,
            grid=(4,),
            in_specs=[pl.BlockSpec(rows.shape, lambda p, order: (0, 0, 0))]
            + part_specs(parts[0].shape),
            out_specs=pl.BlockSpec((count, columns), lambda p, order: (0, order[p])),
        ),
        out_shape=jax.ShapeDtypeStruct((count, 4 * columns), F32),
        compiler_params=pltpu.CompilerParams(vmem_limit_bytes=48 * 2**20),
        cost_estimate=LIGHT,
        name="join",
    )(order, rows, *parts)


def arrange_kernel(order, *refs):
    for part, weight_ref in enumerate(refs[:-1]):

        @pl.when(pl.program_id(0) == part)
        def _():
            refs[-1][...] = weight_ref[...].reshape(refs[-1].shape)


def arrange(order, parts, shape, block, place):
    zeros = (0,) * parts[0].ndim
    return pl.pallas_call(
        arrange_kernel,
        grid_spec=pltpu.PrefetchScalarGridSpec(
            num_scalar_prefetch=1,
            grid=(len(parts),),
            in_specs=[pl.BlockSpec(parts[0].shape, lambda p, order: zeros) for _ in parts],
            out_specs=pl.BlockSpec(block, lambda p, order: place(order[p])),
        ),
        out_shape=jax.ShapeDtypeStruct(shape, parts[0].dtype),
        compiler_params=pltpu.CompilerParams(vmem_limit_bytes=48 * 2**20),
        cost_estimate=LIGHT,
        name="arrange",
    )(order, *parts)


def quarter_row(row, c, half, span):
    if c:
        return half + row
    return row if row < half else row + span


def after(value, *earlier):
    return lax.optimization_barrier((value, earlier))[0]


def line_steps(size):
    return [
        (
            [(i, i + 1) for i in range(step - 1, size - 1)],
            [(i, i - 1) for i in range(1, size - step + 1)],
        )
        for step in range(1, size)
    ]


class Gather:
    def __init__(self, piece):
        self.piece = piece
        self.rights, self.lefts = [piece], [piece]
        self.hops = line_steps(lax.axis_size("tensor"))

    def step(self):
        done = len(self.rights) - 1
        if done < len(self.hops):
            to_right, to_left = self.hops[done]
            self.rights.append(lax.ppermute(self.rights[-1], "tensor", to_right))
            self.lefts.append(lax.ppermute(self.lefts[-1], "tensor", to_left))
        return self.rights[-1], self.lefts[-1]

    def held(self, pair):
        self.rights[-1], self.lefts[-1] = pair

    def place_hop(self, place, target, hop):
        size = lax.axis_size("tensor")
        me = lax.axis_index("tensor")
        if hop == 0:
            return place(target, self.piece, me)
        right, left = self.rights[hop], self.lefts[hop]
        from_left, from_right = me >= hop, me + hop < size
        if 2 * hop >= size:
            piece = jnp.where(from_left, right, jnp.where(from_right, left, self.piece))
            source = jnp.where(from_left, me - hop, jnp.where(from_right, me + hop, me))
            return place(target, piece, source)
        target = place(
            target, jnp.where(from_left, right, self.piece), jnp.where(from_left, me - hop, me)
        )
        return place(
            target, jnp.where(from_right, left, self.piece), jnp.where(from_right, me + hop, me)
        )

    def whole(self):
        size = lax.axis_size("tensor")
        me = lax.axis_index("tensor")
        while len(self.rights) <= len(self.hops):
            self.step()
        parts, order = [self.piece], [me]
        for hop in range(1, size):
            for came, source in ((self.rights[hop], me - hop), (self.lefts[hop], me + hop)):
                parts.append(came)
                order.append(jnp.where((source >= 0) & (source < size), source, me))
        parts, order = parts[::-1], order[::-1]
        shape = self.piece.shape
        return arrange(
            jnp.stack(order).astype(jnp.int32),
            parts,
            (size, *shape),
            (1, *shape),
            lambda i: (i,) + (0,) * len(shape),
        )


def send_blocks(pick, across=False):
    size = lax.axis_size("tensor")
    me = lax.axis_index("tensor")
    arrived = []
    for shift in range(size):
        block = pick(lax.rem(me + shift, size))
        if across:
            block = lax.ppermute(
                block,
                ("ctx", "tensor"),
                [
                    (c * size + i, (1 - c) * size + (i + shift) % size)
                    for c in range(2)
                    for i in range(size)
                ],
            )
        elif shift:
            block = lax.ppermute(block, "tensor", [(i, (i + shift) % size) for i in range(size)])
        arrived.append(block)
    return tuple(arrived)


def stack_blocks(arrived):
    size = len(arrived)
    me = lax.axis_index("tensor")
    out = jnp.zeros((size, *arrived[0].shape), arrived[0].dtype)
    for shift, block in enumerate(arrived):
        out = lax.dynamic_update_index_in_dim(out, block, lax.rem(me - shift + size, size), 0)
    return out


def hold(*values):
    return lax.optimization_barrier(values)


def rows_part(weight, index, count):
    rows = weight.shape[0] // count
    return lax.dynamic_slice_in_dim(weight, index * rows, rows, 0)


def dot(a, b):
    return jnp.dot(a, b, preferred_element_type=F32)


def dot_t(a, b):
    return jnp.einsum("rf,df->rd", a, b, preferred_element_type=F32)


def t_dot(a, b):
    return jnp.einsum("rd,rf->df", a, b, preferred_element_type=F32)


def body(
    tokens,
    cotangent,
    span_order,
    norm_attn,
    w_query,
    w_key,
    w_value,
    w_output,
    norm_mlp,
    w_gate,
    w_up,
    w_down,
):
    tok_rows, width = tokens.shape
    groups = lax.axis_size("tensor")
    member = lax.axis_index("tensor")
    n_ctx = lax.axis_size("ctx")
    assert n_ctx == 2
    ctx_index = lax.axis_index("ctx")
    features = w_query.shape[1]
    kv_count = w_key.shape[1] // HD
    kv_pick = np.arange(groups) * kv_count // groups
    head = (member * kv_count // groups).astype(jnp.int32).reshape(1)
    span = tok_rows // 2
    half = span // 2
    share = span // groups
    over = [(0, 1), (1, 0)]
    chunks = range(2)

    def chunk(array, c):
        if c:
            return array[half : half + span]
        return jnp.concatenate([array[:half], array[half + span :]], axis=0)

    def natural(first, second):
        return jnp.concatenate([first[:half], second, first[half:]], axis=0)

    order = jnp.roll(span_order[0], -2 * ctx_index)
    places = jnp.arange(4, dtype=jnp.int32)
    slot_of = jnp.sum(
        jnp.where(order[None, :] == places[:, None], places[None, :], 0), axis=1, dtype=jnp.int32
    )
    metas = [jnp.concatenate([order[2 * c : 2 * c + 2], slot_of]) for c in chunks]
    offsets = [(0, half), (half, 0)]

    positions = (order[:, None] * span + jnp.arange(span, dtype=jnp.int32)[None, :]).reshape(-1)
    frequency = 10000.0 ** (-jnp.arange(HD // 2, dtype=F32) / (HD // 2))

    def table(positions):
        angles = frequency[:, None] * positions.astype(F32)[None, :]
        cos_part, sin_part = hold(jnp.cos(angles), jnp.sin(angles))
        cos_part, sin_part = cos_part.T, sin_part.T
        return (
            jnp.concatenate([cos_part] * 4, axis=1),
            jnp.concatenate([-sin_part, sin_part] * 2, axis=1),
        )


    upper = lax.axis_index("dp") % 2
    beside = [(i, i ^ 1) for i in range(lax.axis_size("dp"))]
    quarters = jnp.stack(
        [
            2 * upper + ctx_index,
            2 * upper + 1 - ctx_index,
            2 - 2 * upper + ctx_index,
            3 - 2 * upper - ctx_index,
        ]
    ).astype(jnp.int32)

    output_gather = Gather(rows_part(w_output, upper, 2))
    hop = output_gather.step()
    angles = frequency[:, None] * positions[:tok_rows].astype(F32)[None, :]
    cos_part, sin_part = hold(jnp.cos(angles), jnp.sin(angles))
    kv_own, queries, normed, cos_near, sin_near = project(
        head, tokens, norm_attn, w_key, w_value, w_query, cos_part, sin_part
    )
    kv_own, queries, normed, hop, quarters = hold(kv_own, queries, normed, hop, quarters)
    output_gather.held(hop)
    kv_other = lax.ppermute(kv_own, "ctx", over)
    hop = output_gather.step()
    kv_own, kv_other, sent, kept, normed, hop = hold(
        kv_own, kv_other, chunk(queries, 1), chunk(queries, 0), normed, hop
    )
    output_gather.held(hop)
    length = 2 * tok_rows

    foreign = lax.ppermute(sent, "ctx", over)
    hop = output_gather.step()
    first, first_log, *forms = attend_first(metas[0], offsets[0], kept, kv_own, kv_other)
    first, first_log, foreign, forms, hop = hold(first, first_log, foreign, forms, hop)
    output_gather.held(hop)
    *forms, values_t = forms
    first_whole = lax.all_gather(first, "tensor", axis=0, tiled=False)

    output_near = output_gather.whole()
    output_far = lax.ppermute(output_near, "dp", beside)
    second, second_log = attend(metas[1], offsets[1], foreign, forms[0], forms[1], values_t)
    second, second_log, output_near, output_far = hold(
        second, second_log, output_near, output_far
    )

    cos_far, sin_far = table(after(positions[tok_rows:], second))
    cos_pair = jnp.concatenate([cos_near, cos_far], axis=0)
    sin_pair = jnp.concatenate([sin_near, sin_far], axis=0)
    tables = [(chunk(cos_near, 0), chunk(sin_near, 0)), (chunk(cos_far, 1), chunk(sin_far, 1))]
    second_home = lax.ppermute(second, "ctx", over)
    half_rows = output_near.shape[1]
    output_whole = arrange(
        jnp.stack([upper, 1 - upper]).astype(jnp.int32),
        [output_near, output_far],
        (groups, 2 * half_rows, features),
        output_near.shape,
        lambda i: (0, i, 0),
    )
    second_home, output_whole, tables, cos_pair, sin_pair = hold(
        second_home, output_whole, tables, cos_pair, sin_pair
    )
    second_whole = lax.all_gather(second_home, "tensor", axis=0, tiled=False)
    queries = [kept, foreign]
    attention = [first, second]
    log_totals = [first_log, second_log]

    row_of = [
        jnp.asarray([quarter_row(i * share, c, half, span) for i in range(groups)], jnp.int32)
        for c in chunks
    ]

    def own_rows(array, c):
        return lax.dynamic_slice_in_dim(array, row_of[c][member], share, 0)

    def to_attention(c, middle, grad_share):
        middle = own_rows(middle, c)
        inverse_two = lax.rsqrt(jnp.mean(middle * middle, axis=-1, keepdims=True) + EPSILON)
        grad_normed_mlp = grad_share.astype(F32)
        gain = jnp.sum(grad_normed_mlp * middle * inverse_two, axis=0)
        scaled_two = grad_normed_mlp * norm_mlp
        grad_middle = (
            own_rows(cotangent, c).astype(F32)
            + inverse_two * scaled_two
            - middle * inverse_two**3 * jnp.mean(scaled_two * middle, axis=-1, keepdims=True)
        )
        grad_low = grad_middle.astype(BF16)
        blocks = jnp.einsum(
            "rd,tdq->trq", grad_low, output_whole, preferred_element_type=F32
        ).astype(BF16)
        return gain, grad_middle, grad_low, blocks

    def block_of(blocks):
        return lambda j: lax.dynamic_index_in_dim(blocks, j, 0, keepdims=False)

    def rows_of(array):
        return lambda j: lax.dynamic_slice_in_dim(array, j * share, share, 0)

    def line_sum(array):
        return lax.psum_scatter(array, "tensor", scatter_dimension=0, tiled=True)

    def plane_sum(gradient):
        return lax.psum_scatter(
            gradient.astype(BF16), ("dp", "ctx"), scatter_dimension=0, tiled=True
        )

    query_gather = Gather(rows_part(after(w_query, first_whole), 2 * upper + ctx_index, 4))
    hop = query_gather.step()
    weights = (w_gate, w_up, w_down)
    fixed = (tokens, cotangent, norm_mlp, output_whole, weights)
    *fed, down_first, grad_first = feed_forward(0, first_whole, *fixed, ())
    fed, down_first, grad_first, second_whole, hop = hold(
        fed, down_first, grad_first, second_whole, hop
    )
    query_gather.held(hop)

    share_first = line_sum(grad_first)
    hop = query_gather.step()
    *fed, down_second, grad_second = feed_forward(1, second_whole, *fixed, fed)
    fed, down_second, grad_second, hop = hold(fed, down_second, grad_second, hop)
    query_gather.held(hop)
    middle, normed_mlp, hidden, gates = fed

    share_second = line_sum(grad_second)
    hop = query_gather.step()
    w_gates = t_dot(normed_mlp, gates).astype(BF16)
    w_gates, hop, share_first = hold(w_gates, hop, share_first)
    query_gather.held(hop)

    mixed_first = line_sum(after(down_first, w_gates))

    gain_first, middle_first, low_first, blocks = to_attention(0, middle, share_first)
    query_part = query_gather.whole()
    gain_first, middle_first, low_first, blocks, hidden, query_part = hold(
        gain_first, middle_first, low_first, blocks, hidden, query_part
    )

    came_first = send_blocks(block_of(blocks))
    query_over = lax.ppermute(query_part, "ctx", over)
    w_downs = t_dot(cotangent, hidden).astype(BF16)
    middle_own = [own_rows(middle, c) for c in chunks]
    came_first, middle_own, query_part, query_over, w_downs = hold(
        came_first, middle_own, query_part, query_over, w_downs
    )

    query_near = (query_part, query_over)
    query_far = tuple(lax.ppermute(part, "dp", beside) for part in query_near)
    grads_first = stack_blocks(came_first).reshape(span, features)
    query_near, query_far, grads_first, share_second = hold(
        query_near, query_far, grads_first, share_second
    )

    gain_second, middle_second, low_second, blocks = to_attention(1, middle, share_second)
    gain_second, middle_second, low_second, blocks = hold(
        gain_second, middle_second, low_second, blocks
    )
    mixed_second = line_sum(after(down_second, blocks))

    def back_arguments(c, grads):
        return metas[c], offsets[c], queries[c], attention[c], grads, log_totals[c], forms, *tables[c]

    came_second = send_blocks(block_of(blocks), across=True)
    dq_first, dk, dv = attend_back_first(*back_arguments(0, grads_first))
    dq_first, dk, dv, came_second = hold(dq_first, dk, dv, came_second)

    rows_first = send_blocks(rows_of(dq_first))
    grads_second = stack_blocks(came_second).reshape(span, features)
    dq_second, kv_near, kv_far = attend_back_last(
        *back_arguments(1, grads_second), dk, dv, cos_pair, sin_pair
    )
    mixed_gathers = [Gather((middle_own[0] + mixed_first.astype(F32)).astype(BF16)), None]
    mixed_hop = mixed_gathers[0].step()
    dq_second, kv_near, kv_far, rows_first, mixed_hop = hold(
        dq_second, kv_near, kv_far, rows_first, mixed_hop
    )
    mixed_gathers[0].held(mixed_hop)

    def kv_share_of(array, j):
        return [lax.dynamic_slice_in_dim(array, row_of[c][j], share, 0) for c in chunks]

    kv_low = kv_near.astype(BF16)
    near_blocks = send_blocks(lambda j: jnp.concatenate(kv_share_of(kv_low, j), axis=1))
    far_blocks = send_blocks(
        lambda j: jnp.concatenate([rows_of(dq_second)(j), *kv_share_of(kv_far, j)], axis=1),
        across=True,
    )
    query_parts = query_near + query_far
    first_part = join(quarters, stack_blocks(rows_first), query_parts)
    attention_rows = jnp.concatenate(
        [
            lax.dynamic_slice_in_dim(whole, member * share, share, 1)
            for whole in after((first_whole, second_whole), dq_second)
        ],
        axis=1,
    )
    attention_rows = jnp.swapaxes(attention_rows, 0, 1).reshape(2 * share, groups * features)
    w_outs = t_dot(jnp.concatenate([low_first, low_second], axis=0), attention_rows).astype(BF16)
    near_blocks, far_blocks, first_part, w_outs = hold(near_blocks, far_blocks, first_part, w_outs)
    mixed_hop = mixed_gathers[0].step()
    far_blocks = stack_blocks(far_blocks)
    kv_blocks = (
        stack_blocks(near_blocks).astype(F32) + far_blocks[:, :, features:].astype(F32)
    ).astype(BF16)
    kv_blocks = jnp.concatenate([kv_blocks[:, :, : 2 * HD], kv_blocks[:, :, 2 * HD :]], axis=1)
    second_part = join(quarters, far_blocks[:, :, :features], query_parts)
    kv_whole = jnp.stack(
        [
            jnp.concatenate(
                [w_key[:, h * HD : (h + 1) * HD], w_value[:, h * HD : (h + 1) * HD]], axis=1
            )
            for h in kv_pick
        ]
    )

    grad_normed = jnp.concatenate([first_part, second_part], axis=0) + jnp.einsum(
        "trq,tdq->rd", kv_blocks, kv_whole, preferred_element_type=F32
    )
    inputs_own = jnp.concatenate([own_rows(tokens, c) for c in chunks], axis=0).astype(F32)
    inverse_own = lax.rsqrt(jnp.mean(inputs_own * inputs_own, axis=-1, keepdims=True) + EPSILON)
    attn_gain = jnp.sum(grad_normed * inputs_own * inverse_own, axis=0)
    scaled_one = grad_normed * norm_attn
    grad_inputs = (
        jnp.concatenate([middle_first, middle_second], axis=0)
        + inverse_own * scaled_one
        - inputs_own * inverse_own**3 * jnp.mean(scaled_one * inputs_own, axis=-1, keepdims=True)
    ).astype(BF16)

    def put_rows(target, piece, source):
        for c in chunks:
            target = lax.dynamic_update_slice_in_dim(
                target, piece[c * share : (c + 1) * share], row_of[c][source], 0
            )
        return target

    gains = jnp.stack([attn_gain, gain_first + gain_second], axis=1).astype(BF16)
    grad_inputs, gains, dq_second, kv_far, kv_near, w_gates, mixed_hop = hold(
        grad_inputs, gains, dq_second, kv_far, kv_near, w_gates, mixed_hop
    )
    mixed_gathers[0].held(mixed_hop)
    gate_up_grad = plane_sum(w_gates)

    def put_chunk(c):
        def put(target, piece, source):
            return lax.dynamic_update_slice_in_dim(target, piece, row_of[c][source], 0)

        return put

    tokens_gather = Gather(grad_inputs)
    tokens_grad = jnp.zeros((tok_rows, width), BF16)
    mixed = jnp.zeros((tok_rows, width), BF16)
    hop, mixed_hop = tokens_gather.step(), mixed_gathers[0].step()
    home = lax.ppermute(
        jnp.concatenate([dq_second, kv_far[:span], kv_far[span:]], axis=1), "ctx", over
    )
    dq_home, kv_sent = home[:, :features], home[:, features:]
    kv_sent = jnp.concatenate([kv_sent[:, : 2 * HD], kv_sent[:, 2 * HD :]], axis=0)
    grad_kv_raw = (kv_near + kv_sent.astype(F32)).astype(BF16)
    query_kv = t_dot(
        normed, jnp.concatenate([natural(dq_first, dq_home), grad_kv_raw], axis=1)
    ).astype(BF16)
    gains = jnp.pad(gains, ((0, 0), (0, 126)))
    rest = jnp.concatenate([w_downs, w_outs, query_kv, gains], axis=1)
    for count in range(3):
        mixed = mixed_gathers[0].place_hop(put_chunk(0), mixed, count)
    hop, mixed_hop, rest, mixed = hold(hop, mixed_hop, rest, mixed)
    tokens_gather.held(hop)
    mixed_gathers[0].held(mixed_hop)
    rest = plane_sum(rest)

    mixed_gathers[1] = Gather((middle_own[1] + after(mixed_second, hop).astype(F32)).astype(BF16))
    hop, mixed_hop = tokens_gather.step(), mixed_gathers[1].step()
    for count in range(3, groups):
        mixed = mixed_gathers[0].place_hop(put_chunk(0), mixed, count)
        if count + 1 < groups:
            mixed_gathers[0].step()
    tokens_grad = tokens_gather.place_hop(put_rows, tokens_grad, 0)
    tokens_grad = tokens_gather.place_hop(put_rows, tokens_grad, 1)
    mixed = mixed_gathers[1].place_hop(put_chunk(1), mixed, 0)
    hop, mixed_hop, tokens_grad, mixed = hold(hop, mixed_hop, tokens_grad, mixed)
    tokens_gather.held(hop)
    mixed_gathers[1].held(mixed_hop)

    hop, mixed_hop = tokens_gather.step(), mixed_gathers[1].step()
    tokens_grad = tokens_gather.place_hop(put_rows, tokens_grad, 2)
    mixed = mixed_gathers[1].place_hop(put_chunk(1), mixed, 1)
    hop, mixed_hop, tokens_grad, mixed = hold(hop, mixed_hop, tokens_grad, mixed)
    tokens_gather.held(hop)
    mixed_gathers[1].held(mixed_hop)

    mixed_hop = mixed_gathers[1].step()
    if groups > 3:
        tokens_grad = tokens_gather.place_hop(put_rows, tokens_grad, 3)
    mixed = mixed_gathers[1].place_hop(put_chunk(1), mixed, 2)
    hidden_units = w_down.shape[1]
    rest = after(rest, hop)
    down_grad = rest[:, :hidden_units]
    output_plane = rest[:, hidden_units : hidden_units + groups * features]
    query_plane = rest[:, hidden_units + groups * features :]
    query_grad, small = query_plane[:, :features].astype(F32), query_plane[:, features:]
    blocks = send_blocks(
        lambda j: jnp.concatenate(
            [lax.dynamic_slice_in_dim(output_plane, j * features, features, 1), small], axis=1
        )
    )
    mixed_hop, tokens_grad, mixed, blocks = hold(mixed_hop, tokens_grad, mixed, blocks)
    mixed_gathers[1].held(mixed_hop)
    blocks = stack_blocks(blocks).astype(F32)
    output_grad = jnp.sum(blocks[:, :, :features], axis=0)
    kv_share = blocks.shape[1] // groups
    kv_blocks = lax.dynamic_slice_in_dim(
        blocks[:, :, features : features + 2 * HD], member * kv_share, kv_share, 1
    )
    gains = jnp.sum(blocks[:, :, features + 2 * HD : features + 2 * HD + 2], axis=0).T
    for count in range(3, groups):
        mixed = mixed_gathers[1].place_hop(put_chunk(1), mixed, count)
        if count + 1 < groups:
            tokens_gather.step()
            mixed_gathers[1].step()
            tokens_grad = tokens_gather.place_hop(put_rows, tokens_grad, count + 1)

    key_heads, value_heads = [], []
    for h in range(kv_count):
        total = jnp.zeros((kv_share, 2 * HD), F32)
        for g in range(groups):
            if kv_pick[g] == h:
                total = total + kv_blocks[g]
        key_heads.append(total[:, :HD])
        value_heads.append(total[:, HD:])
    key_grad = jnp.concatenate(key_heads, axis=1)
    value_grad = jnp.concatenate(value_heads, axis=1)

    return (
        mixed,
        tokens_grad,
        gains[0],
        query_grad,
        key_grad,
        value_grad,
        output_grad,
        gains[1],
        gate_up_grad[:, :hidden_units].astype(F32),
        gate_up_grad[:, hidden_units:].astype(F32),
        down_grad.astype(F32),
    )


def solution(mesh):
    placed = (
        P(("dp", "ctx"), None),
        P(("dp", "ctx"), None),
        P("dp", None),
        P(),
        P(None, "tensor"),
        P(),
        P(),
        P(None, "tensor"),
        P(),
        P(None, "tensor"),
        P(None, "tensor"),
        P(None, "tensor"),
    )
    return jax.shard_map(
        body,
        mesh=mesh,
        in_specs=placed,
        out_specs=(
            P(("dp", "ctx"), None),
            P(("dp", "ctx"), None),
            P(("dp", "ctx")),
            P(("dp", "ctx"), "tensor"),
            P(("dp", "ctx", "tensor"), None),
            P(("dp", "ctx", "tensor"), None),
            P(("dp", "ctx"), "tensor"),
            P(("dp", "ctx")),
            P(("dp", "ctx"), "tensor"),
            P(("dp", "ctx"), "tensor"),
            P(("dp", "ctx"), "tensor"),
        ),
        check_vma=False,
    )
```

```python
import jax
import jax.numpy as jnp
import numpy as np
from jax import lax
from jax.experimental import pallas as pl
from jax.experimental.pallas import tpu as pltpu
from jax.sharding import PartitionSpec as P

NT = (((1,), (1,)), ((), ()))
F32 = jnp.float32
BF16 = jnp.bfloat16
HD = 64
GROUP = 256
EPSILON = 1e-05
LIGHT = pl.CostEstimate(flops=1, bytes_accessed=1, transcendentals=0)


def turn(values, cos, sin):
    low = (lax.broadcasted_iota(jnp.int32, values.shape, 1) % HD) < HD // 2
    other = jnp.where(
        low, pltpu.roll(values, 128 - HD // 2, 1), pltpu.roll(values, HD // 2, 1)
    )
    return values * cos + other * sin


def project_kernel(
    head,
    tokens_ref,
    gain_ref,
    k_weight,
    v_weight,
    q_weight,
    cos_part,
    sin_part,
    kv_ref,
    q_ref,
    normed_ref,
    cos_ref,
    sin_ref,
):
    inputs = tokens_ref[...].astype(F32)
    inverse = lax.rsqrt(jnp.mean(inputs * inputs, axis=-1, keepdims=True) + EPSILON)
    normed = (inputs * inverse * gain_ref[...]).astype(BF16)
    normed_ref[...] = normed
    cos, sin = cos_part[...], sin_part[...]
    cos = jnp.concatenate([cos, cos, cos, cos], axis=0).T
    sin = jnp.concatenate([-sin, sin, -sin, sin], axis=0).T
    cos_ref[...] = cos
    sin_ref[...] = sin
    first = head[0] % 2 == 0
    key = jnp.dot(normed, k_weight[...], preferred_element_type=F32)
    value = jnp.dot(normed, v_weight[...], preferred_element_type=F32)
    key = jnp.where(first, key, pltpu.roll(key, HD, 1))
    value = jnp.where(first, pltpu.roll(value, HD, 1), value)
    is_key = lax.broadcasted_iota(jnp.int32, key.shape, 1) < HD
    kv_ref[...] = jnp.where(is_key, turn(key, cos, sin), value).astype(BF16)
    raw = jnp.dot(normed, q_weight[...], preferred_element_type=F32)
    for start in range(0, q_ref.shape[1], 128):
        pair = raw[:, start : start + 128]
        q_ref[:, start : start + 128] = (turn(pair, cos, sin) * HD**-0.5).astype(BF16)


def project(head, tokens, gain, k_weight, v_weight, q_weight, cos, sin):
    rows, width = tokens.shape
    columns = q_weight.shape[1]
    block = 256
    two_heads = pl.BlockSpec((width, 128), lambda i, head: (0, head[0] // 2))
    return pl.pallas_call(
        project_kernel,
        grid_spec=pltpu.PrefetchScalarGridSpec(
            num_scalar_prefetch=1,
            grid=(rows // block,),
            in_specs=[
                pl.BlockSpec((block, width), lambda i, head: (i, 0)),
                pl.BlockSpec((1, width), lambda i, head: (0, 0)),
                two_heads,
                two_heads,
                pl.BlockSpec((width, columns), lambda i, head: (0, 0)),
                pl.BlockSpec((HD // 2, block), lambda i, head: (0, i)),
                pl.BlockSpec((HD // 2, block), lambda i, head: (0, i)),
            ],
            out_specs=[
                pl.BlockSpec((block, 128), lambda i, head: (i, 0)),
                pl.BlockSpec((block, columns), lambda i, head: (i, 0)),
                pl.BlockSpec((block, width), lambda i, head: (i, 0)),
                pl.BlockSpec((block, 128), lambda i, head: (i, 0)),
                pl.BlockSpec((block, 128), lambda i, head: (i, 0)),
            ],
        ),
        out_shape=[
            jax.ShapeDtypeStruct((rows, 128), BF16),
            jax.ShapeDtypeStruct((rows, columns), BF16),
            jax.ShapeDtypeStruct((rows, width), BF16),
            jax.ShapeDtypeStruct((rows, 128), F32),
            jax.ShapeDtypeStruct((rows, 128), F32),
        ],
        compiler_params=pltpu.CompilerParams(vmem_limit_bytes=48 * 2**20),
        cost_estimate=LIGHT,
        name="project",
    )(head, tokens, gain.reshape(1, width), k_weight, v_weight, q_weight, cos, sin)


def fwd_kernel(offsets, meta, q_ref, ka_ref, kb_ref, vt_ref, o_ref, lse_ref):
    half = q_ref.shape[0] // 2
    span = 2 * half
    group = min(GROUP, half)
    pairs = q_ref.shape[1] // 128
    for part, offset in enumerate(offsets):
        at = slice(part * half, part * half + half)
        queries = [q_ref[at, p * 128 : p * 128 + 128] for p in range(pairs)]
        chains = [(p, keys_ref) for p in range(pairs) for keys_ref in (ka_ref, kb_ref)]
        seen = meta[part]
        own = pl.multiple_of(meta[2 + seen] * span, span)
        heads = []
        for p, keys_ref in chains:
            tops, sums = [], []
            for first in range(0, half, group):
                count = offset + first + group
                rows = pl.ds(own, count)
                scores = lax.dot_general(
                    keys_ref[rows, :],
                    queries[p][first : first + group],
                    NT,
                    preferred_element_type=F32,
                )
                key_at = lax.broadcasted_iota(jnp.int32, scores.shape, 0)
                row_at = lax.broadcasted_iota(jnp.int32, scores.shape, 1) + (offset + first)
                scores = jnp.where(key_at <= row_at, scores, -1e30)
                top = jnp.max(scores, axis=0, keepdims=True)
                weights = jnp.exp(scores - top).astype(BF16)
                tops.append(top)
                sums.append(jnp.dot(vt_ref[:, rows], weights, preferred_element_type=F32))
            heads += [jnp.concatenate(tops, axis=1), jnp.concatenate(sums, axis=1)]

        def step(index, carry):
            rows = pl.ds(pl.multiple_of(meta[2 + index] * span, span), span)
            out = []
            for chain, (p, keys_ref) in enumerate(chains):
                top, total = carry[2 * chain : 2 * chain + 2]
                scores = lax.dot_general(
                    keys_ref[rows, :], queries[p], NT, preferred_element_type=F32
                )
                new_top = jnp.maximum(top, jnp.max(scores, axis=0, keepdims=True))
                weights = jnp.exp(scores - new_top).astype(BF16)
                total = total * jnp.exp(top - new_top) + jnp.dot(
                    vt_ref[:, rows], weights, preferred_element_type=F32
                )
                out += [new_top, total]
            return tuple(out)

        heads = lax.fori_loop(0, seen, step, tuple(heads))
        for p in range(pairs):
            top0, total0, top1, total1 = heads[4 * p : 4 * p + 4]
            norm0, norm1 = total0[HD : HD + 1], total1[HD : HD + 1]
            o_ref[at, p * 128 : p * 128 + 128] = (
                jnp.concatenate([total0[:HD] / norm0, total1[:HD] / norm1], axis=0).T.astype(BF16)
            )
            lse_ref[p, :, at] = jnp.concatenate(
                [top0 + jnp.log(norm0), top1 + jnp.log(norm1), jnp.zeros((6, half), F32)], axis=0
            )


def spread(kv_refs, ka_ref, kb_ref, va_ref, vb_ref, kt_ref, vt_ref):
    at = 0
    for kv_ref in kv_refs:
        rows = kv_ref.shape[0]
        block = min(512, rows)
        for first in range(0, rows, block):
            here = slice(at + first, at + first + block)
            pair = kv_ref[first : first + block, :].astype(F32)
            other = pltpu.roll(pair, HD, 1)
            left = lax.broadcasted_iota(jnp.int32, pair.shape, 1) < HD
            ka_ref[here, :] = jnp.where(left, pair, 0.0).astype(BF16)
            vb_ref[here, :] = jnp.where(left, 0.0, pair).astype(BF16)
            va_ref[here, :] = jnp.where(left, other, 0.0).astype(BF16)
            kb_ref[here, :] = jnp.where(left, 0.0, other).astype(BF16)
            turned = pair.T
            kt_ref[:, here] = turned[:HD].astype(BF16)
            ones = jnp.where(lax.broadcasted_iota(jnp.int32, (16, block), 0) == 0, 1.0, 0.0)
            vt_ref[:, here] = jnp.concatenate([turned[HD:], ones], axis=0).astype(BF16)
        at += rows


def attend_cost(rows, length, width):
    return pl.CostEstimate(
        flops=8 * rows * length * width, bytes_accessed=2**23, transcendentals=0
    )


def attend_first(meta, offsets, queries, kv_own, kv_other):
    rows, width = queries.shape
    pairs = width // 128
    together = 2 if pairs % 2 == 0 else 1
    length = 2 * kv_own.shape[0]

    def whole(shape):
        return pl.BlockSpec(shape, lambda p, m: (0, 0))

    def kernel(meta, q_ref, own, other, o_ref, lse_ref, ka, kb, va, vb, kt, vt):
        @pl.when(pl.program_id(0) == 0)
        def _():
            spread((own, other), ka, kb, va, vb, kt, vt)

        fwd_kernel(offsets, meta, q_ref, ka, kb, vt, o_ref, lse_ref)

    wide = (length, 128)
    forms = [wide, wide, wide, wide, (HD, length), (HD + 16, length)]
    return pl.pallas_call(
        kernel,
        grid_spec=pltpu.PrefetchScalarGridSpec(
            num_scalar_prefetch=1,
            grid=(pairs // together,),
            in_specs=[
                pl.BlockSpec((rows, 128 * together), lambda p, m: (0, p)),
                whole(kv_own.shape),
                whole(kv_other.shape),
            ],
            out_specs=[
                pl.BlockSpec((rows, 128 * together), lambda p, m: (0, p)),
                pl.BlockSpec((together, 8, rows), lambda p, m: (p, 0, 0)),
            ]
            + [whole(form) for form in forms],
        ),
        out_shape=[
            jax.ShapeDtypeStruct((rows, width), BF16),
            jax.ShapeDtypeStruct((pairs, 8, rows), F32),
        ]
        + [jax.ShapeDtypeStruct(form, BF16) for form in forms],
        compiler_params=pltpu.CompilerParams(vmem_limit_bytes=58 * 2**20),
        cost_estimate=attend_cost(rows, length, width),
        name="attend_first",
    )(meta, queries, kv_own, kv_other)


def attend(meta, offsets, queries, keys_a, keys_b, values_t):
    rows, width = queries.shape
    pairs = width // 128
    together = 2 if pairs % 2 == 0 else 1
    length = keys_a.shape[0]
    whole = pl.BlockSpec((length, 128), lambda p, m: (0, 0))

    def kernel(*refs):
        fwd_kernel(offsets, *refs)

    return pl.pallas_call(
        kernel,
        grid_spec=pltpu.PrefetchScalarGridSpec(
            num_scalar_prefetch=1,
            grid=(pairs // together,),
            in_specs=[
                pl.BlockSpec((rows, 128 * together), lambda p, m: (0, p)),
                whole,
                whole,
                pl.BlockSpec(values_t.shape, lambda p, m: (0, 0)),
            ],
            out_specs=[
                pl.BlockSpec((rows, 128 * together), lambda p, m: (0, p)),
                pl.BlockSpec((together, 8, rows), lambda p, m: (p, 0, 0)),
            ],
        ),
        out_shape=[
            jax.ShapeDtypeStruct((rows, width), BF16),
            jax.ShapeDtypeStruct((pairs, 8, rows), F32),
        ],
        compiler_params=pltpu.CompilerParams(vmem_limit_bytes=58 * 2**20),
        cost_estimate=attend_cost(rows, length, width),
        name="attend",
    )(meta, queries, keys_a, keys_b, values_t)


def bwd_kernel(
    offsets,
    meta,
    q_ref,
    o_ref,
    g_ref,
    lse_ref,
    ka_ref,
    kb_ref,
    va_ref,
    vb_ref,
    kt_ref,
    cos_ref,
    sin_ref,
    dq_ref,
    dk_ref,
    dv_ref,
):
    half = q_ref.shape[0] // 2
    span = 2 * half
    group = min(GROUP, half)

    for part, offset in enumerate(offsets):
        at = slice(part * half, part * half + half)
        queries, grads = q_ref[at, :], g_ref[at, :]
        left = lax.broadcasted_iota(jnp.int32, (half, 128), 1) < HD
        products = (grads.astype(F32) * o_ref[at, :].astype(F32)).T
        zero = jnp.zeros_like(queries)
        sides = []
        for side, (keys_ref, values_ref) in enumerate(((ka_ref, va_ref), (kb_ref, vb_ref))):
            mine = left if side == 0 else jnp.logical_not(left)
            delta = jnp.sum(products[side * HD : side * HD + HD], axis=0, keepdims=True)
            sides.append(
                (
                    keys_ref,
                    values_ref,
                    jnp.where(mine, queries, zero),
                    jnp.where(mine, grads, zero),
                    lse_ref[0, side : side + 1, at],
                    delta,
                )
            )

        def block(rows, first, count, masked):
            cut = slice(first, first + count)
            dqs = []
            dk_add = dv_add = None
            for keys_ref, values_ref, q_mine, g_mine, lse, delta in sides:
                scores = lax.dot_general(
                    keys_ref[rows, :], queries[cut], NT, preferred_element_type=F32
                )
                probs = jnp.exp(scores - lse[:, cut])
                if masked:
                    key_at = lax.broadcasted_iota(jnp.int32, scores.shape, 0)
                    row_at = lax.broadcasted_iota(jnp.int32, scores.shape, 1) + (offset + first)
                    probs = jnp.where(key_at <= row_at, probs, 0.0)
                grad_probs = lax.dot_general(
                    values_ref[rows, :], grads[cut], NT, preferred_element_type=F32
                )
                grad_scores = (probs * (grad_probs - delta[:, cut])).astype(BF16)
                dv_new = jnp.dot(probs.astype(BF16), g_mine[cut], preferred_element_type=F32)
                dk_new = jnp.dot(grad_scores, q_mine[cut], preferred_element_type=F32)
                dv_add = dv_new if dv_add is None else dv_add + dv_new
                dk_add = dk_new if dk_add is None else dk_add + dk_new
                dqs.append(jnp.dot(kt_ref[:, rows], grad_scores, preferred_element_type=F32))
            dv_ref[rows, :] += dv_add
            dk_ref[rows, :] += dk_add
            return jnp.concatenate(dqs, axis=0)

        own = pl.multiple_of(meta[2 + meta[part]] * span, span)
        start = jnp.concatenate(
            [
                block(pl.ds(own, offset + first + group), first, group, True)
                for first in range(0, half, group)
            ],
            axis=1,
        )

        def step(index, total):
            rows = pl.ds(pl.multiple_of(meta[2 + index] * span, span), span)
            return total + block(rows, 0, half, False)

        dq = lax.fori_loop(0, meta[part], step, start).T * (HD**-0.5)
        dq_ref[at, :] = turn(dq, cos_ref[at, :], -sin_ref[at, :]).astype(BF16)


def back_specs(queries, forms):
    rows, width = queries.shape
    pair = pl.BlockSpec((rows, 128), lambda p, m: (0, p))
    table = pl.BlockSpec((rows, 128), lambda p, m: (0, 0))
    specs = [pair, pair, pair, pl.BlockSpec((1, 8, rows), lambda p, m: (p, 0, 0))]
    specs += [pl.BlockSpec(form.shape, lambda p, m: (0, 0)) for form in forms]
    return pair, specs + [table, table]


def attend_back_first(meta, offsets, queries, outputs, grads, lse, forms, cos, sin):
    length = forms[0].shape[0]
    pair, specs = back_specs(queries, forms)
    whole = pl.BlockSpec((length, 128), lambda p, m: (0, 0))

    def kernel(*refs):
        dk_ref, dv_ref = refs[-2:]

        @pl.when(pl.program_id(0) == 0)
        def _():
            dk_ref[...] = jnp.zeros(dk_ref.shape, F32)
            dv_ref[...] = jnp.zeros(dv_ref.shape, F32)

        bwd_kernel(offsets, *refs)

    return pl.pallas_call(
        kernel,
        grid_spec=pltpu.PrefetchScalarGridSpec(
            num_scalar_prefetch=1,
            grid=(queries.shape[1] // 128,),
            in_specs=specs,
            out_specs=[pair, whole, whole],
        ),
        out_shape=[
            jax.ShapeDtypeStruct(queries.shape, BF16),
            jax.ShapeDtypeStruct((length, 128), F32),
            jax.ShapeDtypeStruct((length, 128), F32),
        ],
        compiler_params=pltpu.CompilerParams(vmem_limit_bytes=58 * 2**20),
        cost_estimate=LIGHT,
        name="attend_back_first",
    )(meta, queries, outputs, grads, lse, *forms, cos, sin)


def attend_back_last(
    meta, offsets, queries, outputs, grads, lse, forms, cos, sin, dk, dv, all_cos, all_sin
):
    length = forms[0].shape[0]
    near = length // 2
    pair, specs = back_specs(queries, forms)
    whole = pl.BlockSpec((length, 128), lambda p, m: (0, 0))
    half = pl.BlockSpec((near, 128), lambda p, m: (0, 0))

    def kernel(*refs):
        dk_in, dv_in, cos_ref, sin_ref, dq_ref, near_ref, far_ref, dk_ref, dv_ref = refs[-9:]

        @pl.when(pl.program_id(0) == 0)
        def _():
            dk_ref[...] = dk_in[...]
            dv_ref[...] = dv_in[...]

        bwd_kernel(offsets, *refs[:-9], dq_ref, dk_ref, dv_ref)

        @pl.when(pl.program_id(0) == pl.num_programs(0) - 1)
        def _():
            block = min(512, near)
            for first in range(0, length, block):
                here = slice(first, first + block)
                dk_block, dv_block = dk_ref[here, :], dv_ref[here, :]
                dk_block = dk_block + pltpu.roll(dk_block, HD, 1)
                dv_block = dv_block + pltpu.roll(dv_block, HD, 1)
                left = lax.broadcasted_iota(jnp.int32, dk_block.shape, 1) < HD
                both = jnp.where(
                    left, turn(dk_block, cos_ref[here, :], -sin_ref[here, :]), dv_block
                )
                if first < near:
                    near_ref[here, :] = both
                else:
                    far_ref[first - near : first - near + block, :] = both.astype(BF16)

    return pl.pallas_call(
        kernel,
        grid_spec=pltpu.PrefetchScalarGridSpec(
            num_scalar_prefetch=1,
            grid=(queries.shape[1] // 128,),
            in_specs=specs + [whole] * 4,
            out_specs=[pair, half, half],
            scratch_shapes=[pltpu.VMEM((length, 128), F32), pltpu.VMEM((length, 128), F32)],
        ),
        out_shape=[
            jax.ShapeDtypeStruct(queries.shape, BF16),
            jax.ShapeDtypeStruct((near, 128), F32),
            jax.ShapeDtypeStruct((near, 128), BF16),
        ],
        compiler_params=pltpu.CompilerParams(vmem_limit_bytes=60 * 2**20),
        cost_estimate=LIGHT,
        name="attend_back_last",
    )(meta, queries, outputs, grads, lse, *forms, cos, sin, dk, dv, all_cos, all_sin)


def feed_kernel(
    gathered_ref,
    tokens_ref,
    cotangent_ref,
    gain_ref,
    output_weight,
    gate_weight,
    up_weight,
    down_weight,
    *refs,
):
    middle_ref, normed_ref, hidden_ref, gates_ref, down_ref, grad_ref = refs[-6:]
    middle = tokens_ref[...].astype(F32)
    for source in range(gathered_ref.shape[0]):
        middle = middle + lax.dot_general(
            gathered_ref[source], output_weight[source], NT, preferred_element_type=F32
        )
    middle_ref[...] = middle
    inverse = lax.rsqrt(jnp.mean(middle * middle, axis=-1, keepdims=True) + EPSILON)
    normed = (middle * inverse * gain_ref[...]).astype(BF16)
    normed_ref[...] = normed
    gate = jnp.dot(normed, gate_weight[...], preferred_element_type=F32)
    up = jnp.dot(normed, up_weight[...], preferred_element_type=F32)
    grad_hidden = jnp.dot(cotangent_ref[...], down_weight[...], preferred_element_type=F32)
    sigmoid = jax.nn.sigmoid(gate)
    hidden = (gate * sigmoid * up).astype(BF16)
    hidden_ref[...] = hidden
    grad_gate = (grad_hidden * up * sigmoid * (1.0 + gate * (1.0 - sigmoid))).astype(BF16)
    grad_up = (grad_hidden * gate * sigmoid).astype(BF16)
    units = hidden.shape[1]
    gates_ref[:, :units] = grad_gate
    gates_ref[:, units:] = grad_up
    down_ref[...] = lax.dot_general(
        hidden, down_weight[...], NT, preferred_element_type=F32
    ).astype(BF16)
    grad_ref[...] = (
        lax.dot_general(grad_gate, gate_weight[...], NT, preferred_element_type=F32)
        + lax.dot_general(grad_up, up_weight[...], NT, preferred_element_type=F32)
    ).astype(BF16)


def feed_forward(c, gathered, tokens, cotangent, gain, output_weight, weights, earlier):
    rows, width = tokens.shape
    units = weights[0].shape[1]
    block = min(256, rows // 4)
    quarter = rows // 4 // block
    if c:
        place = lambda i: (i + quarter, 0)
    else:
        place = lambda i: (jnp.where(i < quarter, i, i + 2 * quarter), 0)
    once = pl.Buffered(1)

    def natural(columns):
        return pl.BlockSpec((block, columns), place)

    def whole(array):
        zeros = (0,) * array.ndim
        return pl.BlockSpec(array.shape, lambda i: zeros, pipeline_mode=once)

    shapes = [
        jax.ShapeDtypeStruct((rows, width), F32),
        jax.ShapeDtypeStruct((rows, width), BF16),
        jax.ShapeDtypeStruct((rows, units), BF16),
        jax.ShapeDtypeStruct((rows, 2 * units), BF16),
    ]
    gain = gain.reshape(1, width)
    return pl.pallas_call(
        feed_kernel,
        grid=(2 * quarter,),
        in_specs=[
            pl.BlockSpec((gathered.shape[0], block, gathered.shape[2]), lambda i: (0, i, 0)),
            natural(width),
            natural(width),
            whole(gain),
            whole(output_weight),
        ]
        + [whole(weight) for weight in weights]
        + [pl.BlockSpec(memory_space=pl.ANY) for _ in earlier],
        out_specs=[natural(shape.shape[1]) for shape in shapes]
        + [pl.BlockSpec((block, width), lambda i: (i, 0))] * 2,
        out_shape=shapes + [jax.ShapeDtypeStruct((rows // 2, width), BF16)] * 2,
        input_output_aliases={8 + k: k for k in range(len(earlier))},
        compiler_params=pltpu.CompilerParams(vmem_limit_bytes=60 * 2**20),
        cost_estimate=LIGHT,
        name="feed_forward",
    )(gathered, tokens, cotangent, gain, output_weight, *weights, *earlier)


def part_specs(shape):
    return [pl.BlockSpec(shape, lambda p, order: (0, 0, 0)) for _ in range(4)]


def join_kernel(order, rows_ref, *refs):
    out_ref = refs[4]
    for part, weight_ref in enumerate(refs[:4]):

        @pl.when(pl.program_id(0) == part)
        def _():
            result = None
            for source in range(rows_ref.shape[0]):
                term = lax.dot_general(
                    rows_ref[source], weight_ref[source], NT, preferred_element_type=F32
                )
                result = term if result is None else result + term
            out_ref[...] = result


def join(order, rows, parts):
    size, count, features = rows.shape
    columns = parts[0].shape[1]
    return pl.pallas_call(
        join_kernel,
        grid_spec=pltpu.PrefetchScalarGridSpec(
            num_scalar_prefetch=1,
            grid=(4,),
            in_specs=[pl.BlockSpec(rows.shape, lambda p, order: (0, 0, 0))]
            + part_specs(parts[0].shape),
            out_specs=pl.BlockSpec((count, columns), lambda p, order: (0, order[p])),
        ),
        out_shape=jax.ShapeDtypeStruct((count, 4 * columns), F32),
        compiler_params=pltpu.CompilerParams(vmem_limit_bytes=48 * 2**20),
        cost_estimate=LIGHT,
        name="join",
    )(order, rows, *parts)


def arrange_kernel(order, *refs):
    for part, weight_ref in enumerate(refs[:-1]):

        @pl.when(pl.program_id(0) == part)
        def _():
            refs[-1][...] = weight_ref[...].reshape(refs[-1].shape)


def arrange(order, parts, shape, block, place):
    zeros = (0,) * parts[0].ndim
    return pl.pallas_call(
        arrange_kernel,
        grid_spec=pltpu.PrefetchScalarGridSpec(
            num_scalar_prefetch=1,
            grid=(len(parts),),
            in_specs=[pl.BlockSpec(parts[0].shape, lambda p, order: zeros) for _ in parts],
            out_specs=pl.BlockSpec(block, lambda p, order: place(order[p])),
        ),
        out_shape=jax.ShapeDtypeStruct(shape, parts[0].dtype),
        compiler_params=pltpu.CompilerParams(vmem_limit_bytes=48 * 2**20),
        cost_estimate=LIGHT,
        name="arrange",
    )(order, *parts)


def quarter_row(row, c, half, span):
    if c:
        return half + row
    return row if row < half else row + span


def after(value, *earlier):
    return lax.optimization_barrier((value, earlier))[0]


def line_steps(size):
    return [
        (
            [(i, i + 1) for i in range(step - 1, size - 1)],
            [(i, i - 1) for i in range(1, size - step + 1)],
        )
        for step in range(1, size)
    ]


class Gather:
    def __init__(self, piece):
        self.piece = piece
        self.rights, self.lefts = [piece], [piece]
        self.hops = line_steps(lax.axis_size("tensor"))

    def step(self):
        done = len(self.rights) - 1
        if done < len(self.hops):
            to_right, to_left = self.hops[done]
            self.rights.append(lax.ppermute(self.rights[-1], "tensor", to_right))
            self.lefts.append(lax.ppermute(self.lefts[-1], "tensor", to_left))
        return self.rights[-1], self.lefts[-1]

    def held(self, pair):
        self.rights[-1], self.lefts[-1] = pair

    def place_hop(self, place, target, hop):
        size = lax.axis_size("tensor")
        me = lax.axis_index("tensor")
        if hop == 0:
            return place(target, self.piece, me)
        right, left = self.rights[hop], self.lefts[hop]
        from_left, from_right = me >= hop, me + hop < size
        if 2 * hop >= size:
            piece = jnp.where(from_left, right, jnp.where(from_right, left, self.piece))
            source = jnp.where(from_left, me - hop, jnp.where(from_right, me + hop, me))
            return place(target, piece, source)
        target = place(
            target, jnp.where(from_left, right, self.piece), jnp.where(from_left, me - hop, me)
        )
        return place(
            target, jnp.where(from_right, left, self.piece), jnp.where(from_right, me + hop, me)
        )

    def whole(self):
        size = lax.axis_size("tensor")
        me = lax.axis_index("tensor")
        while len(self.rights) <= len(self.hops):
            self.step()
        parts, order = [self.piece], [me]
        for hop in range(1, size):
            for came, source in ((self.rights[hop], me - hop), (self.lefts[hop], me + hop)):
                parts.append(came)
                order.append(jnp.where((source >= 0) & (source < size), source, me))
        parts, order = parts[::-1], order[::-1]
        shape = self.piece.shape
        return arrange(
            jnp.stack(order).astype(jnp.int32),
            parts,
            (size, *shape),
            (1, *shape),
            lambda i: (i,) + (0,) * len(shape),
        )


def send_blocks(pick, across=False):
    size = lax.axis_size("tensor")
    me = lax.axis_index("tensor")
    arrived = []
    for shift in range(size):
        block = pick(lax.rem(me + shift, size))
        if across:
            block = lax.ppermute(
                block,
                ("ctx", "tensor"),
                [
                    (c * size + i, (1 - c) * size + (i + shift) % size)
                    for c in range(2)
                    for i in range(size)
                ],
            )
        elif shift:
            block = lax.ppermute(block, "tensor", [(i, (i + shift) % size) for i in range(size)])
        arrived.append(block)
    return tuple(arrived)


def stack_blocks(arrived):
    size = len(arrived)
    me = lax.axis_index("tensor")
    out = jnp.zeros((size, *arrived[0].shape), arrived[0].dtype)
    for shift, block in enumerate(arrived):
        out = lax.dynamic_update_index_in_dim(out, block, lax.rem(me - shift + size, size), 0)
    return out


def hold(*values):
    return lax.optimization_barrier(values)


def rows_part(weight, index, count):
    rows = weight.shape[0] // count
    return lax.dynamic_slice_in_dim(weight, index * rows, rows, 0)


def dot(a, b):
    return jnp.dot(a, b, preferred_element_type=F32)


def dot_t(a, b):
    return jnp.einsum("rf,df->rd", a, b, preferred_element_type=F32)


def t_dot(a, b):
    return jnp.einsum("rd,rf->df", a, b, preferred_element_type=F32)


def body(
    tokens,
    cotangent,
    span_order,
    norm_attn,
    w_query,
    w_key,
    w_value,
    w_output,
    norm_mlp,
    w_gate,
    w_up,
    w_down,
):
    tok_rows, width = tokens.shape
    groups = lax.axis_size("tensor")
    member = lax.axis_index("tensor")
    n_ctx = lax.axis_size("ctx")
    assert n_ctx == 2
    ctx_index = lax.axis_index("ctx")
    features = w_query.shape[1]
    kv_count = w_key.shape[1] // HD
    kv_pick = np.arange(groups) * kv_count // groups
    head = (member * kv_count // groups).astype(jnp.int32).reshape(1)
    span = tok_rows // 2
    half = span // 2
    share = span // groups
    over = [(0, 1), (1, 0)]
    chunks = range(2)

    def chunk(array, c):
        if c:
            return array[half : half + span]
        return jnp.concatenate([array[:half], array[half + span :]], axis=0)

    def natural(first, second):
        return jnp.concatenate([first[:half], second, first[half:]], axis=0)

    order = jnp.roll(span_order[0], -2 * ctx_index)
    places = jnp.arange(4, dtype=jnp.int32)
    slot_of = jnp.sum(
        jnp.where(order[None, :] == places[:, None], places[None, :], 0), axis=1, dtype=jnp.int32
    )
    metas = [jnp.concatenate([order[2 * c : 2 * c + 2], slot_of]) for c in chunks]
    offsets = [(0, half), (half, 0)]

    positions = (order[:, None] * span + jnp.arange(span, dtype=jnp.int32)[None, :]).reshape(-1)
    frequency = 10000.0 ** (-jnp.arange(HD // 2, dtype=F32) / (HD // 2))

    def table(positions):
        angles = frequency[:, None] * positions.astype(F32)[None, :]
        cos_part, sin_part = hold(jnp.cos(angles), jnp.sin(angles))
        cos_part, sin_part = cos_part.T, sin_part.T
        return (
            jnp.concatenate([cos_part] * 4, axis=1),
            jnp.concatenate([-sin_part, sin_part] * 2, axis=1),
        )


    upper = lax.axis_index("dp") % 2
    beside = [(i, i ^ 1) for i in range(lax.axis_size("dp"))]
    quarters = jnp.stack(
        [
            2 * upper + ctx_index,
            2 * upper + 1 - ctx_index,
            2 - 2 * upper + ctx_index,
            3 - 2 * upper - ctx_index,
        ]
    ).astype(jnp.int32)

    output_gather = Gather(rows_part(w_output, upper, 2))
    hop = output_gather.step()
    angles = frequency[:, None] * positions[:tok_rows].astype(F32)[None, :]
    cos_part, sin_part = hold(jnp.cos(angles), jnp.sin(angles))
    kv_own, queries, normed, cos_near, sin_near = project(
        head, tokens, norm_attn, w_key, w_value, w_query, cos_part, sin_part
    )
    kv_own, queries, normed, hop, quarters = hold(kv_own, queries, normed, hop, quarters)
    output_gather.held(hop)
    kv_other = lax.ppermute(kv_own, "ctx", over)
    hop = output_gather.step()
    kv_own, kv_other, sent, kept, normed, hop = hold(
        kv_own, kv_other, chunk(queries, 1), chunk(queries, 0), normed, hop
    )
    output_gather.held(hop)
    length = 2 * tok_rows

    foreign = lax.ppermute(sent, "ctx", over)
    hop = output_gather.step()
    first, first_log, *forms = attend_first(metas[0], offsets[0], kept, kv_own, kv_other)
    first, first_log, foreign, forms, hop = hold(first, first_log, foreign, forms, hop)
    output_gather.held(hop)
    *forms, values_t = forms
    first_whole = lax.all_gather(first, "tensor", axis=0, tiled=False)

    output_near = output_gather.whole()
    output_far = lax.ppermute(output_near, "dp", beside)
    second, second_log = attend(metas[1], offsets[1], foreign, forms[0], forms[1], values_t)
    second, second_log, output_near, output_far = hold(
        second, second_log, output_near, output_far
    )

    cos_far, sin_far = table(after(positions[tok_rows:], second))
    cos_pair = jnp.concatenate([cos_near, cos_far], axis=0)
    sin_pair = jnp.concatenate([sin_near, sin_far], axis=0)
    tables = [(chunk(cos_near, 0), chunk(sin_near, 0)), (chunk(cos_far, 1), chunk(sin_far, 1))]
    second_home = lax.ppermute(second, "ctx", over)
    half_rows = output_near.shape[1]
    output_whole = arrange(
        jnp.stack([upper, 1 - upper]).astype(jnp.int32),
        [output_near, output_far],
        (groups, 2 * half_rows, features),
        output_near.shape,
        lambda i: (0, i, 0),
    )
    second_home, output_whole, tables, cos_pair, sin_pair = hold(
        second_home, output_whole, tables, cos_pair, sin_pair
    )
    second_whole = lax.all_gather(second_home, "tensor", axis=0, tiled=False)
    queries = [kept, foreign]
    attention = [first, second]
    log_totals = [first_log, second_log]

    row_of = [
        jnp.asarray([quarter_row(i * share, c, half, span) for i in range(groups)], jnp.int32)
        for c in chunks
    ]

    def own_rows(array, c):
        return lax.dynamic_slice_in_dim(array, row_of[c][member], share, 0)

    def to_attention(c, middle, grad_share):
        middle = own_rows(middle, c)
        inverse_two = lax.rsqrt(jnp.mean(middle * middle, axis=-1, keepdims=True) + EPSILON)
        grad_normed_mlp = grad_share.astype(F32)
        gain = jnp.sum(grad_normed_mlp * middle * inverse_two, axis=0)
        scaled_two = grad_normed_mlp * norm_mlp
        grad_middle = (
            own_rows(cotangent, c).astype(F32)
            + inverse_two * scaled_two
            - middle * inverse_two**3 * jnp.mean(scaled_two * middle, axis=-1, keepdims=True)
        )
        grad_low = grad_middle.astype(BF16)
        blocks = jnp.einsum(
            "rd,tdq->trq", grad_low, output_whole, preferred_element_type=F32
        ).astype(BF16)
        return gain, grad_middle, grad_low, blocks

    def block_of(blocks):
        return lambda j: lax.dynamic_index_in_dim(blocks, j, 0, keepdims=False)

    def rows_of(array):
        return lambda j: lax.dynamic_slice_in_dim(array, j * share, share, 0)

    def line_sum(array):
        return lax.psum_scatter(array, "tensor", scatter_dimension=0, tiled=True)

    def plane_sum(gradient):
        return lax.psum_scatter(
            gradient.astype(BF16), ("dp", "ctx"), scatter_dimension=0, tiled=True
        )

    query_gather = Gather(rows_part(after(w_query, first_whole), 2 * upper + ctx_index, 4))
    hop = query_gather.step()
    weights = (w_gate, w_up, w_down)
    fixed = (tokens, cotangent, norm_mlp, output_whole, weights)
    *fed, down_first, grad_first = feed_forward(0, first_whole, *fixed, ())
    fed, down_first, grad_first, second_whole, hop = hold(
        fed, down_first, grad_first, second_whole, hop
    )
    query_gather.held(hop)

    share_first = line_sum(grad_first)
    hop = query_gather.step()
    *fed, down_second, grad_second = feed_forward(1, second_whole, *fixed, fed)
    fed, down_second, grad_second, hop = hold(fed, down_second, grad_second, hop)
    query_gather.held(hop)
    middle, normed_mlp, hidden, gates = fed

    share_second = line_sum(grad_second)
    hop = query_gather.step()
    w_gates = t_dot(normed_mlp, gates).astype(BF16)
    w_gates, hop, share_first = hold(w_gates, hop, share_first)
    query_gather.held(hop)

    mixed_shares = [line_sum(after(down, w_gates)) for down in (down_first, down_second)]

    gain_first, middle_first, low_first, blocks = to_attention(0, middle, share_first)
    query_part = query_gather.whole()
    gain_first, middle_first, low_first, blocks, hidden, query_part = hold(
        gain_first, middle_first, low_first, blocks, hidden, query_part
    )

    came_first = send_blocks(block_of(blocks))
    query_over = lax.ppermute(query_part, "ctx", over)
    w_downs = t_dot(cotangent, hidden).astype(BF16)
    middle_own = [own_rows(middle, c) for c in chunks]
    came_first, middle_own, query_part, query_over, w_downs = hold(
        came_first, middle_own, query_part, query_over, w_downs
    )

    query_near = (query_part, query_over)
    query_far = tuple(lax.ppermute(part, "dp", beside) for part in query_near)
    grads_first = stack_blocks(came_first).reshape(span, features)
    query_near, query_far, grads_first, share_second = hold(
        query_near, query_far, grads_first, share_second
    )

    gain_second, middle_second, low_second, blocks = to_attention(1, middle, share_second)
    gain_second, middle_second, low_second, blocks = hold(
        gain_second, middle_second, low_second, blocks
    )

    def back_arguments(c, grads):
        return metas[c], offsets[c], queries[c], attention[c], grads, log_totals[c], forms, *tables[c]

    came_second = send_blocks(block_of(blocks), across=True)
    dq_first, dk, dv = attend_back_first(*back_arguments(0, grads_first))
    dq_first, dk, dv, came_second = hold(dq_first, dk, dv, came_second)

    rows_first = send_blocks(rows_of(dq_first))
    grads_second = stack_blocks(came_second).reshape(span, features)
    dq_second, kv_near, kv_far = attend_back_last(
        *back_arguments(1, grads_second), dk, dv, cos_pair, sin_pair
    )
    dq_second, kv_near, kv_far, rows_first = hold(dq_second, kv_near, kv_far, rows_first)

    def kv_share_of(array, j):
        return [lax.dynamic_slice_in_dim(array, row_of[c][j], share, 0) for c in chunks]

    kv_low = kv_near.astype(BF16)
    near_blocks = send_blocks(lambda j: jnp.concatenate(kv_share_of(kv_low, j), axis=1))
    far_blocks = send_blocks(
        lambda j: jnp.concatenate([rows_of(dq_second)(j), *kv_share_of(kv_far, j)], axis=1),
        across=True,
    )
    query_parts = query_near + query_far
    first_part = join(quarters, stack_blocks(rows_first), query_parts)
    attention_rows = jnp.concatenate(
        [
            lax.dynamic_slice_in_dim(whole, member * share, share, 1)
            for whole in after((first_whole, second_whole), dq_second)
        ],
        axis=1,
    )
    attention_rows = jnp.swapaxes(attention_rows, 0, 1).reshape(2 * share, groups * features)
    w_outs = t_dot(jnp.concatenate([low_first, low_second], axis=0), attention_rows).astype(BF16)
    near_blocks, far_blocks, first_part, w_outs = hold(near_blocks, far_blocks, first_part, w_outs)
    far_blocks = stack_blocks(far_blocks)
    kv_blocks = (
        stack_blocks(near_blocks).astype(F32) + far_blocks[:, :, features:].astype(F32)
    ).astype(BF16)
    kv_blocks = jnp.concatenate([kv_blocks[:, :, : 2 * HD], kv_blocks[:, :, 2 * HD :]], axis=1)
    second_part = join(quarters, far_blocks[:, :, :features], query_parts)
    kv_whole = jnp.stack(
        [
            jnp.concatenate(
                [w_key[:, h * HD : (h + 1) * HD], w_value[:, h * HD : (h + 1) * HD]], axis=1
            )
            for h in kv_pick
        ]
    )

    grad_normed = jnp.concatenate([first_part, second_part], axis=0) + jnp.einsum(
        "trq,tdq->rd", kv_blocks, kv_whole, preferred_element_type=F32
    )
    inputs_own = jnp.concatenate([own_rows(tokens, c) for c in chunks], axis=0).astype(F32)
    inverse_own = lax.rsqrt(jnp.mean(inputs_own * inputs_own, axis=-1, keepdims=True) + EPSILON)
    attn_gain = jnp.sum(grad_normed * inputs_own * inverse_own, axis=0)
    scaled_one = grad_normed * norm_attn
    grad_inputs = (
        jnp.concatenate([middle_first, middle_second], axis=0)
        + inverse_own * scaled_one
        - inputs_own * inverse_own**3 * jnp.mean(scaled_one * inputs_own, axis=-1, keepdims=True)
    ).astype(BF16)

    def put_rows(target, piece, source):
        for c in chunks:
            target = lax.dynamic_update_slice_in_dim(
                target, piece[c * share : (c + 1) * share], row_of[c][source], 0
            )
        return target

    gains = jnp.stack([attn_gain, gain_first + gain_second], axis=1).astype(BF16)
    grad_inputs, gains, dq_second, kv_far, kv_near, w_gates = hold(
        grad_inputs, gains, dq_second, kv_far, kv_near, w_gates
    )
    gate_up_grad = plane_sum(w_gates)

    mixed_share = jnp.concatenate(
        [(middle_own[c] + mixed_shares[c].astype(F32)).astype(BF16) for c in chunks], axis=0
    )
    tokens_gather, mixed_gather = Gather(grad_inputs), Gather(mixed_share)
    tokens_grad = jnp.zeros((tok_rows, width), BF16)
    mixed = jnp.zeros((tok_rows, width), BF16)
    hop, mixed_hop = tokens_gather.step(), mixed_gather.step()
    home = lax.ppermute(
        jnp.concatenate([dq_second, kv_far[:span], kv_far[span:]], axis=1), "ctx", over
    )
    dq_home, kv_sent = home[:, :features], home[:, features:]
    kv_sent = jnp.concatenate([kv_sent[:, : 2 * HD], kv_sent[:, 2 * HD :]], axis=0)
    grad_kv_raw = (kv_near + kv_sent.astype(F32)).astype(BF16)
    query_kv = t_dot(
        normed, jnp.concatenate([natural(dq_first, dq_home), grad_kv_raw], axis=1)
    ).astype(BF16)
    gains = jnp.pad(gains, ((0, 0), (0, 126)))
    rest = jnp.concatenate([w_downs, w_outs, query_kv, gains], axis=1)
    hop, mixed_hop, rest = hold(hop, mixed_hop, rest)
    tokens_gather.held(hop)
    mixed_gather.held(mixed_hop)
    rest = plane_sum(rest)

    hop, mixed_hop = tokens_gather.step(), mixed_gather.step()
    for count in range(2):
        tokens_grad = tokens_gather.place_hop(put_rows, tokens_grad, count)
        mixed = mixed_gather.place_hop(put_rows, mixed, count)
    hop, mixed_hop, tokens_grad, mixed = hold(hop, mixed_hop, tokens_grad, mixed)
    tokens_gather.held(hop)
    mixed_gather.held(mixed_hop)

    hop = tokens_gather.step()
    tokens_grad = tokens_gather.place_hop(put_rows, tokens_grad, 2)
    mixed = mixed_gather.place_hop(put_rows, mixed, 2)
    hop, tokens_grad, mixed = hold(hop, tokens_grad, mixed)
    tokens_gather.held(hop)

    mixed_hop = mixed_gather.step()
    if groups > 3:
        tokens_grad = tokens_gather.place_hop(put_rows, tokens_grad, 3)
    hidden_units = w_down.shape[1]
    rest = after(rest, hop)
    down_grad = rest[:, :hidden_units]
    output_plane = rest[:, hidden_units : hidden_units + groups * features]
    query_plane = rest[:, hidden_units + groups * features :]
    query_grad, small = query_plane[:, :features].astype(F32), query_plane[:, features:]
    blocks = send_blocks(
        lambda j: jnp.concatenate(
            [lax.dynamic_slice_in_dim(output_plane, j * features, features, 1), small], axis=1
        )
    )
    mixed_hop, tokens_grad, blocks = hold(mixed_hop, tokens_grad, blocks)
    mixed_gather.held(mixed_hop)
    blocks = stack_blocks(blocks).astype(F32)
    output_grad = jnp.sum(blocks[:, :, :features], axis=0)
    kv_share = blocks.shape[1] // groups
    kv_blocks = lax.dynamic_slice_in_dim(
        blocks[:, :, features : features + 2 * HD], member * kv_share, kv_share, 1
    )
    gains = jnp.sum(blocks[:, :, features + 2 * HD : features + 2 * HD + 2], axis=0).T
    for count in range(3, groups):
        mixed = mixed_gather.place_hop(put_rows, mixed, count)
        if count + 1 < groups:
            tokens_gather.step()
            mixed_gather.step()
            tokens_grad = tokens_gather.place_hop(put_rows, tokens_grad, count + 1)

    key_heads, value_heads = [], []
    for h in range(kv_count):
        total = jnp.zeros((kv_share, 2 * HD), F32)
        for g in range(groups):
            if kv_pick[g] == h:
                total = total + kv_blocks[g]
        key_heads.append(total[:, :HD])
        value_heads.append(total[:, HD:])
    key_grad = jnp.concatenate(key_heads, axis=1)
    value_grad = jnp.concatenate(value_heads, axis=1)

    return (
        mixed,
        tokens_grad,
        gains[0],
        query_grad,
        key_grad,
        value_grad,
        output_grad,
        gains[1],
        gate_up_grad[:, :hidden_units].astype(F32),
        gate_up_grad[:, hidden_units:].astype(F32),
        down_grad.astype(F32),
    )


def solution(mesh):
    placed = (
        P(("dp", "ctx"), None),
        P(("dp", "ctx"), None),
        P("dp", None),
        P(),
        P(None, "tensor"),
        P(),
        P(),
        P(None, "tensor"),
        P(),
        P(None, "tensor"),
        P(None, "tensor"),
        P(None, "tensor"),
    )
    return jax.shard_map(
        body,
        mesh=mesh,
        in_specs=placed,
        out_specs=(
            P(("dp", "ctx"), None),
            P(("dp", "ctx"), None),
            P(("dp", "ctx")),
            P(("dp", "ctx"), "tensor"),
            P(("dp", "ctx", "tensor"), None),
            P(("dp", "ctx", "tensor"), None),
            P(("dp", "ctx"), "tensor"),
            P(("dp", "ctx")),
            P(("dp", "ctx"), "tensor"),
            P(("dp", "ctx"), "tensor"),
            P(("dp", "ctx"), "tensor"),
        ),
        check_vma=False,
    )
```

```python
import jax
import jax.numpy as jnp
import numpy as np
from jax import lax
from jax.experimental import pallas as pl
from jax.experimental.pallas import tpu as pltpu
from jax.sharding import PartitionSpec as P

NT = (((1,), (1,)), ((), ()))
F32 = jnp.float32
BF16 = jnp.bfloat16
HD = 64
GROUP = 256
EPSILON = 1e-05
LIGHT = pl.CostEstimate(flops=1, bytes_accessed=1, transcendentals=0)


def turn(values, cos, sin):
    low = (lax.broadcasted_iota(jnp.int32, values.shape, 1) % HD) < HD // 2
    other = jnp.where(
        low, pltpu.roll(values, 128 - HD // 2, 1), pltpu.roll(values, HD // 2, 1)
    )
    return values * cos + other * sin


def project_kernel(
    head,
    tokens_ref,
    gain_ref,
    k_weight,
    v_weight,
    q_weight,
    cos_part,
    sin_part,
    kv_ref,
    q_ref,
    normed_ref,
    cos_ref,
    sin_ref,
):
    inputs = tokens_ref[...].astype(F32)
    inverse = lax.rsqrt(jnp.mean(inputs * inputs, axis=-1, keepdims=True) + EPSILON)
    normed = (inputs * inverse * gain_ref[...]).astype(BF16)
    normed_ref[...] = normed
    cos, sin = cos_part[...], sin_part[...]
    cos = jnp.concatenate([cos, cos, cos, cos], axis=0).T
    sin = jnp.concatenate([-sin, sin, -sin, sin], axis=0).T
    cos_ref[...] = cos
    sin_ref[...] = sin
    first = head[0] % 2 == 0
    key = jnp.dot(normed, k_weight[...], preferred_element_type=F32)
    value = jnp.dot(normed, v_weight[...], preferred_element_type=F32)
    key = jnp.where(first, key, pltpu.roll(key, HD, 1))
    value = jnp.where(first, pltpu.roll(value, HD, 1), value)
    is_key = lax.broadcasted_iota(jnp.int32, key.shape, 1) < HD
    kv_ref[...] = jnp.where(is_key, turn(key, cos, sin), value).astype(BF16)
    raw = jnp.dot(normed, q_weight[...], preferred_element_type=F32)
    for start in range(0, q_ref.shape[1], 128):
        pair = raw[:, start : start + 128]
        q_ref[:, start : start + 128] = (turn(pair, cos, sin) * HD**-0.5).astype(BF16)


def project(head, tokens, gain, k_weight, v_weight, q_weight, cos, sin):
    rows, width = tokens.shape
    columns = q_weight.shape[1]
    block = 256
    two_heads = pl.BlockSpec((width, 128), lambda i, head: (0, head[0] // 2))
    return pl.pallas_call(
        project_kernel,
        grid_spec=pltpu.PrefetchScalarGridSpec(
            num_scalar_prefetch=1,
            grid=(rows // block,),
            in_specs=[
                pl.BlockSpec((block, width), lambda i, head: (i, 0)),
                pl.BlockSpec((1, width), lambda i, head: (0, 0)),
                two_heads,
                two_heads,
                pl.BlockSpec((width, columns), lambda i, head: (0, 0)),
                pl.BlockSpec((HD // 2, block), lambda i, head: (0, i)),
                pl.BlockSpec((HD // 2, block), lambda i, head: (0, i)),
            ],
            out_specs=[
                pl.BlockSpec((block, 128), lambda i, head: (i, 0)),
                pl.BlockSpec((block, columns), lambda i, head: (i, 0)),
                pl.BlockSpec((block, width), lambda i, head: (i, 0)),
                pl.BlockSpec((block, 128), lambda i, head: (i, 0)),
                pl.BlockSpec((block, 128), lambda i, head: (i, 0)),
            ],
        ),
        out_shape=[
            jax.ShapeDtypeStruct((rows, 128), BF16),
            jax.ShapeDtypeStruct((rows, columns), BF16),
            jax.ShapeDtypeStruct((rows, width), BF16),
            jax.ShapeDtypeStruct((rows, 128), F32),
            jax.ShapeDtypeStruct((rows, 128), F32),
        ],
        compiler_params=pltpu.CompilerParams(vmem_limit_bytes=48 * 2**20),
        cost_estimate=LIGHT,
        name="project",
    )(head, tokens, gain.reshape(1, width), k_weight, v_weight, q_weight, cos, sin)


def fwd_kernel(offsets, meta, q_ref, ka_ref, kb_ref, vt_ref, o_ref, lse_ref):
    half = q_ref.shape[0] // 2
    span = 2 * half
    group = min(GROUP, half)
    pairs = q_ref.shape[1] // 128
    for part, offset in enumerate(offsets):
        at = slice(part * half, part * half + half)
        queries = [q_ref[at, p * 128 : p * 128 + 128] for p in range(pairs)]
        chains = [(p, keys_ref) for p in range(pairs) for keys_ref in (ka_ref, kb_ref)]
        seen = meta[part]
        own = pl.multiple_of(meta[2 + seen] * span, span)
        heads = []
        for p, keys_ref in chains:
            tops, sums = [], []
            for first in range(0, half, group):
                count = offset + first + group
                rows = pl.ds(own, count)
                scores = lax.dot_general(
                    keys_ref[rows, :],
                    queries[p][first : first + group],
                    NT,
                    preferred_element_type=F32,
                )
                key_at = lax.broadcasted_iota(jnp.int32, scores.shape, 0)
                row_at = lax.broadcasted_iota(jnp.int32, scores.shape, 1) + (offset + first)
                scores = jnp.where(key_at <= row_at, scores, -1e30)
                top = jnp.max(scores, axis=0, keepdims=True)
                weights = jnp.exp(scores - top).astype(BF16)
                tops.append(top)
                sums.append(jnp.dot(vt_ref[:, rows], weights, preferred_element_type=F32))
            heads += [jnp.concatenate(tops, axis=1), jnp.concatenate(sums, axis=1)]

        def step(index, carry):
            rows = pl.ds(pl.multiple_of(meta[2 + index] * span, span), span)
            out = []
            for chain, (p, keys_ref) in enumerate(chains):
                top, total = carry[2 * chain : 2 * chain + 2]
                scores = lax.dot_general(
                    keys_ref[rows, :], queries[p], NT, preferred_element_type=F32
                )
                new_top = jnp.maximum(top, jnp.max(scores, axis=0, keepdims=True))
                weights = jnp.exp(scores - new_top).astype(BF16)
                total = total * jnp.exp(top - new_top) + jnp.dot(
                    vt_ref[:, rows], weights, preferred_element_type=F32
                )
                out += [new_top, total]
            return tuple(out)

        heads = lax.fori_loop(0, seen, step, tuple(heads))
        for p in range(pairs):
            top0, total0, top1, total1 = heads[4 * p : 4 * p + 4]
            norm0, norm1 = total0[HD : HD + 1], total1[HD : HD + 1]
            o_ref[at, p * 128 : p * 128 + 128] = (
                jnp.concatenate([total0[:HD] / norm0, total1[:HD] / norm1], axis=0).T.astype(BF16)
            )
            lse_ref[p, :, at] = jnp.concatenate(
                [top0 + jnp.log(norm0), top1 + jnp.log(norm1), jnp.zeros((6, half), F32)], axis=0
            )


def spread(kv_refs, ka_ref, kb_ref, va_ref, vb_ref, kt_ref, vt_ref):
    at = 0
    for kv_ref in kv_refs:
        rows = kv_ref.shape[0]
        block = min(512, rows)
        for first in range(0, rows, block):
            here = slice(at + first, at + first + block)
            pair = kv_ref[first : first + block, :].astype(F32)
            other = pltpu.roll(pair, HD, 1)
            left = lax.broadcasted_iota(jnp.int32, pair.shape, 1) < HD
            ka_ref[here, :] = jnp.where(left, pair, 0.0).astype(BF16)
            vb_ref[here, :] = jnp.where(left, 0.0, pair).astype(BF16)
            va_ref[here, :] = jnp.where(left, other, 0.0).astype(BF16)
            kb_ref[here, :] = jnp.where(left, 0.0, other).astype(BF16)
            turned = pair.T
            kt_ref[:, here] = turned[:HD].astype(BF16)
            ones = jnp.where(lax.broadcasted_iota(jnp.int32, (16, block), 0) == 0, 1.0, 0.0)
            vt_ref[:, here] = jnp.concatenate([turned[HD:], ones], axis=0).astype(BF16)
        at += rows


def attend_cost(rows, length, width):
    return pl.CostEstimate(
        flops=8 * rows * length * width, bytes_accessed=2**23, transcendentals=0
    )


def attend_first(meta, offsets, queries, kv_own, kv_other):
    rows, width = queries.shape
    pairs = width // 128
    together = 2 if pairs % 2 == 0 else 1
    length = 2 * kv_own.shape[0]

    def whole(shape):
        return pl.BlockSpec(shape, lambda p, m: (0, 0))

    def kernel(meta, q_ref, own, other, o_ref, lse_ref, ka, kb, va, vb, kt, vt):
        @pl.when(pl.program_id(0) == 0)
        def _():
            spread((own, other), ka, kb, va, vb, kt, vt)

        fwd_kernel(offsets, meta, q_ref, ka, kb, vt, o_ref, lse_ref)

    wide = (length, 128)
    forms = [wide, wide, wide, wide, (HD, length), (HD + 16, length)]
    return pl.pallas_call(
        kernel,
        grid_spec=pltpu.PrefetchScalarGridSpec(
            num_scalar_prefetch=1,
            grid=(pairs // together,),
            in_specs=[
                pl.BlockSpec((rows, 128 * together), lambda p, m: (0, p)),
                whole(kv_own.shape),
                whole(kv_other.shape),
            ],
            out_specs=[
                pl.BlockSpec((rows, 128 * together), lambda p, m: (0, p)),
                pl.BlockSpec((together, 8, rows), lambda p, m: (p, 0, 0)),
            ]
            + [whole(form) for form in forms],
        ),
        out_shape=[
            jax.ShapeDtypeStruct((rows, width), BF16),
            jax.ShapeDtypeStruct((pairs, 8, rows), F32),
        ]
        + [jax.ShapeDtypeStruct(form, BF16) for form in forms],
        compiler_params=pltpu.CompilerParams(vmem_limit_bytes=58 * 2**20),
        cost_estimate=attend_cost(rows, length, width),
        name="attend_first",
    )(meta, queries, kv_own, kv_other)


def attend(meta, offsets, queries, keys_a, keys_b, values_t):
    rows, width = queries.shape
    pairs = width // 128
    together = 2 if pairs % 2 == 0 else 1
    length = keys_a.shape[0]
    whole = pl.BlockSpec((length, 128), lambda p, m: (0, 0))

    def kernel(*refs):
        fwd_kernel(offsets, *refs)

    return pl.pallas_call(
        kernel,
        grid_spec=pltpu.PrefetchScalarGridSpec(
            num_scalar_prefetch=1,
            grid=(pairs // together,),
            in_specs=[
                pl.BlockSpec((rows, 128 * together), lambda p, m: (0, p)),
                whole,
                whole,
                pl.BlockSpec(values_t.shape, lambda p, m: (0, 0)),
            ],
            out_specs=[
                pl.BlockSpec((rows, 128 * together), lambda p, m: (0, p)),
                pl.BlockSpec((together, 8, rows), lambda p, m: (p, 0, 0)),
            ],
        ),
        out_shape=[
            jax.ShapeDtypeStruct((rows, width), BF16),
            jax.ShapeDtypeStruct((pairs, 8, rows), F32),
        ],
        compiler_params=pltpu.CompilerParams(vmem_limit_bytes=58 * 2**20),
        cost_estimate=attend_cost(rows, length, width),
        name="attend",
    )(meta, queries, keys_a, keys_b, values_t)


def bwd_kernel(
    offsets,
    meta,
    q_ref,
    o_ref,
    g_ref,
    lse_ref,
    ka_ref,
    kb_ref,
    va_ref,
    vb_ref,
    kt_ref,
    cos_ref,
    sin_ref,
    dq_ref,
    dk_ref,
    dv_ref,
):
    half = q_ref.shape[0] // 2
    span = 2 * half
    group = min(GROUP, half)

    for part, offset in enumerate(offsets):
        at = slice(part * half, part * half + half)
        queries, grads = q_ref[at, :], g_ref[at, :]
        left = lax.broadcasted_iota(jnp.int32, (half, 128), 1) < HD
        products = (grads.astype(F32) * o_ref[at, :].astype(F32)).T
        zero = jnp.zeros_like(queries)
        sides = []
        for side, (keys_ref, values_ref) in enumerate(((ka_ref, va_ref), (kb_ref, vb_ref))):
            mine = left if side == 0 else jnp.logical_not(left)
            delta = jnp.sum(products[side * HD : side * HD + HD], axis=0, keepdims=True)
            sides.append(
                (
                    keys_ref,
                    values_ref,
                    jnp.where(mine, queries, zero),
                    jnp.where(mine, grads, zero),
                    lse_ref[0, side : side + 1, at],
                    delta,
                )
            )

        def block(rows, first, count, masked):
            cut = slice(first, first + count)
            dqs = []
            dk_add = dv_add = None
            for keys_ref, values_ref, q_mine, g_mine, lse, delta in sides:
                scores = lax.dot_general(
                    keys_ref[rows, :], queries[cut], NT, preferred_element_type=F32
                )
                probs = jnp.exp(scores - lse[:, cut])
                if masked:
                    key_at = lax.broadcasted_iota(jnp.int32, scores.shape, 0)
                    row_at = lax.broadcasted_iota(jnp.int32, scores.shape, 1) + (offset + first)
                    probs = jnp.where(key_at <= row_at, probs, 0.0)
                grad_probs = lax.dot_general(
                    values_ref[rows, :], grads[cut], NT, preferred_element_type=F32
                )
                grad_scores = (probs * (grad_probs - delta[:, cut])).astype(BF16)
                dv_new = jnp.dot(probs.astype(BF16), g_mine[cut], preferred_element_type=F32)
                dk_new = jnp.dot(grad_scores, q_mine[cut], preferred_element_type=F32)
                dv_add = dv_new if dv_add is None else dv_add + dv_new
                dk_add = dk_new if dk_add is None else dk_add + dk_new
                dqs.append(jnp.dot(kt_ref[:, rows], grad_scores, preferred_element_type=F32))
            dv_ref[rows, :] += dv_add
            dk_ref[rows, :] += dk_add
            return jnp.concatenate(dqs, axis=0)

        own = pl.multiple_of(meta[2 + meta[part]] * span, span)
        start = jnp.concatenate(
            [
                block(pl.ds(own, offset + first + group), first, group, True)
                for first in range(0, half, group)
            ],
            axis=1,
        )

        def step(index, total):
            rows = pl.ds(pl.multiple_of(meta[2 + index] * span, span), span)
            return total + block(rows, 0, half, False)

        dq = lax.fori_loop(0, meta[part], step, start).T * (HD**-0.5)
        dq_ref[at, :] = turn(dq, cos_ref[at, :], -sin_ref[at, :]).astype(BF16)


def back_specs(queries, forms):
    rows, width = queries.shape
    pair = pl.BlockSpec((rows, 128), lambda p, m: (0, p))
    table = pl.BlockSpec((rows, 128), lambda p, m: (0, 0))
    specs = [pair, pair, pair, pl.BlockSpec((1, 8, rows), lambda p, m: (p, 0, 0))]
    specs += [pl.BlockSpec(form.shape, lambda p, m: (0, 0)) for form in forms]
    return pair, specs + [table, table]


def attend_back_first(meta, offsets, queries, outputs, grads, lse, forms, cos, sin):
    length = forms[0].shape[0]
    pair, specs = back_specs(queries, forms)
    whole = pl.BlockSpec((length, 128), lambda p, m: (0, 0))

    def kernel(*refs):
        dk_ref, dv_ref = refs[-2:]

        @pl.when(pl.program_id(0) == 0)
        def _():
            dk_ref[...] = jnp.zeros(dk_ref.shape, F32)
            dv_ref[...] = jnp.zeros(dv_ref.shape, F32)

        bwd_kernel(offsets, *refs)

    return pl.pallas_call(
        kernel,
        grid_spec=pltpu.PrefetchScalarGridSpec(
            num_scalar_prefetch=1,
            grid=(queries.shape[1] // 128,),
            in_specs=specs,
            out_specs=[pair, whole, whole],
        ),
        out_shape=[
            jax.ShapeDtypeStruct(queries.shape, BF16),
            jax.ShapeDtypeStruct((length, 128), F32),
            jax.ShapeDtypeStruct((length, 128), F32),
        ],
        compiler_params=pltpu.CompilerParams(vmem_limit_bytes=58 * 2**20),
        cost_estimate=LIGHT,
        name="attend_back_first",
    )(meta, queries, outputs, grads, lse, *forms, cos, sin)


def attend_back_last(
    meta, offsets, queries, outputs, grads, lse, forms, cos, sin, dk, dv, all_cos, all_sin
):
    length = forms[0].shape[0]
    near = length // 2
    pair, specs = back_specs(queries, forms)
    whole = pl.BlockSpec((length, 128), lambda p, m: (0, 0))
    half = pl.BlockSpec((near, 128), lambda p, m: (0, 0))

    def kernel(*refs):
        dk_in, dv_in, cos_ref, sin_ref, dq_ref, near_ref, far_ref, dk_ref, dv_ref = refs[-9:]

        @pl.when(pl.program_id(0) == 0)
        def _():
            dk_ref[...] = dk_in[...]
            dv_ref[...] = dv_in[...]

        bwd_kernel(offsets, *refs[:-9], dq_ref, dk_ref, dv_ref)

        @pl.when(pl.program_id(0) == pl.num_programs(0) - 1)
        def _():
            block = min(512, near)
            for first in range(0, length, block):
                here = slice(first, first + block)
                dk_block, dv_block = dk_ref[here, :], dv_ref[here, :]
                dk_block = dk_block + pltpu.roll(dk_block, HD, 1)
                dv_block = dv_block + pltpu.roll(dv_block, HD, 1)
                left = lax.broadcasted_iota(jnp.int32, dk_block.shape, 1) < HD
                both = jnp.where(
                    left, turn(dk_block, cos_ref[here, :], -sin_ref[here, :]), dv_block
                )
                if first < near:
                    near_ref[here, :] = both
                else:
                    far_ref[first - near : first - near + block, :] = both.astype(BF16)

    return pl.pallas_call(
        kernel,
        grid_spec=pltpu.PrefetchScalarGridSpec(
            num_scalar_prefetch=1,
            grid=(queries.shape[1] // 128,),
            in_specs=specs + [whole] * 4,
            out_specs=[pair, half, half],
            scratch_shapes=[pltpu.VMEM((length, 128), F32), pltpu.VMEM((length, 128), F32)],
        ),
        out_shape=[
            jax.ShapeDtypeStruct(queries.shape, BF16),
            jax.ShapeDtypeStruct((near, 128), F32),
            jax.ShapeDtypeStruct((near, 128), BF16),
        ],
        compiler_params=pltpu.CompilerParams(vmem_limit_bytes=60 * 2**20),
        cost_estimate=LIGHT,
        name="attend_back_last",
    )(meta, queries, outputs, grads, lse, *forms, cos, sin, dk, dv, all_cos, all_sin)


def feed_kernel(
    gathered_ref,
    tokens_ref,
    cotangent_ref,
    gain_ref,
    output_weight,
    gate_weight,
    up_weight,
    down_weight,
    *refs,
):
    middle_ref, normed_ref, hidden_ref, gates_ref, down_ref, grad_ref = refs[-6:]
    middle = tokens_ref[...].astype(F32)
    for source in range(gathered_ref.shape[0]):
        middle = middle + lax.dot_general(
            gathered_ref[source], output_weight[source], NT, preferred_element_type=F32
        )
    middle_ref[...] = middle
    inverse = lax.rsqrt(jnp.mean(middle * middle, axis=-1, keepdims=True) + EPSILON)
    normed = (middle * inverse * gain_ref[...]).astype(BF16)
    normed_ref[...] = normed
    gate = jnp.dot(normed, gate_weight[...], preferred_element_type=F32)
    up = jnp.dot(normed, up_weight[...], preferred_element_type=F32)
    grad_hidden = jnp.dot(cotangent_ref[...], down_weight[...], preferred_element_type=F32)
    sigmoid = jax.nn.sigmoid(gate)
    hidden = (gate * sigmoid * up).astype(BF16)
    hidden_ref[...] = hidden
    grad_gate = (grad_hidden * up * sigmoid * (1.0 + gate * (1.0 - sigmoid))).astype(BF16)
    grad_up = (grad_hidden * gate * sigmoid).astype(BF16)
    units = hidden.shape[1]
    gates_ref[:, :units] = grad_gate
    gates_ref[:, units:] = grad_up
    down_ref[...] = lax.dot_general(
        hidden, down_weight[...], NT, preferred_element_type=F32
    ).astype(BF16)
    grad_ref[...] = (
        lax.dot_general(grad_gate, gate_weight[...], NT, preferred_element_type=F32)
        + lax.dot_general(grad_up, up_weight[...], NT, preferred_element_type=F32)
    ).astype(BF16)


def feed_forward(c, gathered, tokens, cotangent, gain, output_weight, weights, earlier):
    rows, width = tokens.shape
    units = weights[0].shape[1]
    block = min(256, rows // 4)
    quarter = rows // 4 // block
    if c:
        place = lambda i: (i + quarter, 0)
    else:
        place = lambda i: (jnp.where(i < quarter, i, i + 2 * quarter), 0)
    once = pl.Buffered(1)

    def natural(columns):
        return pl.BlockSpec((block, columns), place)

    def whole(array):
        zeros = (0,) * array.ndim
        return pl.BlockSpec(array.shape, lambda i: zeros, pipeline_mode=once)

    shapes = [
        jax.ShapeDtypeStruct((rows, width), F32),
        jax.ShapeDtypeStruct((rows, width), BF16),
        jax.ShapeDtypeStruct((rows, units), BF16),
        jax.ShapeDtypeStruct((rows, 2 * units), BF16),
        jax.ShapeDtypeStruct((rows, width), BF16),
    ]
    gain = gain.reshape(1, width)
    return pl.pallas_call(
        feed_kernel,
        grid=(2 * quarter,),
        in_specs=[
            pl.BlockSpec((gathered.shape[0], block, gathered.shape[2]), lambda i: (0, i, 0)),
            natural(width),
            natural(width),
            whole(gain),
            whole(output_weight),
        ]
        + [whole(weight) for weight in weights]
        + [pl.BlockSpec(memory_space=pl.ANY) for _ in earlier],
        out_specs=[natural(shape.shape[1]) for shape in shapes]
        + [pl.BlockSpec((block, width), lambda i: (i, 0))],
        out_shape=shapes + [jax.ShapeDtypeStruct((rows // 2, width), BF16)],
        input_output_aliases={8 + k: k for k in range(len(earlier))},
        compiler_params=pltpu.CompilerParams(vmem_limit_bytes=60 * 2**20),
        cost_estimate=LIGHT,
        name="feed_forward",
    )(gathered, tokens, cotangent, gain, output_weight, *weights, *earlier)


def part_specs(shape):
    return [pl.BlockSpec(shape, lambda p, order: (0, 0, 0)) for _ in range(4)]


def join_kernel(order, rows_ref, *refs):
    out_ref = refs[4]
    for part, weight_ref in enumerate(refs[:4]):

        @pl.when(pl.program_id(0) == part)
        def _():
            result = None
            for source in range(rows_ref.shape[0]):
                term = lax.dot_general(
                    rows_ref[source], weight_ref[source], NT, preferred_element_type=F32
                )
                result = term if result is None else result + term
            out_ref[...] = result


def join(order, rows, parts):
    size, count, features = rows.shape
    columns = parts[0].shape[1]
    return pl.pallas_call(
        join_kernel,
        grid_spec=pltpu.PrefetchScalarGridSpec(
            num_scalar_prefetch=1,
            grid=(4,),
            in_specs=[pl.BlockSpec(rows.shape, lambda p, order: (0, 0, 0))]
            + part_specs(parts[0].shape),
            out_specs=pl.BlockSpec((count, columns), lambda p, order: (0, order[p])),
        ),
        out_shape=jax.ShapeDtypeStruct((count, 4 * columns), F32),
        compiler_params=pltpu.CompilerParams(vmem_limit_bytes=48 * 2**20),
        cost_estimate=LIGHT,
        name="join",
    )(order, rows, *parts)


def arrange_kernel(order, *refs):
    for part, weight_ref in enumerate(refs[:-1]):

        @pl.when(pl.program_id(0) == part)
        def _():
            refs[-1][...] = weight_ref[...].reshape(refs[-1].shape)


def arrange(order, parts, shape, block, place):
    zeros = (0,) * parts[0].ndim
    return pl.pallas_call(
        arrange_kernel,
        grid_spec=pltpu.PrefetchScalarGridSpec(
            num_scalar_prefetch=1,
            grid=(len(parts),),
            in_specs=[pl.BlockSpec(parts[0].shape, lambda p, order: zeros) for _ in parts],
            out_specs=pl.BlockSpec(block, lambda p, order: place(order[p])),
        ),
        out_shape=jax.ShapeDtypeStruct(shape, parts[0].dtype),
        compiler_params=pltpu.CompilerParams(vmem_limit_bytes=48 * 2**20),
        cost_estimate=LIGHT,
        name="arrange",
    )(order, *parts)


def quarter_row(row, c, half, span):
    if c:
        return half + row
    return row if row < half else row + span


def after(value, *earlier):
    return lax.optimization_barrier((value, earlier))[0]


def line_steps(size):
    return [
        (
            [(i, i + 1) for i in range(step - 1, size - 1)],
            [(i, i - 1) for i in range(1, size - step + 1)],
        )
        for step in range(1, size)
    ]


class Gather:
    def __init__(self, piece):
        self.piece = piece
        self.rights, self.lefts = [piece], [piece]
        self.hops = line_steps(lax.axis_size("tensor"))

    def step(self):
        done = len(self.rights) - 1
        if done < len(self.hops):
            to_right, to_left = self.hops[done]
            self.rights.append(lax.ppermute(self.rights[-1], "tensor", to_right))
            self.lefts.append(lax.ppermute(self.lefts[-1], "tensor", to_left))
        return self.rights[-1], self.lefts[-1]

    def held(self, pair):
        self.rights[-1], self.lefts[-1] = pair

    def place_hop(self, place, target, hop):
        size = lax.axis_size("tensor")
        me = lax.axis_index("tensor")
        if hop == 0:
            return place(target, self.piece, me)
        right, left = self.rights[hop], self.lefts[hop]
        from_left, from_right = me >= hop, me + hop < size
        if 2 * hop >= size:
            piece = jnp.where(from_left, right, jnp.where(from_right, left, self.piece))
            source = jnp.where(from_left, me - hop, jnp.where(from_right, me + hop, me))
            return place(target, piece, source)
        target = place(
            target, jnp.where(from_left, right, self.piece), jnp.where(from_left, me - hop, me)
        )
        return place(
            target, jnp.where(from_right, left, self.piece), jnp.where(from_right, me + hop, me)
        )

    def whole(self):
        size = lax.axis_size("tensor")
        me = lax.axis_index("tensor")
        while len(self.rights) <= len(self.hops):
            self.step()
        parts, order = [self.piece], [me]
        for hop in range(1, size):
            for came, source in ((self.rights[hop], me - hop), (self.lefts[hop], me + hop)):
                parts.append(came)
                order.append(jnp.where((source >= 0) & (source < size), source, me))
        parts, order = parts[::-1], order[::-1]
        shape = self.piece.shape
        return arrange(
            jnp.stack(order).astype(jnp.int32),
            parts,
            (size, *shape),
            (1, *shape),
            lambda i: (i,) + (0,) * len(shape),
        )


def send_blocks(pick, across=False):
    size = lax.axis_size("tensor")
    me = lax.axis_index("tensor")
    arrived = []
    for shift in range(size):
        block = pick(lax.rem(me + shift, size))
        if across:
            block = lax.ppermute(
                block,
                ("ctx", "tensor"),
                [
                    (c * size + i, (1 - c) * size + (i + shift) % size)
                    for c in range(2)
                    for i in range(size)
                ],
            )
        elif shift:
            block = lax.ppermute(block, "tensor", [(i, (i + shift) % size) for i in range(size)])
        arrived.append(block)
    return tuple(arrived)


def stack_blocks(arrived):
    size = len(arrived)
    me = lax.axis_index("tensor")
    out = jnp.zeros((size, *arrived[0].shape), arrived[0].dtype)
    for shift, block in enumerate(arrived):
        out = lax.dynamic_update_index_in_dim(out, block, lax.rem(me - shift + size, size), 0)
    return out


def hold(*values):
    return lax.optimization_barrier(values)


def rows_part(weight, index, count):
    rows = weight.shape[0] // count
    return lax.dynamic_slice_in_dim(weight, index * rows, rows, 0)


def dot(a, b):
    return jnp.dot(a, b, preferred_element_type=F32)


def dot_t(a, b):
    return jnp.einsum("rf,df->rd", a, b, preferred_element_type=F32)


def t_dot(a, b):
    return jnp.einsum("rd,rf->df", a, b, preferred_element_type=F32)


def body(
    tokens,
    cotangent,
    span_order,
    norm_attn,
    w_query,
    w_key,
    w_value,
    w_output,
    norm_mlp,
    w_gate,
    w_up,
    w_down,
):
    tok_rows, width = tokens.shape
    groups = lax.axis_size("tensor")
    member = lax.axis_index("tensor")
    n_ctx = lax.axis_size("ctx")
    assert n_ctx == 2
    ctx_index = lax.axis_index("ctx")
    features = w_query.shape[1]
    kv_count = w_key.shape[1] // HD
    kv_pick = np.arange(groups) * kv_count // groups
    head = (member * kv_count // groups).astype(jnp.int32).reshape(1)
    span = tok_rows // 2
    half = span // 2
    share = span // groups
    over = [(0, 1), (1, 0)]
    chunks = range(2)

    def chunk(array, c):
        if c:
            return array[half : half + span]
        return jnp.concatenate([array[:half], array[half + span :]], axis=0)

    def natural(first, second):
        return jnp.concatenate([first[:half], second, first[half:]], axis=0)

    order = jnp.roll(span_order[0], -2 * ctx_index)
    places = jnp.arange(4, dtype=jnp.int32)
    slot_of = jnp.sum(
        jnp.where(order[None, :] == places[:, None], places[None, :], 0), axis=1, dtype=jnp.int32
    )
    metas = [jnp.concatenate([order[2 * c : 2 * c + 2], slot_of]) for c in chunks]
    offsets = [(0, half), (half, 0)]

    positions = (order[:, None] * span + jnp.arange(span, dtype=jnp.int32)[None, :]).reshape(-1)
    frequency = 10000.0 ** (-jnp.arange(HD // 2, dtype=F32) / (HD // 2))

    def table(positions):
        angles = frequency[:, None] * positions.astype(F32)[None, :]
        cos_part, sin_part = hold(jnp.cos(angles), jnp.sin(angles))
        cos_part, sin_part = cos_part.T, sin_part.T
        return (
            jnp.concatenate([cos_part] * 4, axis=1),
            jnp.concatenate([-sin_part, sin_part] * 2, axis=1),
        )


    upper = lax.axis_index("dp") % 2
    beside = [(i, i ^ 1) for i in range(lax.axis_size("dp"))]
    quarters = jnp.stack(
        [
            2 * upper + ctx_index,
            2 * upper + 1 - ctx_index,
            2 - 2 * upper + ctx_index,
            3 - 2 * upper - ctx_index,
        ]
    ).astype(jnp.int32)

    output_gather = Gather(rows_part(w_output, upper, 2))
    hop = output_gather.step()
    angles = frequency[:, None] * positions[:tok_rows].astype(F32)[None, :]
    cos_part, sin_part = hold(jnp.cos(angles), jnp.sin(angles))
    kv_own, queries, normed, cos_near, sin_near = project(
        head, tokens, norm_attn, w_key, w_value, w_query, cos_part, sin_part
    )
    kv_own, queries, normed, hop, quarters = hold(kv_own, queries, normed, hop, quarters)
    output_gather.held(hop)
    kv_other = lax.ppermute(kv_own, "ctx", over)
    hop = output_gather.step()
    kv_own, kv_other, sent, kept, normed, hop = hold(
        kv_own, kv_other, chunk(queries, 1), chunk(queries, 0), normed, hop
    )
    output_gather.held(hop)
    length = 2 * tok_rows

    foreign = lax.ppermute(sent, "ctx", over)
    hop = output_gather.step()
    first, first_log, *forms = attend_first(metas[0], offsets[0], kept, kv_own, kv_other)
    first, first_log, foreign, forms, hop = hold(first, first_log, foreign, forms, hop)
    output_gather.held(hop)
    *forms, values_t = forms
    first_whole = lax.all_gather(first, "tensor", axis=0, tiled=False)

    output_near = output_gather.whole()
    output_far = lax.ppermute(output_near, "dp", beside)
    second, second_log = attend(metas[1], offsets[1], foreign, forms[0], forms[1], values_t)
    second, second_log, output_near, output_far = hold(
        second, second_log, output_near, output_far
    )

    cos_far, sin_far = table(after(positions[tok_rows:], second))
    cos_pair = jnp.concatenate([cos_near, cos_far], axis=0)
    sin_pair = jnp.concatenate([sin_near, sin_far], axis=0)
    tables = [(chunk(cos_near, 0), chunk(sin_near, 0)), (chunk(cos_far, 1), chunk(sin_far, 1))]
    second_home = lax.ppermute(second, "ctx", over)
    half_rows = output_near.shape[1]
    output_whole = arrange(
        jnp.stack([upper, 1 - upper]).astype(jnp.int32),
        [output_near, output_far],
        (groups, 2 * half_rows, features),
        output_near.shape,
        lambda i: (0, i, 0),
    )
    second_home, output_whole, tables, cos_pair, sin_pair = hold(
        second_home, output_whole, tables, cos_pair, sin_pair
    )
    second_whole = lax.all_gather(second_home, "tensor", axis=0, tiled=False)
    queries = [kept, foreign]
    attention = [first, second]
    log_totals = [first_log, second_log]

    row_of = [
        jnp.asarray([quarter_row(i * share, c, half, span) for i in range(groups)], jnp.int32)
        for c in chunks
    ]

    def own_rows(array, c):
        return lax.dynamic_slice_in_dim(array, row_of[c][member], share, 0)

    def to_attention(c, middle, grad_share):
        middle = own_rows(middle, c)
        inverse_two = lax.rsqrt(jnp.mean(middle * middle, axis=-1, keepdims=True) + EPSILON)
        grad_normed_mlp = grad_share.astype(F32)
        gain = jnp.sum(grad_normed_mlp * middle * inverse_two, axis=0)
        scaled_two = grad_normed_mlp * norm_mlp
        grad_middle = (
            own_rows(cotangent, c).astype(F32)
            + inverse_two * scaled_two
            - middle * inverse_two**3 * jnp.mean(scaled_two * middle, axis=-1, keepdims=True)
        )
        grad_low = grad_middle.astype(BF16)
        blocks = jnp.einsum(
            "rd,tdq->trq", grad_low, output_whole, preferred_element_type=F32
        ).astype(BF16)
        return gain, grad_middle, grad_low, blocks

    def block_of(blocks):
        return lambda j: lax.dynamic_index_in_dim(blocks, j, 0, keepdims=False)

    def rows_of(array):
        return lambda j: lax.dynamic_slice_in_dim(array, j * share, share, 0)

    def line_sum(array):
        return lax.psum_scatter(array, "tensor", scatter_dimension=0, tiled=True)

    def plane_sum(gradient):
        return lax.psum_scatter(
            gradient.astype(BF16), ("dp", "ctx"), scatter_dimension=0, tiled=True
        )

    query_gather = Gather(rows_part(after(w_query, first_whole), 2 * upper + ctx_index, 4))
    hop = query_gather.step()
    weights = (w_gate, w_up, w_down)
    fixed = (tokens, cotangent, norm_mlp, output_whole, weights)
    *fed, grad_first = feed_forward(0, first_whole, *fixed, ())
    fed, grad_first, second_whole, hop = hold(fed, grad_first, second_whole, hop)
    query_gather.held(hop)

    share_first = line_sum(grad_first)
    hop = query_gather.step()
    *fed, grad_second = feed_forward(1, second_whole, *fixed, fed)
    fed, grad_second, hop = hold(fed, grad_second, hop)
    query_gather.held(hop)
    middle, normed_mlp, hidden, gates, mlp_part = fed

    share_second = line_sum(grad_second)
    hop = query_gather.step()
    w_gates = t_dot(normed_mlp, gates).astype(BF16)
    w_gates, hop, share_first = hold(w_gates, hop, share_first)
    query_gather.held(hop)

    mlp_share = line_sum(after(mlp_part, w_gates))

    gain_first, middle_first, low_first, blocks = to_attention(0, middle, share_first)
    query_part = query_gather.whole()
    gain_first, middle_first, low_first, blocks, hidden, query_part = hold(
        gain_first, middle_first, low_first, blocks, hidden, query_part
    )

    came_first = send_blocks(block_of(blocks))
    query_over = lax.ppermute(query_part, "ctx", over)
    w_downs = t_dot(cotangent, hidden).astype(BF16)
    n_part = tok_rows // groups
    middle_own = lax.dynamic_slice_in_dim(middle, member * n_part, n_part, 0)
    came_first, middle_own, query_part, query_over, w_downs = hold(
        came_first, middle_own, query_part, query_over, w_downs
    )

    query_near = (query_part, query_over)
    query_far = tuple(lax.ppermute(part, "dp", beside) for part in query_near)
    grads_first = stack_blocks(came_first).reshape(span, features)
    query_near, query_far, grads_first, share_second = hold(
        query_near, query_far, grads_first, share_second
    )

    gain_second, middle_second, low_second, blocks = to_attention(1, middle, share_second)
    gain_second, middle_second, low_second, blocks = hold(
        gain_second, middle_second, low_second, blocks
    )

    def back_arguments(c, grads):
        return metas[c], offsets[c], queries[c], attention[c], grads, log_totals[c], forms, *tables[c]

    came_second = send_blocks(block_of(blocks), across=True)
    dq_first, dk, dv = attend_back_first(*back_arguments(0, grads_first))
    dq_first, dk, dv, came_second = hold(dq_first, dk, dv, came_second)

    rows_first = send_blocks(rows_of(dq_first))
    grads_second = stack_blocks(came_second).reshape(span, features)
    dq_second, kv_near, kv_far = attend_back_last(
        *back_arguments(1, grads_second), dk, dv, cos_pair, sin_pair
    )
    dq_second, kv_near, kv_far, rows_first = hold(dq_second, kv_near, kv_far, rows_first)

    def kv_share_of(array, j):
        return [lax.dynamic_slice_in_dim(array, row_of[c][j], share, 0) for c in chunks]

    kv_low = kv_near.astype(BF16)
    near_blocks = send_blocks(lambda j: jnp.concatenate(kv_share_of(kv_low, j), axis=1))
    far_blocks = send_blocks(
        lambda j: jnp.concatenate([rows_of(dq_second)(j), *kv_share_of(kv_far, j)], axis=1),
        across=True,
    )
    query_parts = query_near + query_far
    first_part = join(quarters, stack_blocks(rows_first), query_parts)
    attention_rows = jnp.concatenate(
        [
            lax.dynamic_slice_in_dim(whole, member * share, share, 1)
            for whole in after((first_whole, second_whole), dq_second)
        ],
        axis=1,
    )
    attention_rows = jnp.swapaxes(attention_rows, 0, 1).reshape(2 * share, groups * features)
    w_outs = t_dot(jnp.concatenate([low_first, low_second], axis=0), attention_rows).astype(BF16)
    near_blocks, far_blocks, first_part, w_outs = hold(near_blocks, far_blocks, first_part, w_outs)
    far_blocks = stack_blocks(far_blocks)
    kv_blocks = (
        stack_blocks(near_blocks).astype(F32) + far_blocks[:, :, features:].astype(F32)
    ).astype(BF16)
    kv_blocks = jnp.concatenate([kv_blocks[:, :, : 2 * HD], kv_blocks[:, :, 2 * HD :]], axis=1)
    second_part = join(quarters, far_blocks[:, :, :features], query_parts)
    kv_whole = jnp.stack(
        [
            jnp.concatenate(
                [w_key[:, h * HD : (h + 1) * HD], w_value[:, h * HD : (h + 1) * HD]], axis=1
            )
            for h in kv_pick
        ]
    )

    grad_normed = jnp.concatenate([first_part, second_part], axis=0) + jnp.einsum(
        "trq,tdq->rd", kv_blocks, kv_whole, preferred_element_type=F32
    )
    inputs_own = jnp.concatenate([own_rows(tokens, c) for c in chunks], axis=0).astype(F32)
    inverse_own = lax.rsqrt(jnp.mean(inputs_own * inputs_own, axis=-1, keepdims=True) + EPSILON)
    attn_gain = jnp.sum(grad_normed * inputs_own * inverse_own, axis=0)
    scaled_one = grad_normed * norm_attn
    grad_inputs = (
        jnp.concatenate([middle_first, middle_second], axis=0)
        + inverse_own * scaled_one
        - inputs_own * inverse_own**3 * jnp.mean(scaled_one * inputs_own, axis=-1, keepdims=True)
    ).astype(BF16)

    def put_rows(target, piece, source):
        for c in chunks:
            target = lax.dynamic_update_slice_in_dim(
                target, piece[c * share : (c + 1) * share], row_of[c][source], 0
            )
        return target

    gains = jnp.stack([attn_gain, gain_first + gain_second], axis=1).astype(BF16)
    mixed_share = (middle_own + mlp_share.astype(F32)).astype(BF16)
    grad_inputs, gains, dq_second, kv_far, kv_near, w_gates, mixed_share = hold(
        grad_inputs, gains, dq_second, kv_far, kv_near, w_gates, mixed_share
    )
    gate_up_grad = plane_sum(w_gates)

    def put_share(target, piece, source):
        return lax.dynamic_update_slice_in_dim(target, piece, source * n_part, 0)

    tokens_gather, mixed_gather = Gather(grad_inputs), Gather(mixed_share)
    tokens_grad = jnp.zeros((tok_rows, width), BF16)
    mixed = jnp.zeros((tok_rows, width), BF16)
    hop, mixed_hop = tokens_gather.step(), mixed_gather.step()
    home = lax.ppermute(
        jnp.concatenate([dq_second, kv_far[:span], kv_far[span:]], axis=1), "ctx", over
    )
    dq_home, kv_sent = home[:, :features], home[:, features:]
    kv_sent = jnp.concatenate([kv_sent[:, : 2 * HD], kv_sent[:, 2 * HD :]], axis=0)
    grad_kv_raw = (kv_near + kv_sent.astype(F32)).astype(BF16)
    query_kv = t_dot(
        normed, jnp.concatenate([natural(dq_first, dq_home), grad_kv_raw], axis=1)
    ).astype(BF16)
    gains = jnp.pad(gains, ((0, 0), (0, 126)))
    rest = jnp.concatenate([w_downs, w_outs, query_kv, gains], axis=1)
    hop, mixed_hop, rest = hold(hop, mixed_hop, rest)
    tokens_gather.held(hop)
    mixed_gather.held(mixed_hop)
    rest = plane_sum(rest)

    hop, mixed_hop = tokens_gather.step(), mixed_gather.step()
    for count in range(2):
        tokens_grad = tokens_gather.place_hop(put_rows, tokens_grad, count)
        mixed = mixed_gather.place_hop(put_share, mixed, count)
    hop, mixed_hop, tokens_grad, mixed = hold(hop, mixed_hop, tokens_grad, mixed)
    tokens_gather.held(hop)
    mixed_gather.held(mixed_hop)

    hop = tokens_gather.step()
    tokens_grad = tokens_gather.place_hop(put_rows, tokens_grad, 2)
    mixed = mixed_gather.place_hop(put_share, mixed, 2)
    hop, tokens_grad, mixed = hold(hop, tokens_grad, mixed)
    tokens_gather.held(hop)

    mixed_hop = mixed_gather.step()
    if groups > 3:
        tokens_grad = tokens_gather.place_hop(put_rows, tokens_grad, 3)
    hidden_units = w_down.shape[1]
    rest = after(rest, hop)
    down_grad = rest[:, :hidden_units]
    output_plane = rest[:, hidden_units : hidden_units + groups * features]
    query_plane = rest[:, hidden_units + groups * features :]
    query_grad, small = query_plane[:, :features].astype(F32), query_plane[:, features:]
    blocks = send_blocks(
        lambda j: jnp.concatenate(
            [lax.dynamic_slice_in_dim(output_plane, j * features, features, 1), small], axis=1
        )
    )
    mixed_hop, tokens_grad, blocks = hold(mixed_hop, tokens_grad, blocks)
    mixed_gather.held(mixed_hop)
    blocks = stack_blocks(blocks).astype(F32)
    output_grad = jnp.sum(blocks[:, :, :features], axis=0)
    kv_share = blocks.shape[1] // groups
    kv_blocks = lax.dynamic_slice_in_dim(
        blocks[:, :, features : features + 2 * HD], member * kv_share, kv_share, 1
    )
    gains = jnp.sum(blocks[:, :, features + 2 * HD : features + 2 * HD + 2], axis=0).T
    for count in range(3, groups):
        mixed = mixed_gather.place_hop(put_share, mixed, count)
        if count + 1 < groups:
            tokens_gather.step()
            mixed_gather.step()
            tokens_grad = tokens_gather.place_hop(put_rows, tokens_grad, count + 1)

    key_heads, value_heads = [], []
    for h in range(kv_count):
        total = jnp.zeros((kv_share, 2 * HD), F32)
        for g in range(groups):
            if kv_pick[g] == h:
                total = total + kv_blocks[g]
        key_heads.append(total[:, :HD])
        value_heads.append(total[:, HD:])
    key_grad = jnp.concatenate(key_heads, axis=1)
    value_grad = jnp.concatenate(value_heads, axis=1)

    return (
        mixed,
        tokens_grad,
        gains[0],
        query_grad,
        key_grad,
        value_grad,
        output_grad,
        gains[1],
        gate_up_grad[:, :hidden_units].astype(F32),
        gate_up_grad[:, hidden_units:].astype(F32),
        down_grad.astype(F32),
    )


def solution(mesh):
    placed = (
        P(("dp", "ctx"), None),
        P(("dp", "ctx"), None),
        P("dp", None),
        P(),
        P(None, "tensor"),
        P(),
        P(),
        P(None, "tensor"),
        P(),
        P(None, "tensor"),
        P(None, "tensor"),
        P(None, "tensor"),
    )
    return jax.shard_map(
        body,
        mesh=mesh,
        in_specs=placed,
        out_specs=(
            P(("dp", "ctx"), None),
            P(("dp", "ctx"), None),
            P(("dp", "ctx")),
            P(("dp", "ctx"), "tensor"),
            P(("dp", "ctx", "tensor"), None),
            P(("dp", "ctx", "tensor"), None),
            P(("dp", "ctx"), "tensor"),
            P(("dp", "ctx")),
            P(("dp", "ctx"), "tensor"),
            P(("dp", "ctx"), "tensor"),
            P(("dp", "ctx"), "tensor"),
        ),
        check_vma=False,
    )
```

```python
import jax
import jax.numpy as jnp
import numpy as np
from jax import lax
from jax.experimental import pallas as pl
from jax.experimental.pallas import tpu as pltpu
from jax.sharding import PartitionSpec as P

NT = (((1,), (1,)), ((), ()))
F32 = jnp.float32
BF16 = jnp.bfloat16
HD = 64
GROUP = 256
EPSILON = 1e-05
LIGHT = pl.CostEstimate(flops=1, bytes_accessed=1, transcendentals=0)


def turn(values, cos, sin):
    low = (lax.broadcasted_iota(jnp.int32, values.shape, 1) % HD) < HD // 2
    other = jnp.where(
        low, pltpu.roll(values, 128 - HD // 2, 1), pltpu.roll(values, HD // 2, 1)
    )
    return values * cos + other * sin


def project_kernel(
    head,
    tokens_ref,
    gain_ref,
    k_weight,
    v_weight,
    q_weight,
    cos_part,
    sin_part,
    kv_ref,
    q_ref,
    normed_ref,
    cos_ref,
    sin_ref,
):
    inputs = tokens_ref[...].astype(F32)
    inverse = lax.rsqrt(jnp.mean(inputs * inputs, axis=-1, keepdims=True) + EPSILON)
    normed = (inputs * inverse * gain_ref[...]).astype(BF16)
    normed_ref[...] = normed
    cos, sin = cos_part[...], sin_part[...]
    cos = jnp.concatenate([cos, cos, cos, cos], axis=0).T
    sin = jnp.concatenate([-sin, sin, -sin, sin], axis=0).T
    cos_ref[...] = cos
    sin_ref[...] = sin
    first = head[0] % 2 == 0
    key = jnp.dot(normed, k_weight[...], preferred_element_type=F32)
    value = jnp.dot(normed, v_weight[...], preferred_element_type=F32)
    key = jnp.where(first, key, pltpu.roll(key, HD, 1))
    value = jnp.where(first, pltpu.roll(value, HD, 1), value)
    is_key = lax.broadcasted_iota(jnp.int32, key.shape, 1) < HD
    kv_ref[...] = jnp.where(is_key, turn(key, cos, sin), value).astype(BF16)
    raw = jnp.dot(normed, q_weight[...], preferred_element_type=F32)
    for start in range(0, q_ref.shape[1], 128):
        pair = raw[:, start : start + 128]
        q_ref[:, start : start + 128] = (turn(pair, cos, sin) * HD**-0.5).astype(BF16)


def project(head, tokens, gain, k_weight, v_weight, q_weight, cos, sin):
    rows, width = tokens.shape
    columns = q_weight.shape[1]
    block = 256
    two_heads = pl.BlockSpec((width, 128), lambda i, head: (0, head[0] // 2))
    return pl.pallas_call(
        project_kernel,
        grid_spec=pltpu.PrefetchScalarGridSpec(
            num_scalar_prefetch=1,
            grid=(rows // block,),
            in_specs=[
                pl.BlockSpec((block, width), lambda i, head: (i, 0)),
                pl.BlockSpec((1, width), lambda i, head: (0, 0)),
                two_heads,
                two_heads,
                pl.BlockSpec((width, columns), lambda i, head: (0, 0)),
                pl.BlockSpec((HD // 2, block), lambda i, head: (0, i)),
                pl.BlockSpec((HD // 2, block), lambda i, head: (0, i)),
            ],
            out_specs=[
                pl.BlockSpec((block, 128), lambda i, head: (i, 0)),
                pl.BlockSpec((block, columns), lambda i, head: (i, 0)),
                pl.BlockSpec((block, width), lambda i, head: (i, 0)),
                pl.BlockSpec((block, 128), lambda i, head: (i, 0)),
                pl.BlockSpec((block, 128), lambda i, head: (i, 0)),
            ],
        ),
        out_shape=[
            jax.ShapeDtypeStruct((rows, 128), BF16),
            jax.ShapeDtypeStruct((rows, columns), BF16),
            jax.ShapeDtypeStruct((rows, width), BF16),
            jax.ShapeDtypeStruct((rows, 128), F32),
            jax.ShapeDtypeStruct((rows, 128), F32),
        ],
        compiler_params=pltpu.CompilerParams(vmem_limit_bytes=48 * 2**20),
        cost_estimate=LIGHT,
        name="project",
    )(head, tokens, gain.reshape(1, width), k_weight, v_weight, q_weight, cos, sin)


def fwd_kernel(offsets, meta, q_ref, ka_ref, kb_ref, vt_ref, o_ref, lse_ref):
    half = q_ref.shape[0] // 2
    span = 2 * half
    group = min(GROUP, half)
    pairs = q_ref.shape[1] // 128
    for part, offset in enumerate(offsets):
        at = slice(part * half, part * half + half)
        queries = [q_ref[at, p * 128 : p * 128 + 128] for p in range(pairs)]
        chains = [(p, keys_ref) for p in range(pairs) for keys_ref in (ka_ref, kb_ref)]
        seen = meta[part]
        own = pl.multiple_of(meta[2 + seen] * span, span)
        heads = []
        for p, keys_ref in chains:
            tops, sums = [], []
            for first in range(0, half, group):
                count = offset + first + group
                rows = pl.ds(own, count)
                scores = lax.dot_general(
                    keys_ref[rows, :],
                    queries[p][first : first + group],
                    NT,
                    preferred_element_type=F32,
                )
                key_at = lax.broadcasted_iota(jnp.int32, scores.shape, 0)
                row_at = lax.broadcasted_iota(jnp.int32, scores.shape, 1) + (offset + first)
                scores = jnp.where(key_at <= row_at, scores, -1e30)
                top = jnp.max(scores, axis=0, keepdims=True)
                weights = jnp.exp(scores - top).astype(BF16)
                tops.append(top)
                sums.append(jnp.dot(vt_ref[:, rows], weights, preferred_element_type=F32))
            heads += [jnp.concatenate(tops, axis=1), jnp.concatenate(sums, axis=1)]

        def step(index, carry):
            rows = pl.ds(pl.multiple_of(meta[2 + index] * span, span), span)
            out = []
            for chain, (p, keys_ref) in enumerate(chains):
                top, total = carry[2 * chain : 2 * chain + 2]
                scores = lax.dot_general(
                    keys_ref[rows, :], queries[p], NT, preferred_element_type=F32
                )
                new_top = jnp.maximum(top, jnp.max(scores, axis=0, keepdims=True))
                weights = jnp.exp(scores - new_top).astype(BF16)
                total = total * jnp.exp(top - new_top) + jnp.dot(
                    vt_ref[:, rows], weights, preferred_element_type=F32
                )
                out += [new_top, total]
            return tuple(out)

        heads = lax.fori_loop(0, seen, step, tuple(heads))
        for p in range(pairs):
            top0, total0, top1, total1 = heads[4 * p : 4 * p + 4]
            norm0, norm1 = total0[HD : HD + 1], total1[HD : HD + 1]
            o_ref[at, p * 128 : p * 128 + 128] = (
                jnp.concatenate([total0[:HD] / norm0, total1[:HD] / norm1], axis=0).T.astype(BF16)
            )
            lse_ref[p, :, at] = jnp.concatenate(
                [top0 + jnp.log(norm0), top1 + jnp.log(norm1), jnp.zeros((6, half), F32)], axis=0
            )


def spread(kv_refs, ka_ref, kb_ref, va_ref, vb_ref, kt_ref, vt_ref):
    at = 0
    for kv_ref in kv_refs:
        rows = kv_ref.shape[0]
        block = min(512, rows)
        for first in range(0, rows, block):
            here = slice(at + first, at + first + block)
            pair = kv_ref[first : first + block, :].astype(F32)
            other = pltpu.roll(pair, HD, 1)
            left = lax.broadcasted_iota(jnp.int32, pair.shape, 1) < HD
            ka_ref[here, :] = jnp.where(left, pair, 0.0).astype(BF16)
            vb_ref[here, :] = jnp.where(left, 0.0, pair).astype(BF16)
            va_ref[here, :] = jnp.where(left, other, 0.0).astype(BF16)
            kb_ref[here, :] = jnp.where(left, 0.0, other).astype(BF16)
            turned = pair.T
            kt_ref[:, here] = turned[:HD].astype(BF16)
            ones = jnp.where(lax.broadcasted_iota(jnp.int32, (16, block), 0) == 0, 1.0, 0.0)
            vt_ref[:, here] = jnp.concatenate([turned[HD:], ones], axis=0).astype(BF16)
        at += rows


def attend_cost(rows, length, width):
    return pl.CostEstimate(
        flops=8 * rows * length * width, bytes_accessed=2**23, transcendentals=0
    )


def attend_first(meta, offsets, queries, kv_own, kv_other):
    rows, width = queries.shape
    pairs = width // 128
    together = 2 if pairs % 2 == 0 else 1
    length = 2 * kv_own.shape[0]

    def whole(shape):
        return pl.BlockSpec(shape, lambda p, m: (0, 0))

    def kernel(meta, q_ref, own, other, o_ref, lse_ref, ka, kb, va, vb, kt, vt):
        @pl.when(pl.program_id(0) == 0)
        def _():
            spread((own, other), ka, kb, va, vb, kt, vt)

        fwd_kernel(offsets, meta, q_ref, ka, kb, vt, o_ref, lse_ref)

    wide = (length, 128)
    forms = [wide, wide, wide, wide, (HD, length), (HD + 16, length)]
    return pl.pallas_call(
        kernel,
        grid_spec=pltpu.PrefetchScalarGridSpec(
            num_scalar_prefetch=1,
            grid=(pairs // together,),
            in_specs=[
                pl.BlockSpec((rows, 128 * together), lambda p, m: (0, p)),
                whole(kv_own.shape),
                whole(kv_other.shape),
            ],
            out_specs=[
                pl.BlockSpec((rows, 128 * together), lambda p, m: (0, p)),
                pl.BlockSpec((together, 8, rows), lambda p, m: (p, 0, 0)),
            ]
            + [whole(form) for form in forms],
        ),
        out_shape=[
            jax.ShapeDtypeStruct((rows, width), BF16),
            jax.ShapeDtypeStruct((pairs, 8, rows), F32),
        ]
        + [jax.ShapeDtypeStruct(form, BF16) for form in forms],
        compiler_params=pltpu.CompilerParams(vmem_limit_bytes=58 * 2**20),
        cost_estimate=attend_cost(rows, length, width),
        name="attend_first",
    )(meta, queries, kv_own, kv_other)


def attend(meta, offsets, queries, keys_a, keys_b, values_t):
    rows, width = queries.shape
    pairs = width // 128
    together = 2 if pairs % 2 == 0 else 1
    length = keys_a.shape[0]
    whole = pl.BlockSpec((length, 128), lambda p, m: (0, 0))

    def kernel(*refs):
        fwd_kernel(offsets, *refs)

    return pl.pallas_call(
        kernel,
        grid_spec=pltpu.PrefetchScalarGridSpec(
            num_scalar_prefetch=1,
            grid=(pairs // together,),
            in_specs=[
                pl.BlockSpec((rows, 128 * together), lambda p, m: (0, p)),
                whole,
                whole,
                pl.BlockSpec(values_t.shape, lambda p, m: (0, 0)),
            ],
            out_specs=[
                pl.BlockSpec((rows, 128 * together), lambda p, m: (0, p)),
                pl.BlockSpec((together, 8, rows), lambda p, m: (p, 0, 0)),
            ],
        ),
        out_shape=[
            jax.ShapeDtypeStruct((rows, width), BF16),
            jax.ShapeDtypeStruct((pairs, 8, rows), F32),
        ],
        compiler_params=pltpu.CompilerParams(vmem_limit_bytes=58 * 2**20),
        cost_estimate=attend_cost(rows, length, width),
        name="attend",
    )(meta, queries, keys_a, keys_b, values_t)


def bwd_kernel(
    offsets,
    meta,
    q_ref,
    o_ref,
    g_ref,
    lse_ref,
    ka_ref,
    kb_ref,
    va_ref,
    vb_ref,
    kt_ref,
    cos_ref,
    sin_ref,
    dq_ref,
    dk_ref,
    dv_ref,
):
    half = q_ref.shape[0] // 2
    span = 2 * half
    group = min(GROUP, half)

    for part, offset in enumerate(offsets):
        at = slice(part * half, part * half + half)
        queries, grads = q_ref[at, :], g_ref[at, :]
        left = lax.broadcasted_iota(jnp.int32, (half, 128), 1) < HD
        products = (grads.astype(F32) * o_ref[at, :].astype(F32)).T
        zero = jnp.zeros_like(queries)
        sides = []
        for side, (keys_ref, values_ref) in enumerate(((ka_ref, va_ref), (kb_ref, vb_ref))):
            mine = left if side == 0 else jnp.logical_not(left)
            delta = jnp.sum(products[side * HD : side * HD + HD], axis=0, keepdims=True)
            sides.append(
                (
                    keys_ref,
                    values_ref,
                    jnp.where(mine, queries, zero),
                    jnp.where(mine, grads, zero),
                    lse_ref[0, side : side + 1, at],
                    delta,
                )
            )

        def block(rows, first, count, masked):
            cut = slice(first, first + count)
            dqs = []
            dk_add = dv_add = None
            for keys_ref, values_ref, q_mine, g_mine, lse, delta in sides:
                scores = lax.dot_general(
                    keys_ref[rows, :], queries[cut], NT, preferred_element_type=F32
                )
                probs = jnp.exp(scores - lse[:, cut])
                if masked:
                    key_at = lax.broadcasted_iota(jnp.int32, scores.shape, 0)
                    row_at = lax.broadcasted_iota(jnp.int32, scores.shape, 1) + (offset + first)
                    probs = jnp.where(key_at <= row_at, probs, 0.0)
                grad_probs = lax.dot_general(
                    values_ref[rows, :], grads[cut], NT, preferred_element_type=F32
                )
                grad_scores = (probs * (grad_probs - delta[:, cut])).astype(BF16)
                dv_new = jnp.dot(probs.astype(BF16), g_mine[cut], preferred_element_type=F32)
                dk_new = jnp.dot(grad_scores, q_mine[cut], preferred_element_type=F32)
                dv_add = dv_new if dv_add is None else dv_add + dv_new
                dk_add = dk_new if dk_add is None else dk_add + dk_new
                dqs.append(jnp.dot(kt_ref[:, rows], grad_scores, preferred_element_type=F32))
            dv_ref[rows, :] += dv_add
            dk_ref[rows, :] += dk_add
            return jnp.concatenate(dqs, axis=0)

        own = pl.multiple_of(meta[2 + meta[part]] * span, span)
        start = jnp.concatenate(
            [
                block(pl.ds(own, offset + first + group), first, group, True)
                for first in range(0, half, group)
            ],
            axis=1,
        )

        def step(index, total):
            rows = pl.ds(pl.multiple_of(meta[2 + index] * span, span), span)
            return total + block(rows, 0, half, False)

        dq = lax.fori_loop(0, meta[part], step, start).T * (HD**-0.5)
        dq_ref[at, :] = turn(dq, cos_ref[at, :], -sin_ref[at, :]).astype(BF16)


def back_specs(queries, forms):
    rows, width = queries.shape
    pair = pl.BlockSpec((rows, 128), lambda p, m: (0, p))
    table = pl.BlockSpec((rows, 128), lambda p, m: (0, 0))
    specs = [pair, pair, pair, pl.BlockSpec((1, 8, rows), lambda p, m: (p, 0, 0))]
    specs += [pl.BlockSpec(form.shape, lambda p, m: (0, 0)) for form in forms]
    return pair, specs + [table, table]


def attend_back_first(meta, offsets, queries, outputs, grads, lse, forms, cos, sin):
    length = forms[0].shape[0]
    pair, specs = back_specs(queries, forms)
    whole = pl.BlockSpec((length, 128), lambda p, m: (0, 0))

    def kernel(*refs):
        dk_ref, dv_ref = refs[-2:]

        @pl.when(pl.program_id(0) == 0)
        def _():
            dk_ref[...] = jnp.zeros(dk_ref.shape, F32)
            dv_ref[...] = jnp.zeros(dv_ref.shape, F32)

        bwd_kernel(offsets, *refs)

    return pl.pallas_call(
        kernel,
        grid_spec=pltpu.PrefetchScalarGridSpec(
            num_scalar_prefetch=1,
            grid=(queries.shape[1] // 128,),
            in_specs=specs,
            out_specs=[pair, whole, whole],
        ),
        out_shape=[
            jax.ShapeDtypeStruct(queries.shape, BF16),
            jax.ShapeDtypeStruct((length, 128), F32),
            jax.ShapeDtypeStruct((length, 128), F32),
        ],
        compiler_params=pltpu.CompilerParams(vmem_limit_bytes=58 * 2**20),
        cost_estimate=LIGHT,
        name="attend_back_first",
    )(meta, queries, outputs, grads, lse, *forms, cos, sin)


def attend_back_last(
    meta, offsets, queries, outputs, grads, lse, forms, cos, sin, dk, dv, all_cos, all_sin
):
    length = forms[0].shape[0]
    near = length // 2
    pair, specs = back_specs(queries, forms)
    whole = pl.BlockSpec((length, 128), lambda p, m: (0, 0))
    half = pl.BlockSpec((near, 128), lambda p, m: (0, 0))

    def kernel(*refs):
        dk_in, dv_in, cos_ref, sin_ref, dq_ref, near_ref, far_ref, dk_ref, dv_ref = refs[-9:]

        @pl.when(pl.program_id(0) == 0)
        def _():
            dk_ref[...] = dk_in[...]
            dv_ref[...] = dv_in[...]

        bwd_kernel(offsets, *refs[:-9], dq_ref, dk_ref, dv_ref)

        @pl.when(pl.program_id(0) == pl.num_programs(0) - 1)
        def _():
            block = min(512, near)
            for first in range(0, length, block):
                here = slice(first, first + block)
                dk_block, dv_block = dk_ref[here, :], dv_ref[here, :]
                dk_block = dk_block + pltpu.roll(dk_block, HD, 1)
                dv_block = dv_block + pltpu.roll(dv_block, HD, 1)
                left = lax.broadcasted_iota(jnp.int32, dk_block.shape, 1) < HD
                both = jnp.where(
                    left, turn(dk_block, cos_ref[here, :], -sin_ref[here, :]), dv_block
                )
                if first < near:
                    near_ref[here, :] = both
                else:
                    far_ref[first - near : first - near + block, :] = both.astype(BF16)

    return pl.pallas_call(
        kernel,
        grid_spec=pltpu.PrefetchScalarGridSpec(
            num_scalar_prefetch=1,
            grid=(queries.shape[1] // 128,),
            in_specs=specs + [whole] * 4,
            out_specs=[pair, half, half],
            scratch_shapes=[pltpu.VMEM((length, 128), F32), pltpu.VMEM((length, 128), F32)],
        ),
        out_shape=[
            jax.ShapeDtypeStruct(queries.shape, BF16),
            jax.ShapeDtypeStruct((near, 128), F32),
            jax.ShapeDtypeStruct((near, 128), BF16),
        ],
        compiler_params=pltpu.CompilerParams(vmem_limit_bytes=60 * 2**20),
        cost_estimate=LIGHT,
        name="attend_back_last",
    )(meta, queries, outputs, grads, lse, *forms, cos, sin, dk, dv, all_cos, all_sin)


def feed_kernel(
    gathered_ref,
    tokens_ref,
    cotangent_ref,
    gain_ref,
    output_weight,
    gate_weight,
    up_weight,
    down_weight,
    *refs,
):
    middle_ref, normed_ref, hidden_ref, gates_ref, down_ref, grad_ref = refs[-6:]
    middle = tokens_ref[...].astype(F32)
    for source in range(gathered_ref.shape[0]):
        middle = middle + lax.dot_general(
            gathered_ref[source], output_weight[source], NT, preferred_element_type=F32
        )
    middle_ref[...] = middle
    inverse = lax.rsqrt(jnp.mean(middle * middle, axis=-1, keepdims=True) + EPSILON)
    normed = (middle * inverse * gain_ref[...]).astype(BF16)
    normed_ref[...] = normed
    gate = jnp.dot(normed, gate_weight[...], preferred_element_type=F32)
    up = jnp.dot(normed, up_weight[...], preferred_element_type=F32)
    grad_hidden = jnp.dot(cotangent_ref[...], down_weight[...], preferred_element_type=F32)
    sigmoid = jax.nn.sigmoid(gate)
    hidden = (gate * sigmoid * up).astype(BF16)
    hidden_ref[...] = hidden
    grad_gate = (grad_hidden * up * sigmoid * (1.0 + gate * (1.0 - sigmoid))).astype(BF16)
    grad_up = (grad_hidden * gate * sigmoid).astype(BF16)
    units = hidden.shape[1]
    gates_ref[:, :units] = grad_gate
    gates_ref[:, units:] = grad_up
    down_ref[...] = lax.dot_general(
        hidden, down_weight[...], NT, preferred_element_type=F32
    ).astype(BF16)
    grad_ref[...] = (
        lax.dot_general(grad_gate, gate_weight[...], NT, preferred_element_type=F32)
        + lax.dot_general(grad_up, up_weight[...], NT, preferred_element_type=F32)
    ).astype(BF16)


def feed_forward(c, gathered, tokens, cotangent, gain, output_weight, weights, earlier):
    rows, width = tokens.shape
    units = weights[0].shape[1]
    block = min(256, rows // 4)
    quarter = rows // 4 // block
    if c:
        place = lambda i: (i + quarter, 0)
    else:
        place = lambda i: (jnp.where(i < quarter, i, i + 2 * quarter), 0)
    once = pl.Buffered(1)

    def natural(columns):
        return pl.BlockSpec((block, columns), place)

    def whole(array):
        zeros = (0,) * array.ndim
        return pl.BlockSpec(array.shape, lambda i: zeros, pipeline_mode=once)

    shapes = [
        jax.ShapeDtypeStruct((rows, width), F32),
        jax.ShapeDtypeStruct((rows, width), BF16),
        jax.ShapeDtypeStruct((rows, units), BF16),
        jax.ShapeDtypeStruct((rows, 2 * units), BF16),
        jax.ShapeDtypeStruct((rows, width), BF16),
    ]
    gain = gain.reshape(1, width)
    return pl.pallas_call(
        feed_kernel,
        grid=(2 * quarter,),
        in_specs=[
            pl.BlockSpec((gathered.shape[0], block, gathered.shape[2]), lambda i: (0, i, 0)),
            natural(width),
            natural(width),
            whole(gain),
            whole(output_weight),
        ]
        + [whole(weight) for weight in weights]
        + [pl.BlockSpec(memory_space=pl.ANY) for _ in earlier],
        out_specs=[natural(shape.shape[1]) for shape in shapes]
        + [pl.BlockSpec((block, width), lambda i: (i, 0))],
        out_shape=shapes + [jax.ShapeDtypeStruct((rows // 2, width), BF16)],
        input_output_aliases={8 + k: k for k in range(len(earlier))},
        compiler_params=pltpu.CompilerParams(vmem_limit_bytes=60 * 2**20),
        cost_estimate=LIGHT,
        name="feed_forward",
    )(gathered, tokens, cotangent, gain, output_weight, *weights, *earlier)


def part_specs(shape):
    return [pl.BlockSpec(shape, lambda p, order: (0, 0, 0)) for _ in range(4)]


def join_kernel(order, rows_ref, *refs):
    out_ref = refs[4]
    for part, weight_ref in enumerate(refs[:4]):

        @pl.when(pl.program_id(0) == part)
        def _():
            result = None
            for source in range(rows_ref.shape[0]):
                term = lax.dot_general(
                    rows_ref[source], weight_ref[source], NT, preferred_element_type=F32
                )
                result = term if result is None else result + term
            out_ref[...] = result


def join(order, rows, parts):
    size, count, features = rows.shape
    columns = parts[0].shape[1]
    return pl.pallas_call(
        join_kernel,
        grid_spec=pltpu.PrefetchScalarGridSpec(
            num_scalar_prefetch=1,
            grid=(4,),
            in_specs=[pl.BlockSpec(rows.shape, lambda p, order: (0, 0, 0))]
            + part_specs(parts[0].shape),
            out_specs=pl.BlockSpec((count, columns), lambda p, order: (0, order[p])),
        ),
        out_shape=jax.ShapeDtypeStruct((count, 4 * columns), F32),
        compiler_params=pltpu.CompilerParams(vmem_limit_bytes=48 * 2**20),
        cost_estimate=LIGHT,
        name="join",
    )(order, rows, *parts)


def arrange_kernel(order, *refs):
    for part, weight_ref in enumerate(refs[:-1]):

        @pl.when(pl.program_id(0) == part)
        def _():
            refs[-1][...] = weight_ref[...].reshape(refs[-1].shape)


def arrange(order, parts, shape, block, place):
    zeros = (0,) * parts[0].ndim
    return pl.pallas_call(
        arrange_kernel,
        grid_spec=pltpu.PrefetchScalarGridSpec(
            num_scalar_prefetch=1,
            grid=(len(parts),),
            in_specs=[pl.BlockSpec(parts[0].shape, lambda p, order: zeros) for _ in parts],
            out_specs=pl.BlockSpec(block, lambda p, order: place(order[p])),
        ),
        out_shape=jax.ShapeDtypeStruct(shape, parts[0].dtype),
        compiler_params=pltpu.CompilerParams(vmem_limit_bytes=48 * 2**20),
        cost_estimate=LIGHT,
        name="arrange",
    )(order, *parts)


def quarter_row(row, c, half, span):
    if c:
        return half + row
    return row if row < half else row + span


def after(value, *earlier):
    return lax.optimization_barrier((value, earlier))[0]


def line_steps(size):
    return [
        (
            [(i, i + 1) for i in range(step - 1, size - 1)],
            [(i, i - 1) for i in range(1, size - step + 1)],
        )
        for step in range(1, size)
    ]


class Gather:
    def __init__(self, piece):
        self.piece = piece
        self.rights, self.lefts = [piece], [piece]
        self.hops = line_steps(lax.axis_size("tensor"))

    def step(self):
        done = len(self.rights) - 1
        if done < len(self.hops):
            to_right, to_left = self.hops[done]
            self.rights.append(lax.ppermute(self.rights[-1], "tensor", to_right))
            self.lefts.append(lax.ppermute(self.lefts[-1], "tensor", to_left))
        return self.rights[-1], self.lefts[-1]

    def held(self, pair):
        self.rights[-1], self.lefts[-1] = pair

    def place_hop(self, place, target, hop):
        size = lax.axis_size("tensor")
        me = lax.axis_index("tensor")
        if hop == 0:
            return place(target, self.piece, me)
        right, left = self.rights[hop], self.lefts[hop]
        from_left, from_right = me >= hop, me + hop < size
        if 2 * hop >= size:
            piece = jnp.where(from_left, right, jnp.where(from_right, left, self.piece))
            source = jnp.where(from_left, me - hop, jnp.where(from_right, me + hop, me))
            return place(target, piece, source)
        target = place(
            target, jnp.where(from_left, right, self.piece), jnp.where(from_left, me - hop, me)
        )
        return place(
            target, jnp.where(from_right, left, self.piece), jnp.where(from_right, me + hop, me)
        )

    def whole(self):
        size = lax.axis_size("tensor")
        me = lax.axis_index("tensor")
        while len(self.rights) <= len(self.hops):
            self.step()
        parts, order = [self.piece], [me]
        for hop in range(1, size):
            for came, source in ((self.rights[hop], me - hop), (self.lefts[hop], me + hop)):
                parts.append(came)
                order.append(jnp.where((source >= 0) & (source < size), source, me))
        parts, order = parts[::-1], order[::-1]
        shape = self.piece.shape
        return arrange(
            jnp.stack(order).astype(jnp.int32),
            parts,
            (size, *shape),
            (1, *shape),
            lambda i: (i,) + (0,) * len(shape),
        )


def send_blocks(pick, across=False):
    size = lax.axis_size("tensor")
    me = lax.axis_index("tensor")
    arrived = []
    for shift in range(size):
        block = pick(lax.rem(me + shift, size))
        if across:
            block = lax.ppermute(
                block,
                ("ctx", "tensor"),
                [
                    (c * size + i, (1 - c) * size + (i + shift) % size)
                    for c in range(2)
                    for i in range(size)
                ],
            )
        elif shift:
            block = lax.ppermute(block, "tensor", [(i, (i + shift) % size) for i in range(size)])
        arrived.append(block)
    return tuple(arrived)


def stack_blocks(arrived):
    size = len(arrived)
    me = lax.axis_index("tensor")
    out = jnp.zeros((size, *arrived[0].shape), arrived[0].dtype)
    for shift, block in enumerate(arrived):
        out = lax.dynamic_update_index_in_dim(out, block, lax.rem(me - shift + size, size), 0)
    return out


def hold(*values):
    return lax.optimization_barrier(values)


def rows_part(weight, index, count):
    rows = weight.shape[0] // count
    return lax.dynamic_slice_in_dim(weight, index * rows, rows, 0)


def dot(a, b):
    return jnp.dot(a, b, preferred_element_type=F32)


def dot_t(a, b):
    return jnp.einsum("rf,df->rd", a, b, preferred_element_type=F32)


def t_dot(a, b):
    return jnp.einsum("rd,rf->df", a, b, preferred_element_type=F32)


def body(
    tokens,
    cotangent,
    span_order,
    norm_attn,
    w_query,
    w_key,
    w_value,
    w_output,
    norm_mlp,
    w_gate,
    w_up,
    w_down,
):
    tok_rows, width = tokens.shape
    groups = lax.axis_size("tensor")
    member = lax.axis_index("tensor")
    n_ctx = lax.axis_size("ctx")
    assert n_ctx == 2
    ctx_index = lax.axis_index("ctx")
    features = w_query.shape[1]
    kv_count = w_key.shape[1] // HD
    kv_pick = np.arange(groups) * kv_count // groups
    head = (member * kv_count // groups).astype(jnp.int32).reshape(1)
    span = tok_rows // 2
    half = span // 2
    share = span // groups
    over = [(0, 1), (1, 0)]
    chunks = range(2)

    def chunk(array, c):
        if c:
            return array[half : half + span]
        return jnp.concatenate([array[:half], array[half + span :]], axis=0)

    def natural(first, second):
        return jnp.concatenate([first[:half], second, first[half:]], axis=0)

    order = jnp.roll(span_order[0], -2 * ctx_index)
    places = jnp.arange(4, dtype=jnp.int32)
    slot_of = jnp.sum(
        jnp.where(order[None, :] == places[:, None], places[None, :], 0), axis=1, dtype=jnp.int32
    )
    metas = [jnp.concatenate([order[2 * c : 2 * c + 2], slot_of]) for c in chunks]
    offsets = [(0, half), (half, 0)]

    positions = (order[:, None] * span + jnp.arange(span, dtype=jnp.int32)[None, :]).reshape(-1)
    frequency = 10000.0 ** (-jnp.arange(HD // 2, dtype=F32) / (HD // 2))

    def table(positions):
        angles = frequency[:, None] * positions.astype(F32)[None, :]
        cos_part, sin_part = hold(jnp.cos(angles), jnp.sin(angles))
        cos_part, sin_part = cos_part.T, sin_part.T
        return (
            jnp.concatenate([cos_part] * 4, axis=1),
            jnp.concatenate([-sin_part, sin_part] * 2, axis=1),
        )


    upper = lax.axis_index("dp") % 2
    beside = [(i, i ^ 1) for i in range(lax.axis_size("dp"))]
    quarters = jnp.stack(
        [
            2 * upper + ctx_index,
            2 * upper + 1 - ctx_index,
            2 - 2 * upper + ctx_index,
            3 - 2 * upper - ctx_index,
        ]
    ).astype(jnp.int32)

    output_gather = Gather(rows_part(w_output, upper, 2))
    hop = output_gather.step()
    angles = frequency[:, None] * positions[:tok_rows].astype(F32)[None, :]
    cos_part, sin_part = hold(jnp.cos(angles), jnp.sin(angles))
    kv_own, queries, normed, cos_near, sin_near = project(
        head, tokens, norm_attn, w_key, w_value, w_query, cos_part, sin_part
    )
    kv_own, queries, normed, hop, quarters = hold(kv_own, queries, normed, hop, quarters)
    output_gather.held(hop)
    kv_other = lax.ppermute(kv_own, "ctx", over)
    hop = output_gather.step()
    kv_own, kv_other, sent, kept, normed, hop = hold(
        kv_own, kv_other, chunk(queries, 1), chunk(queries, 0), normed, hop
    )
    output_gather.held(hop)
    length = 2 * tok_rows

    foreign = lax.ppermute(sent, "ctx", over)
    hop = output_gather.step()
    first, first_log, *forms = attend_first(metas[0], offsets[0], kept, kv_own, kv_other)
    first, first_log, foreign, forms, hop = hold(first, first_log, foreign, forms, hop)
    output_gather.held(hop)
    *forms, values_t = forms
    first_whole = lax.all_gather(first, "tensor", axis=0, tiled=False)

    output_near = output_gather.whole()
    output_far = lax.ppermute(output_near, "dp", beside)
    second, second_log = attend(metas[1], offsets[1], foreign, forms[0], forms[1], values_t)
    second, second_log, output_near, output_far = hold(
        second, second_log, output_near, output_far
    )

    cos_far, sin_far = table(after(positions[tok_rows:], second))
    cos_pair = jnp.concatenate([cos_near, cos_far], axis=0)
    sin_pair = jnp.concatenate([sin_near, sin_far], axis=0)
    tables = [(chunk(cos_near, 0), chunk(sin_near, 0)), (chunk(cos_far, 1), chunk(sin_far, 1))]
    second_home = lax.ppermute(second, "ctx", over)
    half_rows = output_near.shape[1]
    output_whole = arrange(
        jnp.stack([upper, 1 - upper]).astype(jnp.int32),
        [output_near, output_far],
        (groups, 2 * half_rows, features),
        output_near.shape,
        lambda i: (0, i, 0),
    )
    second_home, output_whole, tables, cos_pair, sin_pair = hold(
        second_home, output_whole, tables, cos_pair, sin_pair
    )
    second_whole = lax.all_gather(second_home, "tensor", axis=0, tiled=False)
    queries = [kept, foreign]
    attention = [first, second]
    log_totals = [first_log, second_log]

    row_of = [
        jnp.asarray([quarter_row(i * share, c, half, span) for i in range(groups)], jnp.int32)
        for c in chunks
    ]

    def own_rows(array, c):
        return lax.dynamic_slice_in_dim(array, row_of[c][member], share, 0)

    def to_attention(c, middle, grad_share):
        middle = own_rows(middle, c)
        inverse_two = lax.rsqrt(jnp.mean(middle * middle, axis=-1, keepdims=True) + EPSILON)
        grad_normed_mlp = grad_share.astype(F32)
        gain = jnp.sum(grad_normed_mlp * middle * inverse_two, axis=0)
        scaled_two = grad_normed_mlp * norm_mlp
        grad_middle = (
            own_rows(cotangent, c).astype(F32)
            + inverse_two * scaled_two
            - middle * inverse_two**3 * jnp.mean(scaled_two * middle, axis=-1, keepdims=True)
        )
        grad_low = grad_middle.astype(BF16)
        blocks = jnp.einsum(
            "rd,tdq->trq", grad_low, output_whole, preferred_element_type=F32
        ).astype(BF16)
        return gain, grad_middle, grad_low, blocks

    def block_of(blocks):
        return lambda j: lax.dynamic_index_in_dim(blocks, j, 0, keepdims=False)

    def rows_of(array):
        return lambda j: lax.dynamic_slice_in_dim(array, j * share, share, 0)

    def line_sum(array):
        return lax.psum_scatter(array, "tensor", scatter_dimension=0, tiled=True)

    def plane_sum(gradient):
        return lax.psum_scatter(
            gradient.astype(BF16), ("dp", "ctx"), scatter_dimension=0, tiled=True
        )

    query_gather = Gather(rows_part(after(w_query, first_whole), 2 * upper + ctx_index, 4))
    hop = query_gather.step()
    weights = (w_gate, w_up, w_down)
    fixed = (tokens, cotangent, norm_mlp, output_whole, weights)
    *fed, grad_first = feed_forward(0, first_whole, *fixed, ())
    fed, grad_first, second_whole, hop = hold(fed, grad_first, second_whole, hop)
    query_gather.held(hop)

    share_first = line_sum(grad_first)
    hop = query_gather.step()
    *fed, grad_second = feed_forward(1, second_whole, *fixed, fed)
    fed, grad_second, hop = hold(fed, grad_second, hop)
    query_gather.held(hop)
    middle, normed_mlp, hidden, gates, mlp_part = fed

    share_second = line_sum(grad_second)
    hop = query_gather.step()
    w_gates = t_dot(normed_mlp, gates).astype(BF16)
    w_gates, hop, share_first = hold(w_gates, hop, share_first)
    query_gather.held(hop)

    mlp_share = line_sum(after(mlp_part, w_gates))

    gain_first, middle_first, low_first, blocks = to_attention(0, middle, share_first)
    query_part = query_gather.whole()
    gain_first, middle_first, low_first, blocks, hidden, query_part = hold(
        gain_first, middle_first, low_first, blocks, hidden, query_part
    )

    came_first = send_blocks(block_of(blocks))
    query_over = lax.ppermute(query_part, "ctx", over)
    w_downs = t_dot(cotangent, hidden).astype(BF16)
    n_part = tok_rows // groups
    middle_own = lax.dynamic_slice_in_dim(middle, member * n_part, n_part, 0)
    came_first, middle_own, query_part, query_over, w_downs = hold(
        came_first, middle_own, query_part, query_over, w_downs
    )

    query_near = (query_part, query_over)
    query_far = tuple(lax.ppermute(part, "dp", beside) for part in query_near)
    grads_first = stack_blocks(came_first).reshape(span, features)
    query_near, query_far, grads_first, share_second = hold(
        query_near, query_far, grads_first, share_second
    )

    gain_second, middle_second, low_second, blocks = to_attention(1, middle, share_second)
    gain_second, middle_second, low_second, blocks = hold(
        gain_second, middle_second, low_second, blocks
    )

    def back_arguments(c, grads):
        return metas[c], offsets[c], queries[c], attention[c], grads, log_totals[c], forms, *tables[c]

    came_second = send_blocks(block_of(blocks), across=True)
    dq_first, dk, dv = attend_back_first(*back_arguments(0, grads_first))
    dq_first, dk, dv, came_second = hold(dq_first, dk, dv, came_second)

    rows_first = send_blocks(rows_of(dq_first))
    grads_second = stack_blocks(came_second).reshape(span, features)
    dq_second, kv_near, kv_far = attend_back_last(
        *back_arguments(1, grads_second), dk, dv, cos_pair, sin_pair
    )
    dq_second, kv_near, kv_far, rows_first = hold(dq_second, kv_near, kv_far, rows_first)

    def kv_share_of(array, j):
        return [lax.dynamic_slice_in_dim(array, row_of[c][j], share, 0) for c in chunks]

    kv_low = kv_near.astype(BF16)
    near_blocks = send_blocks(lambda j: jnp.concatenate(kv_share_of(kv_low, j), axis=1))
    far_blocks = send_blocks(
        lambda j: jnp.concatenate([rows_of(dq_second)(j), *kv_share_of(kv_far, j)], axis=1),
        across=True,
    )
    query_parts = query_near + query_far
    first_part = join(quarters, stack_blocks(rows_first), query_parts)
    attention_rows = jnp.concatenate(
        [
            lax.dynamic_slice_in_dim(whole, member * share, share, 1)
            for whole in after((first_whole, second_whole), dq_second)
        ],
        axis=1,
    )
    attention_rows = jnp.swapaxes(attention_rows, 0, 1).reshape(2 * share, groups * features)
    w_outs = t_dot(jnp.concatenate([low_first, low_second], axis=0), attention_rows).astype(BF16)
    near_blocks, far_blocks, first_part, w_outs = hold(near_blocks, far_blocks, first_part, w_outs)
    far_blocks = stack_blocks(far_blocks)
    kv_blocks = (
        stack_blocks(near_blocks).astype(F32) + far_blocks[:, :, features:].astype(F32)
    ).astype(BF16)
    kv_blocks = jnp.concatenate([kv_blocks[:, :, : 2 * HD], kv_blocks[:, :, 2 * HD :]], axis=1)
    second_part = join(quarters, far_blocks[:, :, :features], query_parts)
    kv_whole = jnp.stack(
        [
            jnp.concatenate(
                [w_key[:, h * HD : (h + 1) * HD], w_value[:, h * HD : (h + 1) * HD]], axis=1
            )
            for h in kv_pick
        ]
    )

    grad_normed = jnp.concatenate([first_part, second_part], axis=0) + jnp.einsum(
        "trq,tdq->rd", kv_blocks, kv_whole, preferred_element_type=F32
    )
    inputs_own = jnp.concatenate([own_rows(tokens, c) for c in chunks], axis=0).astype(F32)
    inverse_own = lax.rsqrt(jnp.mean(inputs_own * inputs_own, axis=-1, keepdims=True) + EPSILON)
    attn_gain = jnp.sum(grad_normed * inputs_own * inverse_own, axis=0)
    scaled_one = grad_normed * norm_attn
    grad_inputs = (
        jnp.concatenate([middle_first, middle_second], axis=0)
        + inverse_own * scaled_one
        - inputs_own * inverse_own**3 * jnp.mean(scaled_one * inputs_own, axis=-1, keepdims=True)
    ).astype(BF16)

    def put_rows(target, piece, source):
        for c in chunks:
            target = lax.dynamic_update_slice_in_dim(
                target, piece[c * share : (c + 1) * share], row_of[c][source], 0
            )
        return target

    gains = jnp.stack([attn_gain, gain_first + gain_second], axis=1).astype(BF16)
    mixed_share = (middle_own + mlp_share.astype(F32)).astype(BF16)
    grad_inputs, gains, dq_second, kv_far, kv_near, w_gates, mixed_share = hold(
        grad_inputs, gains, dq_second, kv_far, kv_near, w_gates, mixed_share
    )
    gate_up_grad = plane_sum(w_gates)

    def put_share(target, piece, source):
        return lax.dynamic_update_slice_in_dim(target, piece, source * n_part, 0)

    tokens_gather, mixed_gather = Gather(grad_inputs), Gather(mixed_share)
    tokens_grad = jnp.zeros((tok_rows, width), BF16)
    mixed = jnp.zeros((tok_rows, width), BF16)
    hop, mixed_hop = tokens_gather.step(), mixed_gather.step()
    home = lax.ppermute(
        jnp.concatenate([dq_second, kv_far[:span], kv_far[span:]], axis=1), "ctx", over
    )
    dq_home, kv_sent = home[:, :features], home[:, features:]
    kv_sent = jnp.concatenate([kv_sent[:, : 2 * HD], kv_sent[:, 2 * HD :]], axis=0)
    grad_kv_raw = (kv_near + kv_sent.astype(F32)).astype(BF16)
    query_kv = t_dot(
        normed, jnp.concatenate([natural(dq_first, dq_home), grad_kv_raw], axis=1)
    ).astype(BF16)
    gains = jnp.pad(gains, ((0, 0), (0, 126)))
    rest = jnp.concatenate([w_downs, w_outs, query_kv, gains], axis=1)
    tokens_grad = tokens_gather.place_hop(put_rows, tokens_grad, 0)
    mixed = mixed_gather.place_hop(put_share, mixed, 0)
    hop, mixed_hop, rest, tokens_grad, mixed = hold(hop, mixed_hop, rest, tokens_grad, mixed)
    tokens_gather.held(hop)
    mixed_gather.held(mixed_hop)
    rest = plane_sum(rest)

    hop, mixed_hop = tokens_gather.step(), mixed_gather.step()
    hop, mixed_hop = hold(hop, mixed_hop)
    tokens_gather.held(hop)
    mixed_gather.held(mixed_hop)

    hop = tokens_gather.step()
    for count in (1, 2):
        tokens_grad = tokens_gather.place_hop(put_rows, tokens_grad, count)
        mixed = mixed_gather.place_hop(put_share, mixed, count)
    hop, tokens_grad, mixed = hold(hop, tokens_grad, mixed)
    tokens_gather.held(hop)

    mixed_hop = mixed_gather.step()
    if groups > 3:
        tokens_grad = tokens_gather.place_hop(put_rows, tokens_grad, 3)
    hidden_units = w_down.shape[1]
    rest = after(rest, hop)
    down_grad = rest[:, :hidden_units]
    output_plane = rest[:, hidden_units : hidden_units + groups * features]
    query_plane = rest[:, hidden_units + groups * features :]
    query_grad, small = query_plane[:, :features].astype(F32), query_plane[:, features:]
    blocks = send_blocks(
        lambda j: jnp.concatenate(
            [lax.dynamic_slice_in_dim(output_plane, j * features, features, 1), small], axis=1
        )
    )
    mixed_hop, tokens_grad, blocks = hold(mixed_hop, tokens_grad, blocks)
    mixed_gather.held(mixed_hop)
    blocks = stack_blocks(blocks).astype(F32)
    output_grad = jnp.sum(blocks[:, :, :features], axis=0)
    kv_share = blocks.shape[1] // groups
    kv_blocks = lax.dynamic_slice_in_dim(
        blocks[:, :, features : features + 2 * HD], member * kv_share, kv_share, 1
    )
    gains = jnp.sum(blocks[:, :, features + 2 * HD : features + 2 * HD + 2], axis=0).T
    for count in range(3, groups):
        mixed = mixed_gather.place_hop(put_share, mixed, count)
        if count + 1 < groups:
            tokens_gather.step()
            mixed_gather.step()
            tokens_grad = tokens_gather.place_hop(put_rows, tokens_grad, count + 1)

    key_heads, value_heads = [], []
    for h in range(kv_count):
        total = jnp.zeros((kv_share, 2 * HD), F32)
        for g in range(groups):
            if kv_pick[g] == h:
                total = total + kv_blocks[g]
        key_heads.append(total[:, :HD])
        value_heads.append(total[:, HD:])
    key_grad = jnp.concatenate(key_heads, axis=1)
    value_grad = jnp.concatenate(value_heads, axis=1)

    return (
        mixed,
        tokens_grad,
        gains[0],
        query_grad,
        key_grad,
        value_grad,
        output_grad,
        gains[1],
        gate_up_grad[:, :hidden_units].astype(F32),
        gate_up_grad[:, hidden_units:].astype(F32),
        down_grad.astype(F32),
    )


def solution(mesh):
    placed = (
        P(("dp", "ctx"), None),
        P(("dp", "ctx"), None),
        P("dp", None),
        P(),
        P(None, "tensor"),
        P(),
        P(),
        P(None, "tensor"),
        P(),
        P(None, "tensor"),
        P(None, "tensor"),
        P(None, "tensor"),
    )
    return jax.shard_map(
        body,
        mesh=mesh,
        in_specs=placed,
        out_specs=(
            P(("dp", "ctx"), None),
            P(("dp", "ctx"), None),
            P(("dp", "ctx")),
            P(("dp", "ctx"), "tensor"),
            P(("dp", "ctx", "tensor"), None),
            P(("dp", "ctx", "tensor"), None),
            P(("dp", "ctx"), "tensor"),
            P(("dp", "ctx")),
            P(("dp", "ctx"), "tensor"),
            P(("dp", "ctx"), "tensor"),
            P(("dp", "ctx"), "tensor"),
        ),
        check_vma=False,
    )
```
